32 devices in a mesh: src: 2 (over y), tx: 2 (over x), ty: 8 (over z, core).
Axes of the slice: x: 2, y: 2, z: 4, core: 2. Of those that a mesh axis runs over, the one named last changes fastest.
Arguments:
- orders: float32 [8, 2, 512, 512], P('src', None, 'tx', 'ty'), may hold values from -0.00390625 to 0.00390625
- offsets: int32 [8, 2], P('src'), may hold values from -8 to 7
- material: int32 [6, 512, 1024], P(None, 'tx', 'ty'), may hold values from 0 to 3
- e_field: float32 [3, 6, 512, 1024], P(None, None, 'tx', 'ty'), may hold values from -6 to 6
- h_field: float32 [3, 6, 512, 1024], P(None, None, 'tx', 'ty'), may hold values from -6 to 6
Outputs:
- e_out: float32 [3, 6, 512, 1024], P(None, None, 'tx', 'ty')
- h_out: float32 [3, 6, 512, 1024], P(None, None, 'tx', 'ty')
The draws below stay inside these ranges and needn't reach their ends.
All inputs are finite; a program needn't handle non-finite values.
Results may differ from the reference program's by a relative error of at most 0.0003.
Values sent between devices are 32-bit elements; how exact they have to be, the bound alone decides.
No kernel may reach another device: no remote copies, remote signals or barrier semaphores. Data moves between devices by JAX's collectives and lax.ppermute only.
A program may use at most 128 MiB of HBM per device.

```python
import math
import jax
import jax.numpy as jnp
from jax import lax

NZ = 6
MX = 512
MY = 512
STEPS = 4
ZINJ = 1
NX = 512
NY = 1024
P_ALL = 8


def place_ends(entries, own_key, least, high):
    shape = entries.shape
    place = [jax.random.randint(jax.random.fold_in(own_key, axis), (), 0, shape[axis]) for axis in range(len(shape))]
    entries = entries.at[tuple(place)].set(least)
    longest = shape.index(max(shape))
    place[longest] = (place[longest] + 1) % shape[longest]
    return entries.at[tuple(place)].set(high)


def block_levels(own_key, shape, split, least, top_value):
    def one(position, shards_of):
        heights = jax.random.uniform(jax.random.fold_in(jax.random.fold_in(own_key, 6), position), (shards_of,), jnp.float32, least / len(split), top_value / len(split))
        return jnp.repeat(jnp.exp(heights), shape[position] // shards_of).reshape((-1,) + (1,) * (len(shape) - position - 1))

    factor_of = one(*split[0])
    for cut in split[1:]:
        factor_of = factor_of * one(*cut)
    return factor_of


def centred(stream_key, extent, scale, bound, cuts=(), kind=jnp.bfloat16):
    factor_of = block_levels(stream_key, extent, cuts, -0.22, 0.18) if cuts else 1.0
    result = jax.random.normal(stream_key, extent, jnp.float32) * scale * factor_of
    return jnp.minimum(jnp.maximum(result, -bound), bound).astype(kind)


def setup_inputs(seed: int = 0) -> dict:
    arg_keys = jax.random.split(jax.random.key(seed), 6)
    orders = centred(arg_keys[0], (P_ALL, 2, MX, MY), (MX * MY * P_ALL) ** -0.5, 0.00390625, ((0, 2), (2, 2), (3, 8)), jnp.float32)
    offsets = place_ends(jax.random.randint(arg_keys[1], (P_ALL, 2), -8, 8), jax.random.fold_in(arg_keys[1], 1), -8, 7).astype(jnp.int32)
    material = place_ends(jax.random.randint(arg_keys[2], (NZ, NX, NY), 0, 4), jax.random.fold_in(arg_keys[2], 1), 0, 3).astype(jnp.int32)
    e_field = centred(arg_keys[3], (3, NZ, NX, NY), 1.0, 6.0, ((2, 2), (3, 8)), jnp.float32)
    h_field = centred(arg_keys[4], (3, NZ, NX, NY), 1.0, 6.0, ((2, 2), (3, 8)), jnp.float32)
    return dict(orders=orders, offsets=offsets, material=material, e_field=e_field, h_field=h_field)


COURANT = 0.5
OMEGA = 0.7
PERMITTIVITY = (1.0, 2.6, 11.9, 2.1)
HIGH = lax.Precision.HIGHEST


def phase_tables(freqs, positions, length):
    product = jnp.mod(freqs[:, :, None] * positions[None, None, :], length)
    angle = product.astype(jnp.float32) * (2.0 * math.pi / length)
    return jnp.cos(angle), jnp.sin(angle)


def cell_coefficient(material):
    total = jnp.zeros(material.shape, jnp.float32)
    for number in range(len(PERMITTIVITY)):
        total = total + jnp.where(material == number, COURANT / PERMITTIVITY[number], 0.0)
    return total


def ahead(field, axis):
    if axis == 0:
        zero = jnp.zeros((1,) + field.shape[1:], jnp.float32)
        return jnp.concatenate([field[1:], zero], 0) - field
    return jnp.roll(field, -1, axis) - field


def behind(field, axis):
    if axis == 0:
        zero = jnp.zeros((1,) + field.shape[1:], jnp.float32)
        return field - jnp.concatenate([zero, field[:-1]], 0)
    return field - jnp.roll(field, 1, axis)


def reference(orders, offsets, material, e_field, h_field):
    x_pos = jnp.arange(NX, dtype=jnp.int32)
    y_pos = jnp.arange(NY, dtype=jnp.int32)
    kx_base = jnp.arange(MX, dtype=jnp.int32) - MX // 2
    ky_base = jnp.arange(MY, dtype=jnp.int32) - MY // 2

    def one_point(total, item):
        amp, shift = item
        cos_y, sin_y = phase_tables((ky_base + shift[1])[None, :], y_pos, NY)
        cos_x, sin_x = phase_tables((kx_base + shift[0])[None, :], x_pos, NX)
        cos_y, sin_y = cos_y[0], sin_y[0]
        cos_x, sin_x = cos_x[0].T, sin_x[0].T
        inner_re = jnp.dot(amp[0], cos_y, precision=HIGH) - jnp.dot(amp[1], sin_y, precision=HIGH)
        inner_im = jnp.dot(amp[0], sin_y, precision=HIGH) + jnp.dot(amp[1], cos_y, precision=HIGH)
        plane_re = jnp.dot(cos_x, inner_re, precision=HIGH) - jnp.dot(sin_x, inner_im, precision=HIGH)
        plane_im = jnp.dot(cos_x, inner_im, precision=HIGH) + jnp.dot(sin_x, inner_re, precision=HIGH)
        return total + jnp.stack([plane_re, plane_im]), None

    plane, _ = lax.scan(one_point, jnp.zeros((2, NX, NY), jnp.float32), (orders, offsets))
    coefficient = cell_coefficient(material)
    e_x, e_y, e_z = e_field[0], e_field[1], e_field[2]
    h_x, h_y, h_z = h_field[0], h_field[1], h_field[2]
    for step in range(STEPS):
        h_x = h_x - COURANT * (ahead(e_z, 2) - ahead(e_y, 0))
        h_y = h_y - COURANT * (ahead(e_x, 0) - ahead(e_z, 1))
        h_z = h_z - COURANT * (ahead(e_y, 1) - ahead(e_x, 2))
        e_x = e_x + coefficient * (behind(h_z, 2) - behind(h_y, 0))
        e_y = e_y + coefficient * (behind(h_x, 0) - behind(h_z, 1))
        e_z = e_z + coefficient * (behind(h_y, 1) - behind(h_x, 2))
        cosine = math.cos(OMEGA * (step + 1))
        sine = math.sin(OMEGA * (step + 1))
        e_x = e_x.at[ZINJ].add(COURANT * (cosine * plane[0] - sine * plane[1]))
        e_y = e_y.at[ZINJ].add(COURANT * (sine * plane[0] + cosine * plane[1]))
    return jnp.stack([e_x, e_y, e_z]), jnp.stack([h_x, h_y, h_z])
```

```python
import functools
import math

import jax
import jax.numpy as jnp
import ml_dtypes
import numpy as np
from jax import lax
from jax.experimental import pallas as pl
from jax.experimental.pallas import tpu as pltpu
from jax.sharding import PartitionSpec as P

MX = 512
MY = 512
STEPS = 4
ZINJ = 1
LAYERS = 6

COURANT = 0.5
OMEGA = 0.7
PERMITTIVITY = (1.0, 2.6, 11.9, 2.1)

REACH = 8
SPAN = 2 * REACH
PAD = 8
HALO = 4
BASE = 16
SLOT = 32
WIDE = 8
LANES = 128
VMEM_LIMIT = 40 * 1024 * 1024


def split_bf16(table):
    high = table.astype(ml_dtypes.bfloat16)
    low = (table - high.astype(np.float64)).astype(ml_dtypes.bfloat16)
    return high, low


@functools.lru_cache(maxsize=None)
def x_tables(n_tx, rows_kx, cells_x):
    window = rows_kx + SPAN
    rows = cells_x + 2 * PAD
    full = cells_x * n_tx
    table = np.zeros((n_tx, n_tx, rows, 2 * window))
    for own in range(n_tx):
        freq = own * rows_kx - MX // 2 - REACH + np.arange(window)
        for distance in range(n_tx):
            tile = (own + distance) % n_tx
            x = tile * cells_x - PAD + np.arange(rows)
            angle = np.mod(x[:, None] * freq[None, :], full) * (2.0 * math.pi / full)
            table[own, distance] = np.concatenate([np.cos(angle), np.sin(angle)], 1)
    return split_bf16(table)


@functools.lru_cache(maxsize=None)
def y_tables(n_ty, cols_ky, cells_y):
    full = cells_y * n_ty
    window = cols_ky + SPAN
    edge = np.concatenate([np.arange(-HALO, 0), cells_y + np.arange(HALO)])
    y = np.concatenate([np.arange(cells_y), edge])
    table = np.zeros((n_ty, LANES + 2 * SPAN, 2 * cells_y + LANES))
    for block in range(n_ty):
        freq = block * cols_ky - MY // 2 - REACH + np.arange(window)
        angle = np.mod(freq[:, None] * y[None, :], full) * (2.0 * math.pi / full)
        cos, sin = np.cos(angle), np.sin(angle)

        def placed(re_cols, im_cols):
            out = np.zeros((window, 2 * cells_y + LANES))
            out[:, :cells_y] = re_cols[:, :cells_y]
            out[:, cells_y : 2 * cells_y] = im_cols[:, :cells_y]
            out[:, 2 * cells_y : 2 * cells_y + 2 * HALO] = re_cols[:, cells_y:]
            out[:, 2 * cells_y + 2 * HALO : 2 * cells_y + 4 * HALO] = im_cols[:, cells_y:]
            return out

        from_re = placed(cos, sin)
        from_im = placed(-sin, cos)
        table[block, :cols_ky] = from_re[:cols_ky]
        table[block, cols_ky : 2 * cols_ky] = from_im[:cols_ky]
        table[block, LANES : LANES + SPAN] = from_re[cols_ky:]
        table[block, LANES + SPAN :] = from_im[cols_ky:]
    return split_bf16(table)


@functools.lru_cache(maxsize=None)
def y_phases(n_ty, cols_ky, cells_y):
    full = cells_y * n_ty
    out = np.zeros((n_ty, n_ty, 8, LANES), np.float32)
    for own in range(n_ty):
        for block in range(n_ty):
            freq = block * cols_ky - MY // 2 - REACH + np.arange(cols_ky + SPAN)
            angle = np.mod(freq * own * cells_y, full) * (2.0 * math.pi / full)
            cos, sin = np.cos(angle), np.sin(angle)
            out[own, block, 0, :cols_ky] = cos[:cols_ky]
            out[own, block, 0, cols_ky : 2 * cols_ky] = cos[:cols_ky]
            out[own, block, 1, :cols_ky] = -sin[:cols_ky]
            out[own, block, 1, cols_ky : 2 * cols_ky] = sin[:cols_ky]
            for group in range(LANES // (2 * SPAN)):
                at = group * 2 * SPAN
                out[own, block, 2, at : at + SPAN] = cos[cols_ky:]
                out[own, block, 2, at + SPAN : at + 2 * SPAN] = cos[cols_ky:]
                out[own, block, 3, at : at + SPAN] = -sin[cols_ky:]
                out[own, block, 3, at + SPAN : at + 2 * SPAN] = sin[cols_ky:]
    return out


def lane_of(shape):
    return lax.broadcasted_iota(jnp.int32, shape, len(shape) - 1)


def rolled(value, shift):
    shift = shift % LANES
    return value if shift == 0 else pltpu.roll(value, shift, 1)


def halves(value):
    high = value.astype(jnp.bfloat16)
    low = (value - high.astype(jnp.float32)).astype(jnp.bfloat16)
    return high, low


def dot32(a, b):
    return jnp.dot(a, b, preferred_element_type=jnp.float32)


def fold_groups(rows, count):
    tiles = rows // 8
    sizes = [8 * (tiles // count + (1 if g < tiles % count else 0)) for g in range(count)]
    starts = [sum(sizes[:g]) for g in range(count)]
    return list(zip(starts, sizes))


def folded_rows(rows, count):
    return fold_groups(rows, count)[0][1]


def folded(value, count):
    groups = fold_groups(value.shape[0], count)
    tall, wide = groups[0][1], LANES // count
    lane = lane_of((tall, LANES))
    total = jnp.zeros((tall, LANES), value.dtype)
    for g, (start, size) in enumerate(groups):
        part = value[start : start + size]
        if size < tall:
            part = jnp.concatenate([part, jnp.zeros((tall - size, LANES), value.dtype)], 0)
        keep = (lane >= wide * g) & (lane < wide * (g + 1))
        total = jnp.where(keep, rolled(part, wide * g), total)
    return total


def unfolded(value, rows, count, at):
    wide = LANES // count
    parts = []
    for g, (_, size) in enumerate(fold_groups(rows, count)):
        parts.append(rolled(value[:size], at - wide * g))
    return jnp.concatenate(parts, 0)


def x_kernel(place_ref, offs_ref, orders_ref, wh_ref, wl_ref, out_ref, acc_ref, q_ref):
    points, _, cols_ky, rows_kx = orders_ref.shape
    n_tx, rows, _ = wh_ref.shape
    window = rows_kx + SPAN
    half = rows // 2
    acc_ref[...] = jnp.zeros_like(acc_ref)
    blank = jnp.zeros((rows_kx, LANES - cols_ky), jnp.float32)
    for point in range(points):
        down = offs_ref[0, point] + REACH
        across = offs_ref[1, point] + REACH
        for part in range(2):
            amp = jnp.concatenate([orders_ref[point, part].T, blank], 1)
            acc_ref[part, pl.ds(down, rows_kx), :] += pltpu.roll(amp, across, 1)
    s_re = acc_ref[0]
    s_im = acc_ref[1]
    lane = lane_of((window, LANES))

    def main(re, im):
        out = jnp.where(lane < cols_ky, re, rolled(im, cols_ky))
        return out if 2 * cols_ky == LANES else jnp.where(lane < 2 * cols_ky, out, 0.0)

    def spill(re, im):
        out = jnp.where(lane < SPAN, rolled(re, -cols_ky), rolled(im, SPAN - cols_ky))
        return jnp.where(lane < 2 * SPAN, out, 0.0)

    top = jnp.concatenate([main(s_re, s_im), spill(s_re, s_im)], 1)
    bottom = jnp.concatenate([main(-s_im, s_re), spill(-s_im, s_re)], 1)
    right_h, right_l = halves(jnp.concatenate([top, bottom], 0))
    own = place_ref[0]
    for distance in range(n_tx):
        w_h = wh_ref[distance]
        q_ref[...] = dot32(w_h, right_h) + (dot32(wl_ref[distance], right_h) + dot32(w_h, right_l))
        for flip in range(2):
            start = pl.multiple_of((own ^ flip) * half, 8)
            block = q_ref[pl.ds(start, half), :]
            out_ref[2 * distance + flip, :half, :] = block[:, :LANES]
            out_ref[2 * distance + flip, half:, :] = folded(block[:, LANES:], 4)


def x_stage(place, offsets, orders, n_tx, cells_x):
    points, _, cols_ky, rows_kx = orders.shape
    w_h, w_l = x_tables(n_tx, rows_kx, cells_x)
    rows = cells_x + 2 * PAD
    half = rows // 2
    window = rows_kx + SPAN
    height = half + folded_rows(half, 4)
    whole = lambda shape: pl.BlockSpec(shape, lambda i, place, offs: (0,) * len(shape))
    table = pl.BlockSpec((None, n_tx, rows, 2 * window), lambda i, place, offs: (place[1], 0, 0, 0))
    return pl.pallas_call(
        x_kernel,
        grid_spec=pltpu.PrefetchScalarGridSpec(
            num_scalar_prefetch=2,
            grid=(1,),
            in_specs=[whole(orders.shape), table, table],
            out_specs=whole((2 * n_tx, height, LANES)),
            scratch_shapes=[
                pltpu.VMEM((2, window, LANES), jnp.float32),
                pltpu.VMEM((rows, 2 * LANES), jnp.float32),
            ],
        ),
        out_shape=jax.ShapeDtypeStruct((2 * n_tx, height, LANES), jnp.float32),
        compiler_params=pltpu.CompilerParams(vmem_limit_bytes=VMEM_LIMIT),
        name="x_stage",
    )(place, offsets, orders, jnp.asarray(w_h), jnp.asarray(w_l))


def y_kernel(cols_ky, half, place_ref, *refs):
    *block_refs, th_ref, tl_ref, phase_ref, out_ref = refs
    n_ty = len(block_refs)
    lane = lane_of((half, LANES))
    mains, spills, numbers = [], [], []
    for number, ref in enumerate(block_refs):
        block = place_ref[2] ^ number
        numbers.append(block)
        phase = phase_ref[block]
        main = ref[:half, :]
        if 2 * cols_ky == LANES:
            swapped = rolled(main, cols_ky)
        else:
            swapped = jnp.where(lane < cols_ky, rolled(main, -cols_ky), rolled(main, cols_ky))
        mains.append(main * phase[0:1] + swapped * phase[1:2])
        spill = ref[half:, :]
        small = lane_of(spill.shape)
        other = jnp.where(small % (2 * SPAN) < SPAN, rolled(spill, -SPAN), rolled(spill, SPAN))
        spills.append(spill * phase[2:3] + other * phase[3:4])
    packed = []
    for first in range(0, n_ty, 4):
        total = None
        for g in range(4):
            part = unfolded(spills[first + g], half, 4, 32 * g)
            total = part if total is None else jnp.where(lane >= 32 * g, part, total)
        packed.append(total)
    result = None
    for first in range(0, n_ty, 2):
        left_h, left_l = halves(jnp.concatenate(mains[first : first + 2], 1))
        t_h = jnp.concatenate([th_ref[numbers[first + g], :LANES, :] for g in range(2)], 0)
        t_l = jnp.concatenate([tl_ref[numbers[first + g], :LANES, :] for g in range(2)], 0)
        part = dot32(left_h, t_h) + (dot32(left_h, t_l) + dot32(left_l, t_h))
        result = part if result is None else result + part
    for first in range(0, n_ty, 8):
        left_h, left_l = halves(jnp.concatenate(packed[first // 4 : first // 4 + 2], 1))
        t_h = jnp.concatenate([th_ref[numbers[first + g], LANES:, :] for g in range(8)], 0)
        t_l = jnp.concatenate([tl_ref[numbers[first + g], LANES:, :] for g in range(8)], 0)
        result = result + (dot32(left_h, t_h) + (dot32(left_h, t_l) + dot32(left_l, t_h)))
    out_ref[:half, :] = result[:, :LANES]
    out_ref[half : 2 * half, :] = result[:, LANES : 2 * LANES]
    out_ref[2 * half :, :] = folded(result[:, 2 * LANES :], 8)


def y_stage(place, blocks, cols_ky, cells_y, half):
    n_ty = len(blocks)
    t_h, t_l = y_tables(n_ty, cols_ky, cells_y)
    phases = y_phases(n_ty, cols_ky, cells_y)
    whole = lambda shape: pl.BlockSpec(shape, lambda i, place: (0,) * len(shape))
    height = 2 * half + folded_rows(half, 8)
    return pl.pallas_call(
        functools.partial(y_kernel, cols_ky, half),
        grid_spec=pltpu.PrefetchScalarGridSpec(
            num_scalar_prefetch=1,
            grid=(1,),
            in_specs=[whole(b.shape) for b in blocks]
            + [
                whole(t_h.shape),
                whole(t_l.shape),
                pl.BlockSpec((None,) + phases.shape[1:], lambda i, place: (place[2], 0, 0, 0)),
            ],
            out_specs=whole((height, LANES)),
        ),
        out_shape=jax.ShapeDtypeStruct((height, LANES), jnp.float32),
        compiler_params=pltpu.CompilerParams(vmem_limit_bytes=VMEM_LIMIT),
        name="y_stage",
    )(place, *blocks, jnp.asarray(t_h), jnp.asarray(t_l), jnp.asarray(phases))


def coefficient_of(material):
    value = jnp.where(material == 0, COURANT / PERMITTIVITY[0], COURANT / PERMITTIVITY[1])
    value = jnp.where(material == 2, COURANT / PERMITTIVITY[2], value)
    return jnp.where(material == 3, COURANT / PERMITTIVITY[3], value).astype(jnp.float32)


def pack_kernel(e_ref, h_ref, m_ref, x_ref, f_ref, c_ref, w_ref, low_ref, high_ref):
    cells_x = e_ref.shape[2]
    end = BASE + cells_x
    rows = cells_x + 2 * PAD
    lane = lane_of((rows, LANES))
    sub = lane % SLOT
    lows = [jnp.zeros((rows, LANES), jnp.float32)] * 2
    highs = [jnp.zeros((rows, LANES), jnp.float32)] * 2
    blank = jnp.zeros((PAD - HALO, LANES), jnp.float32)
    for j in range(7):
        scale = 1.0 if 3 <= j < 6 else 0.5
        strips = [jnp.zeros((rows, LANES), jnp.float32)] * 2
        for z in range(LAYERS):
            to = f_ref.at[j, z] if j < 6 else c_ref.at[z]
            if j < 3:
                body = e_ref[j, z] * scale
            elif j < 6:
                body = h_ref[j - 3, z]
            else:
                body = coefficient_of(m_ref[z]) * scale
            rims = x_ref[j * LAYERS + z] * scale
            full = jnp.concatenate([blank, rims[HALO:], body, rims[:HALO], blank], 0)
            to[0 : BASE - PAD, :] = jnp.zeros((BASE - PAD, LANES), jnp.float32)
            to[BASE - PAD : end + PAD, :] = full
            to[end + PAD : end + BASE, :] = jnp.zeros((BASE - PAD, LANES), jnp.float32)
            g, at = z % 2, (z // 2) * SLOT
            keep = (lane >= at) & (lane < at + 2 * WIDE)
            strips[g] = jnp.where(keep, rolled(full, at + WIDE), strips[g])
        for g in range(2):
            w_ref[j, g] = strips[g]
            a, b = divmod(2 * j + g, 8)
            keep = (sub >= 4 * b) & (sub < 4 * b + 4)
            lows[a] = jnp.where(keep, rolled(strips[g], 4 * b - 4), lows[a])
            highs[a] = jnp.where(keep, rolled(strips[g], 4 * b - 8), highs[a])
    for a in range(2):
        low_ref[a] = lows[a]
        high_ref[a] = highs[a]


def pack(e_field, h_field, material, x_rims):
    cells_x = e_field.shape[2]
    rows = cells_x + 2 * PAD
    tall = cells_x + 2 * BASE
    f32 = jnp.float32
    return pl.pallas_call(
        pack_kernel,
        out_shape=(
            jax.ShapeDtypeStruct((6, LAYERS, tall, LANES), f32),
            jax.ShapeDtypeStruct((LAYERS, tall, LANES), f32),
            jax.ShapeDtypeStruct((7, 2, rows, LANES), f32),
            jax.ShapeDtypeStruct((2, rows, LANES), f32),
            jax.ShapeDtypeStruct((2, rows, LANES), f32),
        ),
        compiler_params=pltpu.CompilerParams(vmem_limit_bytes=VMEM_LIMIT),
        name="pack",
    )(e_field, h_field, material, x_rims)


def total(terms):
    out = None
    for sign, value in terms:
        if value is None:
            continue
        if out is None:
            out = value if sign > 0 else -value
        else:
            out = out + value if sign > 0 else out - value
    return out


def add(a, b):
    return total([(1, a), (1, b)])


def differ(a, b):
    return total([(1, a), (-1, b)])


def curl_of_e(e, e_z, e_x, e_y):
    return (
        differ(differ(e_z[1], e[1]), differ(e_y[2], e[2])),
        differ(differ(e_x[2], e[2]), differ(e_z[0], e[0])),
        differ(differ(e_y[0], e[0]), differ(e_x[1], e[1])),
    )


def curl_of_h(h, h_z, h_x, h_y):
    return (
        differ(differ(h[2], h_y[2]), differ(h[1], h_z[1])),
        differ(differ(h[0], h_z[0]), differ(h[2], h_x[2])),
        differ(differ(h[1], h_x[1]), differ(h[0], h_y[0])),
    )


def moved(value, shift):
    return None if value is None else rolled(value, shift)


class Tile:
    def __init__(self, ref, live):
        self.ref, self.live = ref, set(live)

    def load(self, j, z, start, size):
        return self.ref[j, z, start : start + size, :] if (j, z) in self.live else None

    def store(self, j, z, start, value):
        if value is not None:
            self.ref[j, z, start : start + value.shape[0], :] = value
            self.live.add((j, z))

    def step_h(self, z, start, size):
        e = [self.load(j, z, start, size) for j in range(3)]
        e_z = [self.load(j, z + 1, start, size) for j in range(2)] + [None]
        e_x = [None] + [self.load(j, z, start + 1, size) for j in (1, 2)]
        e_y = [moved(e[0], -1), None, moved(e[2], -1)]
        new = []
        for j, change in enumerate(curl_of_e(e, e_z, e_x, e_y)):
            new.append(add(self.load(3 + j, z, start, size), change))
            self.store(3 + j, z, start, new[j])
        return new

    def step_e(self, z, start, size, factor):
        h = [self.load(3 + j, z, start, size) for j in range(3)]
        h_z = [self.load(3 + j, z - 1, start, size) for j in range(2)] + [None]
        h_x = [None] + [self.load(3 + j, z, start - 1, size) for j in (1, 2)]
        h_y = [moved(h[0], 1), None, moved(h[2], 1)]
        new = []
        for j, change in enumerate(curl_of_h(h, h_z, h_x, h_y)):
            old = self.load(j, z, start, size)
            new.append(old if change is None else add(old, factor * change))
        return new


class Strip:
    def __init__(self, ref, rows):
        self.ref, self.start, self.rows = ref, BASE - PAD, rows
        self.lane = lane_of((rows, LANES))

    def load(self, j, g, by=0):
        return self.ref[j, g, self.start + by : self.start + by + self.rows, :]

    def store(self, j, g, value):
        self.ref[j, g, self.start : self.start + self.rows, :] = value

    def step_h(self, fresh=False):
        e = [[self.load(j, g) for j in range(3)] for g in range(2)]
        inside = self.lane < 2 * SLOT
        above = [
            [e[1][0], e[1][1], None],
            [jnp.where(inside, rolled(e[0][j], -SLOT), 0.0) for j in range(2)] + [None],
        ]
        for g in range(2):
            e_x = [None, self.load(1, g, 1), self.load(2, g, 1)]
            e_y = [rolled(e[g][0], -1), None, rolled(e[g][2], -1)]
            for j, change in enumerate(curl_of_e(e[g], above[g], e_x, e_y)):
                self.store(3 + j, g, change if fresh else self.load(3 + j, g) + change)

    def step_e(self, factor):
        h = [[self.load(3 + j, g) for j in range(3)] for g in range(2)]
        inside = self.lane >= SLOT
        below = [
            [jnp.where(inside, rolled(h[1][j], SLOT), 0.0) for j in range(2)] + [None],
            [h[0][0], h[0][1], None],
        ]
        new = []
        for g in range(2):
            h_x = [None, self.load(4, g, -1), self.load(5, g, -1)]
            h_y = [rolled(h[g][0], 1), None, rolled(h[g][2], 1)]
            change = curl_of_h(h[g], below[g], h_x, h_y)
            new.append([self.load(j, g) + factor[g] * change[j] for j in range(3)])
        return new

    def edges(self, j, g):
        value = self.ref[j, g, BASE : BASE + self.rows - 2 * PAD, :]
        return jnp.where(lane_of(value.shape) % SLOT < 4, rolled(value, -20), value)


def with_edges(value, edges, z):
    lane = lane_of(edges.shape)
    outer = (lane < HALO) | (lane >= LANES - HALO)
    return jnp.where(outer, rolled(edges, -((z // 2) * SLOT + 4)), 0.0 if value is None else value)


def free_kernel(f_in, c_ref, out_ref, f_ref):
    cells_x = out_ref.shape[2]
    rows = cells_x + 2 * PAD
    first = BASE - PAD
    every = [(j, z) for j in range(6) for z in range(LAYERS)]
    f_ref[...] = f_in[...]
    tile = Tile(f_ref, every)
    for step in range(STEPS):
        last = step == STEPS - 1
        for z in range(LAYERS):
            tile.step_h(z, first, rows - (PAD if last else 0))
            start, size = (BASE, cells_x) if last else (first, rows)
            new = tile.step_e(z, start, size, c_ref[z, start : start + size, :])
            for j in range(3):
                if last:
                    out_ref[j, z] = new[j]
                    out_ref[3 + j, z] = tile.load(3 + j, z, start, size)
                else:
                    tile.store(j, z, start, new[j])


def free_run(f_ext, c_ext, cells_x):
    tall = cells_x + 2 * BASE
    return pl.pallas_call(
        free_kernel,
        out_shape=jax.ShapeDtypeStruct((6, LAYERS, cells_x, LANES), jnp.float32),
        scratch_shapes=[pltpu.VMEM((6, LAYERS, tall, LANES), jnp.float32)],
        compiler_params=pltpu.CompilerParams(vmem_limit_bytes=VMEM_LIMIT),
        name="free_run",
    )(f_ext, c_ext)


def strip_kernel(w_ref, low_ref, high_ref, free_ref, factor_ref, out_ref, s_ref):
    rows = w_ref.shape[2]
    first = BASE - PAD
    lane = lane_of((rows, LANES))
    sub = lane % SLOT
    factor = [None, None]
    for j in range(7):
        for g in range(2):
            a, b = divmod(2 * j + g, 8)
            mine = w_ref[j, g]
            value = jnp.where(sub < 16, rolled(mine, -4), rolled(mine, 16))
            value = jnp.where(sub < 4, rolled(low_ref[a], -4 * b), value)
            value = jnp.where((sub >= 24) & (sub < 28), rolled(high_ref[a], 24 - 4 * b), value)
            if j < 6:
                s_ref[j, g, first : first + rows, :] = value
            else:
                factor[g] = value
                factor_ref[g] = value
    strip = Strip(s_ref, rows)
    for step in range(STEPS):
        strip.step_h()
        new = strip.step_e([factor_ref[g] for g in range(2)])
        for g in range(2):
            for j in range(3):
                strip.store(j, g, new[g][j])
    for j in range(6):
        for g in range(2):
            edges = strip.edges(j, g)
            for z in range(g, LAYERS, 2):
                out_ref[j, z] = with_edges(free_ref[j, z], edges, z)


def strip_run(own_edges, low, high, free):
    rows = own_edges.shape[2]
    f32 = jnp.float32
    return pl.pallas_call(
        strip_kernel,
        out_shape=(
            jax.ShapeDtypeStruct((2, rows, LANES), f32),
            jax.ShapeDtypeStruct(free.shape, f32),
        ),
        scratch_shapes=[pltpu.VMEM((6, 2, rows + 2 * (BASE - PAD), LANES), f32)],
        compiler_params=pltpu.CompilerParams(vmem_limit_bytes=VMEM_LIMIT),
        name="strip_run",
    )(own_edges, low, high, free)


def response_kernel(
    place_ref, c_ref, factor_ref, free_ref, mine_ref, other_ref, e_out, h_out,
    f_ref, s_ref, plane_ref, rim_ref,
):
    cells_x = e_out.shape[2]
    rows = cells_x + 2 * PAD
    half = rows // 2
    first = BASE - PAD
    own = place_ref[0]
    lane = lane_of((half, LANES))
    for ref, which in ((mine_ref, own), (other_ref, 1 - own)):
        at = pl.ds(pl.multiple_of(which * half, 8), half)
        outer = unfolded(ref[2 * half :, :], half, 8, 0)
        for part in range(2):
            plane = ref[part * half : (part + 1) * half, :]
            plane_ref[part, at, :] = plane
            value = jnp.where(lane < 16, rolled(plane, 4), rolled(plane, 24))
            value = jnp.where(lane < 4, rolled(outer, -8 * part), value)
            value = jnp.where((lane >= 24) & (lane < 28), rolled(outer, 20 - 8 * part), value)
            rim_ref[part, at, :] = jnp.where(lane < 28, value, 0.0)

    def injection(ref, step, start, size):
        cosine = 0.5 * COURANT * math.cos(OMEGA * step)
        sine = 0.5 * COURANT * math.sin(OMEGA * step)
        re, im = ref[0, start : start + size, :], ref[1, start : start + size, :]
        return [cosine * re - sine * im, sine * re + cosine * im, None]

    tile = Tile(f_ref, ())
    for j, value in enumerate(injection(plane_ref, 1, 0, rows)):
        tile.store(j, ZINJ, first, value)
    strip = Strip(s_ref, rows)
    s_ref[...] = jnp.zeros_like(s_ref)
    for j, value in enumerate(injection(rim_ref, 1, 0, rows)[:2]):
        strip.store(j, ZINJ % 2, value)
    for step in range(2, STEPS + 1):
        strip.step_h()
        new = strip.step_e([factor_ref[g] for g in range(2)])
        source = injection(rim_ref, step, 0, rows)
        for g in range(2):
            for j in range(3):
                value = add(new[g][j], source[j] if g == ZINJ % 2 else None)
                strip.store(j, g, value)
    for step in range(2, STEPS + 1):
        last = step == STEPS
        start, size = (BASE, cells_x) if last else (first, rows)
        for z in range(LAYERS):
            tile.step_h(z, first, rows - (PAD if last else 0))
            new = tile.step_e(z, start, size, c_ref[z, start : start + size, :])
            if z == ZINJ:
                source = injection(plane_ref, step, start - first, size)
                new = [add(a, b) for a, b in zip(new, source)]
            for j in range(3):
                if not last:
                    tile.store(j, z, start, new[j])
                    continue
                value = free_ref[j, z]
                if new[j] is not None:
                    value = value + with_edges(new[j], strip.edges(j, z % 2), z)
                e_out[j, z] = value * 2.0
                value = free_ref[3 + j, z]
                response = tile.load(3 + j, z, start, size)
                if response is not None:
                    value = value + with_edges(response, strip.edges(3 + j, z % 2), z)
                h_out[j, z] = value


def response(place, c_ext, factor, free, mine, other, cells_x):
    rows = cells_x + 2 * PAD
    tall = cells_x + 2 * BASE
    f32 = jnp.float32
    out = jax.ShapeDtypeStruct((3, LAYERS, cells_x, LANES), f32)
    vmem = pl.BlockSpec(memory_space=pltpu.VMEM)
    return pl.pallas_call(
        response_kernel,
        in_specs=[pl.BlockSpec(memory_space=pltpu.SMEM)] + [vmem] * 5,
        out_shape=(out, out),
        scratch_shapes=[
            pltpu.VMEM((6, LAYERS, tall, LANES), f32),
            pltpu.VMEM((6, 2, tall, LANES), f32),
            pltpu.VMEM((2, rows, LANES), f32),
            pltpu.VMEM((2, rows, LANES), f32),
        ],
        compiler_params=pltpu.CompilerParams(vmem_limit_bytes=VMEM_LIMIT),
        name="response",
    )(place, c_ext, factor, free, mine, other)


def along(block, axis, distance):
    n = lax.axis_size(axis)
    return lax.ppermute(block, axis, [((i - distance) % n, i) for i in range(n)])


def flipped(block, axis, bits):
    return lax.ppermute(block, axis, [(i, i ^ bits) for i in range(lax.axis_size(axis))])


def to_groups(block, n_src, n_tx, flip, distance):
    route = []
    for s in range(n_src):
        for t in range(n_tx):
            route.append((s * n_tx + t, (s ^ flip) * n_tx + (t + distance) % n_tx))
    return lax.ppermute(block, ("src", "tx"), route)


def per_device(orders, offsets, material, e_field, h_field):
    cols_ky = orders.shape[3]
    layers, cells_x, cells_y = material.shape
    n_src, n_tx, n_ty = lax.axis_size("src"), lax.axis_size("tx"), lax.axis_size("ty")
    half = cells_x // 2 + PAD
    place = jnp.stack([lax.axis_index("src"), lax.axis_index("tx"), lax.axis_index("ty")]).astype(
        jnp.int32
    )

    parts = x_stage(place, offsets.T, jnp.swapaxes(orders, 2, 3), n_tx, cells_x)
    block = parts[0]
    for distance in range(n_tx):
        for flip in range(n_src):
            if distance or flip:
                block = block + to_groups(parts[2 * distance + flip], n_src, n_tx, flip, distance)

    def edge_rows(rows):
        c = coefficient_of(material[:, rows])
        return jnp.concatenate(
            [
                e_field[:, :, rows].reshape(-1, HALO, cells_y),
                h_field[:, :, rows].reshape(-1, HALO, cells_y),
                c,
            ],
            0,
        )

    top, bottom = edge_rows(slice(0, HALO)), edge_rows(slice(cells_x - HALO, cells_x))
    if n_tx == 2:
        x_rims = along(jnp.concatenate([top, bottom], 1), "tx", 1)
    else:
        x_rims = jnp.concatenate([along(top, "tx", -1), along(bottom, "tx", 1)], 1)
    f_ext, c_ext, own_edges, to_high, to_low = pack(e_field, h_field, material, x_rims)
    low = along(to_high, "ty", 1)
    high = along(to_low, "ty", -1)

    blocks = {0: block}
    for bits in range(n_ty - 2, 0, -2):
        blocks[bits] = flipped(block, "ty", bits)
    for bits in range(0, n_ty, 2):
        blocks[bits + 1] = flipped(blocks[bits], "ty", 1)
    mine = y_stage(place, [blocks[b] for b in range(n_ty)], cols_ky, cells_y, half)
    other = flipped(mine, "src", 1)
    free = free_run(f_ext, c_ext, cells_x)
    factor, free = strip_run(own_edges, low, high, free)
    return response(place, c_ext, factor, free, mine, other, cells_x)


def solution(mesh):
    in_specs = (
        P("src", None, "tx", "ty"),
        P("src", None),
        P(None, "tx", "ty"),
        P(None, None, "tx", "ty"),
        P(None, None, "tx", "ty"),
    )
    out_specs = (P(None, None, "tx", "ty"), P(None, None, "tx", "ty"))
    return jax.shard_map(
        per_device, mesh=mesh, in_specs=in_specs, out_specs=out_specs, check_vma=False
    )
```

```python
import functools
import math

import jax
import jax.numpy as jnp
import ml_dtypes
import numpy as np
from jax import lax
from jax.experimental import pallas as pl
from jax.experimental.pallas import tpu as pltpu
from jax.sharding import PartitionSpec as P

MX = 512
MY = 512
STEPS = 4
ZINJ = 1
LAYERS = 6

COURANT = 0.5
OMEGA = 0.7
PERMITTIVITY = (1.0, 2.6, 11.9, 2.1)

REACH = 8
SPAN = 2 * REACH
PAD = 8
HALO = 4
BASE = 16
SLOT = 32
WIDE = 8
LANES = 128
VMEM_LIMIT = 40 * 1024 * 1024


def split_bf16(table):
    high = table.astype(ml_dtypes.bfloat16)
    low = (table - high.astype(np.float64)).astype(ml_dtypes.bfloat16)
    return high, low


def padded(lanes):
    return -(-lanes // LANES) * LANES


@functools.lru_cache(maxsize=None)
def x_seeds(n_tx, rows_kx, cells_x):
    window = rows_kx + SPAN
    wide = padded(window)
    full = cells_x * n_tx
    turns = [8 << k for k in range((cells_x // 8).bit_length())]
    count = 8 + len(turns) + n_tx
    table = np.zeros((n_tx, -(-count // 8) * 8, 2 * wide), np.float32)
    for own in range(n_tx):
        freq = own * rows_kx - MX // 2 - REACH + np.arange(window)
        tiles = [(own + distance) % n_tx * cells_x for distance in range(n_tx)]
        x = np.array(list(range(-PAD, 8 - PAD)) + turns + tiles)
        angle = np.mod(x[:, None] * freq[None, :], full) * (2.0 * math.pi / full)
        table[own, :count, :window] = np.cos(angle)
        table[own, :count, wide : wide + window] = np.sin(angle)
    return table, len(turns)


@functools.lru_cache(maxsize=None)
def y_tables(n_ty, cols_ky, cells_y):
    full = cells_y * n_ty
    window = cols_ky + SPAN
    edge = np.concatenate([np.arange(-HALO, 0), cells_y + np.arange(HALO)])
    y = np.concatenate([np.arange(cells_y), edge])
    table = np.zeros((n_ty, LANES + 2 * SPAN, 2 * cells_y + LANES))
    for block in range(n_ty):
        freq = block * cols_ky - MY // 2 - REACH + np.arange(window)
        angle = np.mod(freq[:, None] * y[None, :], full) * (2.0 * math.pi / full)
        cos, sin = np.cos(angle), np.sin(angle)

        def placed(re_cols, im_cols):
            out = np.zeros((window, 2 * cells_y + LANES))
            out[:, :cells_y] = re_cols[:, :cells_y]
            out[:, cells_y : 2 * cells_y] = im_cols[:, :cells_y]
            out[:, 2 * cells_y : 2 * cells_y + 2 * HALO] = re_cols[:, cells_y:]
            out[:, 2 * cells_y + 2 * HALO : 2 * cells_y + 4 * HALO] = im_cols[:, cells_y:]
            return out

        from_re = placed(cos, sin)
        from_im = placed(-sin, cos)
        table[block, :cols_ky] = from_re[:cols_ky]
        table[block, cols_ky : 2 * cols_ky] = from_im[:cols_ky]
        table[block, LANES : LANES + SPAN] = from_re[cols_ky:]
        table[block, LANES + SPAN :] = from_im[cols_ky:]
    return split_bf16(table)


@functools.lru_cache(maxsize=None)
def y_phases(n_ty, cols_ky, cells_y):
    full = cells_y * n_ty
    out = np.zeros((n_ty, n_ty, 8, LANES), np.float32)
    for own in range(n_ty):
        for block in range(n_ty):
            freq = block * cols_ky - MY // 2 - REACH + np.arange(cols_ky + SPAN)
            angle = np.mod(freq * own * cells_y, full) * (2.0 * math.pi / full)
            cos, sin = np.cos(angle), np.sin(angle)
            out[own, block, 0, :cols_ky] = cos[:cols_ky]
            out[own, block, 0, cols_ky : 2 * cols_ky] = cos[:cols_ky]
            out[own, block, 1, :cols_ky] = -sin[:cols_ky]
            out[own, block, 1, cols_ky : 2 * cols_ky] = sin[:cols_ky]
            for group in range(LANES // (2 * SPAN)):
                at = group * 2 * SPAN
                out[own, block, 2, at : at + SPAN] = cos[cols_ky:]
                out[own, block, 2, at + SPAN : at + 2 * SPAN] = cos[cols_ky:]
                out[own, block, 3, at : at + SPAN] = -sin[cols_ky:]
                out[own, block, 3, at + SPAN : at + 2 * SPAN] = sin[cols_ky:]
    return out


def lane_of(shape):
    return lax.broadcasted_iota(jnp.int32, shape, len(shape) - 1)


def rolled(value, shift):
    shift = shift % LANES
    return value if shift == 0 else pltpu.roll(value, shift, 1)


def halves(value):
    high = value.astype(jnp.bfloat16)
    low = (value - high.astype(jnp.float32)).astype(jnp.bfloat16)
    return high, low


def dot32(a, b):
    return jnp.dot(a, b, preferred_element_type=jnp.float32)


def fold_groups(rows, count):
    tiles = rows // 8
    sizes = [8 * (tiles // count + (1 if g < tiles % count else 0)) for g in range(count)]
    starts = [sum(sizes[:g]) for g in range(count)]
    return list(zip(starts, sizes))


def folded_rows(rows, count):
    return fold_groups(rows, count)[0][1]


def folded(value, count):
    groups = fold_groups(value.shape[0], count)
    tall, wide = groups[0][1], LANES // count
    lane = lane_of((tall, LANES))
    total = jnp.zeros((tall, LANES), value.dtype)
    for g, (start, size) in enumerate(groups):
        part = value[start : start + size]
        if size < tall:
            part = jnp.concatenate([part, jnp.zeros((tall - size, LANES), value.dtype)], 0)
        keep = (lane >= wide * g) & (lane < wide * (g + 1))
        total = jnp.where(keep, rolled(part, wide * g), total)
    return total


def unfolded(value, rows, count, at):
    wide = LANES // count
    parts = []
    for g, (_, size) in enumerate(fold_groups(rows, count)):
        parts.append(rolled(value[:size], at - wide * g))
    return jnp.concatenate(parts, 0)


def turned(cos, sin, by_cos, by_sin):
    return cos * by_cos - sin * by_sin, sin * by_cos + cos * by_sin


def table_kernel(n_turns, place_ref, seed_ref, high_ref, low_ref):
    n_tx, rows, both = high_ref.shape
    wide = both // 2

    def row(i):
        return seed_ref[i : i + 1, :wide], seed_ref[i : i + 1, wide:]

    cos, sin = seed_ref[:8, :wide], seed_ref[:8, wide:]
    for k in range(n_turns):
        more = min(8 << k, rows - (8 << k))
        new = turned(cos[:more], sin[:more], *row(8 + k))
        cos, sin = jnp.concatenate([cos, new[0]], 0), jnp.concatenate([sin, new[1]], 0)
    for distance in range(n_tx):
        there = turned(cos, sin, *row(8 + n_turns + distance))
        for part in range(2):
            high, low = halves(there[part])
            high_ref[distance, :, part * wide : (part + 1) * wide] = high
            low_ref[distance, :, part * wide : (part + 1) * wide] = low


def x_table(place, n_tx, rows_kx, cells_x):
    seeds, n_turns = x_seeds(n_tx, rows_kx, cells_x)
    rows = cells_x + 2 * PAD
    shape = (n_tx, rows, seeds.shape[2])
    whole = pl.BlockSpec(shape, lambda i, place: (0, 0, 0))
    return pl.pallas_call(
        functools.partial(table_kernel, n_turns),
        grid_spec=pltpu.PrefetchScalarGridSpec(
            num_scalar_prefetch=1,
            grid=(1,),
            in_specs=[pl.BlockSpec((None,) + seeds.shape[1:], lambda i, place: (place[1], 0, 0))],
            out_specs=(whole, whole),
        ),
        out_shape=(jax.ShapeDtypeStruct(shape, jnp.bfloat16),) * 2,
        compiler_params=pltpu.CompilerParams(vmem_limit_bytes=VMEM_LIMIT),
        name="x_table",
    )(place, jnp.asarray(seeds))


def x_kernel(place_ref, offs_ref, orders_ref, wh_ref, wl_ref, out_ref, line_ref, acc_ref, q_ref):
    points, _, cols_ky, rows_kx = orders_ref.shape
    n_tx, rows, both = wh_ref.shape
    half = rows // 2
    acc_ref[...] = jnp.zeros_like(acc_ref)
    line_ref[...] = jnp.zeros_like(line_ref)
    wide = line_ref.shape[4]
    for point in range(points):
        down = offs_ref[0, point] + REACH
        across = offs_ref[1, point] + REACH
        for part in range(2):
            for tile in range(rows_kx // wide):
                lanes = slice(tile * wide, (tile + 1) * wide)
                line = line_ref.at[point, part, tile]
                line[pl.ds(across, cols_ky), :] = orders_ref[point, part, :, lanes]
                acc_ref[part, pl.ds(down + tile * wide, wide), :] += line[...].T
    s_re = acc_ref[0]
    s_im = acc_ref[1]
    lane = lane_of(s_re.shape)
    re_by, im_by = rolled(s_re, cols_ky), rolled(s_im, cols_ky)

    def main(re, im_by):
        out = jnp.where(lane < cols_ky, re, im_by)
        return out if 2 * cols_ky == LANES else jnp.where(lane < 2 * cols_ky, out, 0.0)

    def spill(re_back, im_back):
        out = jnp.where(lane < SPAN, re_back, im_back)
        return jnp.where(lane < 2 * SPAN, out, 0.0)

    same = 2 * cols_ky == LANES
    re_back = re_by if same else rolled(s_re, -cols_ky)
    im_back = im_by if same else rolled(s_im, -cols_ky)
    top = [main(s_re, im_by), spill(re_back, rolled(s_im, SPAN - cols_ky))]
    bottom = [main(-s_im, re_by), spill(-im_back, rolled(s_re, SPAN - cols_ky))]
    right = jnp.concatenate([jnp.concatenate(top, 1), jnp.concatenate(bottom, 1)], 0)
    right_h, right_l = halves(right)
    own = place_ref[0]
    for distance in range(n_tx):
        w_h = wh_ref[distance]
        q_ref[...] = dot32(w_h, right_h) + (dot32(wl_ref[distance], right_h) + dot32(w_h, right_l))
        for flip in range(2):
            start = pl.multiple_of((own ^ flip) * half, 8)
            block = q_ref[pl.ds(start, half), :]
            out_ref[2 * distance + flip, :half, :] = block[:, :LANES]
            out_ref[2 * distance + flip, half:, :] = folded(block[:, LANES:], 4)


def x_stage(place, offsets, orders, n_tx, cells_x):
    points, _, cols_ky, rows_kx = orders.shape
    wide = min(rows_kx, LANES)
    w_h, w_l = x_table(place, n_tx, rows_kx, cells_x)
    rows = cells_x + 2 * PAD
    half = rows // 2
    height = half + folded_rows(half, 4)
    vmem = pl.BlockSpec(memory_space=pltpu.VMEM)
    smem = pl.BlockSpec(memory_space=pltpu.SMEM)
    return pl.pallas_call(
        x_kernel,
        in_specs=[smem, smem, vmem, vmem, vmem],
        out_shape=jax.ShapeDtypeStruct((2 * n_tx, height, LANES), jnp.float32),
        scratch_shapes=[
            pltpu.VMEM((points, 2, rows_kx // wide, LANES, wide), jnp.float32),
            pltpu.VMEM((2, w_h.shape[2] // 2, LANES), jnp.float32),
            pltpu.VMEM((rows, 2 * LANES), jnp.float32),
        ],
        compiler_params=pltpu.CompilerParams(vmem_limit_bytes=VMEM_LIMIT),
        name="x_stage",
    )(place, offsets, orders, w_h, w_l)


def sum_kernel(*refs):
    *part_refs, _, out_ref = refs
    total = part_refs[0][0]
    for ref in part_refs[1:]:
        total = total + ref[...]
    out_ref[...] = total


def summed(parts, received, after):
    own = pl.BlockSpec((1,) + parts.shape[1:], lambda i: (0, 0, 0))
    each = pl.BlockSpec(parts.shape[1:], lambda i: (0, 0))
    return pl.pallas_call(
        sum_kernel,
        grid=(1,),
        in_specs=[own] + [each] * len(received) + [pl.BlockSpec(memory_space=pl.ANY)],
        out_specs=each,
        out_shape=jax.ShapeDtypeStruct(parts.shape[1:], jnp.float32),
        name="sum_parts",
    )(parts, *received, after)


def y_kernel(cols_ky, half, place_ref, *refs):
    *block_refs, th_ref, tl_ref, phase_ref, _, out_ref = refs
    n_ty = len(block_refs)
    lane = lane_of((half, LANES))
    mains, spills, numbers = [], [], []
    for number, ref in enumerate(block_refs):
        block = place_ref[2] ^ number
        numbers.append(block)
        phase = phase_ref[block]
        main = ref[:half, :]
        if 2 * cols_ky == LANES:
            swapped = rolled(main, cols_ky)
        else:
            swapped = jnp.where(lane < cols_ky, rolled(main, -cols_ky), rolled(main, cols_ky))
        mains.append(main * phase[0:1] + swapped * phase[1:2])
        spill = ref[half:, :]
        small = lane_of(spill.shape)
        other = jnp.where((small & (2 * SPAN - 1)) < SPAN, rolled(spill, -SPAN), rolled(spill, SPAN))
        spills.append(spill * phase[2:3] + other * phase[3:4])
    packed = []
    for first in range(0, n_ty, 4):
        total = None
        for g in range(4):
            part = unfolded(spills[first + g], half, 4, 32 * g)
            total = part if total is None else jnp.where(lane >= 32 * g, part, total)
        packed.append(total)
    result = None
    for first in range(0, n_ty, 2):
        left_h, left_l = halves(jnp.concatenate(mains[first : first + 2], 1))
        t_h = jnp.concatenate([th_ref[numbers[first + g], :LANES, :] for g in range(2)], 0)
        t_l = jnp.concatenate([tl_ref[numbers[first + g], :LANES, :] for g in range(2)], 0)
        part = dot32(left_h, t_h) + (dot32(left_h, t_l) + dot32(left_l, t_h))
        result = part if result is None else result + part
    for first in range(0, n_ty, 8):
        left_h, left_l = halves(jnp.concatenate(packed[first // 4 : first // 4 + 2], 1))
        t_h = jnp.concatenate([th_ref[numbers[first + g], LANES:, :] for g in range(8)], 0)
        t_l = jnp.concatenate([tl_ref[numbers[first + g], LANES:, :] for g in range(8)], 0)
        result = result + (dot32(left_h, t_h) + (dot32(left_h, t_l) + dot32(left_l, t_h)))
    out_ref[:half, :] = result[:, :LANES]
    out_ref[half : 2 * half, :] = result[:, LANES : 2 * LANES]
    out_ref[2 * half :, :] = folded(result[:, 2 * LANES :], 8)


def y_stage(place, blocks, cols_ky, cells_y, half, after):
    n_ty = len(blocks)
    t_h, t_l = y_tables(n_ty, cols_ky, cells_y)
    phases = y_phases(n_ty, cols_ky, cells_y)
    whole = lambda shape: pl.BlockSpec(shape, lambda i, place: (0,) * len(shape))
    height = 2 * half + folded_rows(half, 8)
    return pl.pallas_call(
        functools.partial(y_kernel, cols_ky, half),
        grid_spec=pltpu.PrefetchScalarGridSpec(
            num_scalar_prefetch=1,
            grid=(1,),
            in_specs=[whole(b.shape) for b in blocks]
            + [
                whole(t_h.shape),
                whole(t_l.shape),
                pl.BlockSpec((None,) + phases.shape[1:], lambda i, place: (place[2], 0, 0, 0)),
                pl.BlockSpec(memory_space=pl.ANY),
            ],
            out_specs=whole((height, LANES)),
        ),
        out_shape=jax.ShapeDtypeStruct((height, LANES), jnp.float32),
        compiler_params=pltpu.CompilerParams(vmem_limit_bytes=VMEM_LIMIT),
        name="y_stage",
    )(place, *blocks, jnp.asarray(t_h), jnp.asarray(t_l), jnp.asarray(phases), after)


def coefficient_of(material):
    value = jnp.where(material == 0, COURANT / PERMITTIVITY[0], COURANT / PERMITTIVITY[1])
    value = jnp.where(material == 2, COURANT / PERMITTIVITY[2], value)
    return jnp.where(material == 3, COURANT / PERMITTIVITY[3], value).astype(jnp.float32)


def rim_kernel(e_ref, h_ref, m_ref, out_ref):
    cells_x = e_ref.shape[2]
    for number in range(7 * LAYERS):
        j, z = divmod(number, LAYERS)
        ref = e_ref.at[j, z] if j < 3 else h_ref.at[j - 3, z] if j < 6 else m_ref.at[z]
        first, final = ref[:8, :], ref[cells_x - 8 :, :]
        if j == 6:
            first, final = coefficient_of(first), coefficient_of(final)
        row = lax.broadcasted_iota(jnp.int32, first.shape, 0)
        out_ref[number] = jnp.where(row < HALO, first, final)


def x_rims_of(e_field, h_field, material):
    return pl.pallas_call(
        rim_kernel,
        out_shape=jax.ShapeDtypeStruct((7 * LAYERS, 2 * HALO, LANES), jnp.float32),
        compiler_params=pltpu.CompilerParams(vmem_limit_bytes=VMEM_LIMIT),
        name="x_rims",
    )(e_field, h_field, material)


def pack_kernel(e_ref, h_ref, c_ref, x_ref, ext_ref, w_ref, low_ref, high_ref):
    cells_x = e_ref.shape[2]
    end = BASE + cells_x
    rows = cells_x + 2 * PAD
    lane = lane_of((rows, LANES))
    sub = lane & (SLOT - 1)
    lows = [jnp.zeros((rows, LANES), jnp.float32)] * 2
    highs = [jnp.zeros((rows, LANES), jnp.float32)] * 2
    blank = jnp.zeros((PAD - HALO, LANES), jnp.float32)
    for j in range(7):
        scale = 1.0 if 3 <= j < 6 else 0.5
        strips = [jnp.zeros((rows, LANES), jnp.float32)] * 2
        for z in range(LAYERS):
            if j < 3:
                body = e_ref[j, z] * scale
            elif j < 6:
                body = h_ref[j - 3, z]
            else:
                body = c_ref[z]
            rims = x_ref[j * LAYERS + z] * scale
            full = jnp.concatenate([blank, rims[HALO:], body, rims[:HALO], blank], 0)
            if j == 6:
                ext_ref[z, 0 : BASE - PAD, :] = jnp.zeros((BASE - PAD, LANES), jnp.float32)
                ext_ref[z, BASE - PAD : end + PAD, :] = full
                ext_ref[z, end + PAD : end + BASE, :] = jnp.zeros((BASE - PAD, LANES), jnp.float32)
            g, at = z % 2, (z // 2) * SLOT
            keep = (lane >= at) & (lane < at + 2 * WIDE)
            strips[g] = jnp.where(keep, rolled(full, at + WIDE), strips[g])
        for g in range(2):
            w_ref[j, g] = strips[g]
            a, b = divmod(2 * j + g, 8)
            keep = (sub >= 4 * b) & (sub < 4 * b + 4)
            lows[a] = jnp.where(keep, rolled(strips[g], 4 * b - 4), lows[a])
            highs[a] = jnp.where(keep, rolled(strips[g], 4 * b - 8), highs[a])
    for a in range(2):
        low_ref[a] = lows[a]
        high_ref[a] = highs[a]


def pack(e_field, h_field, coefficient, x_rims):
    cells_x = e_field.shape[2]
    rows = cells_x + 2 * PAD
    tall = cells_x + 2 * BASE
    f32 = jnp.float32
    return pl.pallas_call(
        pack_kernel,
        out_shape=(
            jax.ShapeDtypeStruct((LAYERS, tall, LANES), f32),
            jax.ShapeDtypeStruct((7, 2, rows, LANES), f32),
            jax.ShapeDtypeStruct((2, rows, LANES), f32),
            jax.ShapeDtypeStruct((2, rows, LANES), f32),
        ),
        compiler_params=pltpu.CompilerParams(vmem_limit_bytes=VMEM_LIMIT),
        name="pack",
    )(e_field, h_field, coefficient, x_rims)


def total(terms):
    out = None
    for sign, value in terms:
        if value is None:
            continue
        if out is None:
            out = value if sign > 0 else -value
        else:
            out = out + value if sign > 0 else out - value
    return out


def add(a, b):
    return total([(1, a), (1, b)])


def differ(a, b):
    return total([(1, a), (-1, b)])


def curl_of_e(e, e_z, e_x, e_y):
    return (
        differ(differ(e_z[1], e[1]), differ(e_y[2], e[2])),
        differ(differ(e_x[2], e[2]), differ(e_z[0], e[0])),
        differ(differ(e_y[0], e[0]), differ(e_x[1], e[1])),
    )


def curl_of_h(h, h_z, h_x, h_y):
    return (
        differ(differ(h[2], h_y[2]), differ(h[1], h_z[1])),
        differ(differ(h[0], h_z[0]), differ(h[2], h_x[2])),
        differ(differ(h[1], h_x[1]), differ(h[0], h_y[0])),
    )


def moved(value, shift):
    return None if value is None else rolled(value, shift)


class Tile:
    def __init__(self, ref, live):
        self.ref, self.live = ref, set(live)

    def load(self, j, z, start, size):
        return self.ref[j, z, start : start + size, :] if (j, z) in self.live else None

    def store(self, j, z, start, value):
        if value is not None:
            self.ref[j, z, start : start + value.shape[0], :] = value
            self.live.add((j, z))

    def step_h(self, z, start, size):
        e = [self.load(j, z, start, size) for j in range(3)]
        e_z = [self.load(j, z + 1, start, size) for j in range(2)] + [None]
        e_x = [None] + [self.load(j, z, start + 1, size) for j in (1, 2)]
        e_y = [moved(e[0], -1), None, moved(e[2], -1)]
        new = []
        for j, change in enumerate(curl_of_e(e, e_z, e_x, e_y)):
            new.append(add(self.load(3 + j, z, start, size), change))
            self.store(3 + j, z, start, new[j])
        return new

    def step_e(self, z, start, size, factor):
        h = [self.load(3 + j, z, start, size) for j in range(3)]
        h_z = [self.load(3 + j, z - 1, start, size) for j in range(2)] + [None]
        h_x = [None] + [self.load(3 + j, z, start - 1, size) for j in (1, 2)]
        h_y = [moved(h[0], 1), None, moved(h[2], 1)]
        new = []
        for j, change in enumerate(curl_of_h(h, h_z, h_x, h_y)):
            old = self.load(j, z, start, size)
            new.append(old if change is None else add(old, factor * change))
        return new


class Strip:
    def __init__(self, ref, rows):
        self.ref, self.start, self.rows = ref, BASE - PAD, rows
        self.lane = lane_of((rows, LANES))

    def load(self, j, g, by=0):
        return self.ref[j, g, self.start + by : self.start + by + self.rows, :]

    def store(self, j, g, value):
        self.ref[j, g, self.start : self.start + self.rows, :] = value

    def step_h(self, fresh=False):
        e = [[self.load(j, g) for j in range(3)] for g in range(2)]
        inside = self.lane < 2 * SLOT
        above = [
            [e[1][0], e[1][1], None],
            [jnp.where(inside, rolled(e[0][j], -SLOT), 0.0) for j in range(2)] + [None],
        ]
        for g in range(2):
            e_x = [None, self.load(1, g, 1), self.load(2, g, 1)]
            e_y = [rolled(e[g][0], -1), None, rolled(e[g][2], -1)]
            for j, change in enumerate(curl_of_e(e[g], above[g], e_x, e_y)):
                self.store(3 + j, g, change if fresh else self.load(3 + j, g) + change)

    def step_e(self, factor):
        h = [[self.load(3 + j, g) for j in range(3)] for g in range(2)]
        inside = self.lane >= SLOT
        below = [
            [jnp.where(inside, rolled(h[1][j], SLOT), 0.0) for j in range(2)] + [None],
            [h[0][0], h[0][1], None],
        ]
        new = []
        for g in range(2):
            h_x = [None, self.load(4, g, -1), self.load(5, g, -1)]
            h_y = [rolled(h[g][0], 1), None, rolled(h[g][2], 1)]
            change = curl_of_h(h[g], below[g], h_x, h_y)
            new.append([self.load(j, g) + factor[g] * change[j] for j in range(3)])
        return new

    def edges(self, j, g, cells_x):
        return picked(self.ref[j, g, BASE : BASE + cells_x, :], edge_matrix())


def picked(value, matrix):
    high = value.astype(jnp.bfloat16)
    rest = value - high.astype(jnp.float32)
    middle = rest.astype(jnp.bfloat16)
    low = (rest - middle.astype(jnp.float32)).astype(jnp.bfloat16)
    return dot32(high, matrix) + (dot32(middle, matrix) + dot32(low, matrix))


def matrix_of(pairs, columns):
    row = lax.broadcasted_iota(jnp.int32, (LANES, columns), 0)
    column = lax.broadcasted_iota(jnp.int32, (LANES, columns), 1)
    total = None
    for first_row, first_column, count in pairs:
        here = (column - row == first_column - first_row) & (column >= first_column)
        here = here & (column < first_column + count)
        total = here if total is None else total | here
    return jnp.where(total, 1.0, 0.0).astype(jnp.bfloat16)


def edge_matrix():
    pairs = []
    for slot in range(LAYERS // 2):
        pairs.append((slot * SLOT + 4, slot * LANES, HALO))
        pairs.append((slot * SLOT + 20, slot * LANES + LANES - HALO, HALO))
    return matrix_of(pairs, LAYERS // 2 * LANES)


def with_edges(value, edges, z):
    own = edges[:, (z // 2) * LANES : (z // 2 + 1) * LANES]
    lane = lane_of(own.shape)
    outer = (lane < HALO) | (lane >= LANES - HALO)
    return jnp.where(outer, own, value)


EVERY = [(j, z) for j in range(6) for z in range(LAYERS)]


def free_steps(tile, steps, start, rows, factor_of):
    for _ in range(steps):
        for z in range(LAYERS):
            tile.step_h(z, start, rows)
            for j, value in enumerate(tile.step_e(z, start, rows, factor_of(z))):
                tile.store(j, z, start, value)


def first_kernel(e_ref, h_ref, m_ref, _, c_ref, f_ref):
    cells_x = e_ref.shape[2]
    for z in range(LAYERS):
        c_ref[z] = coefficient_of(m_ref[z]) * 0.5
        for j in range(3):
            f_ref[j, z, PAD : PAD + cells_x, :] = e_ref[j, z] * 0.5
            f_ref[3 + j, z, PAD : PAD + cells_x, :] = h_ref[j, z]
        for j in range(6):
            f_ref[j, z, :PAD, :] = jnp.zeros((PAD, LANES), jnp.float32)
            f_ref[j, z, PAD + cells_x :, :] = jnp.zeros((PAD, LANES), jnp.float32)
    free_steps(Tile(f_ref, EVERY), STEPS // 2, PAD, cells_x, lambda z: c_ref[z])


def first_steps(e_field, h_field, material, after):
    cells_x = e_field.shape[2]
    f32 = jnp.float32
    vmem = pl.BlockSpec(memory_space=pltpu.VMEM)
    return pl.pallas_call(
        first_kernel,
        in_specs=[vmem, vmem, vmem, pl.BlockSpec(memory_space=pl.ANY)],
        out_shape=(
            jax.ShapeDtypeStruct((LAYERS, cells_x, LANES), f32),
            jax.ShapeDtypeStruct((6, LAYERS, cells_x + 2 * PAD, LANES), f32),
        ),
        compiler_params=pltpu.CompilerParams(vmem_limit_bytes=VMEM_LIMIT),
        name="first_steps",
    )(e_field, h_field, material, after)


def later_kernel(f_in, c_ref, e_ref, h_ref, x_ref, out_ref, f_ref, r_ref, rc_ref):
    cells_x = c_ref.shape[1]
    blank = jnp.zeros((PAD - HALO, LANES), jnp.float32)
    zero = jnp.zeros((8, LANES), jnp.float32)
    for j in range(7):
        scale = 1.0 if 3 <= j < 6 else 0.5
        for z in range(LAYERS):
            ref = e_ref.at[j, z] if j < 3 else h_ref.at[j - 3, z] if j < 6 else c_ref.at[z]
            own = 0.5 if j < 3 else 1.0
            rims = x_ref[j * LAYERS + z] * scale
            rows = [
                blank, rims[HALO:], ref[:8, :] * own, ref[cells_x - 8 :, :] * own, rims[:HALO], blank,
            ]
            to = r_ref.at[j, z] if j < 6 else rc_ref.at[z]
            to[...] = jnp.concatenate([zero] + rows + [zero], 0)
    edge = Tile(r_ref, EVERY)
    free_steps(edge, STEPS, 8, 32, lambda z: rc_ref[z, 8:40, :])
    f_ref[...] = f_in[...]
    tile = Tile(f_ref, EVERY)
    free_steps(tile, STEPS - STEPS // 2, PAD, cells_x, lambda z: c_ref[z])
    row = lax.broadcasted_iota(jnp.int32, (8, LANES), 0)
    for j, z in EVERY:
        top = jnp.where(row < HALO, r_ref[j, z, 16:24, :], f_ref[j, z, PAD : PAD + 8, :])
        end = f_ref[j, z, PAD + cells_x - 8 : PAD + cells_x, :]
        end = jnp.where(row >= HALO, r_ref[j, z, 24:32, :], end)
        inner = f_ref[j, z, PAD + 8 : PAD + cells_x - 8, :]
        out_ref[j, z] = jnp.concatenate([top, inner, end], 0)


def later_steps(state, coefficient, e_field, h_field, x_rims):
    cells_x = e_field.shape[2]
    f32 = jnp.float32
    return pl.pallas_call(
        later_kernel,
        out_shape=jax.ShapeDtypeStruct((6, LAYERS, cells_x, LANES), f32),
        scratch_shapes=[
            pltpu.VMEM(state.shape, f32),
            pltpu.VMEM((6, LAYERS, 48, LANES), f32),
            pltpu.VMEM((LAYERS, 48, LANES), f32),
        ],
        compiler_params=pltpu.CompilerParams(vmem_limit_bytes=VMEM_LIMIT),
        name="later_steps",
    )(state, coefficient, e_field, h_field, x_rims)


def strip_kernel(w_ref, low_ref, high_ref, free_ref, _, factor_ref, out_ref, s_ref):
    rows = w_ref.shape[2]
    first = BASE - PAD
    lane = lane_of((rows, LANES))
    sub = lane & (SLOT - 1)
    factor = [None, None]
    for j in range(7):
        for g in range(2):
            a, b = divmod(2 * j + g, 8)
            mine = w_ref[j, g]
            value = jnp.where(sub < 16, rolled(mine, -4), rolled(mine, 16))
            value = jnp.where(sub < 4, rolled(low_ref[a], -4 * b), value)
            value = jnp.where((sub >= 24) & (sub < 28), rolled(high_ref[a], 24 - 4 * b), value)
            if j < 6:
                s_ref[j, g, first : first + rows, :] = value
            else:
                factor[g] = value
                factor_ref[g] = value
    strip = Strip(s_ref, rows)
    for step in range(STEPS):
        strip.step_h()
        new = strip.step_e([factor_ref[g] for g in range(2)])
        for g in range(2):
            for j in range(3):
                strip.store(j, g, new[g][j])
    for j in range(6):
        for g in range(2):
            edges = strip.edges(j, g, out_ref.shape[2])
            for z in range(g, LAYERS, 2):
                out_ref[j, z] = with_edges(free_ref[j, z], edges, z)


def strip_run(own_edges, low, high, free, after):
    rows = own_edges.shape[2]
    f32 = jnp.float32
    return pl.pallas_call(
        strip_kernel,
        in_specs=[pl.BlockSpec(memory_space=pltpu.VMEM)] * 4 + [pl.BlockSpec(memory_space=pl.ANY)],
        out_shape=(
            jax.ShapeDtypeStruct((2, rows, LANES), f32),
            jax.ShapeDtypeStruct(free.shape, f32),
        ),
        scratch_shapes=[pltpu.VMEM((6, 2, rows + 2 * (BASE - PAD), LANES), f32)],
        compiler_params=pltpu.CompilerParams(vmem_limit_bytes=VMEM_LIMIT),
        name="strip_run",
    )(own_edges, low, high, free, after)


def response_kernel(
    place_ref, c_ref, factor_ref, free_ref, mine_ref, other_ref, e_out, h_out,
    f_ref, s_ref, plane_ref, rim_ref, done_ref, sems,
):
    cells_x = e_out.shape[2]
    copies = []

    def send(j, z, source):
        to = e_out.at[j, z] if j < 3 else h_out.at[j - 3, z]
        copies.append(pltpu.make_async_copy(source, to, sems.at[j, z]))
        copies[-1].start()

    far = [(j, z) for j, z in EVERY if z >= ZINJ + STEPS - (0 if j < 2 else 1)]
    for j, z in far:
        if j < 3:
            done_ref[j, z] = free_ref[j, z] * 2.0
            send(j, z, done_ref.at[j, z])
        else:
            send(j, z, free_ref.at[j, z])
    rows = cells_x + 2 * PAD
    half = rows // 2
    first = BASE - PAD
    own = place_ref[0]
    near = matrix_of([(0, 4, WIDE), (LANES - WIDE, 16, WIDE)], LANES)
    outside = matrix_of(
        [(0, 0, HALO), (4, 24, HALO), (8, LANES, HALO), (12, LANES + 24, HALO)], 2 * LANES
    )
    lane = lane_of((half, LANES))
    for ref, which in ((mine_ref, own), (other_ref, 1 - own)):
        at = pl.ds(pl.multiple_of(which * half, 8), half)
        outer = jnp.where(lane < 16, unfolded(ref[2 * half :, :], half, 8, 0), 0.0)
        outer = picked(outer, outside)
        for part in range(2):
            plane = ref[part * half : (part + 1) * half, :]
            plane_ref[part, at, :] = plane
            own_part = outer[:, part * LANES : (part + 1) * LANES]
            rim_ref[part, at, :] = picked(plane, near) + own_part

    def injection(ref, step, start, size):
        cosine = 0.5 * COURANT * math.cos(OMEGA * step)
        sine = 0.5 * COURANT * math.sin(OMEGA * step)
        re, im = ref[0, start : start + size, :], ref[1, start : start + size, :]
        return [cosine * re - sine * im, sine * re + cosine * im, None]

    tile = Tile(f_ref, ())
    for j, value in enumerate(injection(plane_ref, 1, 0, rows)):
        tile.store(j, ZINJ, first, value)
    strip = Strip(s_ref, rows)
    s_ref[...] = jnp.zeros_like(s_ref)
    for j, value in enumerate(injection(rim_ref, 1, 0, rows)[:2]):
        strip.store(j, ZINJ % 2, value)
    for step in range(2, STEPS + 1):
        strip.step_h()
        new = strip.step_e([factor_ref[g] for g in range(2)])
        source = injection(rim_ref, step, 0, rows)
        for g in range(2):
            for j in range(3):
                value = add(new[g][j], source[j] if g == ZINJ % 2 else None)
                strip.store(j, g, value)
    edges = {(j, g): strip.edges(j, g, cells_x) for j in range(6) for g in range(2)}
    for step in range(2, STEPS + 1):
        last = step == STEPS
        start, size = (BASE, cells_x) if last else (first, rows)
        for z in range(LAYERS):
            tile.step_h(z, first, rows - (PAD if last else 0))
            new = tile.step_e(z, start, size, c_ref[z, start : start + size, :])
            if z == ZINJ:
                source = injection(plane_ref, step, start - first, size)
                new = [add(a, b) for a, b in zip(new, source)]
            for j in range(3):
                if not last:
                    tile.store(j, z, start, new[j])
                    continue
                for i, value in ((j, new[j]), (3 + j, tile.load(3 + j, z, start, size))):
                    if (i, z) in far:
                        continue
                    value = with_edges(value, edges[i, z % 2], z) + free_ref[i, z]
                    done_ref[i, z] = value * 2.0 if i < 3 else value
                    send(i, z, done_ref.at[i, z])
    for copy in copies:
        copy.wait()


def response(place, c_ext, factor, free, mine, other, cells_x):
    rows = cells_x + 2 * PAD
    tall = cells_x + 2 * BASE
    f32 = jnp.float32
    out = jax.ShapeDtypeStruct((3, LAYERS, cells_x, LANES), f32)
    vmem = pl.BlockSpec(memory_space=pltpu.VMEM)
    return pl.pallas_call(
        response_kernel,
        in_specs=[pl.BlockSpec(memory_space=pltpu.SMEM)] + [vmem] * 5,
        out_specs=(pl.BlockSpec(memory_space=pl.ANY),) * 2,
        out_shape=(out, out),
        scratch_shapes=[
            pltpu.VMEM((6, LAYERS, tall, LANES), f32),
            pltpu.VMEM((6, 2, tall, LANES), f32),
            pltpu.VMEM((2, rows, LANES), f32),
            pltpu.VMEM((2, rows, LANES), f32),
            pltpu.VMEM((6, LAYERS, cells_x, LANES), f32),
            pltpu.SemaphoreType.DMA((6, LAYERS)),
        ],
        compiler_params=pltpu.CompilerParams(vmem_limit_bytes=VMEM_LIMIT),
        name="response",
    )(place, c_ext, factor, free, mine, other)


def along(block, axis, distance):
    n = lax.axis_size(axis)
    return lax.ppermute(block, axis, [((i - distance) % n, i) for i in range(n)])


def flipped(block, axis, bits):
    return lax.ppermute(block, axis, [(i, i ^ bits) for i in range(lax.axis_size(axis))])


def to_groups(block, n_src, n_tx, flip, distance):
    route = []
    for s in range(n_src):
        for t in range(n_tx):
            route.append((s * n_tx + t, (s ^ flip) * n_tx + (t + distance) % n_tx))
    return lax.ppermute(block, ("src", "tx"), route)


def per_device(orders, offsets, material, e_field, h_field):
    cols_ky = orders.shape[3]
    layers, cells_x, cells_y = material.shape
    n_src, n_tx, n_ty = lax.axis_size("src"), lax.axis_size("tx"), lax.axis_size("ty")
    half = cells_x // 2 + PAD
    place = jnp.stack([lax.axis_index("src"), lax.axis_index("tx"), lax.axis_index("ty")]).astype(
        jnp.int32
    )

    parts = x_stage(place, offsets.T, jnp.swapaxes(orders, 2, 3), n_tx, cells_x)
    received = []
    for distance in range(n_tx):
        for flip in range(n_src):
            if distance or flip:
                part = parts[2 * distance + flip]
                received.append(to_groups(part, n_src, n_tx, flip, distance))
    coefficient, state = first_steps(e_field, h_field, material, parts)

    rims = x_rims_of(e_field, h_field, material)
    if n_tx == 2:
        x_rims = along(rims, "tx", 1)
    else:
        top, bottom = rims[:, :HALO], rims[:, HALO:]
        x_rims = jnp.concatenate([along(top, "tx", -1), along(bottom, "tx", 1)], 1)
    block = summed(parts, received, state)
    c_ext, own_edges, to_high, to_low = pack(e_field, h_field, coefficient, x_rims)
    low = along(to_high, "ty", 1)
    high = along(to_low, "ty", -1)
    free = later_steps(state, coefficient, e_field, h_field, x_rims)

    blocks = {0: block}
    for bits in range(n_ty - 2, 0, -2):
        blocks[bits] = flipped(block, "ty", bits)
    for bits in range(0, n_ty, 2):
        blocks[bits + 1] = flipped(blocks[bits], "ty", 1)
    mine = y_stage(place, [blocks[b] for b in range(n_ty)], cols_ky, cells_y, half, free)
    other = flipped(mine, "src", 1)
    factor, free = strip_run(own_edges, low, high, free, mine)
    return response(place, c_ext, factor, free, mine, other, cells_x)


def solution(mesh):
    in_specs = (
        P("src", None, "tx", "ty"),
        P("src", None),
        P(None, "tx", "ty"),
        P(None, None, "tx", "ty"),
        P(None, None, "tx", "ty"),
    )
    out_specs = (P(None, None, "tx", "ty"), P(None, None, "tx", "ty"))
    return jax.shard_map(
        per_device, mesh=mesh, in_specs=in_specs, out_specs=out_specs, check_vma=False
    )
```

```python
import functools
import math

import jax
import jax.numpy as jnp
import ml_dtypes
import numpy as np
from jax import lax
from jax.experimental import pallas as pl
from jax.experimental.pallas import tpu as pltpu
from jax.sharding import PartitionSpec as P

MX = 512
MY = 512
STEPS = 4
ZINJ = 1
LAYERS = 6

COURANT = 0.5
OMEGA = 0.7
PERMITTIVITY = (1.0, 2.6, 11.9, 2.1)

REACH = 8
SPAN = 2 * REACH
PAD = 8
HALO = 4
BASE = 16
SLOT = 32
WIDE = 8
LANES = 128
VMEM_LIMIT = 24 * 1024 * 1024


def split_bf16(table):
    high = table.astype(ml_dtypes.bfloat16)
    low = (table - high.astype(np.float64)).astype(ml_dtypes.bfloat16)
    return high, low


def padded(lanes):
    return -(-lanes // LANES) * LANES


@functools.lru_cache(maxsize=None)
def x_seeds(n_tx, rows_kx, cells_x):
    window = rows_kx + SPAN
    wide = padded(window)
    full = cells_x * n_tx
    turns = [8 << k for k in range((cells_x // 8).bit_length())]
    count = 8 + len(turns) + n_tx
    table = np.zeros((n_tx, -(-count // 8) * 8, 2 * wide), np.float32)
    for own in range(n_tx):
        freq = own * rows_kx - MX // 2 - REACH + np.arange(window)
        tiles = [(own + distance) % n_tx * cells_x for distance in range(n_tx)]
        x = np.array(list(range(-PAD, 8 - PAD)) + turns + tiles)
        angle = np.mod(x[:, None] * freq[None, :], full) * (2.0 * math.pi / full)
        table[own, :count, :window] = np.cos(angle)
        table[own, :count, wide : wide + window] = np.sin(angle)
    return table, len(turns)


@functools.lru_cache(maxsize=None)
def y_tables(n_ty, cols_ky, cells_y):
    full = cells_y * n_ty
    window = cols_ky + SPAN
    edge = np.concatenate([np.arange(-HALO, 0), cells_y + np.arange(HALO)])
    y = np.concatenate([np.arange(cells_y), edge])
    table = np.zeros((n_ty, LANES + 2 * SPAN, 2 * cells_y + LANES))
    for block in range(n_ty):
        freq = block * cols_ky - MY // 2 - REACH + np.arange(window)
        angle = np.mod(freq[:, None] * y[None, :], full) * (2.0 * math.pi / full)
        cos, sin = np.cos(angle), np.sin(angle)

        def placed(re_cols, im_cols):
            out = np.zeros((window, 2 * cells_y + LANES))
            out[:, :cells_y] = re_cols[:, :cells_y]
            out[:, cells_y : 2 * cells_y] = im_cols[:, :cells_y]
            out[:, 2 * cells_y : 2 * cells_y + 2 * HALO] = re_cols[:, cells_y:]
            out[:, 2 * cells_y + 2 * HALO : 2 * cells_y + 4 * HALO] = im_cols[:, cells_y:]
            return out

        from_re = placed(cos, sin)
        from_im = placed(-sin, cos)
        table[block, :cols_ky] = from_re[:cols_ky]
        table[block, cols_ky : 2 * cols_ky] = from_im[:cols_ky]
        table[block, LANES : LANES + SPAN] = from_re[cols_ky:]
        table[block, LANES + SPAN :] = from_im[cols_ky:]
    return split_bf16(table)


@functools.lru_cache(maxsize=None)
def y_phases(n_ty, cols_ky, cells_y):
    full = cells_y * n_ty
    out = np.zeros((n_ty, n_ty, 8, LANES), np.float32)
    for own in range(n_ty):
        for block in range(n_ty):
            freq = block * cols_ky - MY // 2 - REACH + np.arange(cols_ky + SPAN)
            angle = np.mod(freq * own * cells_y, full) * (2.0 * math.pi / full)
            cos, sin = np.cos(angle), np.sin(angle)
            out[own, block, 0, :cols_ky] = cos[:cols_ky]
            out[own, block, 0, cols_ky : 2 * cols_ky] = cos[:cols_ky]
            out[own, block, 1, :cols_ky] = -sin[:cols_ky]
            out[own, block, 1, cols_ky : 2 * cols_ky] = sin[:cols_ky]
            for group in range(LANES // (2 * SPAN)):
                at = group * 2 * SPAN
                out[own, block, 2, at : at + SPAN] = cos[cols_ky:]
                out[own, block, 2, at + SPAN : at + 2 * SPAN] = cos[cols_ky:]
                out[own, block, 3, at : at + SPAN] = -sin[cols_ky:]
                out[own, block, 3, at + SPAN : at + 2 * SPAN] = sin[cols_ky:]
    return out


def lane_of(shape):
    return lax.broadcasted_iota(jnp.int32, shape, len(shape) - 1)


def rolled(value, shift):
    shift = shift % LANES
    return value if shift == 0 else pltpu.roll(value, shift, 1)


def halves(value):
    high = value.astype(jnp.bfloat16)
    low = (value - high.astype(jnp.float32)).astype(jnp.bfloat16)
    return high, low


def dot32(a, b):
    return jnp.dot(a, b, preferred_element_type=jnp.float32)


def fold_groups(rows, count):
    tiles = rows // 8
    sizes = [8 * (tiles // count + (1 if g < tiles % count else 0)) for g in range(count)]
    starts = [sum(sizes[:g]) for g in range(count)]
    return list(zip(starts, sizes))


def folded_rows(rows, count):
    return fold_groups(rows, count)[0][1]


def folded(value, count):
    groups = fold_groups(value.shape[0], count)
    tall, wide = groups[0][1], LANES // count
    lane = lane_of((tall, LANES))
    total = jnp.zeros((tall, LANES), value.dtype)
    for g, (start, size) in enumerate(groups):
        part = value[start : start + size]
        if size < tall:
            part = jnp.concatenate([part, jnp.zeros((tall - size, LANES), value.dtype)], 0)
        keep = (lane >= wide * g) & (lane < wide * (g + 1))
        total = jnp.where(keep, rolled(part, wide * g), total)
    return total


def unfolded(value, rows, count, at):
    wide = LANES // count
    parts = []
    for g, (_, size) in enumerate(fold_groups(rows, count)):
        parts.append(rolled(value[:size], at - wide * g))
    return jnp.concatenate(parts, 0)


def turned(cos, sin, by_cos, by_sin):
    return cos * by_cos - sin * by_sin, sin * by_cos + cos * by_sin


def fill_table(n_turns, seed_ref, high_ref, low_ref):
    n_tx, rows, both = high_ref.shape
    wide = both // 2

    def row(i):
        return seed_ref[i : i + 1, :wide], seed_ref[i : i + 1, wide:]

    cos, sin = seed_ref[:8, :wide], seed_ref[:8, wide:]
    for k in range(n_turns):
        more = min(8 << k, rows - (8 << k))
        new = turned(cos[:more], sin[:more], *row(8 + k))
        cos, sin = jnp.concatenate([cos, new[0]], 0), jnp.concatenate([sin, new[1]], 0)
    for distance in range(n_tx):
        there = turned(cos, sin, *row(8 + n_turns + distance))
        for part in range(2):
            high, low = halves(there[part])
            high_ref[distance, :, part * wide : (part + 1) * wide] = high
            low_ref[distance, :, part * wide : (part + 1) * wide] = low


def x_kernel(
    n_turns, place_ref, offs_in, orders_in, seeds_in, out_ref, token_ref,
    offs_ref, orders_ref, seed_ref, wh_ref, wl_ref, line_ref, acc_ref, q_ref, sems,
):
    own = place_ref[0]
    copies = [
        pltpu.make_async_copy(seeds_in.at[place_ref[1]], seed_ref, sems.at[0]),
        pltpu.make_async_copy(orders_in, orders_ref, sems.at[1]),
        pltpu.make_async_copy(offs_in, offs_ref, sems.at[2]),
    ]
    for copy in copies:
        copy.start()
    points, _, cols_ky, rows_kx = orders_ref.shape
    n_tx, rows, both = wh_ref.shape
    half = rows // 2
    acc_ref[...] = jnp.zeros_like(acc_ref)
    line_ref[...] = jnp.zeros_like(line_ref)
    token_ref[...] = jnp.zeros_like(token_ref)
    wide = line_ref.shape[4]
    copies[0].wait()
    fill_table(n_turns, seed_ref, wh_ref, wl_ref)
    copies[1].wait()
    copies[2].wait()
    for point in range(points):
        down = offs_ref[0, point] + REACH
        across = offs_ref[1, point] + REACH
        for part in range(2):
            for tile in range(rows_kx // wide):
                lanes = slice(tile * wide, (tile + 1) * wide)
                line = line_ref.at[point, part, tile]
                line[pl.ds(across, cols_ky), :] = orders_ref[point, part, :, lanes]
                acc_ref[part, pl.ds(down + tile * wide, wide), :] += line[...].T
    s_re = acc_ref[0]
    s_im = acc_ref[1]
    lane = lane_of(s_re.shape)
    re_by, im_by = rolled(s_re, cols_ky), rolled(s_im, cols_ky)

    def main(re, im_by):
        out = jnp.where(lane < cols_ky, re, im_by)
        return out if 2 * cols_ky == LANES else jnp.where(lane < 2 * cols_ky, out, 0.0)

    def spill(re_back, im_back):
        out = jnp.where(lane < SPAN, re_back, im_back)
        return jnp.where(lane < 2 * SPAN, out, 0.0)

    same = 2 * cols_ky == LANES
    re_back = re_by if same else rolled(s_re, -cols_ky)
    im_back = im_by if same else rolled(s_im, -cols_ky)
    top = [main(s_re, im_by), spill(re_back, rolled(s_im, SPAN - cols_ky))]
    bottom = [main(-s_im, re_by), spill(-im_back, rolled(s_re, SPAN - cols_ky))]
    right = jnp.concatenate([jnp.concatenate(top, 1), jnp.concatenate(bottom, 1)], 0)
    right_h, right_l = halves(right)
    for distance in range(n_tx):
        w_h = wh_ref[distance]
        q_ref[...] = dot32(w_h, right_h) + (dot32(wl_ref[distance], right_h) + dot32(w_h, right_l))
        for flip in range(2):
            start = pl.multiple_of((own ^ flip) * half, 8)
            block = q_ref[pl.ds(start, half), :]
            out_ref[2 * distance + flip, :half, :] = block[:, :LANES]
            out_ref[2 * distance + flip, half:, :] = folded(block[:, LANES:], 4)


def x_stage(place, offsets, orders, n_tx, cells_x):
    points, _, cols_ky, rows_kx = orders.shape
    wide = min(rows_kx, LANES)
    seeds, n_turns = x_seeds(n_tx, rows_kx, cells_x)
    rows = cells_x + 2 * PAD
    half = rows // 2
    height = half + folded_rows(half, 4)
    f32 = jnp.float32
    table = pltpu.VMEM((n_tx, rows, seeds.shape[2]), jnp.bfloat16)
    return pl.pallas_call(
        functools.partial(x_kernel, n_turns),
        in_specs=[pl.BlockSpec(memory_space=pltpu.SMEM)] + [pl.BlockSpec(memory_space=pl.ANY)] * 3,
        out_shape=(
            jax.ShapeDtypeStruct((2 * n_tx, height, LANES), f32),
            jax.ShapeDtypeStruct((8, LANES), f32),
        ),
        scratch_shapes=[
            pltpu.SMEM(offsets.shape, jnp.int32),
            pltpu.VMEM(orders.shape, f32),
            pltpu.VMEM(seeds.shape[1:], f32),
            table,
            table,
            pltpu.VMEM((points, 2, rows_kx // wide, LANES, wide), f32),
            pltpu.VMEM((2, seeds.shape[2] // 2, LANES), f32),
            pltpu.VMEM((rows, 2 * LANES), f32),
            pltpu.SemaphoreType.DMA((3,)),
        ],
        compiler_params=pltpu.CompilerParams(vmem_limit_bytes=VMEM_LIMIT),
        name="x_stage",
    )(place, offsets, orders, jnp.asarray(seeds))


def sum_kernel(*refs):
    *part_refs, _, out_ref = refs
    total = part_refs[0][0]
    for ref in part_refs[1:]:
        total = total + ref[...]
    out_ref[...] = total


def summed(parts, received, after):
    return pl.pallas_call(
        sum_kernel,
        out_shape=jax.ShapeDtypeStruct(parts.shape[1:], jnp.float32),
        compiler_params=pltpu.CompilerParams(vmem_limit_bytes=VMEM_LIMIT),
        name="sum_parts",
    )(parts, *received, after)


def y_kernel(cols_ky, half, place_ref, *refs):
    *block_refs, th_ref, tl_ref, phase_ref, _, out_ref = refs
    n_ty = len(block_refs)
    lane = lane_of((half, LANES))
    mains, spills, numbers = [], [], []
    for number, ref in enumerate(block_refs):
        block = place_ref[2] ^ number
        numbers.append(block)
        phase = phase_ref[block]
        main = ref[:half, :]
        if 2 * cols_ky == LANES:
            swapped = rolled(main, cols_ky)
        else:
            swapped = jnp.where(lane < cols_ky, rolled(main, -cols_ky), rolled(main, cols_ky))
        mains.append(main * phase[0:1] + swapped * phase[1:2])
        spill = ref[half:, :]
        small = lane_of(spill.shape)
        other = jnp.where((small & (2 * SPAN - 1)) < SPAN, rolled(spill, -SPAN), rolled(spill, SPAN))
        spills.append(spill * phase[2:3] + other * phase[3:4])
    packed = []
    for first in range(0, n_ty, 4):
        total = None
        for g in range(4):
            part = unfolded(spills[first + g], half, 4, 32 * g)
            total = part if total is None else jnp.where(lane >= 32 * g, part, total)
        packed.append(total)
    result = None
    for first in range(0, n_ty, 2):
        left_h, left_l = halves(jnp.concatenate(mains[first : first + 2], 1))
        t_h = jnp.concatenate([th_ref[numbers[first + g], :LANES, :] for g in range(2)], 0)
        t_l = jnp.concatenate([tl_ref[numbers[first + g], :LANES, :] for g in range(2)], 0)
        part = dot32(left_h, t_h) + (dot32(left_h, t_l) + dot32(left_l, t_h))
        result = part if result is None else result + part
    for first in range(0, n_ty, 8):
        left_h, left_l = halves(jnp.concatenate(packed[first // 4 : first // 4 + 2], 1))
        t_h = jnp.concatenate([th_ref[numbers[first + g], LANES:, :] for g in range(8)], 0)
        t_l = jnp.concatenate([tl_ref[numbers[first + g], LANES:, :] for g in range(8)], 0)
        result = result + (dot32(left_h, t_h) + (dot32(left_h, t_l) + dot32(left_l, t_h)))
    out_ref[:half, :] = result[:, :LANES]
    out_ref[half : 2 * half, :] = result[:, LANES : 2 * LANES]
    out_ref[2 * half :, :] = folded(result[:, 2 * LANES :], 8)


def y_stage(place, blocks, cols_ky, cells_y, half, after):
    n_ty = len(blocks)
    t_h, t_l = y_tables(n_ty, cols_ky, cells_y)
    phases = y_phases(n_ty, cols_ky, cells_y)
    whole = lambda shape: pl.BlockSpec(shape, lambda i, place: (0,) * len(shape))
    height = 2 * half + folded_rows(half, 8)
    return pl.pallas_call(
        functools.partial(y_kernel, cols_ky, half),
        grid_spec=pltpu.PrefetchScalarGridSpec(
            num_scalar_prefetch=1,
            grid=(1,),
            in_specs=[whole(b.shape) for b in blocks]
            + [
                whole(t_h.shape),
                whole(t_l.shape),
                pl.BlockSpec((None,) + phases.shape[1:], lambda i, place: (place[2], 0, 0, 0)),
                whole(after.shape),
            ],
            out_specs=whole((height, LANES)),
        ),
        out_shape=jax.ShapeDtypeStruct((height, LANES), jnp.float32),
        compiler_params=pltpu.CompilerParams(vmem_limit_bytes=VMEM_LIMIT),
        name="y_stage",
    )(place, *blocks, jnp.asarray(t_h), jnp.asarray(t_l), jnp.asarray(phases), after)


def coefficient_of(material):
    value = jnp.where(material == 0, COURANT / PERMITTIVITY[0], COURANT / PERMITTIVITY[1])
    value = jnp.where(material == 2, COURANT / PERMITTIVITY[2], value)
    return jnp.where(material == 3, COURANT / PERMITTIVITY[3], value).astype(jnp.float32)


def rim_kernel(e_ref, h_ref, m_ref, _, out_ref, edge_ref, last_ref, sems):
    cells_x = e_ref.shape[2]
    copies = []
    for i, ref in enumerate((e_ref, h_ref)):
        for k, start in enumerate((0, cells_x - 8)):
            here = edge_ref.at[i, k]
            source = ref.at[:, :, pl.ds(start, 8), :]
            copies.append(pltpu.make_async_copy(source, here, sems.at[i, k]))
    for k, start in enumerate((0, cells_x - 8)):
        source = m_ref.at[:, pl.ds(start, 8), :]
        copies.append(pltpu.make_async_copy(source, last_ref.at[k], sems.at[2, k]))
    for copy in copies:
        copy.start()
    for copy in copies:
        copy.wait()
    row = lax.broadcasted_iota(jnp.int32, (LAYERS, 8, LANES), 1)
    for j in range(7):
        if j < 6:
            first, final = (edge_ref[j // 3, k, j % 3] for k in range(2))
        else:
            first, final = (coefficient_of(last_ref[k]) for k in range(2))
        out_ref[j * LAYERS : (j + 1) * LAYERS] = jnp.where(row < HALO, first, final)


def x_rims_of(e_field, h_field, material, after):
    far = pl.BlockSpec(memory_space=pl.ANY)
    f32 = jnp.float32
    return pl.pallas_call(
        rim_kernel,
        in_specs=[far, far, far, pl.BlockSpec(memory_space=pltpu.VMEM)],
        out_shape=jax.ShapeDtypeStruct((7 * LAYERS, 2 * HALO, LANES), f32),
        scratch_shapes=[
            pltpu.VMEM((2, 2, 3, LAYERS, 8, LANES), f32),
            pltpu.VMEM((2, LAYERS, 8, LANES), jnp.int32),
            pltpu.SemaphoreType.DMA((3, 2)),
        ],
        compiler_params=pltpu.CompilerParams(vmem_limit_bytes=VMEM_LIMIT),
        name="x_rims",
    )(e_field, h_field, material, after)


def pack_kernel(e_ref, h_ref, c_ref, x_ref, ext_ref, w_ref, low_ref, high_ref):
    cells_x = e_ref.shape[2]
    end = BASE + cells_x
    rows = cells_x + 2 * PAD
    lane = lane_of((rows, LANES))
    sent = [None, None]
    blank = jnp.zeros((PAD - HALO, LANES), jnp.float32)
    for j in range(7):
        scale = 1.0 if 3 <= j < 6 else 0.5
        strips = [jnp.zeros((rows, LANES), jnp.float32)] * 2
        planes = [[], []]
        for z in range(LAYERS):
            if j < 3:
                body = e_ref[j, z] * scale
            elif j < 6:
                body = h_ref[j - 3, z]
            else:
                body = c_ref[z]
            rims = x_ref[j * LAYERS + z] * scale
            full = jnp.concatenate([blank, rims[HALO:], body, rims[:HALO], blank], 0)
            if j == 6:
                ext_ref[z, 0 : BASE - PAD, :] = jnp.zeros((BASE - PAD, LANES), jnp.float32)
                ext_ref[z, BASE - PAD : end + PAD, :] = full
                ext_ref[z, end + PAD : end + BASE, :] = jnp.zeros((BASE - PAD, LANES), jnp.float32)
            g, at = z % 2, (z // 2) * SLOT
            if j in BY_PRODUCT:
                planes[g].append(full)
                continue
            keep = (lane >= at) & (lane < at + 2 * WIDE)
            strips[g] = jnp.where(keep, rolled(full, at + WIDE), strips[g])
        for g in range(2):
            if j in BY_PRODUCT:
                strips[g] = picked(jnp.concatenate(planes[g], 1), column_matrix())
            w_ref[j, g] = strips[g]
        a = j // 4
        added = picked(jnp.concatenate(strips, 1), message_matrix(j % 4))
        sent[a] = added if sent[a] is None else sent[a] + added
    for a in range(2):
        low_ref[a] = sent[a][:, :LANES]
        high_ref[a] = sent[a][:, LANES:]


def pack(e_field, h_field, coefficient, x_rims):
    cells_x = e_field.shape[2]
    rows = cells_x + 2 * PAD
    tall = cells_x + 2 * BASE
    f32 = jnp.float32
    return pl.pallas_call(
        pack_kernel,
        out_shape=(
            jax.ShapeDtypeStruct((LAYERS, tall, LANES), f32),
            jax.ShapeDtypeStruct((7, 2, rows, LANES), f32),
            jax.ShapeDtypeStruct((2, rows, LANES), f32),
            jax.ShapeDtypeStruct((2, rows, LANES), f32),
        ),
        compiler_params=pltpu.CompilerParams(vmem_limit_bytes=VMEM_LIMIT),
        name="pack",
    )(e_field, h_field, coefficient, x_rims)


def total(terms):
    out = None
    for sign, value in terms:
        if value is None:
            continue
        if out is None:
            out = value if sign > 0 else -value
        else:
            out = out + value if sign > 0 else out - value
    return out


def add(a, b):
    return total([(1, a), (1, b)])


def differ(a, b):
    return total([(1, a), (-1, b)])


def curl_of_e(e, e_z, e_x, e_y):
    return (
        differ(differ(e_z[1], e[1]), differ(e_y[2], e[2])),
        differ(differ(e_x[2], e[2]), differ(e_z[0], e[0])),
        differ(differ(e_y[0], e[0]), differ(e_x[1], e[1])),
    )


def curl_of_h(h, h_z, h_x, h_y):
    return (
        differ(differ(h[2], h_y[2]), differ(h[1], h_z[1])),
        differ(differ(h[0], h_z[0]), differ(h[2], h_x[2])),
        differ(differ(h[1], h_x[1]), differ(h[0], h_y[0])),
    )


def moved(value, shift):
    return None if value is None else rolled(value, shift)


class Tile:
    def __init__(self, ref, live):
        self.ref, self.live = ref, set(live)

    def load(self, j, z, start, size):
        return self.ref[j, z, start : start + size, :] if (j, z) in self.live else None

    def store(self, j, z, start, value):
        if value is not None:
            self.ref[j, z, start : start + value.shape[0], :] = value
            self.live.add((j, z))

    def step_h(self, z, start, size):
        e = [self.load(j, z, start, size) for j in range(3)]
        e_z = [self.load(j, z + 1, start, size) for j in range(2)] + [None]
        e_x = [None] + [self.load(j, z, start + 1, size) for j in (1, 2)]
        e_y = [moved(e[0], -1), None, moved(e[2], -1)]
        new = []
        for j, change in enumerate(curl_of_e(e, e_z, e_x, e_y)):
            new.append(add(self.load(3 + j, z, start, size), change))
            self.store(3 + j, z, start, new[j])
        return new

    def step_e(self, z, start, size, factor):
        h = [self.load(3 + j, z, start, size) for j in range(3)]
        h_z = [self.load(3 + j, z - 1, start, size) for j in range(2)] + [None]
        h_x = [None] + [self.load(3 + j, z, start - 1, size) for j in (1, 2)]
        h_y = [moved(h[0], 1), None, moved(h[2], 1)]
        new = []
        for j, change in enumerate(curl_of_h(h, h_z, h_x, h_y)):
            old = self.load(j, z, start, size)
            new.append(old if change is None else add(old, factor * change))
        return new


class Strip:
    def __init__(self, ref, rows):
        self.ref, self.start, self.rows = ref, BASE - PAD, rows
        self.lane = lane_of((rows, LANES))

    def load(self, j, g, by=0):
        return self.ref[j, g, self.start + by : self.start + by + self.rows, :]

    def store(self, j, g, value):
        self.ref[j, g, self.start : self.start + self.rows, :] = value

    def step_h(self, fresh=False):
        e = [[self.load(j, g) for j in range(3)] for g in range(2)]
        inside = self.lane < 2 * SLOT
        above = [
            [e[1][0], e[1][1], None],
            [jnp.where(inside, rolled(e[0][j], -SLOT), 0.0) for j in range(2)] + [None],
        ]
        for g in range(2):
            e_x = [None, self.load(1, g, 1), self.load(2, g, 1)]
            e_y = [rolled(e[g][0], -1), None, rolled(e[g][2], -1)]
            for j, change in enumerate(curl_of_e(e[g], above[g], e_x, e_y)):
                self.store(3 + j, g, change if fresh else self.load(3 + j, g) + change)

    def step_e(self, factor):
        h = [[self.load(3 + j, g) for j in range(3)] for g in range(2)]
        inside = self.lane >= SLOT
        below = [
            [jnp.where(inside, rolled(h[1][j], SLOT), 0.0) for j in range(2)] + [None],
            [h[0][0], h[0][1], None],
        ]
        new = []
        for g in range(2):
            h_x = [None, self.load(4, g, -1), self.load(5, g, -1)]
            h_y = [rolled(h[g][0], 1), None, rolled(h[g][2], 1)]
            change = curl_of_h(h[g], below[g], h_x, h_y)
            new.append([self.load(j, g) + factor[g] * change[j] for j in range(3)])
        return new

    def edges(self, j, g, cells_x):
        return picked(self.ref[j, g, BASE : BASE + cells_x, :], edge_matrix())


def thirds(value):
    high = value.astype(jnp.bfloat16)
    rest = value - high.astype(jnp.float32)
    middle = rest.astype(jnp.bfloat16)
    low = (rest - middle.astype(jnp.float32)).astype(jnp.bfloat16)
    return high, middle, low


def picked(value, matrix):
    high, middle, low = value if isinstance(value, tuple) else thirds(value)
    return dot32(high, matrix) + (dot32(middle, matrix) + dot32(low, matrix))


def matrix_of(pairs, columns, rows=LANES):
    row = lax.broadcasted_iota(jnp.int32, (rows, columns), 0)
    column = lax.broadcasted_iota(jnp.int32, (rows, columns), 1)
    total = None
    for first_row, first_column, count in pairs:
        here = (column - row == first_column - first_row) & (column >= first_column)
        here = here & (column < first_column + count)
        total = here if total is None else total | here
    return jnp.where(total, 1.0, 0.0).astype(jnp.bfloat16)


def edge_matrix():
    pairs = []
    for slot in range(LAYERS // 2):
        pairs.append((slot * SLOT + 4, slot * LANES, HALO))
        pairs.append((slot * SLOT + 20, slot * LANES + LANES - HALO, HALO))
    return matrix_of(pairs, LAYERS // 2 * LANES)


def column_matrix():
    pairs = []
    for slot in range(LAYERS // 2):
        pairs.append((slot * LANES + LANES - WIDE, slot * SLOT, WIDE))
        pairs.append((slot * LANES, slot * SLOT + WIDE, WIDE))
    return matrix_of(pairs, LANES, LAYERS // 2 * LANES)


def message_matrix(quarter):
    pairs = []
    for g in range(2):
        for slot in range(LAYERS // 2):
            to = slot * SLOT + 4 * (2 * quarter + g)
            pairs.append((g * LANES + slot * SLOT + 4, to, HALO))
            pairs.append((g * LANES + slot * SLOT + 8, LANES + to, HALO))
    return matrix_of(pairs, 2 * LANES, 2 * LANES)


def strip_matrix(place):
    pairs = []
    for slot in range(LAYERS // 2):
        at = slot * SLOT
        pairs.append((at, at + 16, WIDE))
        pairs.append((at + 8, at + 4, WIDE))
        pairs.append((LANES + at + 4 * place, at, HALO))
        pairs.append((2 * LANES + at + 4 * place, at + 24, HALO))
    return matrix_of(pairs, LANES, 3 * LANES)


def with_edges(value, edges, z):
    own = edges[:, (z // 2) * LANES : (z // 2 + 1) * LANES]
    lane = lane_of(own.shape)
    outer = (lane < HALO) | (lane >= LANES - HALO)
    return jnp.where(outer, own, value)


BY_PRODUCT = (0, 1, 2)
EVERY = [(j, z) for j in range(6) for z in range(LAYERS)]


def free_steps(tile, steps, start, rows, factor_of):
    for _ in range(steps):
        for z in range(LAYERS):
            tile.step_h(z, start, rows)
            for j, value in enumerate(tile.step_e(z, start, rows, factor_of(z))):
                tile.store(j, z, start, value)


def first_kernel(e_ref, h_ref, m_ref, _, c_ref, f_ref, token_ref):
    cells_x = e_ref.shape[2]
    token_ref[...] = jnp.zeros_like(token_ref)
    for z in range(LAYERS):
        c_ref[z] = coefficient_of(m_ref[z]) * 0.5
        for j in range(3):
            f_ref[j, z, PAD : PAD + cells_x, :] = e_ref[j, z] * 0.5
            f_ref[3 + j, z, PAD : PAD + cells_x, :] = h_ref[j, z]
        for j in range(6):
            f_ref[j, z, :PAD, :] = jnp.zeros((PAD, LANES), jnp.float32)
            f_ref[j, z, PAD + cells_x :, :] = jnp.zeros((PAD, LANES), jnp.float32)
    free_steps(Tile(f_ref, EVERY), STEPS // 2, PAD, cells_x, lambda z: c_ref[z])


def first_steps(e_field, h_field, material, after):
    cells_x = e_field.shape[2]
    f32 = jnp.float32
    vmem = pl.BlockSpec(memory_space=pltpu.VMEM)
    return pl.pallas_call(
        first_kernel,
        in_specs=[vmem] * 4,
        out_shape=(
            jax.ShapeDtypeStruct((LAYERS, cells_x, LANES), f32),
            jax.ShapeDtypeStruct((6, LAYERS, cells_x + 2 * PAD, LANES), f32),
            jax.ShapeDtypeStruct((8, LANES), f32),
        ),
        compiler_params=pltpu.CompilerParams(vmem_limit_bytes=VMEM_LIMIT),
        name="first_steps",
    )(e_field, h_field, material, after)


class Rows:
    def __init__(self, ref):
        self.ref = ref

    def load(self, j, by=0):
        return self.ref[j, :, 8 + by : 40 + by, :]

    def step(self, factor):
        zero = jnp.zeros((1, 32, LANES), jnp.float32)
        e = [self.load(j) for j in range(3)]
        e_z = [jnp.concatenate([e[j][1:], zero], 0) for j in range(2)] + [None]
        e_x = [None, self.load(1, 1), self.load(2, 1)]
        e_y = [pltpu.roll(e[0], LANES - 1, 2), None, pltpu.roll(e[2], LANES - 1, 2)]
        for j, change in enumerate(curl_of_e(e, e_z, e_x, e_y)):
            self.ref[3 + j, :, 8:40, :] = self.load(3 + j) + change
        h = [self.load(3 + j) for j in range(3)]
        h_z = [jnp.concatenate([zero, h[j][:-1]], 0) for j in range(2)] + [None]
        h_x = [None, self.load(4, -1), self.load(5, -1)]
        h_y = [pltpu.roll(h[0], 1, 2), None, pltpu.roll(h[2], 1, 2)]
        for j, change in enumerate(curl_of_h(h, h_z, h_x, h_y)):
            self.ref[j, :, 8:40, :] = e[j] + factor * change


def later_kernel(f_in, c_ref, e_ref, h_ref, x_ref, out_ref, token_ref, f_ref, r_ref):
    cells_x = c_ref.shape[1]
    token_ref[...] = jnp.zeros_like(token_ref)
    blank = jnp.zeros((LAYERS, PAD - HALO, LANES), jnp.float32)
    zero = jnp.zeros((LAYERS, 8, LANES), jnp.float32)
    factor = None
    for j in range(7):
        ref = e_ref.at[j] if j < 3 else h_ref.at[j - 3] if j < 6 else c_ref
        scale = 1.0 if 3 <= j < 6 else 0.5
        own = 0.5 if j < 3 else 1.0
        rims = x_ref[j * LAYERS : (j + 1) * LAYERS] * scale
        first, final = ref[:, :8, :] * own, ref[:, cells_x - 8 :, :] * own
        rows = [blank, rims[:, HALO:], first, final, rims[:, :HALO], blank]
        if j < 6:
            r_ref[j] = jnp.concatenate([zero] + rows + [zero], 1)
        else:
            factor = jnp.concatenate(rows, 1)
    edge = Rows(r_ref)
    for _ in range(STEPS):
        edge.step(factor)
    f_ref[...] = f_in[...]
    tile = Tile(f_ref, EVERY)
    free_steps(tile, STEPS - STEPS // 2, PAD, cells_x, lambda z: c_ref[z])
    row = lax.broadcasted_iota(jnp.int32, (8, LANES), 0)
    for j, z in EVERY:
        top = jnp.where(row < HALO, r_ref[j, z, 16:24, :], f_ref[j, z, PAD : PAD + 8, :])
        end = f_ref[j, z, PAD + cells_x - 8 : PAD + cells_x, :]
        end = jnp.where(row >= HALO, r_ref[j, z, 24:32, :], end)
        inner = f_ref[j, z, PAD + 8 : PAD + cells_x - 8, :]
        out_ref[j, z] = jnp.concatenate([top, inner, end], 0)


def later_steps(state, coefficient, e_field, h_field, x_rims):
    cells_x = e_field.shape[2]
    f32 = jnp.float32
    return pl.pallas_call(
        later_kernel,
        out_shape=(
            jax.ShapeDtypeStruct((6, LAYERS, cells_x, LANES), f32),
            jax.ShapeDtypeStruct((8, LANES), f32),
        ),
        scratch_shapes=[
            pltpu.VMEM(state.shape, f32),
            pltpu.VMEM((6, LAYERS, 48, LANES), f32),
        ],
        compiler_params=pltpu.CompilerParams(vmem_limit_bytes=VMEM_LIMIT),
        name="later_steps",
    )(state, coefficient, e_field, h_field, x_rims)


def strip_kernel(w_ref, low_ref, high_ref, free_ref, _, factor_ref, out_ref, s_ref):
    rows = w_ref.shape[2]
    first = BASE - PAD
    got = [(thirds(low_ref[a]), thirds(high_ref[a])) for a in range(2)]
    for j in range(7):
        for g in range(2):
            a, b = divmod(2 * j + g, 8)
            lanes = [thirds(w_ref[j, g]), *got[a]]
            parts = tuple(jnp.concatenate([x[i] for x in lanes], 1) for i in range(3))
            value = picked(parts, strip_matrix(b))
            if j < 6:
                s_ref[j, g, first : first + rows, :] = value
            else:
                factor_ref[g] = value
    strip = Strip(s_ref, rows)
    for step in range(STEPS):
        strip.step_h()
        new = strip.step_e([factor_ref[g] for g in range(2)])
        for g in range(2):
            for j in range(3):
                strip.store(j, g, new[g][j])
    for j in range(6):
        for g in range(2):
            edges = strip.edges(j, g, out_ref.shape[2])
            for z in range(g, LAYERS, 2):
                out_ref[j, z] = with_edges(free_ref[j, z], edges, z)


def strip_run(own_edges, low, high, free, after):
    rows = own_edges.shape[2]
    f32 = jnp.float32
    return pl.pallas_call(
        strip_kernel,
        in_specs=[pl.BlockSpec(memory_space=pltpu.VMEM)] * 5,
        out_shape=(
            jax.ShapeDtypeStruct((2, rows, LANES), f32),
            jax.ShapeDtypeStruct(free.shape, f32),
        ),
        scratch_shapes=[pltpu.VMEM((6, 2, rows + 2 * (BASE - PAD), LANES), f32)],
        compiler_params=pltpu.CompilerParams(vmem_limit_bytes=VMEM_LIMIT),
        name="strip_run",
    )(own_edges, low, high, free, after)


def response_kernel(
    place_ref, c_ref, factor_ref, free_ref, mine_ref, other_ref, e_out, h_out,
    f_ref, s_ref, plane_ref, rim_ref, done_ref, sems,
):
    cells_x = e_out.shape[2]
    copies = []

    def send(j, z, source):
        to = e_out.at[j, z] if j < 3 else h_out.at[j - 3, z]
        copies.append(pltpu.make_async_copy(source, to, sems.at[j, z]))
        copies[-1].start()

    far = [(j, z) for j, z in EVERY if z >= ZINJ + STEPS - (0 if j < 2 else 1)]
    for j, z in far:
        if j < 3:
            done_ref[j, z] = free_ref[j, z] * 2.0
            send(j, z, done_ref.at[j, z])
        else:
            send(j, z, free_ref.at[j, z])
    rows = cells_x + 2 * PAD
    half = rows // 2
    first = BASE - PAD
    own = place_ref[0]
    near = matrix_of([(0, 4, WIDE), (LANES - WIDE, 16, WIDE)], LANES)
    outside = matrix_of(
        [(0, 0, HALO), (4, 24, HALO), (8, LANES, HALO), (12, LANES + 24, HALO)], 2 * LANES
    )
    lane = lane_of((half, LANES))
    for ref, which in ((mine_ref, own), (other_ref, 1 - own)):
        at = pl.ds(pl.multiple_of(which * half, 8), half)
        outer = jnp.where(lane < 16, unfolded(ref[2 * half :, :], half, 8, 0), 0.0)
        outer = picked(outer, outside)
        for part in range(2):
            plane = ref[part * half : (part + 1) * half, :]
            plane_ref[part, at, :] = plane
            own_part = outer[:, part * LANES : (part + 1) * LANES]
            rim_ref[part, at, :] = picked(plane, near) + own_part

    def injection(ref, step, start, size):
        cosine = 0.5 * COURANT * math.cos(OMEGA * step)
        sine = 0.5 * COURANT * math.sin(OMEGA * step)
        re, im = ref[0, start : start + size, :], ref[1, start : start + size, :]
        return [cosine * re - sine * im, sine * re + cosine * im, None]

    tile = Tile(f_ref, ())
    for j, value in enumerate(injection(plane_ref, 1, 0, rows)):
        tile.store(j, ZINJ, first, value)
    strip = Strip(s_ref, rows)
    s_ref[...] = jnp.zeros_like(s_ref)
    for j, value in enumerate(injection(rim_ref, 1, 0, rows)[:2]):
        strip.store(j, ZINJ % 2, value)
    for step in range(2, STEPS + 1):
        strip.step_h()
        new = strip.step_e([factor_ref[g] for g in range(2)])
        source = injection(rim_ref, step, 0, rows)
        for g in range(2):
            for j in range(3):
                value = add(new[g][j], source[j] if g == ZINJ % 2 else None)
                strip.store(j, g, value)
    edges = {(j, g): strip.edges(j, g, cells_x) for j in range(6) for g in range(2)}
    for step in range(2, STEPS + 1):
        last = step == STEPS
        start, size = (BASE, cells_x) if last else (first, rows)
        for z in range(LAYERS):
            tile.step_h(z, first, rows - (PAD if last else 0))
            new = tile.step_e(z, start, size, c_ref[z, start : start + size, :])
            if z == ZINJ:
                source = injection(plane_ref, step, start - first, size)
                new = [add(a, b) for a, b in zip(new, source)]
            for j in range(3):
                if not last:
                    tile.store(j, z, start, new[j])
                    continue
                for i, value in ((j, new[j]), (3 + j, tile.load(3 + j, z, start, size))):
                    if (i, z) in far:
                        continue
                    value = with_edges(value, edges[i, z % 2], z) + free_ref[i, z]
                    done_ref[i, z] = value * 2.0 if i < 3 else value
                    send(i, z, done_ref.at[i, z])
    for copy in copies:
        copy.wait()


def response(place, c_ext, factor, free, mine, other, cells_x):
    rows = cells_x + 2 * PAD
    tall = cells_x + 2 * BASE
    f32 = jnp.float32
    out = jax.ShapeDtypeStruct((3, LAYERS, cells_x, LANES), f32)
    vmem = pl.BlockSpec(memory_space=pltpu.VMEM)
    return pl.pallas_call(
        response_kernel,
        in_specs=[pl.BlockSpec(memory_space=pltpu.SMEM)] + [vmem] * 5,
        out_specs=(pl.BlockSpec(memory_space=pl.ANY),) * 2,
        out_shape=(out, out),
        scratch_shapes=[
            pltpu.VMEM((6, LAYERS, tall, LANES), f32),
            pltpu.VMEM((6, 2, tall, LANES), f32),
            pltpu.VMEM((2, rows, LANES), f32),
            pltpu.VMEM((2, rows, LANES), f32),
            pltpu.VMEM((6, LAYERS, cells_x, LANES), f32),
            pltpu.SemaphoreType.DMA((6, LAYERS)),
        ],
        compiler_params=pltpu.CompilerParams(vmem_limit_bytes=VMEM_LIMIT),
        name="response",
    )(place, c_ext, factor, free, mine, other)


def along(block, axis, distance):
    n = lax.axis_size(axis)
    return lax.ppermute(block, axis, [((i - distance) % n, i) for i in range(n)])


def flipped(block, axis, bits):
    return lax.ppermute(block, axis, [(i, i ^ bits) for i in range(lax.axis_size(axis))])


def to_groups(block, n_src, n_tx, flip, distance):
    route = []
    for s in range(n_src):
        for t in range(n_tx):
            route.append((s * n_tx + t, (s ^ flip) * n_tx + (t + distance) % n_tx))
    return lax.ppermute(block, ("src", "tx"), route)


def per_device(orders, offsets, material, e_field, h_field):
    cols_ky = orders.shape[3]
    layers, cells_x, cells_y = material.shape
    n_src, n_tx, n_ty = lax.axis_size("src"), lax.axis_size("tx"), lax.axis_size("ty")
    half = cells_x // 2 + PAD
    place = jnp.stack([lax.axis_index("src"), lax.axis_index("tx"), lax.axis_index("ty")]).astype(
        jnp.int32
    )

    parts, sent = x_stage(place, offsets.T, jnp.swapaxes(orders, 2, 3), n_tx, cells_x)
    received = []
    for distance in range(n_tx):
        for flip in range(n_src):
            if distance or flip:
                part = parts[2 * distance + flip]
                received.append(to_groups(part, n_src, n_tx, flip, distance))
    coefficient, state, begun = first_steps(e_field, h_field, material, sent)

    rims = x_rims_of(e_field, h_field, material, sent)
    if n_tx == 2:
        x_rims = along(rims, "tx", 1)
    else:
        top, bottom = rims[:, :HALO], rims[:, HALO:]
        x_rims = jnp.concatenate([along(top, "tx", -1), along(bottom, "tx", 1)], 1)
    block = summed(parts, received, begun)
    c_ext, own_edges, to_high, to_low = pack(e_field, h_field, coefficient, x_rims)
    low = along(to_high, "ty", 1)
    high = along(to_low, "ty", -1)
    free, run = later_steps(state, coefficient, e_field, h_field, x_rims)

    blocks = {0: block}
    for bits in range(n_ty - 2, 0, -2):
        blocks[bits] = flipped(block, "ty", bits)
    for bits in range(0, n_ty, 2):
        blocks[bits + 1] = flipped(blocks[bits], "ty", 1)
    mine = y_stage(place, [blocks[b] for b in range(n_ty)], cols_ky, cells_y, half, run)
    other = flipped(mine, "src", 1)
    factor, free = strip_run(own_edges, low, high, free, mine)
    return response(place, c_ext, factor, free, mine, other, cells_x)


def solution(mesh):
    in_specs = (
        P("src", None, "tx", "ty"),
        P("src", None),
        P(None, "tx", "ty"),
        P(None, None, "tx", "ty"),
        P(None, None, "tx", "ty"),
    )
    out_specs = (P(None, None, "tx", "ty"), P(None, None, "tx", "ty"))
    return jax.shard_map(
        per_device, mesh=mesh, in_specs=in_specs, out_specs=out_specs, check_vma=False
    )
```

```python
import functools
import math

import jax
import jax.numpy as jnp
import ml_dtypes
import numpy as np
from jax import lax
from jax.experimental import pallas as pl
from jax.experimental.pallas import tpu as pltpu
from jax.sharding import PartitionSpec as P

MX = 512
MY = 512
STEPS = 4
ZINJ = 1
LAYERS = 6

COURANT = 0.5
OMEGA = 0.7
PERMITTIVITY = (1.0, 2.6, 11.9, 2.1)

REACH = 8
SPAN = 2 * REACH
PAD = 8
HALO = 4
BASE = 16
SLOT = 32
WIDE = 8
LANES = 128
VMEM_LIMIT = 24 * 1024 * 1024
X_LIMIT = 63_000_000


def split_bf16(table):
    high = table.astype(ml_dtypes.bfloat16)
    low = (table - high.astype(np.float64)).astype(ml_dtypes.bfloat16)
    return high, low


def padded(lanes):
    return -(-lanes // LANES) * LANES


@functools.lru_cache(maxsize=None)
def x_seeds(n_tx, rows_kx, cells_x):
    window = rows_kx + SPAN
    wide = padded(window)
    full = cells_x * n_tx
    turns = [8 << k for k in range((cells_x // 8).bit_length())]
    count = 8 + len(turns) + n_tx
    table = np.zeros((n_tx, -(-count // 8) * 8, 2 * wide), np.float32)
    for own in range(n_tx):
        freq = own * rows_kx - MX // 2 - REACH + np.arange(window)
        tiles = [(own + distance) % n_tx * cells_x for distance in range(n_tx)]
        x = np.array(list(range(-PAD, 8 - PAD)) + turns + tiles)
        angle = np.mod(x[:, None] * freq[None, :], full) * (2.0 * math.pi / full)
        table[own, :count, :window] = np.cos(angle)
        table[own, :count, wide : wide + window] = np.sin(angle)
    return table, len(turns)


@functools.lru_cache(maxsize=None)
def y_tables(n_ty, cols_ky, cells_y):
    full = cells_y * n_ty
    window = cols_ky + SPAN
    edge = np.concatenate([np.arange(-HALO, 0), cells_y + np.arange(HALO)])
    y = np.concatenate([np.arange(cells_y), edge])
    table = np.zeros((n_ty, LANES + 2 * SPAN, 2 * cells_y + LANES))
    for block in range(n_ty):
        freq = block * cols_ky - MY // 2 - REACH + np.arange(window)
        angle = np.mod(freq[:, None] * y[None, :], full) * (2.0 * math.pi / full)
        cos, sin = np.cos(angle), np.sin(angle)

        def placed(re_cols, im_cols):
            out = np.zeros((window, 2 * cells_y + LANES))
            out[:, :cells_y] = re_cols[:, :cells_y]
            out[:, cells_y : 2 * cells_y] = im_cols[:, :cells_y]
            out[:, 2 * cells_y : 2 * cells_y + 2 * HALO] = re_cols[:, cells_y:]
            out[:, 2 * cells_y + 2 * HALO : 2 * cells_y + 4 * HALO] = im_cols[:, cells_y:]
            return out

        from_re = placed(cos, sin)
        from_im = placed(-sin, cos)
        table[block, :cols_ky] = from_re[:cols_ky]
        table[block, cols_ky : 2 * cols_ky] = from_im[:cols_ky]
        table[block, LANES : LANES + SPAN] = from_re[cols_ky:]
        table[block, LANES + SPAN :] = from_im[cols_ky:]
    return split_bf16(table)


@functools.lru_cache(maxsize=None)
def y_phases(n_ty, cols_ky, cells_y):
    full = cells_y * n_ty
    out = np.zeros((n_ty, n_ty, 8, LANES), np.float32)
    for own in range(n_ty):
        for block in range(n_ty):
            freq = block * cols_ky - MY // 2 - REACH + np.arange(cols_ky + SPAN)
            angle = np.mod(freq * own * cells_y, full) * (2.0 * math.pi / full)
            cos, sin = np.cos(angle), np.sin(angle)
            out[own, block, 0, :cols_ky] = cos[:cols_ky]
            out[own, block, 0, cols_ky : 2 * cols_ky] = cos[:cols_ky]
            out[own, block, 1, :cols_ky] = -sin[:cols_ky]
            out[own, block, 1, cols_ky : 2 * cols_ky] = sin[:cols_ky]
            for group in range(LANES // (2 * SPAN)):
                at = group * 2 * SPAN
                out[own, block, 2, at : at + SPAN] = cos[cols_ky:]
                out[own, block, 2, at + SPAN : at + 2 * SPAN] = cos[cols_ky:]
                out[own, block, 3, at : at + SPAN] = -sin[cols_ky:]
                out[own, block, 3, at + SPAN : at + 2 * SPAN] = sin[cols_ky:]
    return out


def lasting(microseconds):
    moved = int(microseconds * 3.69e6)
    return pl.CostEstimate(flops=0, transcendentals=0, bytes_accessed=moved)


def lane_of(shape):
    return lax.broadcasted_iota(jnp.int32, shape, len(shape) - 1)


def rolled(value, shift):
    shift = shift % LANES
    return value if shift == 0 else pltpu.roll(value, shift, 1)


def halves(value):
    high = value.astype(jnp.bfloat16)
    low = (value - high.astype(jnp.float32)).astype(jnp.bfloat16)
    return high, low


def dot32(a, b):
    return jnp.dot(a, b, preferred_element_type=jnp.float32)


def fold_groups(rows, count):
    tiles = rows // 8
    sizes = [8 * (tiles // count + (1 if g < tiles % count else 0)) for g in range(count)]
    starts = [sum(sizes[:g]) for g in range(count)]
    return list(zip(starts, sizes))


def folded_rows(rows, count):
    return fold_groups(rows, count)[0][1]


def folded(value, count):
    groups = fold_groups(value.shape[0], count)
    tall, wide = groups[0][1], LANES // count
    lane = lane_of((tall, LANES))
    total = jnp.zeros((tall, LANES), value.dtype)
    for g, (start, size) in enumerate(groups):
        part = value[start : start + size]
        if size < tall:
            part = jnp.concatenate([part, jnp.zeros((tall - size, LANES), value.dtype)], 0)
        keep = (lane >= wide * g) & (lane < wide * (g + 1))
        total = jnp.where(keep, rolled(part, wide * g), total)
    return total


def unfolded(value, rows, count, at):
    wide = LANES // count
    parts = []
    for g, (_, size) in enumerate(fold_groups(rows, count)):
        parts.append(rolled(value[:size], at - wide * g))
    return jnp.concatenate(parts, 0)


def turned(cos, sin, by_cos, by_sin):
    return cos * by_cos - sin * by_sin, sin * by_cos + cos * by_sin


def fill_table(n_turns, seed_ref, high_ref, low_ref):
    n_tx, rows, both = high_ref.shape
    wide = both // 2

    def row(i):
        return seed_ref[i : i + 1, :wide], seed_ref[i : i + 1, wide:]

    cos, sin = seed_ref[:8, :wide], seed_ref[:8, wide:]
    for k in range(n_turns):
        more = min(8 << k, rows - (8 << k))
        new = turned(cos[:more], sin[:more], *row(8 + k))
        cos, sin = jnp.concatenate([cos, new[0]], 0), jnp.concatenate([sin, new[1]], 0)
    for distance in range(n_tx):
        there = turned(cos, sin, *row(8 + n_turns + distance))
        for part in range(2):
            high, low = halves(there[part])
            high_ref[distance, :, part * wide : (part + 1) * wide] = high
            low_ref[distance, :, part * wide : (part + 1) * wide] = low


def x_kernel(
    n_turns, place_ref, offs_in, orders_in, seeds_in, e_in, h_in, m_in, *refs,
):
    *out_refs, rim_ref = refs[:-12]
    (
        edge_ref, last_ref, offs_ref, orders_ref, seed_ref, wh_ref, wl_ref, line_ref, acc_ref,
        q_ref, sems, rim_sems,
    ) = refs[-12:]
    own = place_ref[0]
    copies = [
        pltpu.make_async_copy(seeds_in.at[place_ref[1]], seed_ref, sems.at[0]),
        pltpu.make_async_copy(orders_in, orders_ref, sems.at[1]),
        pltpu.make_async_copy(offs_in, offs_ref, sems.at[2]),
    ]
    cells_x = e_in.shape[2]
    for k, start in enumerate((0, cells_x - 8)):
        at = pl.ds(start, 8)
        for i, ref in enumerate((e_in, h_in)):
            source = ref.at[:, :, at, :]
            copies.append(pltpu.make_async_copy(source, edge_ref.at[i, k], rim_sems.at[i, k]))
        copies.append(pltpu.make_async_copy(m_in.at[:, at, :], last_ref.at[k], rim_sems.at[2, k]))
    for copy in copies:
        copy.start()
    points, _, cols_ky, rows_kx = orders_ref.shape
    n_tx, rows, both = wh_ref.shape
    half = rows // 2
    acc_ref[...] = jnp.zeros_like(acc_ref)
    line_ref[...] = jnp.zeros_like(line_ref)
    wide = line_ref.shape[4]
    copies[0].wait()
    fill_table(n_turns, seed_ref, wh_ref, wl_ref)
    copies[1].wait()
    copies[2].wait()
    for point in range(points):
        down = offs_ref[0, point] + REACH
        across = offs_ref[1, point] + REACH
        for part in range(2):
            for tile in range(rows_kx // wide):
                lanes = slice(tile * wide, (tile + 1) * wide)
                line = line_ref.at[point, part, tile]
                line[pl.ds(across, cols_ky), :] = orders_ref[point, part, :, lanes]
                acc_ref[part, pl.ds(down + tile * wide, wide), :] += line[...].T
    s_re = acc_ref[0]
    s_im = acc_ref[1]
    lane = lane_of(s_re.shape)
    re_by, im_by = rolled(s_re, cols_ky), rolled(s_im, cols_ky)

    def main(re, im_by):
        out = jnp.where(lane < cols_ky, re, im_by)
        return out if 2 * cols_ky == LANES else jnp.where(lane < 2 * cols_ky, out, 0.0)

    def spill(re_back, im_back):
        out = jnp.where(lane < SPAN, re_back, im_back)
        return jnp.where(lane < 2 * SPAN, out, 0.0)

    same = 2 * cols_ky == LANES
    re_back = re_by if same else rolled(s_re, -cols_ky)
    im_back = im_by if same else rolled(s_im, -cols_ky)
    top = [main(s_re, im_by), spill(re_back, rolled(s_im, SPAN - cols_ky))]
    bottom = [main(-s_im, re_by), spill(-im_back, rolled(s_re, SPAN - cols_ky))]
    right = jnp.concatenate([jnp.concatenate(top, 1), jnp.concatenate(bottom, 1)], 0)
    right_h, right_l = halves(right)
    for distance in range(n_tx):
        w_h = wh_ref[distance]
        q_ref[...] = dot32(w_h, right_h) + (dot32(wl_ref[distance], right_h) + dot32(w_h, right_l))
        for flip in range(2):
            start = pl.multiple_of((own ^ flip) * half, 8)
            block = q_ref[pl.ds(start, half), :]
            out_refs[2 * distance + flip][:half, :] = block[:, :LANES]
            out_refs[2 * distance + flip][half:, :] = folded(block[:, LANES:], 4)
    for copy in copies[3:]:
        copy.wait()
    row = lax.broadcasted_iota(jnp.int32, (LAYERS, 8, LANES), 1)
    for j in range(7):
        if j < 6:
            first, final = (edge_ref[j // 3, k, j % 3] for k in range(2))
        else:
            first, final = (coefficient_of(last_ref[k]) for k in range(2))
        rim_ref[j * LAYERS : (j + 1) * LAYERS] = jnp.where(row < HALO, first, final)


def x_stage(place, offsets, orders, n_tx, e_field, h_field, material):
    points, _, cols_ky, rows_kx = orders.shape
    cells_x = e_field.shape[2]
    wide = min(rows_kx, LANES)
    seeds, n_turns = x_seeds(n_tx, rows_kx, cells_x)
    rows = cells_x + 2 * PAD
    half = rows // 2
    height = half + folded_rows(half, 4)
    f32 = jnp.float32
    table = pltpu.VMEM((n_tx, rows, seeds.shape[2]), jnp.bfloat16)
    return pl.pallas_call(
        functools.partial(x_kernel, n_turns),
        in_specs=[pl.BlockSpec(memory_space=pltpu.SMEM)] + [pl.BlockSpec(memory_space=pltpu.HBM)] * 6,
        out_shape=(jax.ShapeDtypeStruct((height, LANES), f32),) * (2 * n_tx)
        + (jax.ShapeDtypeStruct((7 * LAYERS, 2 * HALO, LANES), f32),),
        scratch_shapes=[
            pltpu.VMEM((2, 2, 3, LAYERS, 8, LANES), f32),
            pltpu.VMEM((2, LAYERS, 8, LANES), jnp.int32),
            pltpu.SMEM(offsets.shape, jnp.int32),
            pltpu.VMEM(orders.shape, f32),
            pltpu.VMEM(seeds.shape[1:], f32),
            table,
            table,
            pltpu.VMEM((points, 2, rows_kx // wide, LANES, wide), f32),
            pltpu.VMEM((2, seeds.shape[2] // 2, LANES), f32),
            pltpu.VMEM((rows, 2 * LANES), f32),
            pltpu.SemaphoreType.DMA((3,)),
            pltpu.SemaphoreType.DMA((3, 2)),
        ],
        compiler_params=pltpu.CompilerParams(vmem_limit_bytes=X_LIMIT),
        cost_estimate=lasting(3.5),
        name="x_stage",
    )(place, offsets, orders, jnp.asarray(seeds), e_field, h_field, material)


def sum_kernel(*refs):
    *part_refs, _, out_ref = refs
    total = part_refs[0][...]
    for ref in part_refs[1:]:
        total = total + ref[...]
    out_ref[...] = total


def summed(parts, after):
    return pl.pallas_call(
        sum_kernel,
        out_shape=jax.ShapeDtypeStruct(parts[0].shape, jnp.float32),
        compiler_params=pltpu.CompilerParams(vmem_limit_bytes=VMEM_LIMIT),
        cost_estimate=lasting(0.4),
        name="sum_parts",
    )(*parts, after)


def y_kernel(cols_ky, half, place_ref, *refs):
    *block_refs, th_ref, tl_ref, phase_ref, _, out_ref = refs
    n_ty = len(block_refs)
    lane = lane_of((half, LANES))
    mains, spills, numbers = [], [], []
    for number, ref in enumerate(block_refs):
        block = place_ref[2] ^ number
        numbers.append(block)
        phase = phase_ref[block]
        main = ref[:half, :]
        if 2 * cols_ky == LANES:
            swapped = rolled(main, cols_ky)
        else:
            swapped = jnp.where(lane < cols_ky, rolled(main, -cols_ky), rolled(main, cols_ky))
        mains.append(main * phase[0:1] + swapped * phase[1:2])
        spill = ref[half:, :]
        small = lane_of(spill.shape)
        other = jnp.where((small & (2 * SPAN - 1)) < SPAN, rolled(spill, -SPAN), rolled(spill, SPAN))
        spills.append(spill * phase[2:3] + other * phase[3:4])
    packed = []
    for first in range(0, n_ty, 4):
        total = None
        for g in range(4):
            part = unfolded(spills[first + g], half, 4, 32 * g)
            total = part if total is None else jnp.where(lane >= 32 * g, part, total)
        packed.append(total)
    result = None
    for first in range(0, n_ty, 2):
        left_h, left_l = halves(jnp.concatenate(mains[first : first + 2], 1))
        t_h = jnp.concatenate([th_ref[numbers[first + g], :LANES, :] for g in range(2)], 0)
        t_l = jnp.concatenate([tl_ref[numbers[first + g], :LANES, :] for g in range(2)], 0)
        part = dot32(left_h, t_h) + (dot32(left_h, t_l) + dot32(left_l, t_h))
        result = part if result is None else result + part
    for first in range(0, n_ty, 8):
        left_h, left_l = halves(jnp.concatenate(packed[first // 4 : first // 4 + 2], 1))
        t_h = jnp.concatenate([th_ref[numbers[first + g], LANES:, :] for g in range(8)], 0)
        t_l = jnp.concatenate([tl_ref[numbers[first + g], LANES:, :] for g in range(8)], 0)
        result = result + (dot32(left_h, t_h) + (dot32(left_h, t_l) + dot32(left_l, t_h)))
    out_ref[:half, :] = result[:, :LANES]
    out_ref[half : 2 * half, :] = result[:, LANES : 2 * LANES]
    out_ref[2 * half :, :] = folded(result[:, 2 * LANES :], 8)


def y_stage(place, blocks, cols_ky, cells_y, half, after):
    n_ty = len(blocks)
    t_h, t_l = y_tables(n_ty, cols_ky, cells_y)
    phases = y_phases(n_ty, cols_ky, cells_y)
    whole = lambda shape: pl.BlockSpec(shape, lambda i, place: (0,) * len(shape))
    height = 2 * half + folded_rows(half, 8)
    return pl.pallas_call(
        functools.partial(y_kernel, cols_ky, half),
        grid_spec=pltpu.PrefetchScalarGridSpec(
            num_scalar_prefetch=1,
            grid=(1,),
            in_specs=[whole(b.shape) for b in blocks]
            + [
                whole(t_h.shape),
                whole(t_l.shape),
                pl.BlockSpec((None,) + phases.shape[1:], lambda i, place: (place[2], 0, 0, 0)),
                whole(after.shape),
            ],
            out_specs=whole((height, LANES)),
        ),
        out_shape=jax.ShapeDtypeStruct((height, LANES), jnp.float32),
        compiler_params=pltpu.CompilerParams(vmem_limit_bytes=VMEM_LIMIT),
        cost_estimate=lasting(1.5),
        name="y_stage",
    )(place, *blocks, jnp.asarray(t_h), jnp.asarray(t_l), jnp.asarray(phases), after)


def coefficient_of(material):
    value = jnp.where(material == 0, COURANT / PERMITTIVITY[0], COURANT / PERMITTIVITY[1])
    value = jnp.where(material == 2, COURANT / PERMITTIVITY[2], value)
    return jnp.where(material == 3, COURANT / PERMITTIVITY[3], value).astype(jnp.float32)


def pack_kernel(
    e_ref, h_ref, c_ref, x_ref, column_ref, message_ref, ext_ref, w_ref, low_ref, high_ref
):
    cells_x = e_ref.shape[2]
    end = BASE + cells_x
    rows = cells_x + 2 * PAD
    lane = lane_of((rows, LANES))
    by_product = []
    blank = jnp.zeros((PAD - HALO, LANES), jnp.float32)
    for j in range(7):
        scale = 1.0 if 3 <= j < 6 else 0.5
        strips = [jnp.zeros((rows, LANES), jnp.float32)] * 2
        planes = [[], []]
        for z in range(LAYERS):
            if j < 3:
                body = e_ref[j, z] * scale
            elif j < 6:
                body = h_ref[j - 3, z]
            else:
                body = c_ref[z]
            rims = x_ref[j * LAYERS + z] * scale
            full = jnp.concatenate([blank, rims[HALO:], body, rims[:HALO], blank], 0)
            if j == 6:
                ext_ref[z, 0 : BASE - PAD, :] = jnp.zeros((BASE - PAD, LANES), jnp.float32)
                ext_ref[z, BASE - PAD : end + PAD, :] = full
                ext_ref[z, end + PAD : end + BASE, :] = jnp.zeros((BASE - PAD, LANES), jnp.float32)
            g, at = z % 2, (z // 2) * SLOT
            if j in BY_PRODUCT:
                planes[g].append(beside(full))
                continue
            keep = (lane >= at) & (lane < at + 2 * WIDE)
            strips[g] = jnp.where(keep, rolled(full, at + WIDE), strips[g])
        for g in range(2):
            if j in BY_PRODUCT:
                by_product.append(jnp.concatenate(planes[g], 1))
            else:
                w_ref[j, g] = strips[g]
    taken = dot32(jnp.concatenate(by_product, 0), column_ref[...])
    for i, (j, g) in enumerate((j, g) for j in BY_PRODUCT for g in range(2)):
        w_ref[j, g] = taken[i * rows : (i + 1) * rows]
    items = [beside(w_ref[j, g]) for j in range(7) for g in range(2)]
    items += [jnp.zeros_like(items[0])] * (16 - len(items))
    sides = [jnp.concatenate(items[8 * a : 8 * a + 8], 1) for a in range(2)]
    sent = dot32(jnp.concatenate(sides, 0), message_ref[...])
    for a in range(2):
        low_ref[a] = sent[a * rows : (a + 1) * rows, :LANES]
        high_ref[a] = sent[a * rows : (a + 1) * rows, LANES:]


def pack(e_field, h_field, coefficient, x_rims):
    cells_x = e_field.shape[2]
    rows = cells_x + 2 * PAD
    tall = cells_x + 2 * BASE
    f32 = jnp.float32
    return pl.pallas_call(
        pack_kernel,
        out_shape=(
            jax.ShapeDtypeStruct((LAYERS, tall, LANES), f32),
            jax.ShapeDtypeStruct((7, 2, rows, LANES), f32),
            jax.ShapeDtypeStruct((2, rows, LANES), f32),
            jax.ShapeDtypeStruct((2, rows, LANES), f32),
        ),
        compiler_params=pltpu.CompilerParams(vmem_limit_bytes=VMEM_LIMIT),
        cost_estimate=lasting(2.2),
        name="pack",
    )(
        e_field, h_field, coefficient, x_rims,
        jnp.asarray(column_matrix()),
        jnp.asarray(message_matrix()),
    )


def total(terms):
    out = None
    for sign, value in terms:
        if value is None:
            continue
        if out is None:
            out = value if sign > 0 else -value
        else:
            out = out + value if sign > 0 else out - value
    return out


def add(a, b):
    return total([(1, a), (1, b)])


def differ(a, b):
    return total([(1, a), (-1, b)])


def curl_of_e(e, e_z, e_x, e_y):
    return (
        differ(differ(e_z[1], e[1]), differ(e_y[2], e[2])),
        differ(differ(e_x[2], e[2]), differ(e_z[0], e[0])),
        differ(differ(e_y[0], e[0]), differ(e_x[1], e[1])),
    )


def curl_of_h(h, h_z, h_x, h_y):
    return (
        differ(differ(h[2], h_y[2]), differ(h[1], h_z[1])),
        differ(differ(h[0], h_z[0]), differ(h[2], h_x[2])),
        differ(differ(h[1], h_x[1]), differ(h[0], h_y[0])),
    )


def moved(value, shift):
    return None if value is None else rolled(value, shift)


class Tile:
    def __init__(self, ref, live):
        self.ref, self.live = ref, set(live)

    def load(self, j, z, start, size):
        return self.ref[j, z, start : start + size, :] if (j, z) in self.live else None

    def store(self, j, z, start, value):
        if value is not None:
            self.ref[j, z, start : start + value.shape[0], :] = value
            self.live.add((j, z))

    def step_h(self, z, start, size):
        e = [self.load(j, z, start, size) for j in range(3)]
        e_z = [self.load(j, z + 1, start, size) for j in range(2)] + [None]
        e_x = [None] + [self.load(j, z, start + 1, size) for j in (1, 2)]
        e_y = [moved(e[0], -1), None, moved(e[2], -1)]
        new = []
        for j, change in enumerate(curl_of_e(e, e_z, e_x, e_y)):
            new.append(add(self.load(3 + j, z, start, size), change))
            self.store(3 + j, z, start, new[j])
        return new

    def step_e(self, z, start, size, factor):
        h = [self.load(3 + j, z, start, size) for j in range(3)]
        h_z = [self.load(3 + j, z - 1, start, size) for j in range(2)] + [None]
        h_x = [None] + [self.load(3 + j, z, start - 1, size) for j in (1, 2)]
        h_y = [moved(h[0], 1), None, moved(h[2], 1)]
        new = []
        for j, change in enumerate(curl_of_h(h, h_z, h_x, h_y)):
            old = self.load(j, z, start, size)
            new.append(old if change is None else add(old, factor * change))
        return new


class Strip:
    def __init__(self, ref, rows):
        self.ref, self.start, self.rows = ref, BASE - PAD, rows
        self.lane = lane_of((rows, LANES))

    def load(self, j, g, by=0):
        return self.ref[j, g, self.start + by : self.start + by + self.rows, :]

    def store(self, j, g, value):
        self.ref[j, g, self.start : self.start + self.rows, :] = value

    def step_h(self, fresh=False):
        e = [[self.load(j, g) for j in range(3)] for g in range(2)]
        inside = self.lane < 2 * SLOT
        above = [
            [e[1][0], e[1][1], None],
            [jnp.where(inside, rolled(e[0][j], -SLOT), 0.0) for j in range(2)] + [None],
        ]
        for g in range(2):
            e_x = [None, self.load(1, g, 1), self.load(2, g, 1)]
            e_y = [rolled(e[g][0], -1), None, rolled(e[g][2], -1)]
            for j, change in enumerate(curl_of_e(e[g], above[g], e_x, e_y)):
                self.store(3 + j, g, change if fresh else self.load(3 + j, g) + change)

    def step_e(self, factor):
        h = [[self.load(3 + j, g) for j in range(3)] for g in range(2)]
        inside = self.lane >= SLOT
        below = [
            [jnp.where(inside, rolled(h[1][j], SLOT), 0.0) for j in range(2)] + [None],
            [h[0][0], h[0][1], None],
        ]
        new = []
        for g in range(2):
            h_x = [None, self.load(4, g, -1), self.load(5, g, -1)]
            h_y = [rolled(h[g][0], 1), None, rolled(h[g][2], 1)]
            change = curl_of_h(h[g], below[g], h_x, h_y)
            new.append([self.load(j, g) + factor[g] * change[j] for j in range(3)])
        return new

    def all_edges(self, cells_x, matrix):
        values = [
            beside(self.ref[j, g, BASE : BASE + cells_x, :]) for j in range(6) for g in range(2)
        ]
        return dot32(jnp.concatenate(values, 0), matrix)


def beside(value):
    return jnp.concatenate(halves(value), 1)


def matrix_of(pairs, columns, rows=LANES):
    out = np.zeros((rows, columns), ml_dtypes.bfloat16)
    for first_row, first_column, count in pairs:
        for i in range(count):
            out[first_row + i, first_column + i] = 1
    return out


def doubled(matrix):
    blocks = matrix.reshape(-1, LANES, matrix.shape[1])
    return np.concatenate([m for block in blocks for m in (block, block)], 0)


def near_matrix():
    return doubled(matrix_of([(0, 4, WIDE), (LANES - WIDE, 16, WIDE)], LANES))


def outside_matrix():
    pairs = [(0, 0, HALO), (4, 24, HALO), (8, LANES, HALO), (12, LANES + 24, HALO)]
    return doubled(matrix_of(pairs, 2 * LANES))


def edge_matrix():
    pairs = []
    for slot in range(LAYERS // 2):
        pairs.append((slot * SLOT + 4, slot * LANES, HALO))
        pairs.append((slot * SLOT + 20, slot * LANES + LANES - HALO, HALO))
    return doubled(matrix_of(pairs, LAYERS // 2 * LANES))


def column_matrix():
    pairs = []
    for slot in range(LAYERS // 2):
        pairs.append((slot * LANES + LANES - WIDE, slot * SLOT, WIDE))
        pairs.append((slot * LANES, slot * SLOT + WIDE, WIDE))
    return doubled(matrix_of(pairs, LANES, LAYERS // 2 * LANES))


def message_matrix():
    pairs = []
    for item in range(8):
        for slot in range(LAYERS // 2):
            at, to = item * LANES + slot * SLOT, slot * SLOT + HALO * item
            pairs.append((at + 4, to, HALO))
            pairs.append((at + 8, LANES + to, HALO))
    return doubled(matrix_of(pairs, 2 * LANES, 8 * LANES))


def strip_matrices():
    own, got = [], []
    for slot in range(LAYERS // 2):
        at = slot * SLOT
        own += [(at, at + 16, WIDE), (at + 8, at + 4, WIDE)]
        for item in range(8):
            to = item * LANES + at
            got.append((at + HALO * item, to, HALO))
            got.append((LANES + at + HALO * item, to + 24, HALO))
    return doubled(matrix_of(own, LANES)), doubled(matrix_of(got, 8 * LANES, 2 * LANES))


def with_edges(value, edges_ref, j, z):
    start = (2 * j + z % 2) * value.shape[0]
    lanes = slice((z // 2) * LANES, (z // 2 + 1) * LANES)
    own = edges_ref[start : start + value.shape[0], lanes]
    lane = lane_of(own.shape)
    outer = (lane < HALO) | (lane >= LANES - HALO)
    return jnp.where(outer, own, value)


BY_PRODUCT = (0, 1, 2)
EVERY = [(j, z) for j in range(6) for z in range(LAYERS)]


def free_steps(tile, steps, start, rows, factor_of):
    for _ in range(steps):
        for z in range(LAYERS):
            tile.step_h(z, start, rows)
            for j, value in enumerate(tile.step_e(z, start, rows, factor_of(z))):
                tile.store(j, z, start, value)


def first_kernel(e_ref, h_ref, m_ref, c_ref, f_ref, token_ref):
    cells_x = e_ref.shape[2]
    token_ref[...] = jnp.zeros_like(token_ref)
    for z in range(LAYERS):
        c_ref[z] = coefficient_of(m_ref[z]) * 0.5
        for j in range(3):
            f_ref[j, z, PAD : PAD + cells_x, :] = e_ref[j, z] * 0.5
            f_ref[3 + j, z, PAD : PAD + cells_x, :] = h_ref[j, z]
        for j in range(6):
            f_ref[j, z, :PAD, :] = jnp.zeros((PAD, LANES), jnp.float32)
            f_ref[j, z, PAD + cells_x :, :] = jnp.zeros((PAD, LANES), jnp.float32)
    free_steps(Tile(f_ref, EVERY), STEPS // 2, PAD, cells_x, lambda z: c_ref[z])


def first_steps(e_field, h_field, material):
    cells_x = e_field.shape[2]
    f32 = jnp.float32
    return pl.pallas_call(
        first_kernel,
        out_shape=(
            jax.ShapeDtypeStruct((LAYERS, cells_x, LANES), f32),
            jax.ShapeDtypeStruct((6, LAYERS, cells_x + 2 * PAD, LANES), f32),
            jax.ShapeDtypeStruct((8, LANES), f32),
        ),
        compiler_params=pltpu.CompilerParams(vmem_limit_bytes=VMEM_LIMIT),
        cost_estimate=lasting(3.3),
        name="first_steps",
    )(e_field, h_field, material)


class Rows:
    def __init__(self, ref):
        self.ref = ref

    def load(self, j, by=0):
        return self.ref[j, :, 8 + by : 40 + by, :]

    def step(self, factor):
        zero = jnp.zeros((1, 32, LANES), jnp.float32)
        e = [self.load(j) for j in range(3)]
        e_z = [jnp.concatenate([e[j][1:], zero], 0) for j in range(2)] + [None]
        e_x = [None, self.load(1, 1), self.load(2, 1)]
        e_y = [pltpu.roll(e[0], LANES - 1, 2), None, pltpu.roll(e[2], LANES - 1, 2)]
        for j, change in enumerate(curl_of_e(e, e_z, e_x, e_y)):
            self.ref[3 + j, :, 8:40, :] = self.load(3 + j) + change
        h = [self.load(3 + j) for j in range(3)]
        h_z = [jnp.concatenate([zero, h[j][:-1]], 0) for j in range(2)] + [None]
        h_x = [None, self.load(4, -1), self.load(5, -1)]
        h_y = [pltpu.roll(h[0], 1, 2), None, pltpu.roll(h[2], 1, 2)]
        for j, change in enumerate(curl_of_h(h, h_z, h_x, h_y)):
            self.ref[j, :, 8:40, :] = e[j] + factor * change


def later_kernel(f_in, c_ref, e_ref, h_ref, x_ref, out_ref, token_ref, f_ref, r_ref):
    cells_x = c_ref.shape[1]
    token_ref[...] = jnp.zeros_like(token_ref)
    blank = jnp.zeros((LAYERS, PAD - HALO, LANES), jnp.float32)
    zero = jnp.zeros((LAYERS, 8, LANES), jnp.float32)
    factor = None
    for j in range(7):
        ref = e_ref.at[j] if j < 3 else h_ref.at[j - 3] if j < 6 else c_ref
        scale = 1.0 if 3 <= j < 6 else 0.5
        own = 0.5 if j < 3 else 1.0
        rims = x_ref[j * LAYERS : (j + 1) * LAYERS] * scale
        first, final = ref[:, :8, :] * own, ref[:, cells_x - 8 :, :] * own
        rows = [blank, rims[:, HALO:], first, final, rims[:, :HALO], blank]
        if j < 6:
            r_ref[j] = jnp.concatenate([zero] + rows + [zero], 1)
        else:
            factor = jnp.concatenate(rows, 1)
    edge = Rows(r_ref)
    for _ in range(STEPS):
        edge.step(factor)
    f_ref[...] = f_in[...]
    tile = Tile(f_ref, EVERY)
    free_steps(tile, STEPS - STEPS // 2, PAD, cells_x, lambda z: c_ref[z])
    row = lax.broadcasted_iota(jnp.int32, (8, LANES), 0)
    for j, z in EVERY:
        top = jnp.where(row < HALO, r_ref[j, z, 16:24, :], f_ref[j, z, PAD : PAD + 8, :])
        end = f_ref[j, z, PAD + cells_x - 8 : PAD + cells_x, :]
        end = jnp.where(row >= HALO, r_ref[j, z, 24:32, :], end)
        inner = f_ref[j, z, PAD + 8 : PAD + cells_x - 8, :]
        out_ref[j, z] = jnp.concatenate([top, inner, end], 0)


def later_steps(state, coefficient, e_field, h_field, x_rims):
    cells_x = e_field.shape[2]
    f32 = jnp.float32
    return pl.pallas_call(
        later_kernel,
        out_shape=(
            jax.ShapeDtypeStruct((6, LAYERS, cells_x, LANES), f32),
            jax.ShapeDtypeStruct((8, LANES), f32),
        ),
        scratch_shapes=[
            pltpu.VMEM(state.shape, f32),
            pltpu.VMEM((6, LAYERS, 48, LANES), f32),
        ],
        compiler_params=pltpu.CompilerParams(vmem_limit_bytes=VMEM_LIMIT),
        cost_estimate=lasting(3.7),
        name="later_steps",
    )(state, coefficient, e_field, h_field, x_rims)


def strip_kernel(
    w_ref, low_ref, high_ref, free_ref, own_ref, got_ref, edge_ref, _, factor_ref, out_ref,
    s_ref, edges_ref,
):
    rows = w_ref.shape[2]
    first = BASE - PAD
    mine = [beside(w_ref[j, g]) for j in range(7) for g in range(2)]
    mine = dot32(jnp.concatenate(mine, 0), own_ref[...])
    got = [jnp.concatenate([beside(low_ref[a]), beside(high_ref[a])], 1) for a in range(2)]
    got = dot32(jnp.concatenate(got, 0), got_ref[...])
    for j in range(7):
        for g in range(2):
            i = 2 * j + g
            a, b = divmod(i, 8)
            value = mine[i * rows : (i + 1) * rows]
            value = value + got[a * rows : (a + 1) * rows, b * LANES : (b + 1) * LANES]
            if j < 6:
                s_ref[j, g, first : first + rows, :] = value
            else:
                factor_ref[g] = value
    strip = Strip(s_ref, rows)
    for step in range(STEPS):
        strip.step_h()
        new = strip.step_e([factor_ref[g] for g in range(2)])
        for g in range(2):
            for j in range(3):
                strip.store(j, g, new[g][j])
    edges_ref[...] = strip.all_edges(out_ref.shape[2], edge_ref[...])
    for j, z in EVERY:
        out_ref[j, z] = with_edges(free_ref[j, z], edges_ref, j, z)


def strip_run(own_edges, low, high, free, after):
    rows = own_edges.shape[2]
    f32 = jnp.float32
    return pl.pallas_call(
        strip_kernel,
        out_shape=(
            jax.ShapeDtypeStruct((2, rows, LANES), f32),
            jax.ShapeDtypeStruct(free.shape, f32),
        ),
        scratch_shapes=[
            pltpu.VMEM((6, 2, rows + 2 * (BASE - PAD), LANES), f32),
            pltpu.VMEM((12 * free.shape[2], LAYERS // 2 * LANES), f32),
        ],
        compiler_params=pltpu.CompilerParams(vmem_limit_bytes=VMEM_LIMIT),
        cost_estimate=lasting(4),
        name="strip_run",
    )(
        own_edges, low, high, free, *(jnp.asarray(m) for m in strip_matrices()),
        jnp.asarray(edge_matrix()), after,
    )


def response_kernel(
    place_ref, c_ref, factor_ref, free_ref, mine_ref, other_ref, near_ref, outside_ref, edge_ref,
    e_out, h_out,
    f_ref, s_ref, plane_ref, rim_ref, done_ref, edges_ref, sems,
):
    cells_x = e_out.shape[2]
    copies = []

    def send(j, z, source):
        to = e_out.at[j, z] if j < 3 else h_out.at[j - 3, z]
        copies.append(pltpu.make_async_copy(source, to, sems.at[j, z]))
        copies[-1].start()

    far = [(j, z) for j, z in EVERY if z >= ZINJ + STEPS - (0 if j < 2 else 1)]
    for j, z in far:
        if j < 3:
            done_ref[j, z] = free_ref[j, z] * 2.0
            send(j, z, done_ref.at[j, z])
        else:
            send(j, z, free_ref.at[j, z])
    rows = cells_x + 2 * PAD
    half = rows // 2
    first = BASE - PAD
    own = place_ref[0]
    lane = lane_of((half, LANES))
    for ref, which in ((mine_ref, own), (other_ref, 1 - own)):
        at = pl.ds(pl.multiple_of(which * half, 8), half)
        for part in range(2):
            plane_ref[part, at, :] = ref[part * half : (part + 1) * half, :]
        rim_ref[0, at, :] = jnp.where(lane < 16, unfolded(ref[2 * half :, :], half, 8, 0), 0.0)
    outer = dot32(beside(rim_ref[0]), outside_ref[...])
    planes = jnp.concatenate([beside(plane_ref[part]) for part in range(2)], 0)
    inner = dot32(planes, near_ref[...])
    for part in range(2):
        own_part = outer[:, part * LANES : (part + 1) * LANES]
        rim_ref[part] = inner[part * rows : (part + 1) * rows] + own_part

    def injection(ref, step, start, size):
        cosine = 0.5 * COURANT * math.cos(OMEGA * step)
        sine = 0.5 * COURANT * math.sin(OMEGA * step)
        re, im = ref[0, start : start + size, :], ref[1, start : start + size, :]
        return [cosine * re - sine * im, sine * re + cosine * im, None]

    tile = Tile(f_ref, ())
    for j, value in enumerate(injection(plane_ref, 1, 0, rows)):
        tile.store(j, ZINJ, first, value)
    strip = Strip(s_ref, rows)
    s_ref[...] = jnp.zeros_like(s_ref)
    for j, value in enumerate(injection(rim_ref, 1, 0, rows)[:2]):
        strip.store(j, ZINJ % 2, value)
    for step in range(2, STEPS + 1):
        strip.step_h()
        new = strip.step_e([factor_ref[g] for g in range(2)])
        source = injection(rim_ref, step, 0, rows)
        for g in range(2):
            for j in range(3):
                value = add(new[g][j], source[j] if g == ZINJ % 2 else None)
                strip.store(j, g, value)
    edges_ref[...] = strip.all_edges(cells_x, edge_ref[...])
    for step in range(2, STEPS + 1):
        last = step == STEPS
        start, size = (BASE, cells_x) if last else (first, rows)
        for z in range(LAYERS):
            tile.step_h(z, first, rows - (PAD if last else 0))
            new = tile.step_e(z, start, size, c_ref[z, start : start + size, :])
            if z == ZINJ:
                source = injection(plane_ref, step, start - first, size)
                new = [add(a, b) for a, b in zip(new, source)]
            for j in range(3):
                if not last:
                    tile.store(j, z, start, new[j])
                    continue
                for i, value in ((j, new[j]), (3 + j, tile.load(3 + j, z, start, size))):
                    if (i, z) in far:
                        continue
                    value = with_edges(value, edges_ref, i, z) + free_ref[i, z]
                    done_ref[i, z] = value * 2.0 if i < 3 else value
                    send(i, z, done_ref.at[i, z])
    for copy in copies:
        copy.wait()


def response(place, c_ext, factor, free, mine, other, cells_x):
    rows = cells_x + 2 * PAD
    tall = cells_x + 2 * BASE
    f32 = jnp.float32
    out = jax.ShapeDtypeStruct((3, LAYERS, cells_x, LANES), f32)
    vmem = pl.BlockSpec(memory_space=pltpu.VMEM)
    return pl.pallas_call(
        response_kernel,
        in_specs=[pl.BlockSpec(memory_space=pltpu.SMEM)] + [vmem] * 8,
        out_specs=(pl.BlockSpec(memory_space=pl.ANY),) * 2,
        out_shape=(out, out),
        scratch_shapes=[
            pltpu.VMEM((6, LAYERS, tall, LANES), f32),
            pltpu.VMEM((6, 2, tall, LANES), f32),
            pltpu.VMEM((2, rows, LANES), f32),
            pltpu.VMEM((2, rows, LANES), f32),
            pltpu.VMEM((6, LAYERS, cells_x, LANES), f32),
            pltpu.VMEM((12 * cells_x, LAYERS // 2 * LANES), f32),
            pltpu.SemaphoreType.DMA((6, LAYERS)),
        ],
        compiler_params=pltpu.CompilerParams(vmem_limit_bytes=VMEM_LIMIT),
        cost_estimate=lasting(6.5),
        name="response",
    )(
        place, c_ext, factor, free, mine, other,
        jnp.asarray(near_matrix()), jnp.asarray(outside_matrix()), jnp.asarray(edge_matrix()),
    )


def along(block, axis, distance):
    n = lax.axis_size(axis)
    return lax.ppermute(block, axis, [((i - distance) % n, i) for i in range(n)])


def flipped(block, axis, bits):
    return lax.ppermute(block, axis, [(i, i ^ bits) for i in range(lax.axis_size(axis))])


def to_groups(block, n_src, n_tx, flip, distance):
    route = []
    for s in range(n_src):
        for t in range(n_tx):
            route.append((s * n_tx + t, (s ^ flip) * n_tx + (t + distance) % n_tx))
    return lax.ppermute(block, ("src", "tx"), route)


def per_device(orders, offsets, material, e_field, h_field):
    cols_ky = orders.shape[3]
    layers, cells_x, cells_y = material.shape
    n_src, n_tx, n_ty = lax.axis_size("src"), lax.axis_size("tx"), lax.axis_size("ty")
    half = cells_x // 2 + PAD
    place = jnp.stack([lax.axis_index("src"), lax.axis_index("tx"), lax.axis_index("ty")]).astype(
        jnp.int32
    )

    *parts, rims = x_stage(
        place, offsets.T, jnp.swapaxes(orders, 2, 3), n_tx, e_field, h_field, material
    )
    received = [parts[0]]
    for distance in range(n_tx):
        for flip in range(n_src):
            if distance or flip:
                part = parts[2 * distance + flip]
                received.append(to_groups(part, n_src, n_tx, flip, distance))
    coefficient, state, begun = first_steps(e_field, h_field, material)

    if n_tx == 2:
        x_rims = along(rims, "tx", 1)
    else:
        top, bottom = rims[:, :HALO], rims[:, HALO:]
        x_rims = jnp.concatenate([along(top, "tx", -1), along(bottom, "tx", 1)], 1)
    block = summed(received, begun)
    c_ext, own_edges, to_high, to_low = pack(e_field, h_field, coefficient, x_rims)
    low = along(to_high, "ty", 1)
    high = along(to_low, "ty", -1)
    free, run = later_steps(state, coefficient, e_field, h_field, x_rims)

    blocks = {0: block}
    for bits in range(n_ty - 2, 0, -2):
        blocks[bits] = flipped(block, "ty", bits)
    for bits in range(0, n_ty, 2):
        blocks[bits + 1] = flipped(blocks[bits], "ty", 1)
    mine = y_stage(place, [blocks[b] for b in range(n_ty)], cols_ky, cells_y, half, run)
    other = flipped(mine, "src", 1)
    factor, free = strip_run(own_edges, low, high, free, mine)
    return response(place, c_ext, factor, free, mine, other, cells_x)


def solution(mesh):
    in_specs = (
        P("src", None, "tx", "ty"),
        P("src", None),
        P(None, "tx", "ty"),
        P(None, None, "tx", "ty"),
        P(None, None, "tx", "ty"),
    )
    out_specs = (P(None, None, "tx", "ty"), P(None, None, "tx", "ty"))
    return jax.shard_map(
        per_device, mesh=mesh, in_specs=in_specs, out_specs=out_specs, check_vma=False
    )
```

```python
import functools
import math

import jax
import jax.numpy as jnp
import ml_dtypes
import numpy as np
from jax import lax
from jax.experimental import pallas as pl
from jax.experimental.pallas import tpu as pltpu
from jax.sharding import PartitionSpec as P

MX = 512
MY = 512
STEPS = 4
ZINJ = 1
LAYERS = 6

COURANT = 0.5
OMEGA = 0.7
PERMITTIVITY = (1.0, 2.6, 11.9, 2.1)

REACH = 8
SPAN = 2 * REACH
PAD = 8
HALO = 4
BASE = 16
SLOT = 32
WIDE = 8
REACHED = STEPS - 1
RESPONSE_SLOT = 21
HIGH_SIDE = 10
LANES = 128
VMEM_LIMIT = 24 * 1024 * 1024
X_LIMIT = 60_700_000


def split_bf16(table):
    high = table.astype(ml_dtypes.bfloat16)
    low = (table - high.astype(np.float64)).astype(ml_dtypes.bfloat16)
    return high, low


def padded(lanes):
    return -(-lanes // LANES) * LANES


@functools.lru_cache(maxsize=None)
def x_seeds(n_tx, rows_kx, cells_x):
    window = rows_kx + SPAN
    wide = padded(window)
    full = cells_x * n_tx
    turns = [8 << k for k in range((cells_x // 8).bit_length())]
    count = 8 + len(turns) + n_tx
    table = np.zeros((n_tx, -(-count // 8) * 8, 2 * wide), np.float32)
    for own in range(n_tx):
        freq = own * rows_kx - MX // 2 - REACH + np.arange(window)
        tiles = [(own + distance) % n_tx * cells_x for distance in range(n_tx)]
        x = np.array(list(range(-PAD, 8 - PAD)) + turns + tiles)
        angle = np.mod(x[:, None] * freq[None, :], full) * (2.0 * math.pi / full)
        table[own, :count, :window] = np.cos(angle)
        table[own, :count, wide : wide + window] = np.sin(angle)
    return table, len(turns)


@functools.lru_cache(maxsize=None)
def y_tables(n_ty, cols_ky, cells_y):
    full = cells_y * n_ty
    window = cols_ky + SPAN
    edge = np.concatenate([np.arange(-HALO, 0), cells_y + np.arange(HALO)])
    y = np.concatenate([np.arange(cells_y), edge])
    table = np.zeros((n_ty, LANES + 2 * SPAN, 2 * cells_y + LANES))
    for block in range(n_ty):
        freq = block * cols_ky - MY // 2 - REACH + np.arange(window)
        angle = np.mod(freq[:, None] * y[None, :], full) * (2.0 * math.pi / full)
        cos, sin = np.cos(angle), np.sin(angle)

        def placed(re_cols, im_cols):
            out = np.zeros((window, 2 * cells_y + LANES))
            out[:, :cells_y] = re_cols[:, :cells_y]
            out[:, cells_y : 2 * cells_y] = im_cols[:, :cells_y]
            out[:, 2 * cells_y : 2 * cells_y + 2 * HALO] = re_cols[:, cells_y:]
            out[:, 2 * cells_y + 2 * HALO : 2 * cells_y + 4 * HALO] = im_cols[:, cells_y:]
            return out

        from_re = placed(cos, sin)
        from_im = placed(-sin, cos)
        table[block, :cols_ky] = from_re[:cols_ky]
        table[block, cols_ky : 2 * cols_ky] = from_im[:cols_ky]
        table[block, LANES : LANES + SPAN] = from_re[cols_ky:]
        table[block, LANES + SPAN :] = from_im[cols_ky:]
    return split_bf16(table)


@functools.lru_cache(maxsize=None)
def y_phases(n_ty, cols_ky, cells_y):
    full = cells_y * n_ty
    out = np.zeros((n_ty, n_ty, 8, LANES), np.float32)
    for own in range(n_ty):
        for block in range(n_ty):
            freq = block * cols_ky - MY // 2 - REACH + np.arange(cols_ky + SPAN)
            angle = np.mod(freq * own * cells_y, full) * (2.0 * math.pi / full)
            cos, sin = np.cos(angle), np.sin(angle)
            out[own, block, 0, :cols_ky] = cos[:cols_ky]
            out[own, block, 0, cols_ky : 2 * cols_ky] = cos[:cols_ky]
            out[own, block, 1, :cols_ky] = -sin[:cols_ky]
            out[own, block, 1, cols_ky : 2 * cols_ky] = sin[:cols_ky]
            for group in range(LANES // (2 * SPAN)):
                at = group * 2 * SPAN
                out[own, block, 2, at : at + SPAN] = cos[cols_ky:]
                out[own, block, 2, at + SPAN : at + 2 * SPAN] = cos[cols_ky:]
                out[own, block, 3, at : at + SPAN] = -sin[cols_ky:]
                out[own, block, 3, at + SPAN : at + 2 * SPAN] = sin[cols_ky:]
    return out


def lasting(microseconds):
    moved = int(microseconds * 3.69e6)
    return pl.CostEstimate(flops=0, transcendentals=0, bytes_accessed=moved)


def lane_of(shape):
    return lax.broadcasted_iota(jnp.int32, shape, len(shape) - 1)


def rolled(value, shift):
    shift = shift % LANES
    return value if shift == 0 else pltpu.roll(value, shift, 1)


def halves(value):
    high = value.astype(jnp.bfloat16)
    low = (value - high.astype(jnp.float32)).astype(jnp.bfloat16)
    return high, low


def dot32(a, b):
    return jnp.dot(a, b, preferred_element_type=jnp.float32)


def fold_groups(rows, count):
    tiles = rows // 8
    sizes = [8 * (tiles // count + (1 if g < tiles % count else 0)) for g in range(count)]
    starts = [sum(sizes[:g]) for g in range(count)]
    return list(zip(starts, sizes))


def folded_rows(rows, count):
    return fold_groups(rows, count)[0][1]


def folded(value, count):
    groups = fold_groups(value.shape[0], count)
    tall, wide = groups[0][1], LANES // count
    lane = lane_of((tall, LANES))
    total = jnp.zeros((tall, LANES), value.dtype)
    for g, (start, size) in enumerate(groups):
        part = value[start : start + size]
        if size < tall:
            part = jnp.concatenate([part, jnp.zeros((tall - size, LANES), value.dtype)], 0)
        keep = (lane >= wide * g) & (lane < wide * (g + 1))
        total = jnp.where(keep, rolled(part, wide * g), total)
    return total


def unfolded(value, rows, count, at):
    wide = LANES // count
    parts = []
    for g, (_, size) in enumerate(fold_groups(rows, count)):
        parts.append(rolled(value[:size], at - wide * g))
    return jnp.concatenate(parts, 0)


def turned(cos, sin, by_cos, by_sin):
    return cos * by_cos - sin * by_sin, sin * by_cos + cos * by_sin


def fill_table(n_turns, seed_ref, high_ref, low_ref):
    n_tx, rows, both = high_ref.shape
    wide = both // 2

    def row(i):
        return seed_ref[i : i + 1, :wide], seed_ref[i : i + 1, wide:]

    cos, sin = seed_ref[:8, :wide], seed_ref[:8, wide:]
    for k in range(n_turns):
        more = min(8 << k, rows - (8 << k))
        new = turned(cos[:more], sin[:more], *row(8 + k))
        cos, sin = jnp.concatenate([cos, new[0]], 0), jnp.concatenate([sin, new[1]], 0)
    for distance in range(n_tx):
        there = turned(cos, sin, *row(8 + n_turns + distance))
        for part in range(2):
            high, low = halves(there[part])
            high_ref[distance, :, part * wide : (part + 1) * wide] = high
            low_ref[distance, :, part * wide : (part + 1) * wide] = low


def x_kernel(
    n_turns, place_ref, offs_in, orders_in, seeds_in, e_in, h_in, m_in, *refs,
):
    *out_refs, rim_ref = refs[:-12]
    (
        edge_ref, last_ref, offs_ref, orders_ref, seed_ref, wh_ref, wl_ref, line_ref, acc_ref,
        q_ref, sems, rim_sems,
    ) = refs[-12:]
    own = place_ref[0]
    copies = [
        pltpu.make_async_copy(seeds_in.at[place_ref[1]], seed_ref, sems.at[0]),
        pltpu.make_async_copy(orders_in, orders_ref, sems.at[1]),
        pltpu.make_async_copy(offs_in, offs_ref, sems.at[2]),
    ]
    cells_x = e_in.shape[2]
    for k, start in enumerate((0, cells_x - 8)):
        at = pl.ds(start, 8)
        for i, ref in enumerate((e_in, h_in)):
            source = ref.at[:, :, at, :]
            copies.append(pltpu.make_async_copy(source, edge_ref.at[i, k], rim_sems.at[i, k]))
        copies.append(pltpu.make_async_copy(m_in.at[:, at, :], last_ref.at[k], rim_sems.at[2, k]))
    for copy in copies:
        copy.start()
    points, _, cols_ky, rows_kx = orders_ref.shape
    n_tx, rows, both = wh_ref.shape
    half = rows // 2
    acc_ref[...] = jnp.zeros_like(acc_ref)
    line_ref[...] = jnp.zeros_like(line_ref)
    wide = line_ref.shape[4]
    copies[0].wait()
    fill_table(n_turns, seed_ref, wh_ref, wl_ref)
    copies[1].wait()
    copies[2].wait()
    for point in range(points):
        down = offs_ref[0, point] + REACH
        across = offs_ref[1, point] + REACH
        for part in range(2):
            for tile in range(rows_kx // wide):
                lanes = slice(tile * wide, (tile + 1) * wide)
                line = line_ref.at[point, part, tile]
                line[pl.ds(across, cols_ky), :] = orders_ref[point, part, :, lanes]
                acc_ref[part, pl.ds(down + tile * wide, wide), :] += line[...].T
    s_re = acc_ref[0]
    s_im = acc_ref[1]
    lane = lane_of(s_re.shape)
    re_by, im_by = rolled(s_re, cols_ky), rolled(s_im, cols_ky)

    def main(re, im_by):
        out = jnp.where(lane < cols_ky, re, im_by)
        return out if 2 * cols_ky == LANES else jnp.where(lane < 2 * cols_ky, out, 0.0)

    def spill(re_back, im_back):
        out = jnp.where(lane < SPAN, re_back, im_back)
        return jnp.where(lane < 2 * SPAN, out, 0.0)

    same = 2 * cols_ky == LANES
    re_back = re_by if same else rolled(s_re, -cols_ky)
    im_back = im_by if same else rolled(s_im, -cols_ky)
    top = [main(s_re, im_by), spill(re_back, rolled(s_im, SPAN - cols_ky))]
    bottom = [main(-s_im, re_by), spill(-im_back, rolled(s_re, SPAN - cols_ky))]
    right = jnp.concatenate([jnp.concatenate(top, 1), jnp.concatenate(bottom, 1)], 0)
    right_h, right_l = halves(right)
    for distance in range(n_tx):
        w_h = wh_ref[distance]
        q_ref[...] = dot32(w_h, right_h) + (dot32(wl_ref[distance], right_h) + dot32(w_h, right_l))
        for flip in range(2):
            start = pl.multiple_of((own ^ flip) * half, 8)
            block = q_ref[pl.ds(start, half), :]
            out_refs[2 * distance + flip][:half, :] = block[:, :LANES]
            out_refs[2 * distance + flip][half:, :] = folded(block[:, LANES:], 4)
    for copy in copies[3:]:
        copy.wait()
    row = lax.broadcasted_iota(jnp.int32, (LAYERS, 8, LANES), 1)
    for j in range(7):
        if j < 6:
            first, final = (edge_ref[j // 3, k, j % 3] for k in range(2))
        else:
            first, final = (coefficient_of(last_ref[k]) for k in range(2))
        rim_ref[j * LAYERS : (j + 1) * LAYERS] = jnp.where(row < HALO, first, final)


def x_stage(place, offsets, orders, n_tx, e_field, h_field, material):
    points, _, cols_ky, rows_kx = orders.shape
    cells_x = e_field.shape[2]
    wide = min(rows_kx, LANES)
    seeds, n_turns = x_seeds(n_tx, rows_kx, cells_x)
    rows = cells_x + 2 * PAD
    half = rows // 2
    height = half + folded_rows(half, 4)
    f32 = jnp.float32
    table = pltpu.VMEM((n_tx, rows, seeds.shape[2]), jnp.bfloat16)
    return pl.pallas_call(
        functools.partial(x_kernel, n_turns),
        in_specs=[pl.BlockSpec(memory_space=pltpu.SMEM)] + [pl.BlockSpec(memory_space=pltpu.HBM)] * 6,
        out_shape=(jax.ShapeDtypeStruct((height, LANES), f32),) * (2 * n_tx)
        + (jax.ShapeDtypeStruct((7 * LAYERS, 2 * HALO, LANES), f32),),
        scratch_shapes=[
            pltpu.VMEM((2, 2, 3, LAYERS, 8, LANES), f32),
            pltpu.VMEM((2, LAYERS, 8, LANES), jnp.int32),
            pltpu.SMEM(offsets.shape, jnp.int32),
            pltpu.VMEM(orders.shape, f32),
            pltpu.VMEM(seeds.shape[1:], f32),
            table,
            table,
            pltpu.VMEM((points, 2, rows_kx // wide, LANES, wide), f32),
            pltpu.VMEM((2, seeds.shape[2] // 2, LANES), f32),
            pltpu.VMEM((rows, 2 * LANES), f32),
            pltpu.SemaphoreType.DMA((3,)),
            pltpu.SemaphoreType.DMA((3, 2)),
        ],
        compiler_params=pltpu.CompilerParams(vmem_limit_bytes=X_LIMIT),
        cost_estimate=lasting(3.5),
        name="x_stage",
    )(place, offsets, orders, jnp.asarray(seeds), e_field, h_field, material)


def sum_kernel(*refs):
    *part_refs, _, out_ref = refs
    total = part_refs[0][...]
    for ref in part_refs[1:]:
        total = total + ref[...]
    out_ref[...] = total


def summed(parts, after):
    return pl.pallas_call(
        sum_kernel,
        out_shape=jax.ShapeDtypeStruct(parts[0].shape, jnp.float32),
        compiler_params=pltpu.CompilerParams(vmem_limit_bytes=VMEM_LIMIT),
        cost_estimate=lasting(0.4),
        name="sum_parts",
    )(*parts, after)


def y_kernel(cols_ky, half, place_ref, *refs):
    *block_refs, th_ref, tl_ref, phase_ref, _, out_ref = refs
    n_ty = len(block_refs)
    lane = lane_of((half, LANES))
    mains, spills, numbers = [], [], []
    for number, ref in enumerate(block_refs):
        block = place_ref[2] ^ number
        numbers.append(block)
        phase = phase_ref[block]
        main = ref[:half, :]
        if 2 * cols_ky == LANES:
            swapped = rolled(main, cols_ky)
        else:
            swapped = jnp.where(lane < cols_ky, rolled(main, -cols_ky), rolled(main, cols_ky))
        mains.append(main * phase[0:1] + swapped * phase[1:2])
        spill = ref[half:, :]
        small = lane_of(spill.shape)
        other = jnp.where((small & (2 * SPAN - 1)) < SPAN, rolled(spill, -SPAN), rolled(spill, SPAN))
        spills.append(spill * phase[2:3] + other * phase[3:4])
    packed = []
    for first in range(0, n_ty, 4):
        total = None
        for g in range(4):
            part = unfolded(spills[first + g], half, 4, 32 * g)
            total = part if total is None else jnp.where(lane >= 32 * g, part, total)
        packed.append(total)
    result = None
    for first in range(0, n_ty, 2):
        left_h, left_l = halves(jnp.concatenate(mains[first : first + 2], 1))
        t_h = jnp.concatenate([th_ref[numbers[first + g], :LANES, :] for g in range(2)], 0)
        t_l = jnp.concatenate([tl_ref[numbers[first + g], :LANES, :] for g in range(2)], 0)
        part = dot32(left_h, t_h) + (dot32(left_h, t_l) + dot32(left_l, t_h))
        result = part if result is None else result + part
    for first in range(0, n_ty, 8):
        left_h, left_l = halves(jnp.concatenate(packed[first // 4 : first // 4 + 2], 1))
        t_h = jnp.concatenate([th_ref[numbers[first + g], LANES:, :] for g in range(8)], 0)
        t_l = jnp.concatenate([tl_ref[numbers[first + g], LANES:, :] for g in range(8)], 0)
        result = result + (dot32(left_h, t_h) + (dot32(left_h, t_l) + dot32(left_l, t_h)))
    out_ref[:half, :] = result[:, :LANES]
    out_ref[half : 2 * half, :] = result[:, LANES : 2 * LANES]
    out_ref[2 * half :, :] = folded(result[:, 2 * LANES :], 8)


def y_stage(place, blocks, cols_ky, cells_y, half, after):
    n_ty = len(blocks)
    t_h, t_l = y_tables(n_ty, cols_ky, cells_y)
    phases = y_phases(n_ty, cols_ky, cells_y)
    whole = lambda shape: pl.BlockSpec(shape, lambda i, place: (0,) * len(shape))
    height = 2 * half + folded_rows(half, 8)
    return pl.pallas_call(
        functools.partial(y_kernel, cols_ky, half),
        grid_spec=pltpu.PrefetchScalarGridSpec(
            num_scalar_prefetch=1,
            grid=(1,),
            in_specs=[whole(b.shape) for b in blocks]
            + [
                whole(t_h.shape),
                whole(t_l.shape),
                pl.BlockSpec((None,) + phases.shape[1:], lambda i, place: (place[2], 0, 0, 0)),
                whole(after.shape),
            ],
            out_specs=whole((height, LANES)),
        ),
        out_shape=jax.ShapeDtypeStruct((height, LANES), jnp.float32),
        compiler_params=pltpu.CompilerParams(vmem_limit_bytes=VMEM_LIMIT),
        cost_estimate=lasting(1.5),
        name="y_stage",
    )(place, *blocks, jnp.asarray(t_h), jnp.asarray(t_l), jnp.asarray(phases), after)


def coefficient_of(material):
    value = jnp.where(material == 0, COURANT / PERMITTIVITY[0], COURANT / PERMITTIVITY[1])
    value = jnp.where(material == 2, COURANT / PERMITTIVITY[2], value)
    return jnp.where(material == 3, COURANT / PERMITTIVITY[3], value).astype(jnp.float32)


def pack_kernel(
    e_ref, h_ref, c_ref, x_ref, column_ref, message_ref, ext_ref, w_ref, low_ref, high_ref
):
    cells_x = e_ref.shape[2]
    end = BASE + cells_x
    rows = cells_x + 2 * PAD
    lane = lane_of((rows, LANES))
    by_product = []
    blank = jnp.zeros((PAD - HALO, LANES), jnp.float32)
    for j in range(7):
        scale = 1.0 if 3 <= j < 6 else 0.5
        strips = [jnp.zeros((rows, LANES), jnp.float32)] * 2
        planes = [[], []]
        for z in range(LAYERS):
            if j < 3:
                body = e_ref[j, z] * scale
            elif j < 6:
                body = h_ref[j - 3, z]
            else:
                body = c_ref[z]
            rims = x_ref[j * LAYERS + z] * scale
            full = jnp.concatenate([blank, rims[HALO:], body, rims[:HALO], blank], 0)
            if j == 6:
                ext_ref[z, 0 : BASE - PAD, :] = jnp.zeros((BASE - PAD, LANES), jnp.float32)
                ext_ref[z, BASE - PAD : end + PAD, :] = full
                ext_ref[z, end + PAD : end + BASE, :] = jnp.zeros((BASE - PAD, LANES), jnp.float32)
            g, at = z % 2, (z // 2) * SLOT
            if j in BY_PRODUCT:
                planes[g].append(beside(full))
                continue
            keep = (lane >= at) & (lane < at + 2 * WIDE)
            strips[g] = jnp.where(keep, rolled(full, at + WIDE), strips[g])
        for g in range(2):
            if j in BY_PRODUCT:
                by_product.append(jnp.concatenate(planes[g], 1))
            else:
                w_ref[j, g] = strips[g]
    taken = dot32(jnp.concatenate(by_product, 0), column_ref[...])
    for i, (j, g) in enumerate((j, g) for j in BY_PRODUCT for g in range(2)):
        w_ref[j, g] = taken[i * rows : (i + 1) * rows]
    items = [beside(w_ref[j, g]) for j in range(7) for g in range(2)]
    items += [jnp.zeros_like(items[0])] * (16 - len(items))
    sides = [jnp.concatenate(items[8 * a : 8 * a + 8], 1) for a in range(2)]
    sent = dot32(jnp.concatenate(sides, 0), message_ref[...])
    for a in range(2):
        low_ref[a] = sent[a * rows : (a + 1) * rows, :LANES]
        high_ref[a] = sent[a * rows : (a + 1) * rows, LANES:]


def pack(e_field, h_field, coefficient, x_rims):
    cells_x = e_field.shape[2]
    rows = cells_x + 2 * PAD
    tall = cells_x + 2 * BASE
    f32 = jnp.float32
    return pl.pallas_call(
        pack_kernel,
        out_shape=(
            jax.ShapeDtypeStruct((LAYERS, tall, LANES), f32),
            jax.ShapeDtypeStruct((7, 2, rows, LANES), f32),
            jax.ShapeDtypeStruct((2, rows, LANES), f32),
            jax.ShapeDtypeStruct((2, rows, LANES), f32),
        ),
        compiler_params=pltpu.CompilerParams(vmem_limit_bytes=VMEM_LIMIT),
        cost_estimate=lasting(2.2),
        name="pack",
    )(
        e_field, h_field, coefficient, x_rims,
        jnp.asarray(column_matrix()),
        jnp.asarray(message_matrix()),
    )


def total(terms):
    out = None
    for sign, value in terms:
        if value is None:
            continue
        if out is None:
            out = value if sign > 0 else -value
        else:
            out = out + value if sign > 0 else out - value
    return out


def add(a, b):
    return total([(1, a), (1, b)])


def differ(a, b):
    return total([(1, a), (-1, b)])


def curl_of_e(e, e_z, e_x, e_y):
    return (
        differ(differ(e_z[1], e[1]), differ(e_y[2], e[2])),
        differ(differ(e_x[2], e[2]), differ(e_z[0], e[0])),
        differ(differ(e_y[0], e[0]), differ(e_x[1], e[1])),
    )


def curl_of_h(h, h_z, h_x, h_y):
    return (
        differ(differ(h[2], h_y[2]), differ(h[1], h_z[1])),
        differ(differ(h[0], h_z[0]), differ(h[2], h_x[2])),
        differ(differ(h[1], h_x[1]), differ(h[0], h_y[0])),
    )


def moved(value, shift):
    return None if value is None else rolled(value, shift)


class Tile:
    def __init__(self, ref, live):
        self.ref, self.live = ref, set(live)

    def load(self, j, z, start, size):
        return self.ref[j, z, start : start + size, :] if (j, z) in self.live else None

    def store(self, j, z, start, value):
        if value is not None:
            self.ref[j, z, start : start + value.shape[0], :] = value
            self.live.add((j, z))

    def step_h(self, z, start, size):
        e = [self.load(j, z, start, size) for j in range(3)]
        e_z = [self.load(j, z + 1, start, size) for j in range(2)] + [None]
        e_x = [None] + [self.load(j, z, start + 1, size) for j in (1, 2)]
        e_y = [moved(e[0], -1), None, moved(e[2], -1)]
        new = []
        for j, change in enumerate(curl_of_e(e, e_z, e_x, e_y)):
            new.append(add(self.load(3 + j, z, start, size), change))
            self.store(3 + j, z, start, new[j])
        return new

    def step_e(self, z, start, size, factor):
        h = [self.load(3 + j, z, start, size) for j in range(3)]
        h_z = [self.load(3 + j, z - 1, start, size) for j in range(2)] + [None]
        h_x = [None] + [self.load(3 + j, z, start - 1, size) for j in (1, 2)]
        h_y = [moved(h[0], 1), None, moved(h[2], 1)]
        new = []
        for j, change in enumerate(curl_of_h(h, h_z, h_x, h_y)):
            old = self.load(j, z, start, size)
            new.append(old if change is None else add(old, factor * change))
        return new


class Strip:
    def __init__(self, ref, rows):
        self.ref, self.start, self.rows = ref, BASE - PAD, rows
        self.lane = lane_of((rows, LANES))

    def load(self, j, g, by=0):
        return self.ref[j, g, self.start + by : self.start + by + self.rows, :]

    def store(self, j, g, value):
        self.ref[j, g, self.start : self.start + self.rows, :] = value

    def step_h(self, fresh=False):
        e = [[self.load(j, g) for j in range(3)] for g in range(2)]
        inside = self.lane < 2 * SLOT
        above = [
            [e[1][0], e[1][1], None],
            [jnp.where(inside, rolled(e[0][j], -SLOT), 0.0) for j in range(2)] + [None],
        ]
        for g in range(2):
            e_x = [None, self.load(1, g, 1), self.load(2, g, 1)]
            e_y = [rolled(e[g][0], -1), None, rolled(e[g][2], -1)]
            for j, change in enumerate(curl_of_e(e[g], above[g], e_x, e_y)):
                self.store(3 + j, g, change if fresh else self.load(3 + j, g) + change)

    def step_e(self, factor):
        h = [[self.load(3 + j, g) for j in range(3)] for g in range(2)]
        inside = self.lane >= SLOT
        below = [
            [jnp.where(inside, rolled(h[1][j], SLOT), 0.0) for j in range(2)] + [None],
            [h[0][0], h[0][1], None],
        ]
        new = []
        for g in range(2):
            h_x = [None, self.load(4, g, -1), self.load(5, g, -1)]
            h_y = [rolled(h[g][0], 1), None, rolled(h[g][2], 1)]
            change = curl_of_h(h[g], below[g], h_x, h_y)
            new.append([self.load(j, g) + factor[g] * change[j] for j in range(3)])
        return new

    def all_edges(self, cells_x, matrix):
        values = [
            beside(self.ref[j, g, BASE : BASE + cells_x, :]) for j in range(6) for g in range(2)
        ]
        return dot32(jnp.concatenate(values, 0), matrix)


def beside(value):
    return jnp.concatenate(halves(value), 1)


def matrix_of(pairs, columns, rows=LANES):
    out = np.zeros((rows, columns), ml_dtypes.bfloat16)
    for first_row, first_column, count in pairs:
        for i in range(count):
            out[first_row + i, first_column + i] = 1
    return out


def doubled(matrix):
    blocks = matrix.reshape(-1, LANES, matrix.shape[1])
    return np.concatenate([m for block in blocks for m in (block, block)], 0)


def near_matrix():
    own, at = 2 * REACHED, ZINJ * RESPONSE_SLOT
    pairs = [(0, at + REACHED, own), (LANES - own, at + HIGH_SIDE, own)]
    return doubled(matrix_of(pairs, LANES))


def outside_matrix():
    pairs = []
    for part in range(2):
        lane, at = part * 2 * HALO, part * LANES + ZINJ * RESPONSE_SLOT
        pairs.append((lane + HALO - REACHED, at, REACHED))
        pairs.append((lane + HALO, at + HIGH_SIDE + 2 * REACHED, REACHED))
    return doubled(matrix_of(pairs, 2 * LANES))


def response_edge_matrix():
    pairs = []
    for z in range(min(LAYERS, ZINJ + STEPS)):
        at = z * RESPONSE_SLOT + REACHED
        pairs.append((at, z * LANES, REACHED))
        pairs.append((at + HIGH_SIDE, (z + 1) * LANES - REACHED, REACHED))
    return doubled(matrix_of(pairs, min(LAYERS, ZINJ + STEPS) * LANES))


def factor_matrix():
    pairs = []
    for z in range(LAYERS):
        at, to = z % 2 * LANES + z // 2 * SLOT, z * RESPONSE_SLOT
        pairs.append((at + HALO - REACHED, to, 3 * REACHED))
        pairs.append((at + 16 + WIDE - 2 * REACHED, to + HIGH_SIDE, 3 * REACHED))
    return doubled(matrix_of(pairs, LANES, 2 * LANES))


def edge_matrix():
    pairs = []
    for slot in range(LAYERS // 2):
        pairs.append((slot * SLOT + 4, slot * LANES, HALO))
        pairs.append((slot * SLOT + 20, slot * LANES + LANES - HALO, HALO))
    return doubled(matrix_of(pairs, LAYERS // 2 * LANES))


def column_matrix():
    pairs = []
    for slot in range(LAYERS // 2):
        pairs.append((slot * LANES + LANES - WIDE, slot * SLOT, WIDE))
        pairs.append((slot * LANES, slot * SLOT + WIDE, WIDE))
    return doubled(matrix_of(pairs, LANES, LAYERS // 2 * LANES))


def message_matrix():
    pairs = []
    for item in range(8):
        for slot in range(LAYERS // 2):
            at, to = item * LANES + slot * SLOT, slot * SLOT + HALO * item
            pairs.append((at + 4, to, HALO))
            pairs.append((at + 8, LANES + to, HALO))
    return doubled(matrix_of(pairs, 2 * LANES, 8 * LANES))


def strip_matrices():
    own, got = [], []
    for slot in range(LAYERS // 2):
        at = slot * SLOT
        own += [(at, at + 16, WIDE), (at + 8, at + 4, WIDE)]
        for item in range(8):
            to = item * LANES + at
            got.append((at + HALO * item, to, HALO))
            got.append((LANES + at + HALO * item, to + 24, HALO))
    return doubled(matrix_of(own, LANES)), doubled(matrix_of(got, 8 * LANES, 2 * LANES))


class ResponseStrip:
    def __init__(self, ref, rows):
        self.ref, self.start, self.rows = ref, BASE - PAD, rows
        self.lane = lane_of((rows, LANES))

    def load(self, j, by=0):
        return self.ref[j, self.start + by : self.start + by + self.rows, :]

    def store(self, j, value):
        self.ref[j, self.start : self.start + self.rows, :] = value

    def step_h(self, fresh):
        e = [self.load(j) for j in range(3)]
        inside = self.lane < (LAYERS - 1) * RESPONSE_SLOT
        e_z = [jnp.where(inside, rolled(e[j], -RESPONSE_SLOT), 0.0) for j in range(2)] + [None]
        e_x = [None, self.load(1, 1), self.load(2, 1)]
        e_y = [rolled(e[0], -1), None, rolled(e[2], -1)]
        for j, change in enumerate(curl_of_e(e, e_z, e_x, e_y)):
            self.store(3 + j, change if fresh else self.load(3 + j) + change)

    def step_e(self, factor):
        h = [self.load(3 + j) for j in range(3)]
        inside = self.lane >= RESPONSE_SLOT
        h_z = [jnp.where(inside, rolled(h[j], RESPONSE_SLOT), 0.0) for j in range(2)] + [None]
        h_x = [None, self.load(4, -1), self.load(5, -1)]
        h_y = [rolled(h[0], 1), None, rolled(h[2], 1)]
        change = curl_of_h(h, h_z, h_x, h_y)
        return [self.load(j) + factor * change[j] for j in range(3)]

    def all_edges(self, cells_x, matrix):
        values = [beside(self.ref[j, BASE : BASE + cells_x, :]) for j in range(6)]
        return dot32(jnp.concatenate(values, 0), matrix)


def with_edges(value, edges_ref, strip, block, width):
    start = strip * value.shape[0]
    own = edges_ref[start : start + value.shape[0], block * LANES : (block + 1) * LANES]
    lane = lane_of(own.shape)
    outer = (lane < width) | (lane >= LANES - width)
    return jnp.where(outer, own, value)


BY_PRODUCT = (0, 1, 2)
EVERY = [(j, z) for j in range(6) for z in range(LAYERS)]


def free_steps(tile, steps, start, rows, factor_of):
    for _ in range(steps):
        for z in range(LAYERS):
            tile.step_h(z, start, rows)
            for j, value in enumerate(tile.step_e(z, start, rows, factor_of(z))):
                tile.store(j, z, start, value)


def first_kernel(e_ref, h_ref, m_ref, c_ref, f_ref, token_ref):
    cells_x = e_ref.shape[2]
    token_ref[...] = jnp.zeros_like(token_ref)
    for z in range(LAYERS):
        c_ref[z] = coefficient_of(m_ref[z]) * 0.5
        for j in range(3):
            f_ref[j, z, PAD : PAD + cells_x, :] = e_ref[j, z] * 0.5
            f_ref[3 + j, z, PAD : PAD + cells_x, :] = h_ref[j, z]
        for j in range(6):
            f_ref[j, z, :PAD, :] = jnp.zeros((PAD, LANES), jnp.float32)
            f_ref[j, z, PAD + cells_x :, :] = jnp.zeros((PAD, LANES), jnp.float32)
    free_steps(Tile(f_ref, EVERY), STEPS // 2, PAD, cells_x, lambda z: c_ref[z])


def first_steps(e_field, h_field, material):
    cells_x = e_field.shape[2]
    f32 = jnp.float32
    return pl.pallas_call(
        first_kernel,
        out_shape=(
            jax.ShapeDtypeStruct((LAYERS, cells_x, LANES), f32),
            jax.ShapeDtypeStruct((6, LAYERS, cells_x + 2 * PAD, LANES), f32),
            jax.ShapeDtypeStruct((8, LANES), f32),
        ),
        compiler_params=pltpu.CompilerParams(vmem_limit_bytes=VMEM_LIMIT),
        cost_estimate=lasting(3.3),
        name="first_steps",
    )(e_field, h_field, material)


class Rows:
    def __init__(self, ref):
        self.ref = ref

    def load(self, j, by=0):
        return self.ref[j, :, 8 + by : 40 + by, :]

    def step(self, factor):
        zero = jnp.zeros((1, 32, LANES), jnp.float32)
        e = [self.load(j) for j in range(3)]
        e_z = [jnp.concatenate([e[j][1:], zero], 0) for j in range(2)] + [None]
        e_x = [None, self.load(1, 1), self.load(2, 1)]
        e_y = [pltpu.roll(e[0], LANES - 1, 2), None, pltpu.roll(e[2], LANES - 1, 2)]
        for j, change in enumerate(curl_of_e(e, e_z, e_x, e_y)):
            self.ref[3 + j, :, 8:40, :] = self.load(3 + j) + change
        h = [self.load(3 + j) for j in range(3)]
        h_z = [jnp.concatenate([zero, h[j][:-1]], 0) for j in range(2)] + [None]
        h_x = [None, self.load(4, -1), self.load(5, -1)]
        h_y = [pltpu.roll(h[0], 1, 2), None, pltpu.roll(h[2], 1, 2)]
        for j, change in enumerate(curl_of_h(h, h_z, h_x, h_y)):
            self.ref[j, :, 8:40, :] = e[j] + factor * change


def later_kernel(f_in, c_ref, e_ref, h_ref, x_ref, out_ref, token_ref, f_ref, r_ref):
    cells_x = c_ref.shape[1]
    token_ref[...] = jnp.zeros_like(token_ref)
    blank = jnp.zeros((LAYERS, PAD - HALO, LANES), jnp.float32)
    zero = jnp.zeros((LAYERS, 8, LANES), jnp.float32)
    factor = None
    for j in range(7):
        ref = e_ref.at[j] if j < 3 else h_ref.at[j - 3] if j < 6 else c_ref
        scale = 1.0 if 3 <= j < 6 else 0.5
        own = 0.5 if j < 3 else 1.0
        rims = x_ref[j * LAYERS : (j + 1) * LAYERS] * scale
        first, final = ref[:, :8, :] * own, ref[:, cells_x - 8 :, :] * own
        rows = [blank, rims[:, HALO:], first, final, rims[:, :HALO], blank]
        if j < 6:
            r_ref[j] = jnp.concatenate([zero] + rows + [zero], 1)
        else:
            factor = jnp.concatenate(rows, 1)
    edge = Rows(r_ref)
    for _ in range(STEPS):
        edge.step(factor)
    f_ref[...] = f_in[...]
    tile = Tile(f_ref, EVERY)
    free_steps(tile, STEPS - STEPS // 2, PAD, cells_x, lambda z: c_ref[z])
    row = lax.broadcasted_iota(jnp.int32, (8, LANES), 0)
    for j, z in EVERY:
        top = jnp.where(row < HALO, r_ref[j, z, 16:24, :], f_ref[j, z, PAD : PAD + 8, :])
        end = f_ref[j, z, PAD + cells_x - 8 : PAD + cells_x, :]
        end = jnp.where(row >= HALO, r_ref[j, z, 24:32, :], end)
        inner = f_ref[j, z, PAD + 8 : PAD + cells_x - 8, :]
        out_ref[j, z] = jnp.concatenate([top, inner, end], 0)


def later_steps(state, coefficient, e_field, h_field, x_rims):
    cells_x = e_field.shape[2]
    f32 = jnp.float32
    return pl.pallas_call(
        later_kernel,
        out_shape=(
            jax.ShapeDtypeStruct((6, LAYERS, cells_x, LANES), f32),
            jax.ShapeDtypeStruct((8, LANES), f32),
        ),
        scratch_shapes=[
            pltpu.VMEM(state.shape, f32),
            pltpu.VMEM((6, LAYERS, 48, LANES), f32),
        ],
        compiler_params=pltpu.CompilerParams(vmem_limit_bytes=VMEM_LIMIT),
        cost_estimate=lasting(3.7),
        name="later_steps",
    )(state, coefficient, e_field, h_field, x_rims)


def strip_kernel(
    w_ref, low_ref, high_ref, free_ref, own_ref, got_ref, edge_ref, to_ref, _, factor_ref, out_ref,
    s_ref, edges_ref,
):
    rows = w_ref.shape[2]
    first = BASE - PAD
    mine = [beside(w_ref[j, g]) for j in range(7) for g in range(2)]
    mine = dot32(jnp.concatenate(mine, 0), own_ref[...])
    got = [jnp.concatenate([beside(low_ref[a]), beside(high_ref[a])], 1) for a in range(2)]
    got = dot32(jnp.concatenate(got, 0), got_ref[...])
    factor = []
    for j in range(7):
        for g in range(2):
            i = 2 * j + g
            a, b = divmod(i, 8)
            value = mine[i * rows : (i + 1) * rows]
            value = value + got[a * rows : (a + 1) * rows, b * LANES : (b + 1) * LANES]
            if j < 6:
                s_ref[j, g, first : first + rows, :] = value
            else:
                factor.append(value)
    factor_ref[...] = dot32(jnp.concatenate([beside(f) for f in factor], 1), to_ref[...])
    strip = Strip(s_ref, rows)
    for step in range(STEPS):
        strip.step_h()
        new = strip.step_e(factor)
        for g in range(2):
            for j in range(3):
                strip.store(j, g, new[g][j])
    edges_ref[...] = strip.all_edges(out_ref.shape[2], edge_ref[...])
    for j, z in EVERY:
        out_ref[j, z] = with_edges(free_ref[j, z], edges_ref, 2 * j + z % 2, z // 2, HALO)


def strip_run(own_edges, low, high, free, after):
    rows = own_edges.shape[2]
    f32 = jnp.float32
    return pl.pallas_call(
        strip_kernel,
        out_shape=(
            jax.ShapeDtypeStruct((rows, LANES), f32),
            jax.ShapeDtypeStruct(free.shape, f32),
        ),
        scratch_shapes=[
            pltpu.VMEM((6, 2, rows + 2 * (BASE - PAD), LANES), f32),
            pltpu.VMEM((12 * free.shape[2], LAYERS // 2 * LANES), f32),
        ],
        compiler_params=pltpu.CompilerParams(vmem_limit_bytes=VMEM_LIMIT),
        cost_estimate=lasting(4),
        name="strip_run",
    )(
        own_edges, low, high, free, *(jnp.asarray(m) for m in strip_matrices()),
        jnp.asarray(edge_matrix()), jnp.asarray(factor_matrix()), after,
    )


def response_kernel(
    place_ref, c_ref, factor_ref, free_ref, mine_ref, other_ref, near_ref, outside_ref, edge_ref,
    e_out, h_out,
    f_ref, s_ref, plane_ref, rim_ref, done_ref, edges_ref, sems,
):
    cells_x = e_out.shape[2]
    copies = []

    def send(j, z, source):
        to = e_out.at[j, z] if j < 3 else h_out.at[j - 3, z]
        copies.append(pltpu.make_async_copy(source, to, sems.at[j, z]))
        copies[-1].start()

    far = [(j, z) for j, z in EVERY if z >= ZINJ + STEPS - (0 if j < 2 else 1)]
    for j, z in far:
        if j < 3:
            done_ref[j, z] = free_ref[j, z] * 2.0
            send(j, z, done_ref.at[j, z])
        else:
            send(j, z, free_ref.at[j, z])
    rows = cells_x + 2 * PAD
    half = rows // 2
    first = BASE - PAD
    own = place_ref[0]
    lane = lane_of((half, LANES))
    for ref, which in ((mine_ref, own), (other_ref, 1 - own)):
        at = pl.ds(pl.multiple_of(which * half, 8), half)
        for part in range(2):
            plane_ref[part, at, :] = ref[part * half : (part + 1) * half, :]
        rim_ref[0, at, :] = jnp.where(lane < 16, unfolded(ref[2 * half :, :], half, 8, 0), 0.0)
    outer = dot32(beside(rim_ref[0]), outside_ref[...])
    planes = jnp.concatenate([beside(plane_ref[part]) for part in range(2)], 0)
    inner = dot32(planes, near_ref[...])
    for part in range(2):
        own_part = outer[:, part * LANES : (part + 1) * LANES]
        rim_ref[part] = inner[part * rows : (part + 1) * rows] + own_part

    def injection(ref, step, start, size):
        cosine = 0.5 * COURANT * math.cos(OMEGA * step)
        sine = 0.5 * COURANT * math.sin(OMEGA * step)
        re, im = ref[0, start : start + size, :], ref[1, start : start + size, :]
        return [cosine * re - sine * im, sine * re + cosine * im, None]

    tile = Tile(f_ref, ())
    for j, value in enumerate(injection(plane_ref, 1, 0, rows)):
        tile.store(j, ZINJ, first, value)
    strip = ResponseStrip(s_ref, rows)
    s_ref[...] = jnp.zeros_like(s_ref)
    for j, value in enumerate(injection(rim_ref, 1, 0, rows)[:2]):
        strip.store(j, value)
    for step in range(2, STEPS + 1):
        strip.step_h(step == 2)
        new = strip.step_e(factor_ref[...])
        for j, value in enumerate(injection(rim_ref, step, 0, rows)):
            strip.store(j, add(new[j], value))
    edges_ref[...] = strip.all_edges(cells_x, edge_ref[...])
    for step in range(2, STEPS + 1):
        last = step == STEPS
        start, size = (BASE, cells_x) if last else (first, rows)
        for z in range(LAYERS):
            tile.step_h(z, first, rows - (PAD if last else 0))
            new = tile.step_e(z, start, size, c_ref[z, start : start + size, :])
            if z == ZINJ:
                source = injection(plane_ref, step, start - first, size)
                new = [add(a, b) for a, b in zip(new, source)]
            for j in range(3):
                if not last:
                    tile.store(j, z, start, new[j])
                    continue
                for i, value in ((j, new[j]), (3 + j, tile.load(3 + j, z, start, size))):
                    if (i, z) in far:
                        continue
                    value = with_edges(value, edges_ref, i, z, REACHED) + free_ref[i, z]
                    done_ref[i, z] = value * 2.0 if i < 3 else value
                    send(i, z, done_ref.at[i, z])
    for copy in copies:
        copy.wait()


def response(place, c_ext, factor, free, mine, other, cells_x):
    rows = cells_x + 2 * PAD
    tall = cells_x + 2 * BASE
    f32 = jnp.float32
    out = jax.ShapeDtypeStruct((3, LAYERS, cells_x, LANES), f32)
    vmem = pl.BlockSpec(memory_space=pltpu.VMEM)
    return pl.pallas_call(
        response_kernel,
        in_specs=[pl.BlockSpec(memory_space=pltpu.SMEM)] + [vmem] * 8,
        out_specs=(pl.BlockSpec(memory_space=pl.ANY),) * 2,
        out_shape=(out, out),
        scratch_shapes=[
            pltpu.VMEM((6, LAYERS, tall, LANES), f32),
            pltpu.VMEM((6, tall, LANES), f32),
            pltpu.VMEM((2, rows, LANES), f32),
            pltpu.VMEM((2, rows, LANES), f32),
            pltpu.VMEM((6, LAYERS, cells_x, LANES), f32),
            pltpu.VMEM((6 * cells_x, min(LAYERS, ZINJ + STEPS) * LANES), f32),
            pltpu.SemaphoreType.DMA((6, LAYERS)),
        ],
        compiler_params=pltpu.CompilerParams(vmem_limit_bytes=VMEM_LIMIT),
        cost_estimate=lasting(6.5),
        name="response",
    )(
        place, c_ext, factor, free, mine, other,
        jnp.asarray(near_matrix()), jnp.asarray(outside_matrix()),
        jnp.asarray(response_edge_matrix()),
    )


def along(block, axis, distance):
    n = lax.axis_size(axis)
    return lax.ppermute(block, axis, [((i - distance) % n, i) for i in range(n)])


def flipped(block, axis, bits):
    return lax.ppermute(block, axis, [(i, i ^ bits) for i in range(lax.axis_size(axis))])


def to_groups(block, n_src, n_tx, flip, distance):
    route = []
    for s in range(n_src):
        for t in range(n_tx):
            route.append((s * n_tx + t, (s ^ flip) * n_tx + (t + distance) % n_tx))
    return lax.ppermute(block, ("src", "tx"), route)


def per_device(orders, offsets, material, e_field, h_field):
    cols_ky = orders.shape[3]
    layers, cells_x, cells_y = material.shape
    n_src, n_tx, n_ty = lax.axis_size("src"), lax.axis_size("tx"), lax.axis_size("ty")
    half = cells_x // 2 + PAD
    place = jnp.stack([lax.axis_index("src"), lax.axis_index("tx"), lax.axis_index("ty")]).astype(
        jnp.int32
    )

    *parts, rims = x_stage(
        place, offsets.T, jnp.swapaxes(orders, 2, 3), n_tx, e_field, h_field, material
    )
    received = [parts[0]]
    for distance in range(n_tx):
        for flip in range(n_src):
            if distance or flip:
                part = parts[2 * distance + flip]
                received.append(to_groups(part, n_src, n_tx, flip, distance))
    coefficient, state, begun = first_steps(e_field, h_field, material)

    if n_tx == 2:
        x_rims = along(rims, "tx", 1)
    else:
        top, bottom = rims[:, :HALO], rims[:, HALO:]
        x_rims = jnp.concatenate([along(top, "tx", -1), along(bottom, "tx", 1)], 1)
    block = summed(received, begun)
    c_ext, own_edges, to_high, to_low = pack(e_field, h_field, coefficient, x_rims)
    low = along(to_high, "ty", 1)
    high = along(to_low, "ty", -1)
    free, run = later_steps(state, coefficient, e_field, h_field, x_rims)

    blocks = {0: block}
    for bits in range(n_ty - 2, 0, -2):
        blocks[bits] = flipped(block, "ty", bits)
    for bits in range(0, n_ty, 2):
        blocks[bits + 1] = flipped(blocks[bits], "ty", 1)
    mine = y_stage(place, [blocks[b] for b in range(n_ty)], cols_ky, cells_y, half, run)
    other = flipped(mine, "src", 1)
    factor, free = strip_run(own_edges, low, high, free, mine)
    return response(place, c_ext, factor, free, mine, other, cells_x)


def solution(mesh):
    in_specs = (
        P("src", None, "tx", "ty"),
        P("src", None),
        P(None, "tx", "ty"),
        P(None, None, "tx", "ty"),
        P(None, None, "tx", "ty"),
    )
    out_specs = (P(None, None, "tx", "ty"), P(None, None, "tx", "ty"))
    return jax.shard_map(
        per_device, mesh=mesh, in_specs=in_specs, out_specs=out_specs, check_vma=False
    )
```

```python
import functools
import math

import jax
import jax.numpy as jnp
import ml_dtypes
import numpy as np
from jax import lax
from jax.experimental import pallas as pl
from jax.experimental.pallas import tpu as pltpu
from jax.sharding import PartitionSpec as P

MX = 512
MY = 512
STEPS = 4
ZINJ = 1
LAYERS = 6

COURANT = 0.5
OMEGA = 0.7
PERMITTIVITY = (1.0, 2.6, 11.9, 2.1)

REACH = 8
SPAN = 2 * REACH
PAD = 8
HALO = 4
BASE = 16
SLOT = 32
WIDE = 8
REACHED = STEPS - 1
RESPONSE_SLOT = 21
HIGH_SIDE = 10
LANES = 128
VMEM_LIMIT = 24 * 1024 * 1024
X_LIMIT = 60_700_000


def split_bf16(table):
    high = table.astype(ml_dtypes.bfloat16)
    low = (table - high.astype(np.float64)).astype(ml_dtypes.bfloat16)
    return high, low


def padded(lanes):
    return -(-lanes // LANES) * LANES


@functools.lru_cache(maxsize=None)
def x_seeds(n_tx, rows_kx, cells_x):
    window = rows_kx + SPAN
    wide = padded(window)
    full = cells_x * n_tx
    turns = [8 << k for k in range((cells_x // 8).bit_length())]
    count = 8 + len(turns) + n_tx
    table = np.zeros((n_tx, -(-count // 8) * 8, 2 * wide), np.float32)
    for own in range(n_tx):
        freq = own * rows_kx - MX // 2 - REACH + np.arange(window)
        tiles = [(own + distance) % n_tx * cells_x for distance in range(n_tx)]
        x = np.array(list(range(-PAD, 8 - PAD)) + turns + tiles)
        angle = np.mod(x[:, None] * freq[None, :], full) * (2.0 * math.pi / full)
        table[own, :count, :window] = np.cos(angle)
        table[own, :count, wide : wide + window] = np.sin(angle)
    return table, len(turns)


@functools.lru_cache(maxsize=None)
def y_tables(n_ty, cols_ky, cells_y):
    full = cells_y * n_ty
    window = cols_ky + SPAN
    edge = np.concatenate([np.arange(-HALO, 0), cells_y + np.arange(HALO)])
    y = np.concatenate([np.arange(cells_y), edge])
    table = np.zeros((n_ty, LANES + 2 * SPAN, 2 * cells_y + LANES))
    for block in range(n_ty):
        freq = block * cols_ky - MY // 2 - REACH + np.arange(window)
        angle = np.mod(freq[:, None] * y[None, :], full) * (2.0 * math.pi / full)
        cos, sin = np.cos(angle), np.sin(angle)

        def placed(re_cols, im_cols):
            out = np.zeros((window, 2 * cells_y + LANES))
            out[:, :cells_y] = re_cols[:, :cells_y]
            out[:, cells_y : 2 * cells_y] = im_cols[:, :cells_y]
            out[:, 2 * cells_y : 2 * cells_y + 2 * HALO] = re_cols[:, cells_y:]
            out[:, 2 * cells_y + 2 * HALO : 2 * cells_y + 4 * HALO] = im_cols[:, cells_y:]
            return out

        from_re = placed(cos, sin)
        from_im = placed(-sin, cos)
        table[block, :cols_ky] = from_re[:cols_ky]
        table[block, cols_ky : 2 * cols_ky] = from_im[:cols_ky]
        table[block, LANES : LANES + SPAN] = from_re[cols_ky:]
        table[block, LANES + SPAN :] = from_im[cols_ky:]
    return split_bf16(table)


@functools.lru_cache(maxsize=None)
def y_phases(n_ty, cols_ky, cells_y):
    full = cells_y * n_ty
    out = np.zeros((n_ty, n_ty, 8, LANES), np.float32)
    for own in range(n_ty):
        for block in range(n_ty):
            freq = block * cols_ky - MY // 2 - REACH + np.arange(cols_ky + SPAN)
            angle = np.mod(freq * own * cells_y, full) * (2.0 * math.pi / full)
            cos, sin = np.cos(angle), np.sin(angle)
            out[own, block, 0, :cols_ky] = cos[:cols_ky]
            out[own, block, 0, cols_ky : 2 * cols_ky] = cos[:cols_ky]
            out[own, block, 1, :cols_ky] = -sin[:cols_ky]
            out[own, block, 1, cols_ky : 2 * cols_ky] = sin[:cols_ky]
            for group in range(LANES // (2 * SPAN)):
                at = group * 2 * SPAN
                out[own, block, 2, at : at + SPAN] = cos[cols_ky:]
                out[own, block, 2, at + SPAN : at + 2 * SPAN] = cos[cols_ky:]
                out[own, block, 3, at : at + SPAN] = -sin[cols_ky:]
                out[own, block, 3, at + SPAN : at + 2 * SPAN] = sin[cols_ky:]
    return out


def lasting(microseconds):
    moved = int(microseconds * 3.69e6)
    return pl.CostEstimate(flops=0, transcendentals=0, bytes_accessed=moved)


def lane_of(shape):
    return lax.broadcasted_iota(jnp.int32, shape, len(shape) - 1)


def rolled(value, shift):
    shift = shift % LANES
    return value if shift == 0 else pltpu.roll(value, shift, 1)


def halves(value):
    high = value.astype(jnp.bfloat16)
    low = (value - high.astype(jnp.float32)).astype(jnp.bfloat16)
    return high, low


def dot32(a, b):
    return jnp.dot(a, b, preferred_element_type=jnp.float32)


def fold_groups(rows, count):
    tiles = rows // 8
    sizes = [8 * (tiles // count + (1 if g < tiles % count else 0)) for g in range(count)]
    starts = [sum(sizes[:g]) for g in range(count)]
    return list(zip(starts, sizes))


def folded_rows(rows, count):
    return fold_groups(rows, count)[0][1]


def folded(value, count):
    groups = fold_groups(value.shape[0], count)
    tall, wide = groups[0][1], LANES // count
    lane = lane_of((tall, LANES))
    total = jnp.zeros((tall, LANES), value.dtype)
    for g, (start, size) in enumerate(groups):
        part = value[start : start + size]
        if size < tall:
            part = jnp.concatenate([part, jnp.zeros((tall - size, LANES), value.dtype)], 0)
        keep = (lane >= wide * g) & (lane < wide * (g + 1))
        total = jnp.where(keep, rolled(part, wide * g), total)
    return total


def unfolded(value, rows, count, at):
    wide = LANES // count
    parts = []
    for g, (_, size) in enumerate(fold_groups(rows, count)):
        parts.append(rolled(value[:size], at - wide * g))
    return jnp.concatenate(parts, 0)


def turned(cos, sin, by_cos, by_sin):
    return cos * by_cos - sin * by_sin, sin * by_cos + cos * by_sin


def fill_table(n_turns, seed_ref, table_ref):
    _, n_tx, rows, both = table_ref.shape
    wide = both // 2

    def row(i):
        return seed_ref[i : i + 1, :wide], seed_ref[i : i + 1, wide:]

    cos, sin = seed_ref[:8, :wide], seed_ref[:8, wide:]
    for k in range(n_turns):
        more = min(8 << k, rows - (8 << k))
        new = turned(cos[:more], sin[:more], *row(8 + k))
        cos, sin = jnp.concatenate([cos, new[0]], 0), jnp.concatenate([sin, new[1]], 0)
    for distance in range(n_tx):
        there = turned(cos, sin, *row(8 + n_turns + distance))
        for part in range(2):
            high, low = halves(there[part])
            table_ref[0, distance, :, part * wide : (part + 1) * wide] = high
            table_ref[1, distance, :, part * wide : (part + 1) * wide] = low


def x_kernel(
    n_turns, offs_in, orders_in, seeds_in, e_in, h_in, m_in, *refs,
):
    *out_refs, rim_ref = refs[:-11]
    (
        edge_ref, last_ref, offs_ref, orders_ref, seed_ref, table_ref, line_ref, acc_ref, q_ref,
        sems, rim_sems,
    ) = refs[-11:]
    own = lax.axis_index("src")
    copies = [
        pltpu.make_async_copy(seeds_in.at[lax.axis_index("tx")], seed_ref, sems.at[0]),
        pltpu.make_async_copy(orders_in, orders_ref, sems.at[1]),
        pltpu.make_async_copy(offs_in, offs_ref, sems.at[2]),
    ]
    cells_x = e_in.shape[2]
    for k, start in enumerate((0, cells_x - 8)):
        at = pl.ds(start, 8)
        for i, ref in enumerate((e_in, h_in)):
            source = ref.at[:, :, at, :]
            copies.append(pltpu.make_async_copy(source, edge_ref.at[i, k], rim_sems.at[i, k]))
        copies.append(pltpu.make_async_copy(m_in.at[:, at, :], last_ref.at[k], rim_sems.at[2, k]))
    for copy in copies:
        copy.start()
    points, _, cols_ky, rows_kx = orders_ref.shape
    _, n_tx, rows, both = table_ref.shape
    half = rows // 2
    acc_ref[...] = jnp.zeros_like(acc_ref)
    line_ref[...] = jnp.zeros_like(line_ref)
    wide = line_ref.shape[4]
    copies[0].wait()
    fill_table(n_turns, seed_ref, table_ref)
    copies[1].wait()
    copies[2].wait()
    for point in range(points):
        down = offs_ref[0, point] + REACH
        across = offs_ref[1, point] + REACH
        for part in range(2):
            for tile in range(rows_kx // wide):
                lanes = slice(tile * wide, (tile + 1) * wide)
                line = line_ref.at[point, part, tile]
                line[pl.ds(across, cols_ky), :] = orders_ref[point, part, :, lanes]
                acc_ref[part, pl.ds(down + tile * wide, wide), :] += line[...].T
    s_re = acc_ref[0]
    s_im = acc_ref[1]
    lane = lane_of(s_re.shape)
    re_by, im_by = rolled(s_re, cols_ky), rolled(s_im, cols_ky)

    def main(re, im_by):
        out = jnp.where(lane < cols_ky, re, im_by)
        return out if 2 * cols_ky == LANES else jnp.where(lane < 2 * cols_ky, out, 0.0)

    def spill(re_back, im_back):
        out = jnp.where(lane < SPAN, re_back, im_back)
        return jnp.where(lane < 2 * SPAN, out, 0.0)

    same = 2 * cols_ky == LANES
    re_back = re_by if same else rolled(s_re, -cols_ky)
    im_back = im_by if same else rolled(s_im, -cols_ky)
    top = [main(s_re, im_by), spill(re_back, rolled(s_im, SPAN - cols_ky))]
    bottom = [main(-s_im, re_by), spill(-im_back, rolled(s_re, SPAN - cols_ky))]
    right = jnp.concatenate([jnp.concatenate(top, 1), jnp.concatenate(bottom, 1)], 0)
    right_h, right_l = halves(right)
    tall = n_tx * rows
    by_high = dot32(table_ref[...].reshape(2 * tall, both), right_h)
    by_low = dot32(table_ref[0].reshape(tall, both), right_l)
    q_ref[...] = by_high[:tall] + (by_high[tall:] + by_low)
    for distance in range(n_tx):
        for flip in range(2):
            start = pl.multiple_of(distance * rows + (own ^ flip) * half, 8)
            block = q_ref[pl.ds(start, half), :]
            out_refs[2 * distance + flip][:half, :] = block[:, :LANES]
            out_refs[2 * distance + flip][half:, :] = folded(block[:, LANES:], 4)
    for copy in copies[3:]:
        copy.wait()
    row = lax.broadcasted_iota(jnp.int32, (LAYERS, 8, LANES), 1)
    for j in range(7):
        if j < 6:
            first, final = (edge_ref[j // 3, k, j % 3] for k in range(2))
        else:
            first, final = (coefficient_of(last_ref[k]) for k in range(2))
        rim_ref[j * LAYERS : (j + 1) * LAYERS] = jnp.where(row < HALO, first, final)


def x_stage(offsets, orders, n_tx, e_field, h_field, material):
    points, _, cols_ky, rows_kx = orders.shape
    cells_x = e_field.shape[2]
    wide = min(rows_kx, LANES)
    seeds, n_turns = x_seeds(n_tx, rows_kx, cells_x)
    rows = cells_x + 2 * PAD
    half = rows // 2
    height = half + folded_rows(half, 4)
    f32 = jnp.float32
    return pl.pallas_call(
        functools.partial(x_kernel, n_turns),
        in_specs=[pl.BlockSpec(memory_space=pltpu.HBM)] * 6,
        out_shape=(jax.ShapeDtypeStruct((height, LANES), f32),) * (2 * n_tx)
        + (jax.ShapeDtypeStruct((7 * LAYERS, 2 * HALO, LANES), f32),),
        scratch_shapes=[
            pltpu.VMEM((2, 2, 3, LAYERS, 8, LANES), f32),
            pltpu.VMEM((2, LAYERS, 8, LANES), jnp.int32),
            pltpu.SMEM(offsets.shape, jnp.int32),
            pltpu.VMEM(orders.shape, f32),
            pltpu.VMEM(seeds.shape[1:], f32),
            pltpu.VMEM((2, n_tx, rows, seeds.shape[2]), jnp.bfloat16),
            pltpu.VMEM((points, 2, rows_kx // wide, LANES, wide), f32),
            pltpu.VMEM((2, seeds.shape[2] // 2, LANES), f32),
            pltpu.VMEM((n_tx * rows, 2 * LANES), f32),
            pltpu.SemaphoreType.DMA((3,)),
            pltpu.SemaphoreType.DMA((3, 2)),
        ],
        compiler_params=pltpu.CompilerParams(vmem_limit_bytes=X_LIMIT),
        cost_estimate=lasting(3.5),
        name="x_stage",
    )(offsets, orders, jnp.asarray(seeds), e_field, h_field, material)


def sum_kernel(*refs):
    *part_refs, _, out_ref = refs
    total = part_refs[0][...]
    for ref in part_refs[1:]:
        total = total + ref[...]
    out_ref[...] = total


def summed(parts, after):
    return pl.pallas_call(
        sum_kernel,
        out_shape=jax.ShapeDtypeStruct(parts[0].shape, jnp.float32),
        compiler_params=pltpu.CompilerParams(vmem_limit_bytes=VMEM_LIMIT),
        cost_estimate=lasting(0.4),
        name="sum_parts",
    )(*parts, after)


def y_kernel(cols_ky, half, *refs):
    *block_refs, th_ref, tl_ref, phase_ref, _, out_ref = refs
    n_ty = len(block_refs)
    lane = lane_of((half, LANES))
    mains, spills, numbers = [], [], []
    own = lax.axis_index("ty")
    for number, ref in enumerate(block_refs):
        block = own ^ number
        numbers.append(block)
        phase = phase_ref[own, block]
        main = ref[:half, :]
        if 2 * cols_ky == LANES:
            swapped = rolled(main, cols_ky)
        else:
            swapped = jnp.where(lane < cols_ky, rolled(main, -cols_ky), rolled(main, cols_ky))
        mains.append(main * phase[0:1] + swapped * phase[1:2])
        spill = ref[half:, :]
        small = lane_of(spill.shape)
        other = jnp.where((small & (2 * SPAN - 1)) < SPAN, rolled(spill, -SPAN), rolled(spill, SPAN))
        spills.append(spill * phase[2:3] + other * phase[3:4])
    packed = []
    for first in range(0, n_ty, 4):
        total = None
        for g in range(4):
            part = unfolded(spills[first + g], half, 4, 32 * g)
            total = part if total is None else jnp.where(lane >= 32 * g, part, total)
        packed.append(total)
    left = jnp.concatenate(mains + packed, 1)
    high = left.astype(jnp.bfloat16)
    low = left - high.astype(jnp.float32)
    both = jnp.concatenate([left, low], 0).astype(jnp.bfloat16)

    def table(ref):
        parts = [ref[block, :LANES, :] for block in numbers]
        return jnp.concatenate(parts + [ref[block, LANES:, :] for block in numbers], 0)

    by_high = dot32(both, table(th_ref))
    result = by_high[:half] + (by_high[half:] + dot32(high, table(tl_ref)))
    out_ref[:half, :] = result[:, :LANES]
    out_ref[half : 2 * half, :] = result[:, LANES : 2 * LANES]
    out_ref[2 * half :, :] = folded(result[:, 2 * LANES :], 8)


def y_stage(blocks, cols_ky, cells_y, half, after):
    n_ty = len(blocks)
    t_h, t_l = y_tables(n_ty, cols_ky, cells_y)
    phases = y_phases(n_ty, cols_ky, cells_y)
    height = 2 * half + folded_rows(half, 8)
    return pl.pallas_call(
        functools.partial(y_kernel, cols_ky, half),
        out_shape=jax.ShapeDtypeStruct((height, LANES), jnp.float32),
        compiler_params=pltpu.CompilerParams(vmem_limit_bytes=VMEM_LIMIT),
        cost_estimate=lasting(1.5),
        name="y_stage",
    )(*blocks, jnp.asarray(t_h), jnp.asarray(t_l), jnp.asarray(phases), after)


def coefficient_of(material):
    value = jnp.where(material == 0, COURANT / PERMITTIVITY[0], COURANT / PERMITTIVITY[1])
    value = jnp.where(material == 2, COURANT / PERMITTIVITY[2], value)
    return jnp.where(material == 3, COURANT / PERMITTIVITY[3], value).astype(jnp.float32)


def pack_kernel(
    e_ref, h_ref, c_ref, x_ref, column_ref, message_ref, ext_ref, w_ref, low_ref, high_ref
):
    cells_x = e_ref.shape[2]
    end = BASE + cells_x
    rows = cells_x + 2 * PAD
    lane = lane_of((rows, LANES))
    by_product = []
    blank = jnp.zeros((PAD - HALO, LANES), jnp.float32)
    for j in range(7):
        scale = 1.0 if 3 <= j < 6 else 0.5
        strips = [jnp.zeros((rows, LANES), jnp.float32)] * 2
        planes = [[], []]
        for z in range(LAYERS):
            if j < 3:
                body = e_ref[j, z] * scale
            elif j < 6:
                body = h_ref[j - 3, z]
            else:
                body = c_ref[z]
            rims = x_ref[j * LAYERS + z] * scale
            full = jnp.concatenate([blank, rims[HALO:], body, rims[:HALO], blank], 0)
            if j == 6:
                ext_ref[z, 0 : BASE - PAD, :] = jnp.zeros((BASE - PAD, LANES), jnp.float32)
                ext_ref[z, BASE - PAD : end + PAD, :] = full
                ext_ref[z, end + PAD : end + BASE, :] = jnp.zeros((BASE - PAD, LANES), jnp.float32)
            g, at = z % 2, (z // 2) * SLOT
            if j in BY_PRODUCT:
                planes[g].append(beside(full))
                continue
            keep = (lane >= at) & (lane < at + 2 * WIDE)
            strips[g] = jnp.where(keep, rolled(full, at + WIDE), strips[g])
        for g in range(2):
            if j in BY_PRODUCT:
                by_product.append(jnp.concatenate(planes[g], 1))
            else:
                w_ref[j, g] = strips[g]
    taken = dot32(jnp.concatenate(by_product, 0), column_ref[...])
    for i, (j, g) in enumerate((j, g) for j in BY_PRODUCT for g in range(2)):
        w_ref[j, g] = taken[i * rows : (i + 1) * rows]
    items = [beside(w_ref[j, g]) for j in range(7) for g in range(2)]
    items += [jnp.zeros_like(items[0])] * (16 - len(items))
    sides = [jnp.concatenate(items[8 * a : 8 * a + 8], 1) for a in range(2)]
    sent = dot32(jnp.concatenate(sides, 0), message_ref[...])
    for a in range(2):
        low_ref[a] = sent[a * rows : (a + 1) * rows, :LANES]
        high_ref[a] = sent[a * rows : (a + 1) * rows, LANES:]


def pack(e_field, h_field, coefficient, x_rims):
    cells_x = e_field.shape[2]
    rows = cells_x + 2 * PAD
    tall = cells_x + 2 * BASE
    f32 = jnp.float32
    return pl.pallas_call(
        pack_kernel,
        out_shape=(
            jax.ShapeDtypeStruct((LAYERS, tall, LANES), f32),
            jax.ShapeDtypeStruct((7, 2, rows, LANES), f32),
            jax.ShapeDtypeStruct((2, rows, LANES), f32),
            jax.ShapeDtypeStruct((2, rows, LANES), f32),
        ),
        compiler_params=pltpu.CompilerParams(vmem_limit_bytes=VMEM_LIMIT),
        cost_estimate=lasting(2.2),
        name="pack",
    )(
        e_field, h_field, coefficient, x_rims,
        jnp.asarray(column_matrix()),
        jnp.asarray(message_matrix()),
    )


def total(terms):
    out = None
    for sign, value in terms:
        if value is None:
            continue
        if out is None:
            out = value if sign > 0 else -value
        else:
            out = out + value if sign > 0 else out - value
    return out


def add(a, b):
    return total([(1, a), (1, b)])


def differ(a, b):
    return total([(1, a), (-1, b)])


def curl_of_e(e, e_z, e_x, e_y):
    return (
        differ(differ(e_z[1], e[1]), differ(e_y[2], e[2])),
        differ(differ(e_x[2], e[2]), differ(e_z[0], e[0])),
        differ(differ(e_y[0], e[0]), differ(e_x[1], e[1])),
    )


def curl_of_h(h, h_z, h_x, h_y):
    return (
        differ(differ(h[2], h_y[2]), differ(h[1], h_z[1])),
        differ(differ(h[0], h_z[0]), differ(h[2], h_x[2])),
        differ(differ(h[1], h_x[1]), differ(h[0], h_y[0])),
    )


def moved(value, shift):
    return None if value is None else rolled(value, shift)


class Tile:
    def __init__(self, ref, live):
        self.ref, self.live = ref, set(live)

    def load(self, j, z, start, size):
        return self.ref[j, z, start : start + size, :] if (j, z) in self.live else None

    def store(self, j, z, start, value):
        if value is not None:
            self.ref[j, z, start : start + value.shape[0], :] = value
            self.live.add((j, z))

    def step_h(self, z, start, size):
        e = [self.load(j, z, start, size) for j in range(3)]
        e_z = [self.load(j, z + 1, start, size) for j in range(2)] + [None]
        e_x = [None] + [self.load(j, z, start + 1, size) for j in (1, 2)]
        e_y = [moved(e[0], -1), None, moved(e[2], -1)]
        new = []
        for j, change in enumerate(curl_of_e(e, e_z, e_x, e_y)):
            new.append(add(self.load(3 + j, z, start, size), change))
            self.store(3 + j, z, start, new[j])
        return new

    def step_e(self, z, start, size, factor):
        h = [self.load(3 + j, z, start, size) for j in range(3)]
        h_z = [self.load(3 + j, z - 1, start, size) for j in range(2)] + [None]
        h_x = [None] + [self.load(3 + j, z, start - 1, size) for j in (1, 2)]
        h_y = [moved(h[0], 1), None, moved(h[2], 1)]
        new = []
        for j, change in enumerate(curl_of_h(h, h_z, h_x, h_y)):
            old = self.load(j, z, start, size)
            new.append(old if change is None else add(old, factor * change))
        return new


class Strip:
    def __init__(self, ref, rows):
        self.ref, self.start, self.rows = ref, BASE - PAD, rows
        self.lane = lane_of((rows, LANES))

    def load(self, j, g, by=0):
        return self.ref[j, g, self.start + by : self.start + by + self.rows, :]

    def store(self, j, g, value):
        self.ref[j, g, self.start : self.start + self.rows, :] = value

    def step_h(self, fresh=False):
        e = [[self.load(j, g) for j in range(3)] for g in range(2)]
        inside = self.lane < 2 * SLOT
        above = [
            [e[1][0], e[1][1], None],
            [jnp.where(inside, rolled(e[0][j], -SLOT), 0.0) for j in range(2)] + [None],
        ]
        for g in range(2):
            e_x = [None, self.load(1, g, 1), self.load(2, g, 1)]
            e_y = [rolled(e[g][0], -1), None, rolled(e[g][2], -1)]
            for j, change in enumerate(curl_of_e(e[g], above[g], e_x, e_y)):
                self.store(3 + j, g, change if fresh else self.load(3 + j, g) + change)

    def step_e(self, factor):
        h = [[self.load(3 + j, g) for j in range(3)] for g in range(2)]
        inside = self.lane >= SLOT
        below = [
            [jnp.where(inside, rolled(h[1][j], SLOT), 0.0) for j in range(2)] + [None],
            [h[0][0], h[0][1], None],
        ]
        new = []
        for g in range(2):
            h_x = [None, self.load(4, g, -1), self.load(5, g, -1)]
            h_y = [rolled(h[g][0], 1), None, rolled(h[g][2], 1)]
            change = curl_of_h(h[g], below[g], h_x, h_y)
            new.append([self.load(j, g) + factor[g] * change[j] for j in range(3)])
        return new

    def all_edges(self, cells_x, matrix):
        values = [
            beside(self.ref[j, g, BASE : BASE + cells_x, :]) for j in range(6) for g in range(2)
        ]
        return dot32(jnp.concatenate(values, 0), matrix)


def beside(value):
    return jnp.concatenate(halves(value), 1)


def matrix_of(pairs, columns, rows=LANES):
    out = np.zeros((rows, columns), ml_dtypes.bfloat16)
    for first_row, first_column, count in pairs:
        for i in range(count):
            out[first_row + i, first_column + i] = 1
    return out


def doubled(matrix):
    blocks = matrix.reshape(-1, LANES, matrix.shape[1])
    return np.concatenate([m for block in blocks for m in (block, block)], 0)


def near_matrix():
    own, at = 2 * REACHED, ZINJ * RESPONSE_SLOT
    pairs = [(0, at + REACHED, own), (LANES - own, at + HIGH_SIDE, own)]
    return doubled(matrix_of(pairs, LANES))


def outside_matrix():
    pairs = []
    for part in range(2):
        lane, at = part * 2 * HALO, part * LANES + ZINJ * RESPONSE_SLOT
        pairs.append((lane + HALO - REACHED, at, REACHED))
        pairs.append((lane + HALO, at + HIGH_SIDE + 2 * REACHED, REACHED))
    return doubled(matrix_of(pairs, 2 * LANES))


def response_edge_matrix():
    pairs = []
    for z in range(min(LAYERS, ZINJ + STEPS)):
        at = z * RESPONSE_SLOT + REACHED
        pairs.append((at, z * LANES, REACHED))
        pairs.append((at + HIGH_SIDE, (z + 1) * LANES - REACHED, REACHED))
    return doubled(matrix_of(pairs, min(LAYERS, ZINJ + STEPS) * LANES))


def factor_matrix():
    pairs = []
    for z in range(LAYERS):
        at, to = z % 2 * LANES + z // 2 * SLOT, z * RESPONSE_SLOT
        pairs.append((at + HALO - REACHED, to, 3 * REACHED))
        pairs.append((at + 16 + WIDE - 2 * REACHED, to + HIGH_SIDE, 3 * REACHED))
    return doubled(matrix_of(pairs, LANES, 2 * LANES))


def edge_matrix():
    pairs = []
    for slot in range(LAYERS // 2):
        pairs.append((slot * SLOT + 4, slot * LANES, HALO))
        pairs.append((slot * SLOT + 20, slot * LANES + LANES - HALO, HALO))
    return doubled(matrix_of(pairs, LAYERS // 2 * LANES))


def column_matrix():
    pairs = []
    for slot in range(LAYERS // 2):
        pairs.append((slot * LANES + LANES - WIDE, slot * SLOT, WIDE))
        pairs.append((slot * LANES, slot * SLOT + WIDE, WIDE))
    return doubled(matrix_of(pairs, LANES, LAYERS // 2 * LANES))


def message_matrix():
    pairs = []
    for item in range(8):
        for slot in range(LAYERS // 2):
            at, to = item * LANES + slot * SLOT, slot * SLOT + HALO * item
            pairs.append((at + 4, to, HALO))
            pairs.append((at + 8, LANES + to, HALO))
    return doubled(matrix_of(pairs, 2 * LANES, 8 * LANES))


def strip_matrices():
    own, got = [], []
    for slot in range(LAYERS // 2):
        at = slot * SLOT
        own += [(at, at + 16, WIDE), (at + 8, at + 4, WIDE)]
        for item in range(8):
            to = item * LANES + at
            got.append((at + HALO * item, to, HALO))
            got.append((LANES + at + HALO * item, to + 24, HALO))
    return doubled(matrix_of(own, LANES)), doubled(matrix_of(got, 8 * LANES, 2 * LANES))


class ResponseStrip:
    def __init__(self, ref, rows):
        self.ref, self.start, self.rows = ref, BASE - PAD, rows
        self.lane = lane_of((rows, LANES))

    def load(self, j, by=0):
        return self.ref[j, self.start + by : self.start + by + self.rows, :]

    def store(self, j, value):
        self.ref[j, self.start : self.start + self.rows, :] = value

    def step_h(self, fresh):
        e = [self.load(j) for j in range(3)]
        inside = self.lane < (LAYERS - 1) * RESPONSE_SLOT
        e_z = [jnp.where(inside, rolled(e[j], -RESPONSE_SLOT), 0.0) for j in range(2)] + [None]
        e_x = [None, self.load(1, 1), self.load(2, 1)]
        e_y = [rolled(e[0], -1), None, rolled(e[2], -1)]
        for j, change in enumerate(curl_of_e(e, e_z, e_x, e_y)):
            self.store(3 + j, change if fresh else self.load(3 + j) + change)

    def step_e(self, factor):
        h = [self.load(3 + j) for j in range(3)]
        inside = self.lane >= RESPONSE_SLOT
        h_z = [jnp.where(inside, rolled(h[j], RESPONSE_SLOT), 0.0) for j in range(2)] + [None]
        h_x = [None, self.load(4, -1), self.load(5, -1)]
        h_y = [rolled(h[0], 1), None, rolled(h[2], 1)]
        change = curl_of_h(h, h_z, h_x, h_y)
        return [self.load(j) + factor * change[j] for j in range(3)]

    def all_edges(self, cells_x, matrix):
        values = [beside(self.ref[j, BASE : BASE + cells_x, :]) for j in range(6)]
        return dot32(jnp.concatenate(values, 0), matrix)


def with_edges(value, edges_ref, strip, block, width):
    start = strip * value.shape[0]
    own = edges_ref[start : start + value.shape[0], block * LANES : (block + 1) * LANES]
    lane = lane_of(own.shape)
    outer = (lane < width) | (lane >= LANES - width)
    return jnp.where(outer, own, value)


BY_PRODUCT = (0, 1, 2)
EVERY = [(j, z) for j in range(6) for z in range(LAYERS)]


def free_steps(tile, steps, start, rows, factor_of):
    for _ in range(steps):
        for z in range(LAYERS):
            tile.step_h(z, start, rows)
            for j, value in enumerate(tile.step_e(z, start, rows, factor_of(z))):
                tile.store(j, z, start, value)


def first_kernel(e_ref, h_ref, m_ref, c_ref, f_ref, token_ref):
    cells_x = e_ref.shape[2]
    token_ref[...] = jnp.zeros_like(token_ref)
    for z in range(LAYERS):
        c_ref[z] = coefficient_of(m_ref[z]) * 0.5
        for j in range(3):
            f_ref[j, z, PAD : PAD + cells_x, :] = e_ref[j, z] * 0.5
            f_ref[3 + j, z, PAD : PAD + cells_x, :] = h_ref[j, z]
        for j in range(6):
            f_ref[j, z, :PAD, :] = jnp.zeros((PAD, LANES), jnp.float32)
            f_ref[j, z, PAD + cells_x :, :] = jnp.zeros((PAD, LANES), jnp.float32)
    free_steps(Tile(f_ref, EVERY), STEPS // 2, PAD, cells_x, lambda z: c_ref[z])


def first_steps(e_field, h_field, material):
    cells_x = e_field.shape[2]
    f32 = jnp.float32
    return pl.pallas_call(
        first_kernel,
        out_shape=(
            jax.ShapeDtypeStruct((LAYERS, cells_x, LANES), f32),
            jax.ShapeDtypeStruct((6, LAYERS, cells_x + 2 * PAD, LANES), f32),
            jax.ShapeDtypeStruct((8, LANES), f32),
        ),
        compiler_params=pltpu.CompilerParams(vmem_limit_bytes=VMEM_LIMIT),
        cost_estimate=lasting(3.3),
        name="first_steps",
    )(e_field, h_field, material)


class Rows:
    def __init__(self, ref):
        self.ref = ref

    def load(self, j, by=0):
        return self.ref[j, :, 8 + by : 40 + by, :]

    def step(self, factor):
        zero = jnp.zeros((1, 32, LANES), jnp.float32)
        e = [self.load(j) for j in range(3)]
        e_z = [jnp.concatenate([e[j][1:], zero], 0) for j in range(2)] + [None]
        e_x = [None, self.load(1, 1), self.load(2, 1)]
        e_y = [pltpu.roll(e[0], LANES - 1, 2), None, pltpu.roll(e[2], LANES - 1, 2)]
        for j, change in enumerate(curl_of_e(e, e_z, e_x, e_y)):
            self.ref[3 + j, :, 8:40, :] = self.load(3 + j) + change
        h = [self.load(3 + j) for j in range(3)]
        h_z = [jnp.concatenate([zero, h[j][:-1]], 0) for j in range(2)] + [None]
        h_x = [None, self.load(4, -1), self.load(5, -1)]
        h_y = [pltpu.roll(h[0], 1, 2), None, pltpu.roll(h[2], 1, 2)]
        for j, change in enumerate(curl_of_h(h, h_z, h_x, h_y)):
            self.ref[j, :, 8:40, :] = e[j] + factor * change


def later_kernel(f_in, c_ref, e_ref, h_ref, x_ref, out_ref, token_ref, f_ref, r_ref):
    cells_x = c_ref.shape[1]
    token_ref[...] = jnp.zeros_like(token_ref)
    blank = jnp.zeros((LAYERS, PAD - HALO, LANES), jnp.float32)
    zero = jnp.zeros((LAYERS, 8, LANES), jnp.float32)
    factor = None
    for j in range(7):
        ref = e_ref.at[j] if j < 3 else h_ref.at[j - 3] if j < 6 else c_ref
        scale = 1.0 if 3 <= j < 6 else 0.5
        own = 0.5 if j < 3 else 1.0
        rims = x_ref[j * LAYERS : (j + 1) * LAYERS] * scale
        first, final = ref[:, :8, :] * own, ref[:, cells_x - 8 :, :] * own
        rows = [blank, rims[:, HALO:], first, final, rims[:, :HALO], blank]
        if j < 6:
            r_ref[j] = jnp.concatenate([zero] + rows + [zero], 1)
        else:
            factor = jnp.concatenate(rows, 1)
    edge = Rows(r_ref)
    for _ in range(STEPS):
        edge.step(factor)
    f_ref[...] = f_in[...]
    tile = Tile(f_ref, EVERY)
    free_steps(tile, STEPS - STEPS // 2, PAD, cells_x, lambda z: c_ref[z])
    row = lax.broadcasted_iota(jnp.int32, (8, LANES), 0)
    for j, z in EVERY:
        top = jnp.where(row < HALO, r_ref[j, z, 16:24, :], f_ref[j, z, PAD : PAD + 8, :])
        end = f_ref[j, z, PAD + cells_x - 8 : PAD + cells_x, :]
        end = jnp.where(row >= HALO, r_ref[j, z, 24:32, :], end)
        inner = f_ref[j, z, PAD + 8 : PAD + cells_x - 8, :]
        out_ref[j, z] = jnp.concatenate([top, inner, end], 0)


def later_steps(state, coefficient, e_field, h_field, x_rims):
    cells_x = e_field.shape[2]
    f32 = jnp.float32
    return pl.pallas_call(
        later_kernel,
        out_shape=(
            jax.ShapeDtypeStruct((6, LAYERS, cells_x, LANES), f32),
            jax.ShapeDtypeStruct((8, LANES), f32),
        ),
        scratch_shapes=[
            pltpu.VMEM(state.shape, f32),
            pltpu.VMEM((6, LAYERS, 48, LANES), f32),
        ],
        compiler_params=pltpu.CompilerParams(vmem_limit_bytes=VMEM_LIMIT),
        cost_estimate=lasting(3.7),
        name="later_steps",
    )(state, coefficient, e_field, h_field, x_rims)


def strip_kernel(
    w_ref, low_ref, high_ref, free_ref, own_ref, got_ref, edge_ref, to_ref, _, factor_ref, out_ref,
    s_ref, edges_ref,
):
    rows = w_ref.shape[2]
    first = BASE - PAD
    mine = [beside(w_ref[j, g]) for j in range(7) for g in range(2)]
    mine = dot32(jnp.concatenate(mine, 0), own_ref[...])
    got = [jnp.concatenate([beside(low_ref[a]), beside(high_ref[a])], 1) for a in range(2)]
    got = dot32(jnp.concatenate(got, 0), got_ref[...])
    factor = []
    for j in range(7):
        for g in range(2):
            i = 2 * j + g
            a, b = divmod(i, 8)
            value = mine[i * rows : (i + 1) * rows]
            value = value + got[a * rows : (a + 1) * rows, b * LANES : (b + 1) * LANES]
            if j < 6:
                s_ref[j, g, first : first + rows, :] = value
            else:
                factor.append(value)
    factor_ref[...] = dot32(jnp.concatenate([beside(f) for f in factor], 1), to_ref[...])
    strip = Strip(s_ref, rows)
    for step in range(STEPS):
        strip.step_h()
        new = strip.step_e(factor)
        for g in range(2):
            for j in range(3):
                strip.store(j, g, new[g][j])
    edges_ref[...] = strip.all_edges(out_ref.shape[2], edge_ref[...])
    for j, z in EVERY:
        out_ref[j, z] = with_edges(free_ref[j, z], edges_ref, 2 * j + z % 2, z // 2, HALO)


def strip_run(own_edges, low, high, free, after):
    rows = own_edges.shape[2]
    f32 = jnp.float32
    return pl.pallas_call(
        strip_kernel,
        out_shape=(
            jax.ShapeDtypeStruct((rows, LANES), f32),
            jax.ShapeDtypeStruct(free.shape, f32),
        ),
        scratch_shapes=[
            pltpu.VMEM((6, 2, rows + 2 * (BASE - PAD), LANES), f32),
            pltpu.VMEM((12 * free.shape[2], LAYERS // 2 * LANES), f32),
        ],
        compiler_params=pltpu.CompilerParams(vmem_limit_bytes=VMEM_LIMIT),
        cost_estimate=lasting(4),
        name="strip_run",
    )(
        own_edges, low, high, free, *(jnp.asarray(m) for m in strip_matrices()),
        jnp.asarray(edge_matrix()), jnp.asarray(factor_matrix()), after,
    )


def response_kernel(
    c_ref, factor_ref, free_ref, mine_ref, other_ref, near_ref, outside_ref, edge_ref,
    e_out, h_out,
    f_ref, s_ref, plane_ref, rim_ref, done_ref, edges_ref, sems,
):
    cells_x = e_out.shape[2]
    copies = []

    def send(j, z, source):
        to = e_out.at[j, z] if j < 3 else h_out.at[j - 3, z]
        copies.append(pltpu.make_async_copy(source, to, sems.at[j, z]))
        copies[-1].start()

    far = [(j, z) for j, z in EVERY if z >= ZINJ + STEPS - (0 if j < 2 else 1)]
    for j, z in far:
        if j < 3:
            done_ref[j, z] = free_ref[j, z] * 2.0
            send(j, z, done_ref.at[j, z])
        else:
            send(j, z, free_ref.at[j, z])
    rows = cells_x + 2 * PAD
    half = rows // 2
    first = BASE - PAD
    own = lax.axis_index("src")
    lane = lane_of((half, LANES))
    for ref, which in ((mine_ref, own), (other_ref, 1 - own)):
        at = pl.ds(pl.multiple_of(which * half, 8), half)
        for part in range(2):
            plane_ref[part, at, :] = ref[part * half : (part + 1) * half, :]
        rim_ref[0, at, :] = jnp.where(lane < 16, unfolded(ref[2 * half :, :], half, 8, 0), 0.0)
    outer = dot32(beside(rim_ref[0]), outside_ref[...])
    planes = jnp.concatenate([beside(plane_ref[part]) for part in range(2)], 0)
    inner = dot32(planes, near_ref[...])
    for part in range(2):
        own_part = outer[:, part * LANES : (part + 1) * LANES]
        rim_ref[part] = inner[part * rows : (part + 1) * rows] + own_part

    def injection(ref, step, start, size):
        cosine = 0.5 * COURANT * math.cos(OMEGA * step)
        sine = 0.5 * COURANT * math.sin(OMEGA * step)
        re, im = ref[0, start : start + size, :], ref[1, start : start + size, :]
        return [cosine * re - sine * im, sine * re + cosine * im, None]

    tile = Tile(f_ref, ())
    for j, value in enumerate(injection(plane_ref, 1, 0, rows)):
        tile.store(j, ZINJ, first, value)
    strip = ResponseStrip(s_ref, rows)
    s_ref[...] = jnp.zeros_like(s_ref)
    for j, value in enumerate(injection(rim_ref, 1, 0, rows)[:2]):
        strip.store(j, value)
    for step in range(2, STEPS + 1):
        strip.step_h(step == 2)
        new = strip.step_e(factor_ref[...])
        for j, value in enumerate(injection(rim_ref, step, 0, rows)):
            strip.store(j, add(new[j], value))
    edges_ref[...] = strip.all_edges(cells_x, edge_ref[...])
    for step in range(2, STEPS + 1):
        last = step == STEPS
        start, size = (BASE, cells_x) if last else (first, rows)
        for z in range(LAYERS):
            tile.step_h(z, first, rows - (PAD if last else 0))
            new = tile.step_e(z, start, size, c_ref[z, start : start + size, :])
            if z == ZINJ:
                source = injection(plane_ref, step, start - first, size)
                new = [add(a, b) for a, b in zip(new, source)]
            for j in range(3):
                if not last:
                    tile.store(j, z, start, new[j])
                    continue
                for i, value in ((j, new[j]), (3 + j, tile.load(3 + j, z, start, size))):
                    if (i, z) in far:
                        continue
                    value = with_edges(value, edges_ref, i, z, REACHED) + free_ref[i, z]
                    done_ref[i, z] = value * 2.0 if i < 3 else value
                    send(i, z, done_ref.at[i, z])
    for copy in copies:
        copy.wait()


def response(c_ext, factor, free, mine, other, cells_x):
    rows = cells_x + 2 * PAD
    tall = cells_x + 2 * BASE
    f32 = jnp.float32
    out = jax.ShapeDtypeStruct((3, LAYERS, cells_x, LANES), f32)
    vmem = pl.BlockSpec(memory_space=pltpu.VMEM)
    return pl.pallas_call(
        response_kernel,
        in_specs=[vmem] * 8,
        out_specs=(pl.BlockSpec(memory_space=pl.ANY),) * 2,
        out_shape=(out, out),
        scratch_shapes=[
            pltpu.VMEM((6, LAYERS, tall, LANES), f32),
            pltpu.VMEM((6, tall, LANES), f32),
            pltpu.VMEM((2, rows, LANES), f32),
            pltpu.VMEM((2, rows, LANES), f32),
            pltpu.VMEM((6, LAYERS, cells_x, LANES), f32),
            pltpu.VMEM((6 * cells_x, min(LAYERS, ZINJ + STEPS) * LANES), f32),
            pltpu.SemaphoreType.DMA((6, LAYERS)),
        ],
        compiler_params=pltpu.CompilerParams(vmem_limit_bytes=VMEM_LIMIT),
        cost_estimate=lasting(6.5),
        name="response",
    )(
        c_ext, factor, free, mine, other,
        jnp.asarray(near_matrix()), jnp.asarray(outside_matrix()),
        jnp.asarray(response_edge_matrix()),
    )


def along(block, axis, distance):
    n = lax.axis_size(axis)
    return lax.ppermute(block, axis, [((i - distance) % n, i) for i in range(n)])


def flipped(block, axis, bits):
    return lax.ppermute(block, axis, [(i, i ^ bits) for i in range(lax.axis_size(axis))])


def to_groups(block, n_src, n_tx, flip, distance):
    route = []
    for s in range(n_src):
        for t in range(n_tx):
            route.append((s * n_tx + t, (s ^ flip) * n_tx + (t + distance) % n_tx))
    return lax.ppermute(block, ("src", "tx"), route)


def per_device(orders, offsets, material, e_field, h_field):
    cols_ky = orders.shape[3]
    layers, cells_x, cells_y = material.shape
    n_src, n_tx, n_ty = lax.axis_size("src"), lax.axis_size("tx"), lax.axis_size("ty")
    half = cells_x // 2 + PAD
    *parts, rims = x_stage(
        offsets.T, jnp.swapaxes(orders, 2, 3), n_tx, e_field, h_field, material
    )
    received = [parts[0]]
    for distance in range(n_tx):
        for flip in range(n_src):
            if distance or flip:
                part = parts[2 * distance + flip]
                received.append(to_groups(part, n_src, n_tx, flip, distance))
    coefficient, state, begun = first_steps(e_field, h_field, material)

    if n_tx == 2:
        x_rims = along(rims, "tx", 1)
    else:
        top, bottom = rims[:, :HALO], rims[:, HALO:]
        x_rims = jnp.concatenate([along(top, "tx", -1), along(bottom, "tx", 1)], 1)
    block = summed(received, begun)
    c_ext, own_edges, to_high, to_low = pack(e_field, h_field, coefficient, x_rims)
    low = along(to_high, "ty", 1)
    high = along(to_low, "ty", -1)
    free, run = later_steps(state, coefficient, e_field, h_field, x_rims)

    blocks = {0: block}
    for bits in range(n_ty - 2, 0, -2):
        blocks[bits] = flipped(block, "ty", bits)
    for bits in range(0, n_ty, 2):
        blocks[bits + 1] = flipped(blocks[bits], "ty", 1)
    mine = y_stage([blocks[b] for b in range(n_ty)], cols_ky, cells_y, half, run)
    other = flipped(mine, "src", 1)
    factor, free = strip_run(own_edges, low, high, free, mine)
    return response(c_ext, factor, free, mine, other, cells_x)


def solution(mesh):
    in_specs = (
        P("src", None, "tx", "ty"),
        P("src", None),
        P(None, "tx", "ty"),
        P(None, None, "tx", "ty"),
        P(None, None, "tx", "ty"),
    )
    out_specs = (P(None, None, "tx", "ty"), P(None, None, "tx", "ty"))
    return jax.shard_map(
        per_device, mesh=mesh, in_specs=in_specs, out_specs=out_specs, check_vma=False
    )
```

```python
import functools
import math

import jax
import jax.numpy as jnp
import ml_dtypes
import numpy as np
from jax import lax
from jax.experimental import pallas as pl
from jax.experimental.pallas import tpu as pltpu
from jax.sharding import PartitionSpec as P

MX = 512
MY = 512
STEPS = 4
ZINJ = 1
LAYERS = 6

COURANT = 0.5
OMEGA = 0.7
PERMITTIVITY = (1.0, 2.6, 11.9, 2.1)

REACH = 8
SPAN = 2 * REACH
PAD = 8
HALO = 4
CHUNK = 64
BASE = 16
SLOT = 32
WIDE = 8
REACHED = STEPS - 1
RESPONSE_SLOT = 21
HIGH_SIDE = 10
LANES = 128
VMEM_LIMIT = 24 * 1024 * 1024
RESPONSE_LIMIT = 40 * 1024 * 1024
X_LIMIT = 60_700_000


def split_bf16(table):
    high = table.astype(ml_dtypes.bfloat16)
    low = (table - high.astype(np.float64)).astype(ml_dtypes.bfloat16)
    return high, low


def padded(lanes):
    return -(-lanes // LANES) * LANES


@functools.lru_cache(maxsize=None)
def x_seeds(n_tx, rows_kx, cells_x):
    window = rows_kx + SPAN
    wide = padded(window)
    full = cells_x * n_tx
    turns = [8 << k for k in range((cells_x // 8).bit_length())]
    count = 8 + len(turns) + n_tx
    table = np.zeros((n_tx, -(-count // 8) * 8, 2 * wide), np.float32)
    for own in range(n_tx):
        freq = own * rows_kx - MX // 2 - REACH + np.arange(window)
        tiles = [(own + distance) % n_tx * cells_x for distance in range(n_tx)]
        x = np.array(list(range(-PAD, 8 - PAD)) + turns + tiles)
        angle = np.mod(x[:, None] * freq[None, :], full) * (2.0 * math.pi / full)
        table[own, :count, :window] = np.cos(angle)
        table[own, :count, wide : wide + window] = np.sin(angle)
    return table, len(turns)


@functools.lru_cache(maxsize=None)
def y_tables(n_ty, cols_ky, cells_y):
    full = cells_y * n_ty
    window = cols_ky + SPAN
    edge = np.concatenate([np.arange(-HALO, 0), cells_y + np.arange(HALO)])
    y = np.concatenate([np.arange(cells_y), edge])
    table = np.zeros((n_ty, LANES + 2 * SPAN, 2 * cells_y + LANES))
    for block in range(n_ty):
        freq = block * cols_ky - MY // 2 - REACH + np.arange(window)
        angle = np.mod(freq[:, None] * y[None, :], full) * (2.0 * math.pi / full)
        cos, sin = np.cos(angle), np.sin(angle)

        def placed(re_cols, im_cols):
            out = np.zeros((window, 2 * cells_y + LANES))
            out[:, :cells_y] = re_cols[:, :cells_y]
            out[:, cells_y : 2 * cells_y] = im_cols[:, :cells_y]
            out[:, 2 * cells_y : 2 * cells_y + 2 * HALO] = re_cols[:, cells_y:]
            out[:, 2 * cells_y + 2 * HALO : 2 * cells_y + 4 * HALO] = im_cols[:, cells_y:]
            return out

        from_re = placed(cos, sin)
        from_im = placed(-sin, cos)
        table[block, :cols_ky] = from_re[:cols_ky]
        table[block, cols_ky : 2 * cols_ky] = from_im[:cols_ky]
        table[block, LANES : LANES + SPAN] = from_re[cols_ky:]
        table[block, LANES + SPAN :] = from_im[cols_ky:]
    return split_bf16(table)


@functools.lru_cache(maxsize=None)
def y_phases(n_ty, cols_ky, cells_y):
    full = cells_y * n_ty
    out = np.zeros((n_ty, n_ty, 8, LANES), np.float32)
    for own in range(n_ty):
        for block in range(n_ty):
            freq = block * cols_ky - MY // 2 - REACH + np.arange(cols_ky + SPAN)
            angle = np.mod(freq * own * cells_y, full) * (2.0 * math.pi / full)
            cos, sin = np.cos(angle), np.sin(angle)
            out[own, block, 0, :cols_ky] = cos[:cols_ky]
            out[own, block, 0, cols_ky : 2 * cols_ky] = cos[:cols_ky]
            out[own, block, 1, :cols_ky] = -sin[:cols_ky]
            out[own, block, 1, cols_ky : 2 * cols_ky] = sin[:cols_ky]
            for group in range(LANES // (2 * SPAN)):
                at = group * 2 * SPAN
                out[own, block, 2, at : at + SPAN] = cos[cols_ky:]
                out[own, block, 2, at + SPAN : at + 2 * SPAN] = cos[cols_ky:]
                out[own, block, 3, at : at + SPAN] = -sin[cols_ky:]
                out[own, block, 3, at + SPAN : at + 2 * SPAN] = sin[cols_ky:]
    return out


def lasting(microseconds):
    moved = int(microseconds * 3.69e6)
    return pl.CostEstimate(flops=0, transcendentals=0, bytes_accessed=moved)


def lane_of(shape):
    return lax.broadcasted_iota(jnp.int32, shape, len(shape) - 1)


def rolled(value, shift):
    shift = shift % LANES
    return value if shift == 0 else pltpu.roll(value, shift, 1)


def halves(value):
    high = value.astype(jnp.bfloat16)
    low = (value - high.astype(jnp.float32)).astype(jnp.bfloat16)
    return high, low


def dot32(a, b):
    return jnp.dot(a, b, preferred_element_type=jnp.float32)


def fold_groups(rows, count):
    tiles = rows // 8
    sizes = [8 * (tiles // count + (1 if g < tiles % count else 0)) for g in range(count)]
    starts = [sum(sizes[:g]) for g in range(count)]
    return list(zip(starts, sizes))


def folded_rows(rows, count):
    return fold_groups(rows, count)[0][1]


def folded(value, count):
    groups = fold_groups(value.shape[0], count)
    tall, wide = groups[0][1], LANES // count
    lane = lane_of((tall, LANES))
    total = jnp.zeros((tall, LANES), value.dtype)
    for g, (start, size) in enumerate(groups):
        part = value[start : start + size]
        if size < tall:
            part = jnp.concatenate([part, jnp.zeros((tall - size, LANES), value.dtype)], 0)
        keep = (lane >= wide * g) & (lane < wide * (g + 1))
        total = jnp.where(keep, rolled(part, wide * g), total)
    return total


def unfolded(value, rows, count, at):
    wide = LANES // count
    parts = []
    for g, (_, size) in enumerate(fold_groups(rows, count)):
        parts.append(rolled(value[:size], at - wide * g))
    return jnp.concatenate(parts, 0)


def turned(cos, sin, by_cos, by_sin):
    return cos * by_cos - sin * by_sin, sin * by_cos + cos * by_sin


def fill_table(n_turns, seed_ref, table_ref):
    _, n_tx, rows, both = table_ref.shape
    wide = both // 2

    def row(i):
        return seed_ref[i : i + 1, :wide], seed_ref[i : i + 1, wide:]

    cos, sin = seed_ref[:8, :wide], seed_ref[:8, wide:]
    for k in range(n_turns):
        more = min(8 << k, rows - (8 << k))
        new = turned(cos[:more], sin[:more], *row(8 + k))
        cos, sin = jnp.concatenate([cos, new[0]], 0), jnp.concatenate([sin, new[1]], 0)
    for distance in range(n_tx):
        there = turned(cos, sin, *row(8 + n_turns + distance))
        for part in range(2):
            high, low = halves(there[part])
            table_ref[0, distance, :, part * wide : (part + 1) * wide] = high
            table_ref[1, distance, :, part * wide : (part + 1) * wide] = low


def x_kernel(
    n_turns, offs_in, orders_in, seeds_in, _e, _h, _m, *refs
):
    *out_refs, offs_ref, orders_ref, seed_ref, table_ref, line_ref, acc_ref, q_ref, sems = refs
    own = lax.axis_index("src")
    copies = [
        pltpu.make_async_copy(seeds_in.at[lax.axis_index("tx")], seed_ref, sems.at[0]),
        pltpu.make_async_copy(orders_in, orders_ref, sems.at[1]),
        pltpu.make_async_copy(offs_in, offs_ref, sems.at[2]),
    ]
    for copy in copies:
        copy.start()
    points, _, cols_ky, rows_kx = orders_ref.shape
    _, n_tx, rows, both = table_ref.shape
    half = rows // 2
    acc_ref[...] = jnp.zeros_like(acc_ref)
    line_ref[...] = jnp.zeros_like(line_ref)
    wide = line_ref.shape[4]
    copies[0].wait()
    fill_table(n_turns, seed_ref, table_ref)
    copies[1].wait()
    copies[2].wait()
    for point in range(points):
        down = offs_ref[0, point] + REACH
        across = offs_ref[1, point] + REACH
        for part in range(2):
            for tile in range(rows_kx // wide):
                lanes = slice(tile * wide, (tile + 1) * wide)
                line = line_ref.at[point, part, tile]
                line[pl.ds(across, cols_ky), :] = orders_ref[point, part, :, lanes]
                acc_ref[part, pl.ds(down + tile * wide, wide), :] += line[...].T
    s_re = acc_ref[0]
    s_im = acc_ref[1]
    lane = lane_of(s_re.shape)
    re_by, im_by = rolled(s_re, cols_ky), rolled(s_im, cols_ky)

    def main(re, im_by):
        out = jnp.where(lane < cols_ky, re, im_by)
        return out if 2 * cols_ky == LANES else jnp.where(lane < 2 * cols_ky, out, 0.0)

    def spill(re_back, im_back):
        out = jnp.where(lane < SPAN, re_back, im_back)
        return jnp.where(lane < 2 * SPAN, out, 0.0)

    same = 2 * cols_ky == LANES
    re_back = re_by if same else rolled(s_re, -cols_ky)
    im_back = im_by if same else rolled(s_im, -cols_ky)
    top = [main(s_re, im_by), spill(re_back, rolled(s_im, SPAN - cols_ky))]
    bottom = [main(-s_im, re_by), spill(-im_back, rolled(s_re, SPAN - cols_ky))]
    right = jnp.concatenate([jnp.concatenate(top, 1), jnp.concatenate(bottom, 1)], 0)
    right_h, right_l = halves(right)
    tall = n_tx * rows
    by_high = dot32(table_ref[...].reshape(2 * tall, both), right_h)
    by_low = dot32(table_ref[0].reshape(tall, both), right_l)
    q_ref[...] = by_high[:tall] + (by_high[tall:] + by_low)
    for distance in range(n_tx):
        for flip in range(2):
            start = pl.multiple_of(distance * rows + (own ^ flip) * half, 8)
            block = q_ref[pl.ds(start, half), :]
            out_refs[2 * distance + flip][:half, :] = block[:, :LANES]
            out_refs[2 * distance + flip][half:, :] = folded(block[:, LANES:], 4)


def x_stage(offsets, orders, n_tx, cells_x, beside):
    points, _, cols_ky, rows_kx = orders.shape
    wide = min(rows_kx, LANES)
    seeds, n_turns = x_seeds(n_tx, rows_kx, cells_x)
    rows = cells_x + 2 * PAD
    half = rows // 2
    height = half + folded_rows(half, 4)
    f32 = jnp.float32
    return pl.pallas_call(
        functools.partial(x_kernel, n_turns),
        in_specs=[pl.BlockSpec(memory_space=pltpu.HBM)] * 6,
        out_shape=(jax.ShapeDtypeStruct((height, LANES), f32),) * (2 * n_tx),
        scratch_shapes=[
            pltpu.SMEM(offsets.shape, jnp.int32),
            pltpu.VMEM(orders.shape, f32),
            pltpu.VMEM(seeds.shape[1:], f32),
            pltpu.VMEM((2, n_tx, rows, seeds.shape[2]), jnp.bfloat16),
            pltpu.VMEM((points, 2, rows_kx // wide, LANES, wide), f32),
            pltpu.VMEM((2, seeds.shape[2] // 2, LANES), f32),
            pltpu.VMEM((n_tx * rows, 2 * LANES), f32),
            pltpu.SemaphoreType.DMA((3,)),
        ],
        compiler_params=pltpu.CompilerParams(vmem_limit_bytes=X_LIMIT),
        cost_estimate=lasting(3.5),
        name="x_stage",
    )(offsets, orders, jnp.asarray(seeds), *beside)


def sum_kernel(*refs):
    *part_refs, _, out_ref = refs
    total = part_refs[0][...]
    for ref in part_refs[1:]:
        total = total + ref[...]
    out_ref[...] = total


def summed(parts, after):
    return pl.pallas_call(
        sum_kernel,
        out_shape=jax.ShapeDtypeStruct(parts[0].shape, jnp.float32),
        compiler_params=pltpu.CompilerParams(vmem_limit_bytes=VMEM_LIMIT),
        cost_estimate=lasting(0.4),
        name="sum_parts",
    )(*parts, after)


def y_kernel(cols_ky, half, *refs):
    *block_refs, th_ref, tl_ref, phase_ref, _, out_ref = refs
    n_ty = len(block_refs)
    lane = lane_of((half, LANES))
    mains, spills, numbers = [], [], []
    own = lax.axis_index("ty")
    for number, ref in enumerate(block_refs):
        block = own ^ number
        numbers.append(block)
        phase = phase_ref[own, block]
        main = ref[:half, :]
        if 2 * cols_ky == LANES:
            swapped = rolled(main, cols_ky)
        else:
            swapped = jnp.where(lane < cols_ky, rolled(main, -cols_ky), rolled(main, cols_ky))
        mains.append(main * phase[0:1] + swapped * phase[1:2])
        spill = ref[half:, :]
        small = lane_of(spill.shape)
        other = jnp.where((small & (2 * SPAN - 1)) < SPAN, rolled(spill, -SPAN), rolled(spill, SPAN))
        spills.append(spill * phase[2:3] + other * phase[3:4])
    packed = []
    for first in range(0, n_ty, 4):
        total = None
        for g in range(4):
            part = unfolded(spills[first + g], half, 4, 32 * g)
            total = part if total is None else jnp.where(lane >= 32 * g, part, total)
        packed.append(total)
    left = jnp.concatenate(mains + packed, 1)
    high = left.astype(jnp.bfloat16)
    low = left - high.astype(jnp.float32)
    both = jnp.concatenate([left, low], 0).astype(jnp.bfloat16)

    def table(ref):
        parts = [ref[block, :LANES, :] for block in numbers]
        return jnp.concatenate(parts + [ref[block, LANES:, :] for block in numbers], 0)

    by_high = dot32(both, table(th_ref))
    result = by_high[:half] + (by_high[half:] + dot32(high, table(tl_ref)))
    out_ref[:half, :] = result[:, :LANES]
    out_ref[half : 2 * half, :] = result[:, LANES : 2 * LANES]
    out_ref[2 * half :, :] = folded(result[:, 2 * LANES :], 8)


def y_stage(blocks, cols_ky, cells_y, half, after):
    n_ty = len(blocks)
    t_h, t_l = y_tables(n_ty, cols_ky, cells_y)
    phases = y_phases(n_ty, cols_ky, cells_y)
    height = 2 * half + folded_rows(half, 8)
    return pl.pallas_call(
        functools.partial(y_kernel, cols_ky, half),
        out_shape=jax.ShapeDtypeStruct((height, LANES), jnp.float32),
        compiler_params=pltpu.CompilerParams(vmem_limit_bytes=VMEM_LIMIT),
        cost_estimate=lasting(1.5),
        name="y_stage",
    )(*blocks, jnp.asarray(t_h), jnp.asarray(t_l), jnp.asarray(phases), after)


def coefficient_of(material):
    value = jnp.where(material == 0, COURANT / PERMITTIVITY[0], COURANT / PERMITTIVITY[1])
    value = jnp.where(material == 2, COURANT / PERMITTIVITY[2], value)
    return jnp.where(material == 3, COURANT / PERMITTIVITY[3], value).astype(jnp.float32)


def pack_kernel(
    e_ref, h_ref, c_ref, x_ref, column_ref, message_ref, ext_ref, w_ref, low_ref, high_ref
):
    cells_x = h_ref.shape[2]
    end = BASE + cells_x
    rows = cells_x + 2 * PAD
    lane = lane_of((rows, LANES))
    by_product = []
    blank = jnp.zeros((PAD - HALO, LANES), jnp.float32)
    for j in range(7):
        scale = SCALES[j]
        strips = [jnp.zeros((rows, LANES), jnp.float32)] * 2
        planes = [[], []]
        for z in range(LAYERS):
            if j < 3:
                body = e_ref[pl.ds((j * LAYERS + z) * cells_x, cells_x), :]
            elif j < 6:
                body = h_ref[j - 3, z] * scale
            else:
                body = c_ref[z]
            rims = x_ref[j * LAYERS + z]
            rims = rims if scale == 1 else rims * scale
            full = jnp.concatenate([blank, rims[HALO:], body, rims[:HALO], blank], 0)
            if j == 6:
                ext_ref[z, 0 : BASE - PAD, :] = jnp.zeros((BASE - PAD, LANES), jnp.float32)
                ext_ref[z, BASE - PAD : end + PAD, :] = full
                ext_ref[z, end + PAD : end + BASE, :] = jnp.zeros((BASE - PAD, LANES), jnp.float32)
            g, at = z % 2, (z // 2) * SLOT
            if j in BY_PRODUCT:
                planes[g].append(beside(full))
                continue
            keep = (lane >= at) & (lane < at + 2 * WIDE)
            strips[g] = jnp.where(keep, rolled(full, at + WIDE), strips[g])
        for g in range(2):
            if j in BY_PRODUCT:
                by_product.append(jnp.concatenate(planes[g], 1))
            else:
                w_ref[j, g] = strips[g]
    taken = dot32(jnp.concatenate(by_product, 0), column_ref[...])
    for i, (j, g) in enumerate((j, g) for j in BY_PRODUCT for g in range(2)):
        w_ref[j, g] = taken[i * rows : (i + 1) * rows]
    items = [beside(w_ref[j, g]) for j in range(7) for g in range(2)]
    items += [jnp.zeros_like(items[0])] * (16 - len(items))
    sides = [jnp.concatenate(items[8 * a : 8 * a + 8], 1) for a in range(2)]
    sent = dot32(jnp.concatenate(sides, 0), message_ref[...])
    for a in range(2):
        low_ref[a] = sent[a * rows : (a + 1) * rows, :LANES]
        high_ref[a] = sent[a * rows : (a + 1) * rows, LANES:]


def pack(e_field, h_field, coefficient, x_rims):
    cells_x = h_field.shape[2]
    rows = cells_x + 2 * PAD
    tall = cells_x + 2 * BASE
    f32 = jnp.float32
    return pl.pallas_call(
        pack_kernel,
        out_shape=(
            jax.ShapeDtypeStruct((LAYERS, tall, LANES), f32),
            jax.ShapeDtypeStruct((7, 2, rows, LANES), f32),
            jax.ShapeDtypeStruct((2, rows, LANES), f32),
            jax.ShapeDtypeStruct((2, rows, LANES), f32),
        ),
        compiler_params=pltpu.CompilerParams(vmem_limit_bytes=VMEM_LIMIT),
        cost_estimate=lasting(2.2),
        name="pack",
    )(
        e_field, h_field, coefficient, x_rims,
        jnp.asarray(column_matrix()),
        jnp.asarray(message_matrix()),
    )


def total(terms):
    out = None
    for sign, value in terms:
        if value is None:
            continue
        if out is None:
            out = value if sign > 0 else -value
        else:
            out = out + value if sign > 0 else out - value
    return out


def add(a, b):
    return total([(1, a), (1, b)])


def differ(a, b):
    return total([(1, a), (-1, b)])


def curl_of_e(e, e_z, e_x, e_y):
    return (
        differ(differ(e_z[1], e[1]), differ(e_y[2], e[2])),
        differ(differ(e_x[2], e[2]), differ(e_z[0], e[0])),
        differ(differ(e_y[0], e[0]), differ(e_x[1], e[1])),
    )


def curl_of_h(h, h_z, h_x, h_y):
    return (
        differ(differ(h[2], h_y[2]), differ(h[1], h_z[1])),
        differ(differ(h[0], h_z[0]), differ(h[2], h_x[2])),
        differ(differ(h[1], h_x[1]), differ(h[0], h_y[0])),
    )


def moved(value, shift):
    return None if value is None else rolled(value, shift)


class Planes:
    def __init__(self, ref, live=()):
        self.ref, self.live = ref, set(live)

    def get(self, j, z, start, size):
        return self.ref[j, z, start : start + size, :] if (j, z) in self.live else None

    def put(self, j, z, start, value):
        if value is not None:
            self.ref[j, z, start : start + value.shape[0], :] = value
            self.live.add((j, z))


def chunks(start, size):
    return [(at, min(CHUNK, start + size - at)) for at in range(start, start + size, CHUNK)]


def step_h(e, h, to, start, size):
    for z in range(LAYERS):
        for at, rows in chunks(start, size):
            own = [e.get(j, z, at, rows) for j in range(3)]
            above = [e.get(j, z + 1, at, rows) for j in range(2)] + [None]
            e_x = [None] + [e.get(j, z, at + 1, rows) for j in (1, 2)]
            e_y = [moved(own[0], -1), None, moved(own[2], -1)]
            for j, change in enumerate(curl_of_e(own, above, e_x, e_y)):
                to.put(j, z, at, add(h.get(j, z, at, rows), change))


def step_e(e, h, put, start, size, factor_of):
    for z in range(LAYERS):
        for at, rows in chunks(start, size):
            own = [h.get(j, z, at, rows) for j in range(3)]
            below = [h.get(j, z - 1, at, rows) for j in range(2)] + [None]
            h_x = [None] + [h.get(j, z, at - 1, rows) for j in (1, 2)]
            h_y = [moved(own[0], 1), None, moved(own[2], 1)]
            for j, change in enumerate(curl_of_h(own, below, h_x, h_y)):
                value = e.get(j, z, at, rows)
                if change is not None:
                    value = add(value, factor_of(z, at, rows) * change)
                put(j, z, at, value)


class Strip:
    def __init__(self, ref, rows):
        self.ref, self.start, self.rows = ref, BASE - PAD, rows
        self.lane = lane_of((rows, LANES))

    def load(self, j, g, by=0):
        return self.ref[j, g, self.start + by : self.start + by + self.rows, :]

    def store(self, j, g, value):
        self.ref[j, g, self.start : self.start + self.rows, :] = value

    def step_h(self, fresh=False):
        e = [[self.load(j, g) for j in range(3)] for g in range(2)]
        inside = self.lane < 2 * SLOT
        above = [
            [e[1][0], e[1][1], None],
            [jnp.where(inside, rolled(e[0][j], -SLOT), 0.0) for j in range(2)] + [None],
        ]
        for g in range(2):
            e_x = [None, self.load(1, g, 1), self.load(2, g, 1)]
            e_y = [rolled(e[g][0], -1), None, rolled(e[g][2], -1)]
            for j, change in enumerate(curl_of_e(e[g], above[g], e_x, e_y)):
                self.store(3 + j, g, change if fresh else self.load(3 + j, g) + change)

    def step_e(self, factor):
        h = [[self.load(3 + j, g) for j in range(3)] for g in range(2)]
        inside = self.lane >= SLOT
        below = [
            [jnp.where(inside, rolled(h[1][j], SLOT), 0.0) for j in range(2)] + [None],
            [h[0][0], h[0][1], None],
        ]
        new = []
        for g in range(2):
            h_x = [None, self.load(4, g, -1), self.load(5, g, -1)]
            h_y = [rolled(h[g][0], 1), None, rolled(h[g][2], 1)]
            change = curl_of_h(h[g], below[g], h_x, h_y)
            new.append([self.load(j, g) + factor[g] * change[j] for j in range(3)])
        return new

    def all_edges(self, cells_x, matrix):
        values = [
            beside(self.ref[j, g, BASE : BASE + cells_x, :]) for j in range(6) for g in range(2)
        ]
        return dot32(jnp.concatenate(values, 0), matrix)


def beside(value):
    return jnp.concatenate(halves(value), 1)


def matrix_of(pairs, columns, rows=LANES):
    out = np.zeros((rows, columns), ml_dtypes.bfloat16)
    for first_row, first_column, count in pairs:
        for i in range(count):
            out[first_row + i, first_column + i] = 1
    return out


def doubled(matrix):
    blocks = matrix.reshape(-1, LANES, matrix.shape[1])
    return np.concatenate([m for block in blocks for m in (block, block)], 0)


def near_matrix():
    own, at = 2 * REACHED, ZINJ * RESPONSE_SLOT
    pairs = [(0, at + REACHED, own), (LANES - own, at + HIGH_SIDE, own)]
    return doubled(matrix_of(pairs, LANES))


def outside_matrix():
    pairs = []
    for part in range(2):
        lane, at = part * 2 * HALO, part * LANES + ZINJ * RESPONSE_SLOT
        pairs.append((lane + HALO - REACHED, at, REACHED))
        pairs.append((lane + HALO, at + HIGH_SIDE + 2 * REACHED, REACHED))
    return doubled(matrix_of(pairs, 2 * LANES))


def response_edge_matrix():
    pairs = []
    for z in range(min(LAYERS, ZINJ + STEPS)):
        at = z * RESPONSE_SLOT + REACHED
        pairs.append((at, z * LANES, REACHED))
        pairs.append((at + HIGH_SIDE, (z + 1) * LANES - REACHED, REACHED))
    return doubled(matrix_of(pairs, min(LAYERS, ZINJ + STEPS) * LANES))


def factor_matrix():
    pairs = []
    for z in range(LAYERS):
        at, to = z % 2 * LANES + z // 2 * SLOT, z * RESPONSE_SLOT
        pairs.append((at + HALO - REACHED, to, 3 * REACHED))
        pairs.append((at + 16 + WIDE - 2 * REACHED, to + HIGH_SIDE, 3 * REACHED))
    return doubled(matrix_of(pairs, LANES, 2 * LANES))


def edge_matrix():
    pairs = []
    for slot in range(LAYERS // 2):
        pairs.append((slot * SLOT + 4, slot * LANES, HALO))
        pairs.append((slot * SLOT + 20, slot * LANES + LANES - HALO, HALO))
    return doubled(matrix_of(pairs, LAYERS // 2 * LANES))


def column_matrix():
    pairs = []
    for slot in range(LAYERS // 2):
        pairs.append((slot * LANES + LANES - WIDE, slot * SLOT, WIDE))
        pairs.append((slot * LANES, slot * SLOT + WIDE, WIDE))
    return doubled(matrix_of(pairs, LANES, LAYERS // 2 * LANES))


def message_matrix():
    pairs = []
    for item in range(8):
        for slot in range(LAYERS // 2):
            at, to = item * LANES + slot * SLOT, slot * SLOT + HALO * item
            pairs.append((at + 4, to, HALO))
            pairs.append((at + 8, LANES + to, HALO))
    return doubled(matrix_of(pairs, 2 * LANES, 8 * LANES))


def strip_matrices():
    own, got = [], []
    for slot in range(LAYERS // 2):
        at = slot * SLOT
        own += [(at, at + 16, WIDE), (at + 8, at + 4, WIDE)]
        for item in range(8):
            to = item * LANES + at
            got.append((at + HALO * item, to, HALO))
            got.append((LANES + at + HALO * item, to + 24, HALO))
    return doubled(matrix_of(own, LANES)), doubled(matrix_of(got, 8 * LANES, 2 * LANES))


class ResponseStrip:
    def __init__(self, ref, rows):
        self.ref, self.start, self.rows = ref, BASE - PAD, rows
        self.lane = lane_of((rows, LANES))

    def load(self, j, by=0):
        return self.ref[j, self.start + by : self.start + by + self.rows, :]

    def store(self, j, value):
        self.ref[j, self.start : self.start + self.rows, :] = value

    def step_h(self, fresh):
        e = [self.load(j) for j in range(3)]
        inside = self.lane < (LAYERS - 1) * RESPONSE_SLOT
        e_z = [jnp.where(inside, rolled(e[j], -RESPONSE_SLOT), 0.0) for j in range(2)] + [None]
        e_x = [None, self.load(1, 1), self.load(2, 1)]
        e_y = [rolled(e[0], -1), None, rolled(e[2], -1)]
        for j, change in enumerate(curl_of_e(e, e_z, e_x, e_y)):
            self.store(3 + j, change if fresh else self.load(3 + j) + change)

    def step_e(self, factor):
        h = [self.load(3 + j) for j in range(3)]
        inside = self.lane >= RESPONSE_SLOT
        h_z = [jnp.where(inside, rolled(h[j], RESPONSE_SLOT), 0.0) for j in range(2)] + [None]
        h_x = [None, self.load(4, -1), self.load(5, -1)]
        h_y = [rolled(h[0], 1), None, rolled(h[2], 1)]
        change = curl_of_h(h, h_z, h_x, h_y)
        return [self.load(j) + factor * change[j] for j in range(3)]

    def all_edges(self, cells_x, matrix):
        values = [beside(self.ref[j, BASE : BASE + cells_x, :]) for j in range(6)]
        return dot32(jnp.concatenate(values, 0), matrix)


def with_edges(value, edges_ref, start, block, width):
    own = edges_ref[start : start + value.shape[0], block * LANES : (block + 1) * LANES]
    lane = lane_of(own.shape)
    outer = (lane < width) | (lane >= LANES - width)
    return jnp.where(outer, own, value)


SCALES = (1.0, 1.0, 1.0, 2.0, 2.0, 2.0, 0.5)
BY_PRODUCT = (0, 1, 2)
EVERY = [(j, z) for j in range(6) for z in range(LAYERS)]
ALL_PLANES = EVERY[: 3 * LAYERS]


def blank_rims(ref):
    tall = ref.shape[2]
    for j in range(3):
        for z in range(LAYERS):
            ref[j, z, :PAD, :] = jnp.zeros((PAD, LANES), jnp.float32)
            ref[j, z, tall - PAD :, :] = jnp.zeros((PAD, LANES), jnp.float32)


class Inputs:
    def __init__(self, get):
        self.get = get


def first_kernel(
    e_ref, h_ref, m_ref, c_ref, e_out, h_out, token_ref, rim_ref, e_mid, h_mid
):
    cells_x = h_ref.shape[2]
    token_ref[...] = jnp.zeros_like(token_ref)
    row = lax.broadcasted_iota(jnp.int32, (8, LANES), 0)
    for j in range(7):
        for z in range(LAYERS):
            base = (j * LAYERS + z) * cells_x
            if j < 3:
                first, final = e_ref[base : base + 8, :], e_ref[base + cells_x - 8 : base + cells_x, :]
            else:
                ref = h_ref.at[j - 3, z] if j < 6 else m_ref.at[z]
                first, final = ref[:8, :], ref[cells_x - 8 :, :]
            if j == 6:
                first, final = coefficient_of(first), coefficient_of(final)
                c_ref[z] = coefficient_of(m_ref[z]) * 0.5
            rim_ref[j * LAYERS + z] = jnp.where(row < HALO, first, final)
    for ref in (e_out, h_out, e_mid, h_mid):
        blank_rims(ref)

    def get_e(j, z, start, size):
        if z >= LAYERS:
            return None
        base = (j * LAYERS + z) * cells_x + start - PAD
        if base + size <= e_ref.shape[0]:
            return e_ref[base : base + size, :]
        return pltpu.roll(e_ref[base - 1 : base - 1 + size, :], size - 1, 0)

    def get_h(j, z, start, size):
        return h_ref[j, z, start - PAD : start - PAD + size, :] * 2.0

    def factor(z, start, size):
        return c_ref[z, start - PAD : start - PAD + size, :]

    e, h = Inputs(get_e), Inputs(get_h)
    for new_e, new_h in ((e_mid, h_mid), (e_out, h_out)):
        to_e, to_h = Planes(new_e, ALL_PLANES), Planes(new_h, ALL_PLANES)
        step_h(e, h, to_h, PAD, cells_x)
        step_e(e, to_h, to_e.put, PAD, cells_x, factor)
        e, h = to_e, to_h


def first_steps(e_rows, h_field, material):
    cells_x = h_field.shape[2]
    f32 = jnp.float32
    planes = jax.ShapeDtypeStruct((3, LAYERS, cells_x + 2 * PAD, LANES), f32)
    return pl.pallas_call(
        first_kernel,
        out_shape=(
            jax.ShapeDtypeStruct((LAYERS, cells_x, LANES), f32),
            planes,
            planes,
            jax.ShapeDtypeStruct((8, LANES), f32),
            jax.ShapeDtypeStruct((7 * LAYERS, 2 * HALO, LANES), f32),
        ),
        scratch_shapes=[pltpu.VMEM(planes.shape, f32)] * 2,
        compiler_params=pltpu.CompilerParams(vmem_limit_bytes=VMEM_LIMIT),
        cost_estimate=lasting(2.7),
        name="first_steps",
    )(e_rows, h_field, material)


class Rows:
    def __init__(self, ref):
        self.ref = ref

    def load(self, j, by=0):
        return self.ref[j, :, 8 + by : 40 + by, :]

    def step(self, factor):
        zero = jnp.zeros((1, 32, LANES), jnp.float32)
        e = [self.load(j) for j in range(3)]
        e_z = [jnp.concatenate([e[j][1:], zero], 0) for j in range(2)] + [None]
        e_x = [None, self.load(1, 1), self.load(2, 1)]
        e_y = [pltpu.roll(e[0], LANES - 1, 2), None, pltpu.roll(e[2], LANES - 1, 2)]
        for j, change in enumerate(curl_of_e(e, e_z, e_x, e_y)):
            self.ref[3 + j, :, 8:40, :] = self.load(3 + j) + change
        h = [self.load(3 + j) for j in range(3)]
        h_z = [jnp.concatenate([zero, h[j][:-1]], 0) for j in range(2)] + [None]
        h_x = [None, self.load(4, -1), self.load(5, -1)]
        h_y = [pltpu.roll(h[0], 1, 2), None, pltpu.roll(h[2], 1, 2)]
        for j, change in enumerate(curl_of_h(h, h_z, h_x, h_y)):
            self.ref[j, :, 8:40, :] = e[j] + factor * change


def edge_rows(e_ref, h_ref, c_ref, x_ref, r_ref):
    cells_x = c_ref.shape[1]
    blank = jnp.zeros((LAYERS, PAD - HALO, LANES), jnp.float32)
    zero = jnp.zeros((LAYERS, 8, LANES), jnp.float32)
    for j in range(7):
        rims = x_ref[j * LAYERS : (j + 1) * LAYERS] * SCALES[j]
        if j < 3:
            bases = [(j * LAYERS + z) * cells_x for z in range(LAYERS)]
            first = jnp.stack([e_ref[b : b + 8, :] for b in bases])
            final = jnp.stack([e_ref[b + cells_x - 8 : b + cells_x, :] for b in bases])
        elif j < 6:
            first, final = h_ref[j - 3, :, :8, :] * 2.0, h_ref[j - 3, :, cells_x - 8 :, :] * 2.0
        else:
            first, final = c_ref[:, :8, :], c_ref[:, cells_x - 8 :, :]
        rows = [blank, rims[:, HALO:], first, final, rims[:, :HALO], blank]
        if j < 6:
            r_ref[j] = jnp.concatenate([zero] + rows + [zero], 1)
        else:
            factor = jnp.concatenate(rows, 1)
    edge = Rows(r_ref)
    for _ in range(STEPS):
        edge.step(factor)


def with_rows(value, r_ref, j, z):
    row = lax.broadcasted_iota(jnp.int32, (8, LANES), 0)
    top = jnp.where(row < HALO, r_ref[j, z, 16:24, :], value[:8])
    end = jnp.where(row >= HALO, r_ref[j, z, 24:32, :], value[-8:])
    return jnp.concatenate([top, value[8:-8], end], 0)


def later_kernel(e_in, h_in, c_ref, _, out_ref, token_ref, e_mid, h_mid, h_last):
    cells_x = c_ref.shape[1]
    token_ref[...] = jnp.zeros_like(token_ref)
    for ref in (e_mid, h_mid, h_last):
        blank_rims(ref)

    def finish(j, z, start, value):
        out_ref[j, z, start - PAD : start - PAD + value.shape[0], :] = value

    def factor(z, start, size):
        return c_ref[z, start - PAD : start - PAD + size, :]

    e, h = Planes(e_in, ALL_PLANES), Planes(h_in, ALL_PLANES)
    to_e, to_h = Planes(e_mid, ALL_PLANES), Planes(h_mid, ALL_PLANES)
    step_h(e, h, to_h, PAD, cells_x)
    step_e(e, to_h, to_e.put, PAD, cells_x, factor)
    last_h = Planes(h_last, ALL_PLANES)
    step_h(to_e, to_h, last_h, PAD, cells_x)
    step_e(to_e, last_h, finish, PAD, cells_x, factor)
    for j, z in ALL_PLANES:
        out_ref[3 + j, z] = h_last[j, z, PAD : PAD + cells_x, :]


def later_steps(e, h, coefficient, after):
    cells_x = coefficient.shape[1]
    f32 = jnp.float32
    return pl.pallas_call(
        later_kernel,
        out_shape=(
            jax.ShapeDtypeStruct((6, LAYERS, cells_x, LANES), f32),
            jax.ShapeDtypeStruct((8, LANES), f32),
        ),
        scratch_shapes=[pltpu.VMEM(e.shape, f32)] * 3,
        compiler_params=pltpu.CompilerParams(vmem_limit_bytes=VMEM_LIMIT),
        cost_estimate=lasting(2.7),
        name="later_steps",
    )(e, h, coefficient, after)


def strip_kernel(
    w_ref, low_ref, high_ref, free_ref, e_ref, h_ref, c_ref, x_ref, own_ref, got_ref, edge_ref,
    to_ref, _, factor_ref, out_ref, s_ref, edges_ref, r_ref,
):
    rows = w_ref.shape[2]
    first = BASE - PAD
    mine = [beside(w_ref[j, g]) for j in range(7) for g in range(2)]
    mine = dot32(jnp.concatenate(mine, 0), own_ref[...])
    got = [jnp.concatenate([beside(low_ref[a]), beside(high_ref[a])], 1) for a in range(2)]
    got = dot32(jnp.concatenate(got, 0), got_ref[...])
    factor = []
    for j in range(7):
        for g in range(2):
            i = 2 * j + g
            a, b = divmod(i, 8)
            value = mine[i * rows : (i + 1) * rows]
            value = value + got[a * rows : (a + 1) * rows, b * LANES : (b + 1) * LANES]
            if j < 6:
                s_ref[j, g, first : first + rows, :] = value
            else:
                factor.append(value)
    factor_ref[...] = dot32(jnp.concatenate([beside(f) for f in factor], 1), to_ref[...])
    strip = Strip(s_ref, rows)
    for step in range(STEPS):
        strip.step_h()
        new = strip.step_e(factor)
        for g in range(2):
            for j in range(3):
                strip.store(j, g, new[g][j])
    cells_x = out_ref.shape[2]
    edges_ref[...] = strip.all_edges(cells_x, edge_ref[...])
    edge_rows(e_ref, h_ref, c_ref, x_ref, r_ref)
    for j, z in EVERY:
        value = with_rows(free_ref[j, z], r_ref, j, z)
        value = with_edges(value, edges_ref, (2 * j + z % 2) * cells_x, z // 2, HALO)
        out_ref[j, z] = value if j < 3 else value * 0.5


def strip_run(own_edges, low, high, free, e_field, h_field, coefficient, x_rims, after):
    rows = own_edges.shape[2]
    f32 = jnp.float32
    return pl.pallas_call(
        strip_kernel,
        out_shape=(
            jax.ShapeDtypeStruct((rows, LANES), f32),
            jax.ShapeDtypeStruct(free.shape, f32),
        ),
        scratch_shapes=[
            pltpu.VMEM((6, 2, rows + 2 * (BASE - PAD), LANES), f32),
            pltpu.VMEM((12 * free.shape[2], LAYERS // 2 * LANES), f32),
            pltpu.VMEM((6, LAYERS, 48, LANES), f32),
        ],
        compiler_params=pltpu.CompilerParams(vmem_limit_bytes=VMEM_LIMIT),
        cost_estimate=lasting(4),
        name="strip_run",
    )(
        own_edges, low, high, free, e_field, h_field, coefficient, x_rims,
        *(jnp.asarray(m) for m in strip_matrices()),
        jnp.asarray(edge_matrix()), jnp.asarray(factor_matrix()), after,
    )


def response_kernel(
    c_ref, factor_ref, free_ref, mine_ref, other_ref, near_ref, outside_ref, edge_ref,
    e_out, h_out,
    e_refs, h_refs, s_ref, plane_ref, rim_ref, done_ref, edges_ref, sems,
):
    cells_x = e_out.shape[2]
    copies = []

    def send(j, z, source):
        to = e_out.at[j, z] if j < 3 else h_out.at[j - 3, z]
        copies.append(pltpu.make_async_copy(source, to, sems.at[j, z]))
        copies[-1].start()

    far = [(j, z) for j, z in EVERY if z >= ZINJ + STEPS - (0 if j < 2 else 1)]
    for j, z in far:
        send(j, z, free_ref.at[j, z])
    rows = cells_x + 2 * PAD
    half = rows // 2
    first = BASE - PAD
    own = lax.axis_index("src")
    lane = lane_of((half, LANES))
    for ref, which in ((mine_ref, own), (other_ref, 1 - own)):
        at = pl.ds(pl.multiple_of(which * half, 8), half)
        for part in range(2):
            plane_ref[part, at, :] = ref[part * half : (part + 1) * half, :]
        rim_ref[0, at, :] = jnp.where(lane < 16, unfolded(ref[2 * half :, :], half, 8, 0), 0.0)
    outer = dot32(beside(rim_ref[0]), outside_ref[...])
    planes = jnp.concatenate([beside(plane_ref[part]) for part in range(2)], 0)
    inner = dot32(planes, near_ref[...])
    for part in range(2):
        own_part = outer[:, part * LANES : (part + 1) * LANES]
        rim_ref[part] = inner[part * rows : (part + 1) * rows] + own_part

    def injection(ref, step, start, size):
        cosine = COURANT * math.cos(OMEGA * step)
        sine = COURANT * math.sin(OMEGA * step)
        re, im = ref[0, start : start + size, :], ref[1, start : start + size, :]
        return [cosine * re - sine * im, sine * re + cosine * im, None]

    e, h = Planes(e_refs.at[0]), Planes(h_refs.at[0])
    for j, value in enumerate(injection(plane_ref, 1, 0, rows)):
        e.put(j, ZINJ, first, value)
    strip = ResponseStrip(s_ref, rows)
    s_ref[...] = jnp.zeros_like(s_ref)
    for j, value in enumerate(injection(rim_ref, 1, 0, rows)[:2]):
        strip.store(j, value)
    for step in range(2, STEPS + 1):
        strip.step_h(step == 2)
        new = strip.step_e(factor_ref[...])
        for j, value in enumerate(injection(rim_ref, step, 0, rows)):
            strip.store(j, add(new[j], value))
    edges_ref[...] = strip.all_edges(cells_x, edge_ref[...])

    def factor(z, start, size):
        return c_ref[z, start : start + size, :]

    def finish(j, z, start, value):
        if (j, z) in far:
            return
        size, at = value.shape[0], start - BASE
        if j < 3 and z == ZINJ:
            value = add(value, injection(plane_ref, STEPS, start - first, size)[j])
        value = with_edges(value, edges_ref, j * cells_x + at, z, REACHED)
        value = (value if j < 3 else value * 0.5) + free_ref[j, z, at : at + size, :]
        done_ref[j, z, at : at + size, :] = value
        if at + size == cells_x:
            send(j, z, done_ref.at[j, z])

    for step in range(2, STEPS + 1):
        last = step == STEPS
        new_h = Planes(h_refs.at[step - 1])
        step_h(e, h, new_h, first, rows - (PAD if last else 0))
        if last:
            for j, z in ALL_PLANES:
                for at, size in chunks(BASE, cells_x):
                    value = new_h.get(j, z, at, size)
                    if value is not None:
                        finish(3 + j, z, at, value)
            step_e(e, new_h, finish, BASE, cells_x, factor)
            break
        new_e = Planes(e_refs.at[step - 1])

        def put(j, z, start, value):
            if z == ZINJ:
                size = value.shape[0]
                value = add(value, injection(plane_ref, step, start - first, size)[j])
            new_e.put(j, z, start, value)

        step_e(e, new_h, put, first, rows, factor)
        e, h = new_e, new_h
    for copy in copies:
        copy.wait()


def response(c_ext, factor, free, mine, other, cells_x):
    rows = cells_x + 2 * PAD
    tall = cells_x + 2 * BASE
    f32 = jnp.float32
    out = jax.ShapeDtypeStruct((3, LAYERS, cells_x, LANES), f32)
    vmem = pl.BlockSpec(memory_space=pltpu.VMEM)
    return pl.pallas_call(
        response_kernel,
        in_specs=[vmem] * 8,
        out_specs=(pl.BlockSpec(memory_space=pl.ANY),) * 2,
        out_shape=(out, out),
        scratch_shapes=[
            pltpu.VMEM((STEPS - 1, 3, LAYERS, tall, LANES), f32),
            pltpu.VMEM((STEPS, 3, LAYERS, tall, LANES), f32),
            pltpu.VMEM((6, tall, LANES), f32),
            pltpu.VMEM((2, rows, LANES), f32),
            pltpu.VMEM((2, rows, LANES), f32),
            pltpu.VMEM((6, LAYERS, cells_x, LANES), f32),
            pltpu.VMEM((6 * cells_x, min(LAYERS, ZINJ + STEPS) * LANES), f32),
            pltpu.SemaphoreType.DMA((6, LAYERS)),
        ],
        compiler_params=pltpu.CompilerParams(vmem_limit_bytes=RESPONSE_LIMIT),
        cost_estimate=lasting(6.5),
        name="response",
    )(
        c_ext, factor, free, mine, other,
        jnp.asarray(near_matrix()), jnp.asarray(outside_matrix()),
        jnp.asarray(response_edge_matrix()),
    )


def along(block, axis, distance):
    n = lax.axis_size(axis)
    return lax.ppermute(block, axis, [((i - distance) % n, i) for i in range(n)])


def flipped(block, axis, bits):
    return lax.ppermute(block, axis, [(i, i ^ bits) for i in range(lax.axis_size(axis))])


def to_groups(block, n_src, n_tx, flip, distance):
    route = []
    for s in range(n_src):
        for t in range(n_tx):
            route.append((s * n_tx + t, (s ^ flip) * n_tx + (t + distance) % n_tx))
    return lax.ppermute(block, ("src", "tx"), route)


def per_device(orders, offsets, material, e_field, h_field):
    cols_ky = orders.shape[3]
    layers, cells_x, cells_y = material.shape
    n_src, n_tx, n_ty = lax.axis_size("src"), lax.axis_size("tx"), lax.axis_size("ty")
    half = cells_x // 2 + PAD
    e_field = e_field.reshape(-1, cells_y)
    parts = x_stage(
        offsets.T, jnp.swapaxes(orders, 2, 3), n_tx, cells_x, (e_field, h_field, material)
    )
    received = [parts[0]]
    for distance in range(n_tx):
        for flip in range(n_src):
            if distance or flip:
                part = parts[2 * distance + flip]
                received.append(to_groups(part, n_src, n_tx, flip, distance))
    coefficient, e_half, h_half, begun, rims = first_steps(e_field, h_field, material)

    if n_tx == 2:
        x_rims = along(rims, "tx", 1)
    else:
        top, bottom = rims[:, :HALO], rims[:, HALO:]
        x_rims = jnp.concatenate([along(top, "tx", -1), along(bottom, "tx", 1)], 1)
    block = summed(received, begun)
    c_ext, own_edges, to_high, to_low = pack(e_field, h_field, coefficient, x_rims)
    low = along(to_high, "ty", 1)
    high = along(to_low, "ty", -1)
    free, run = later_steps(e_half, h_half, coefficient, to_high)

    blocks = {0: block}
    for bits in range(n_ty - 2, 0, -2):
        blocks[bits] = flipped(block, "ty", bits)
    for bits in range(0, n_ty, 2):
        blocks[bits + 1] = flipped(blocks[bits], "ty", 1)
    mine = y_stage([blocks[b] for b in range(n_ty)], cols_ky, cells_y, half, run)
    other = flipped(mine, "src", 1)
    factor, free = strip_run(
        own_edges, low, high, free, e_field, h_field, coefficient, x_rims, mine
    )
    return response(c_ext, factor, free, mine, other, cells_x)


def solution(mesh):
    in_specs = (
        P("src", None, "tx", "ty"),
        P("src", None),
        P(None, "tx", "ty"),
        P(None, None, "tx", "ty"),
        P(None, None, "tx", "ty"),
    )
    out_specs = (P(None, None, "tx", "ty"), P(None, None, "tx", "ty"))
    return jax.shard_map(
        per_device, mesh=mesh, in_specs=in_specs, out_specs=out_specs, check_vma=False
    )
```

```python
import functools
import math

import jax
import jax.numpy as jnp
import ml_dtypes
import numpy as np
from jax import lax
from jax.experimental import pallas as pl
from jax.experimental.pallas import tpu as pltpu
from jax.sharding import PartitionSpec as P

MX = 512
MY = 512
STEPS = 4
ZINJ = 1
LAYERS = 6

COURANT = 0.5
OMEGA = 0.7
PERMITTIVITY = (1.0, 2.6, 11.9, 2.1)

REACH = 8
SPAN = 2 * REACH
PAD = 8
HALO = 4
CHUNK = 16
RESPONSE_CHUNK = 64
BASE = 16
SLOT = 32
WIDE = 8
REACHED = STEPS - 1
RESPONSE_SLOT = 21
HIGH_SIDE = 10
LANES = 128
VMEM_LIMIT = 24 * 1024 * 1024
RESPONSE_LIMIT = 40 * 1024 * 1024
X_LIMIT = 60_700_000


def split_bf16(table):
    high = table.astype(ml_dtypes.bfloat16)
    low = (table - high.astype(np.float64)).astype(ml_dtypes.bfloat16)
    return high, low


def padded(lanes):
    return -(-lanes // LANES) * LANES


@functools.lru_cache(maxsize=None)
def x_seeds(n_tx, rows_kx, cells_x):
    window = rows_kx + SPAN
    wide = padded(window)
    full = cells_x * n_tx
    turns = [8 << k for k in range((cells_x // 8).bit_length())]
    count = 8 + len(turns) + n_tx
    table = np.zeros((n_tx, -(-count // 8) * 8, 2 * wide), np.float32)
    for own in range(n_tx):
        freq = own * rows_kx - MX // 2 - REACH + np.arange(window)
        tiles = [(own + distance) % n_tx * cells_x for distance in range(n_tx)]
        x = np.array(list(range(-PAD, 8 - PAD)) + turns + tiles)
        angle = np.mod(x[:, None] * freq[None, :], full) * (2.0 * math.pi / full)
        table[own, :count, :window] = np.cos(angle)
        table[own, :count, wide : wide + window] = np.sin(angle)
    return table, len(turns)


@functools.lru_cache(maxsize=None)
def y_tables(n_ty, cols_ky, cells_y):
    full = cells_y * n_ty
    window = cols_ky + SPAN
    edge = np.concatenate([np.arange(-HALO, 0), cells_y + np.arange(HALO)])
    y = np.concatenate([np.arange(cells_y), edge])
    table = np.zeros((n_ty, LANES + 2 * SPAN, 2 * cells_y + LANES))
    for block in range(n_ty):
        freq = block * cols_ky - MY // 2 - REACH + np.arange(window)
        angle = np.mod(freq[:, None] * y[None, :], full) * (2.0 * math.pi / full)
        cos, sin = np.cos(angle), np.sin(angle)

        def placed(re_cols, im_cols):
            out = np.zeros((window, 2 * cells_y + LANES))
            out[:, :cells_y] = re_cols[:, :cells_y]
            out[:, cells_y : 2 * cells_y] = im_cols[:, :cells_y]
            out[:, 2 * cells_y : 2 * cells_y + 2 * HALO] = re_cols[:, cells_y:]
            out[:, 2 * cells_y + 2 * HALO : 2 * cells_y + 4 * HALO] = im_cols[:, cells_y:]
            return out

        from_re = placed(cos, sin)
        from_im = placed(-sin, cos)
        table[block, :cols_ky] = from_re[:cols_ky]
        table[block, cols_ky : 2 * cols_ky] = from_im[:cols_ky]
        table[block, LANES : LANES + SPAN] = from_re[cols_ky:]
        table[block, LANES + SPAN :] = from_im[cols_ky:]
    return split_bf16(table)


@functools.lru_cache(maxsize=None)
def y_phases(n_ty, cols_ky, cells_y):
    full = cells_y * n_ty
    out = np.zeros((n_ty, n_ty, 8, LANES), np.float32)
    for own in range(n_ty):
        for block in range(n_ty):
            freq = block * cols_ky - MY // 2 - REACH + np.arange(cols_ky + SPAN)
            angle = np.mod(freq * own * cells_y, full) * (2.0 * math.pi / full)
            cos, sin = np.cos(angle), np.sin(angle)
            out[own, block, 0, :cols_ky] = cos[:cols_ky]
            out[own, block, 0, cols_ky : 2 * cols_ky] = cos[:cols_ky]
            out[own, block, 1, :cols_ky] = -sin[:cols_ky]
            out[own, block, 1, cols_ky : 2 * cols_ky] = sin[:cols_ky]
            for group in range(LANES // (2 * SPAN)):
                at = group * 2 * SPAN
                out[own, block, 2, at : at + SPAN] = cos[cols_ky:]
                out[own, block, 2, at + SPAN : at + 2 * SPAN] = cos[cols_ky:]
                out[own, block, 3, at : at + SPAN] = -sin[cols_ky:]
                out[own, block, 3, at + SPAN : at + 2 * SPAN] = sin[cols_ky:]
    return out


def lasting(microseconds):
    moved = int(microseconds * 3.69e6)
    return pl.CostEstimate(flops=0, transcendentals=0, bytes_accessed=moved)


def lane_of(shape):
    return lax.broadcasted_iota(jnp.int32, shape, len(shape) - 1)


def rolled(value, shift):
    shift = shift % LANES
    return value if shift == 0 else pltpu.roll(value, shift, 1)


def halves(value):
    high = value.astype(jnp.bfloat16)
    low = (value - high.astype(jnp.float32)).astype(jnp.bfloat16)
    return high, low


def dot32(a, b):
    return jnp.dot(a, b, preferred_element_type=jnp.float32)


def fold_groups(rows, count):
    tiles = rows // 8
    sizes = [8 * (tiles // count + (1 if g < tiles % count else 0)) for g in range(count)]
    starts = [sum(sizes[:g]) for g in range(count)]
    return list(zip(starts, sizes))


def folded_rows(rows, count):
    return fold_groups(rows, count)[0][1]


def folded(value, count):
    groups = fold_groups(value.shape[0], count)
    tall, wide = groups[0][1], LANES // count
    lane = lane_of((tall, LANES))
    total = jnp.zeros((tall, LANES), value.dtype)
    for g, (start, size) in enumerate(groups):
        part = value[start : start + size]
        if size < tall:
            part = jnp.concatenate([part, jnp.zeros((tall - size, LANES), value.dtype)], 0)
        keep = (lane >= wide * g) & (lane < wide * (g + 1))
        total = jnp.where(keep, rolled(part, wide * g), total)
    return total


def unfolded(value, rows, count, at):
    wide = LANES // count
    parts = []
    for g, (_, size) in enumerate(fold_groups(rows, count)):
        parts.append(rolled(value[:size], at - wide * g))
    return jnp.concatenate(parts, 0)


def turned(cos, sin, by_cos, by_sin):
    return cos * by_cos - sin * by_sin, sin * by_cos + cos * by_sin


def fill_table(n_turns, seed_ref, table_ref):
    _, n_tx, rows, both = table_ref.shape
    wide = both // 2

    def row(i):
        return seed_ref[i : i + 1, :wide], seed_ref[i : i + 1, wide:]

    cos, sin = seed_ref[:8, :wide], seed_ref[:8, wide:]
    for k in range(n_turns):
        more = min(8 << k, rows - (8 << k))
        new = turned(cos[:more], sin[:more], *row(8 + k))
        cos, sin = jnp.concatenate([cos, new[0]], 0), jnp.concatenate([sin, new[1]], 0)
    for distance in range(n_tx):
        there = turned(cos, sin, *row(8 + n_turns + distance))
        for part in range(2):
            high, low = halves(there[part])
            table_ref[0, distance, :, part * wide : (part + 1) * wide] = high
            table_ref[1, distance, :, part * wide : (part + 1) * wide] = low


def x_kernel(
    n_turns, offs_in, orders_in, seeds_in, _e, _h, _m, *refs
):
    *out_refs, offs_ref, orders_ref, seed_ref, table_ref, line_ref, acc_ref, q_ref, sems = refs
    own = lax.axis_index("src")
    copies = [
        pltpu.make_async_copy(seeds_in.at[lax.axis_index("tx")], seed_ref, sems.at[0]),
        pltpu.make_async_copy(orders_in, orders_ref, sems.at[1]),
        pltpu.make_async_copy(offs_in, offs_ref, sems.at[2]),
    ]
    for copy in copies:
        copy.start()
    points, _, cols_ky, rows_kx = orders_ref.shape
    _, n_tx, rows, both = table_ref.shape
    half = rows // 2
    acc_ref[...] = jnp.zeros_like(acc_ref)
    line_ref[...] = jnp.zeros_like(line_ref)
    wide = line_ref.shape[4]
    copies[0].wait()
    fill_table(n_turns, seed_ref, table_ref)
    copies[1].wait()
    copies[2].wait()
    for point in range(points):
        down = offs_ref[0, point] + REACH
        across = offs_ref[1, point] + REACH
        for part in range(2):
            for tile in range(rows_kx // wide):
                lanes = slice(tile * wide, (tile + 1) * wide)
                line = line_ref.at[point, part, tile]
                line[pl.ds(across, cols_ky), :] = orders_ref[point, part, :, lanes]
                acc_ref[part, pl.ds(down + tile * wide, wide), :] += line[...].T
    s_re = acc_ref[0]
    s_im = acc_ref[1]
    lane = lane_of(s_re.shape)
    re_by, im_by = rolled(s_re, cols_ky), rolled(s_im, cols_ky)

    def main(re, im_by):
        out = jnp.where(lane < cols_ky, re, im_by)
        return out if 2 * cols_ky == LANES else jnp.where(lane < 2 * cols_ky, out, 0.0)

    def spill(re_back, im_back):
        out = jnp.where(lane < SPAN, re_back, im_back)
        return jnp.where(lane < 2 * SPAN, out, 0.0)

    same = 2 * cols_ky == LANES
    re_back = re_by if same else rolled(s_re, -cols_ky)
    im_back = im_by if same else rolled(s_im, -cols_ky)
    top = [main(s_re, im_by), spill(re_back, rolled(s_im, SPAN - cols_ky))]
    bottom = [main(-s_im, re_by), spill(-im_back, rolled(s_re, SPAN - cols_ky))]
    right = jnp.concatenate([jnp.concatenate(top, 1), jnp.concatenate(bottom, 1)], 0)
    right_h, right_l = halves(right)
    tall = n_tx * rows
    by_high = dot32(table_ref[...].reshape(2 * tall, both), right_h)
    by_low = dot32(table_ref[0].reshape(tall, both), right_l)
    q_ref[...] = by_high[:tall] + (by_high[tall:] + by_low)
    for distance in range(n_tx):
        for flip in range(2):
            start = pl.multiple_of(distance * rows + (own ^ flip) * half, 8)
            block = q_ref[pl.ds(start, half), :]
            out_refs[2 * distance + flip][:half, :] = block[:, :LANES]
            out_refs[2 * distance + flip][half:, :] = folded(block[:, LANES:], 4)


def x_stage(offsets, orders, n_tx, cells_x, beside):
    points, _, cols_ky, rows_kx = orders.shape
    wide = min(rows_kx, LANES)
    seeds, n_turns = x_seeds(n_tx, rows_kx, cells_x)
    rows = cells_x + 2 * PAD
    half = rows // 2
    height = half + folded_rows(half, 4)
    f32 = jnp.float32
    return pl.pallas_call(
        functools.partial(x_kernel, n_turns),
        in_specs=[pl.BlockSpec(memory_space=pltpu.HBM)] * 6,
        out_shape=(jax.ShapeDtypeStruct((height, LANES), f32),) * (2 * n_tx),
        scratch_shapes=[
            pltpu.SMEM(offsets.shape, jnp.int32),
            pltpu.VMEM(orders.shape, f32),
            pltpu.VMEM(seeds.shape[1:], f32),
            pltpu.VMEM((2, n_tx, rows, seeds.shape[2]), jnp.bfloat16),
            pltpu.VMEM((points, 2, rows_kx // wide, LANES, wide), f32),
            pltpu.VMEM((2, seeds.shape[2] // 2, LANES), f32),
            pltpu.VMEM((n_tx * rows, 2 * LANES), f32),
            pltpu.SemaphoreType.DMA((3,)),
        ],
        compiler_params=pltpu.CompilerParams(vmem_limit_bytes=X_LIMIT),
        cost_estimate=lasting(3.5),
        name="x_stage",
    )(offsets, orders, jnp.asarray(seeds), *beside)


def sum_kernel(*refs):
    *part_refs, _, out_ref = refs
    total = part_refs[0][...]
    for ref in part_refs[1:]:
        total = total + ref[...]
    out_ref[...] = total


def summed(parts, after):
    return pl.pallas_call(
        sum_kernel,
        out_shape=jax.ShapeDtypeStruct(parts[0].shape, jnp.float32),
        compiler_params=pltpu.CompilerParams(vmem_limit_bytes=VMEM_LIMIT),
        cost_estimate=lasting(0.4),
        name="sum_parts",
    )(*parts, after)


def y_kernel(cols_ky, half, *refs):
    *block_refs, th_ref, tl_ref, phase_ref, _, out_ref = refs
    n_ty = len(block_refs)
    lane = lane_of((half, LANES))
    mains, spills, numbers = [], [], []
    own = lax.axis_index("ty")
    for number, ref in enumerate(block_refs):
        block = own ^ number
        numbers.append(block)
        phase = phase_ref[own, block]
        main = ref[:half, :]
        if 2 * cols_ky == LANES:
            swapped = rolled(main, cols_ky)
        else:
            swapped = jnp.where(lane < cols_ky, rolled(main, -cols_ky), rolled(main, cols_ky))
        mains.append(main * phase[0:1] + swapped * phase[1:2])
        spill = ref[half:, :]
        small = lane_of(spill.shape)
        other = jnp.where((small & (2 * SPAN - 1)) < SPAN, rolled(spill, -SPAN), rolled(spill, SPAN))
        spills.append(spill * phase[2:3] + other * phase[3:4])
    packed = []
    for first in range(0, n_ty, 4):
        total = None
        for g in range(4):
            part = unfolded(spills[first + g], half, 4, 32 * g)
            total = part if total is None else jnp.where(lane >= 32 * g, part, total)
        packed.append(total)
    left = jnp.concatenate(mains + packed, 1)
    high = left.astype(jnp.bfloat16)
    low = left - high.astype(jnp.float32)
    both = jnp.concatenate([left, low], 0).astype(jnp.bfloat16)

    def table(ref):
        parts = [ref[block, :LANES, :] for block in numbers]
        return jnp.concatenate(parts + [ref[block, LANES:, :] for block in numbers], 0)

    by_high = dot32(both, table(th_ref))
    result = by_high[:half] + (by_high[half:] + dot32(high, table(tl_ref)))
    out_ref[:half, :] = result[:, :LANES]
    out_ref[half : 2 * half, :] = result[:, LANES : 2 * LANES]
    out_ref[2 * half :, :] = folded(result[:, 2 * LANES :], 8)


def y_stage(blocks, cols_ky, cells_y, half, after):
    n_ty = len(blocks)
    t_h, t_l = y_tables(n_ty, cols_ky, cells_y)
    phases = y_phases(n_ty, cols_ky, cells_y)
    height = 2 * half + folded_rows(half, 8)
    return pl.pallas_call(
        functools.partial(y_kernel, cols_ky, half),
        out_shape=jax.ShapeDtypeStruct((height, LANES), jnp.float32),
        compiler_params=pltpu.CompilerParams(vmem_limit_bytes=VMEM_LIMIT),
        cost_estimate=lasting(1.5),
        name="y_stage",
    )(*blocks, jnp.asarray(t_h), jnp.asarray(t_l), jnp.asarray(phases), after)


def coefficient_of(material):
    value = jnp.where(material == 0, COURANT / PERMITTIVITY[0], COURANT / PERMITTIVITY[1])
    value = jnp.where(material == 2, COURANT / PERMITTIVITY[2], value)
    return jnp.where(material == 3, COURANT / PERMITTIVITY[3], value).astype(jnp.float32)


def pack_kernel(
    e_ref, h_ref, c_ref, x_ref, column_ref, message_ref, ext_ref, w_ref, low_ref, high_ref
):
    cells_x = h_ref.shape[2]
    end = BASE + cells_x
    rows = cells_x + 2 * PAD
    lane = lane_of((rows, LANES))
    by_product = []
    blank = jnp.zeros((PAD - HALO, LANES), jnp.float32)
    for j in range(7):
        scale = SCALES[j]
        strips = [jnp.zeros((rows, LANES), jnp.float32)] * 2
        planes = [[], []]
        for z in range(LAYERS):
            if j < 3:
                body = e_ref[pl.ds((j * LAYERS + z) * cells_x, cells_x), :]
            elif j < 6:
                body = h_ref[j - 3, z] * scale
            else:
                body = c_ref[z]
            rims = x_ref[j * LAYERS + z]
            rims = rims if scale == 1 else rims * scale
            full = jnp.concatenate([blank, rims[HALO:], body, rims[:HALO], blank], 0)
            if j == 6:
                ext_ref[z, 0 : BASE - PAD, :] = jnp.zeros((BASE - PAD, LANES), jnp.float32)
                ext_ref[z, BASE - PAD : end + PAD, :] = full
                ext_ref[z, end + PAD : end + BASE, :] = jnp.zeros((BASE - PAD, LANES), jnp.float32)
            g, at = z % 2, (z // 2) * SLOT
            if j in BY_PRODUCT:
                planes[g].append(beside(full))
                continue
            keep = (lane >= at) & (lane < at + 2 * WIDE)
            strips[g] = jnp.where(keep, rolled(full, at + WIDE), strips[g])
        for g in range(2):
            if j in BY_PRODUCT:
                by_product.append(jnp.concatenate(planes[g], 1))
            else:
                w_ref[j, g] = strips[g]
    taken = dot32(jnp.concatenate(by_product, 0), column_ref[...])
    for i, (j, g) in enumerate((j, g) for j in BY_PRODUCT for g in range(2)):
        w_ref[j, g] = taken[i * rows : (i + 1) * rows]
    items = [beside(w_ref[j, g]) for j in range(7) for g in range(2)]
    items += [jnp.zeros_like(items[0])] * (16 - len(items))
    sides = [jnp.concatenate(items[8 * a : 8 * a + 8], 1) for a in range(2)]
    sent = dot32(jnp.concatenate(sides, 0), message_ref[...])
    for a in range(2):
        low_ref[a] = sent[a * rows : (a + 1) * rows, :LANES]
        high_ref[a] = sent[a * rows : (a + 1) * rows, LANES:]


def pack(e_field, h_field, coefficient, x_rims):
    cells_x = h_field.shape[2]
    rows = cells_x + 2 * PAD
    tall = cells_x + 2 * BASE
    f32 = jnp.float32
    return pl.pallas_call(
        pack_kernel,
        out_shape=(
            jax.ShapeDtypeStruct((LAYERS, tall, LANES), f32),
            jax.ShapeDtypeStruct((7, 2, rows, LANES), f32),
            jax.ShapeDtypeStruct((2, rows, LANES), f32),
            jax.ShapeDtypeStruct((2, rows, LANES), f32),
        ),
        compiler_params=pltpu.CompilerParams(vmem_limit_bytes=VMEM_LIMIT),
        cost_estimate=lasting(2.2),
        name="pack",
    )(
        e_field, h_field, coefficient, x_rims,
        jnp.asarray(column_matrix()),
        jnp.asarray(message_matrix()),
    )


def total(terms):
    out = None
    for sign, value in terms:
        if value is None:
            continue
        if out is None:
            out = value if sign > 0 else -value
        else:
            out = out + value if sign > 0 else out - value
    return out


def add(a, b):
    return total([(1, a), (1, b)])


def differ(a, b):
    return total([(1, a), (-1, b)])


def curl_of_e(e, e_z, e_x, e_y):
    return (
        differ(differ(e_z[1], e[1]), differ(e_y[2], e[2])),
        differ(differ(e_x[2], e[2]), differ(e_z[0], e[0])),
        differ(differ(e_y[0], e[0]), differ(e_x[1], e[1])),
    )


def curl_of_h(h, h_z, h_x, h_y):
    return (
        differ(differ(h[2], h_y[2]), differ(h[1], h_z[1])),
        differ(differ(h[0], h_z[0]), differ(h[2], h_x[2])),
        differ(differ(h[1], h_x[1]), differ(h[0], h_y[0])),
    )


def moved(value, shift):
    return None if value is None else rolled(value, shift)


class Planes:
    def __init__(self, ref, live=()):
        self.ref, self.live = ref, set(live)

    def get(self, j, z, start, size):
        return self.ref[j, z, start : start + size, :] if (j, z) in self.live else None

    def put(self, j, z, start, value):
        if value is not None:
            self.ref[j, z, start : start + value.shape[0], :] = value
            self.live.add((j, z))


def chunks(start, size, height):
    return [(at, min(height, start + size - at)) for at in range(start, start + size, height)]


def step_h(e, h, to, start, size, height):
    for at, rows in chunks(start, size, height):
        above = [e.get(j, 0, at, rows) for j in range(3)]
        for z in range(LAYERS):
            own, above = above, [e.get(j, z + 1, at, rows) for j in range(3)]
            e_x = [None] + [e.get(j, z, at + 1, rows) for j in (1, 2)]
            e_y = [moved(own[0], -1), None, moved(own[2], -1)]
            for j, change in enumerate(curl_of_e(own, above[:2] + [None], e_x, e_y)):
                to.put(j, z, at, add(h.get(j, z, at, rows), change))


def step_e(e, h, put, start, size, factor_of, height):
    for at, rows in chunks(start, size, height):
        own = [None] * 3
        for z in range(LAYERS):
            below, own = own, [h.get(j, z, at, rows) for j in range(3)]
            h_x = [None] + [h.get(j, z, at - 1, rows) for j in (1, 2)]
            h_y = [moved(own[0], 1), None, moved(own[2], 1)]
            factor = factor_of(z, at, rows)
            for j, change in enumerate(curl_of_h(own, below[:2] + [None], h_x, h_y)):
                value = e.get(j, z, at, rows)
                put(j, z, at, value if change is None else add(value, factor * change))


class Strip:
    def __init__(self, ref, rows):
        self.ref, self.start, self.rows = ref, BASE - PAD, rows
        self.lane = lane_of((rows, LANES))

    def load(self, j, g, by=0):
        return self.ref[j, g, self.start + by : self.start + by + self.rows, :]

    def store(self, j, g, value):
        self.ref[j, g, self.start : self.start + self.rows, :] = value

    def step_h(self, fresh=False):
        e = [[self.load(j, g) for j in range(3)] for g in range(2)]
        inside = self.lane < 2 * SLOT
        above = [
            [e[1][0], e[1][1], None],
            [jnp.where(inside, rolled(e[0][j], -SLOT), 0.0) for j in range(2)] + [None],
        ]
        for g in range(2):
            e_x = [None, self.load(1, g, 1), self.load(2, g, 1)]
            e_y = [rolled(e[g][0], -1), None, rolled(e[g][2], -1)]
            for j, change in enumerate(curl_of_e(e[g], above[g], e_x, e_y)):
                self.store(3 + j, g, change if fresh else self.load(3 + j, g) + change)

    def step_e(self, factor):
        h = [[self.load(3 + j, g) for j in range(3)] for g in range(2)]
        inside = self.lane >= SLOT
        below = [
            [jnp.where(inside, rolled(h[1][j], SLOT), 0.0) for j in range(2)] + [None],
            [h[0][0], h[0][1], None],
        ]
        new = []
        for g in range(2):
            h_x = [None, self.load(4, g, -1), self.load(5, g, -1)]
            h_y = [rolled(h[g][0], 1), None, rolled(h[g][2], 1)]
            change = curl_of_h(h[g], below[g], h_x, h_y)
            new.append([self.load(j, g) + factor[g] * change[j] for j in range(3)])
        return new

    def all_edges(self, cells_x, matrix):
        values = [
            beside(self.ref[j, g, BASE : BASE + cells_x, :]) for j in range(6) for g in range(2)
        ]
        return dot32(jnp.concatenate(values, 0), matrix)


def beside(value):
    return jnp.concatenate(halves(value), 1)


def matrix_of(pairs, columns, rows=LANES):
    out = np.zeros((rows, columns), ml_dtypes.bfloat16)
    for first_row, first_column, count in pairs:
        for i in range(count):
            out[first_row + i, first_column + i] = 1
    return out


def doubled(matrix):
    blocks = matrix.reshape(-1, LANES, matrix.shape[1])
    return np.concatenate([m for block in blocks for m in (block, block)], 0)


def near_matrix():
    own, at = 2 * REACHED, ZINJ * RESPONSE_SLOT
    pairs = [(0, at + REACHED, own), (LANES - own, at + HIGH_SIDE, own)]
    return doubled(matrix_of(pairs, LANES))


def outside_matrix():
    pairs = []
    for part in range(2):
        lane, at = part * 2 * HALO, part * LANES + ZINJ * RESPONSE_SLOT
        pairs.append((lane + HALO - REACHED, at, REACHED))
        pairs.append((lane + HALO, at + HIGH_SIDE + 2 * REACHED, REACHED))
    return doubled(matrix_of(pairs, 2 * LANES))


def response_edge_matrix():
    pairs = []
    for z in range(min(LAYERS, ZINJ + STEPS)):
        at = z * RESPONSE_SLOT + REACHED
        pairs.append((at, z * LANES, REACHED))
        pairs.append((at + HIGH_SIDE, (z + 1) * LANES - REACHED, REACHED))
    return doubled(matrix_of(pairs, min(LAYERS, ZINJ + STEPS) * LANES))


def factor_matrix():
    pairs = []
    for z in range(LAYERS):
        at, to = z % 2 * LANES + z // 2 * SLOT, z * RESPONSE_SLOT
        pairs.append((at + HALO - REACHED, to, 3 * REACHED))
        pairs.append((at + 16 + WIDE - 2 * REACHED, to + HIGH_SIDE, 3 * REACHED))
    return doubled(matrix_of(pairs, LANES, 2 * LANES))


def edge_matrix():
    pairs = []
    for slot in range(LAYERS // 2):
        pairs.append((slot * SLOT + 4, slot * LANES, HALO))
        pairs.append((slot * SLOT + 20, slot * LANES + LANES - HALO, HALO))
    return doubled(matrix_of(pairs, LAYERS // 2 * LANES))


def column_matrix():
    pairs = []
    for slot in range(LAYERS // 2):
        pairs.append((slot * LANES + LANES - WIDE, slot * SLOT, WIDE))
        pairs.append((slot * LANES, slot * SLOT + WIDE, WIDE))
    return doubled(matrix_of(pairs, LANES, LAYERS // 2 * LANES))


def message_matrix():
    pairs = []
    for item in range(8):
        for slot in range(LAYERS // 2):
            at, to = item * LANES + slot * SLOT, slot * SLOT + HALO * item
            pairs.append((at + 4, to, HALO))
            pairs.append((at + 8, LANES + to, HALO))
    return doubled(matrix_of(pairs, 2 * LANES, 8 * LANES))


def strip_matrices():
    own, got = [], []
    for slot in range(LAYERS // 2):
        at = slot * SLOT
        own += [(at, at + 16, WIDE), (at + 8, at + 4, WIDE)]
        for item in range(8):
            to = item * LANES + at
            got.append((at + HALO * item, to, HALO))
            got.append((LANES + at + HALO * item, to + 24, HALO))
    return doubled(matrix_of(own, LANES)), doubled(matrix_of(got, 8 * LANES, 2 * LANES))


class ResponseStrip:
    def __init__(self, ref, rows):
        self.ref, self.start, self.rows = ref, BASE - PAD, rows
        self.lane = lane_of((rows, LANES))

    def load(self, j, by=0):
        return self.ref[j, self.start + by : self.start + by + self.rows, :]

    def store(self, j, value):
        self.ref[j, self.start : self.start + self.rows, :] = value

    def step_h(self, fresh):
        e = [self.load(j) for j in range(3)]
        inside = self.lane < (LAYERS - 1) * RESPONSE_SLOT
        e_z = [jnp.where(inside, rolled(e[j], -RESPONSE_SLOT), 0.0) for j in range(2)] + [None]
        e_x = [None, self.load(1, 1), self.load(2, 1)]
        e_y = [rolled(e[0], -1), None, rolled(e[2], -1)]
        for j, change in enumerate(curl_of_e(e, e_z, e_x, e_y)):
            self.store(3 + j, change if fresh else self.load(3 + j) + change)

    def step_e(self, factor):
        h = [self.load(3 + j) for j in range(3)]
        inside = self.lane >= RESPONSE_SLOT
        h_z = [jnp.where(inside, rolled(h[j], RESPONSE_SLOT), 0.0) for j in range(2)] + [None]
        h_x = [None, self.load(4, -1), self.load(5, -1)]
        h_y = [rolled(h[0], 1), None, rolled(h[2], 1)]
        change = curl_of_h(h, h_z, h_x, h_y)
        return [self.load(j) + factor * change[j] for j in range(3)]

    def all_edges(self, cells_x, matrix):
        values = [beside(self.ref[j, BASE : BASE + cells_x, :]) for j in range(6)]
        return dot32(jnp.concatenate(values, 0), matrix)


def with_edges(value, edges_ref, start, block, width):
    own = edges_ref[start : start + value.shape[0], block * LANES : (block + 1) * LANES]
    lane = lane_of(own.shape)
    outer = (lane < width) | (lane >= LANES - width)
    return jnp.where(outer, own, value)


SCALES = (1.0, 1.0, 1.0, 2.0, 2.0, 2.0, 0.5)
BY_PRODUCT = (0,)
EVERY = [(j, z) for j in range(6) for z in range(LAYERS)]
ALL_PLANES = EVERY[: 3 * LAYERS]


def blank_rims(ref):
    tall = ref.shape[2]
    for j in range(3):
        for z in range(LAYERS):
            ref[j, z, :PAD, :] = jnp.zeros((PAD, LANES), jnp.float32)
            ref[j, z, tall - PAD :, :] = jnp.zeros((PAD, LANES), jnp.float32)


class Inputs:
    def __init__(self, get):
        self.get = get


def first_kernel(
    e_ref, h_ref, m_ref, c_ref, e_out, h_out, token_ref, rim_ref, e_mid, h_mid
):
    cells_x = h_ref.shape[2]
    token_ref[...] = jnp.zeros_like(token_ref)
    row = lax.broadcasted_iota(jnp.int32, (8, LANES), 0)
    for j in range(7):
        for z in range(LAYERS):
            base = (j * LAYERS + z) * cells_x
            if j < 3:
                first, final = e_ref[base : base + 8, :], e_ref[base + cells_x - 8 : base + cells_x, :]
            else:
                ref = h_ref.at[j - 3, z] if j < 6 else m_ref.at[z]
                first, final = ref[:8, :], ref[cells_x - 8 :, :]
            if j == 6:
                first, final = coefficient_of(first), coefficient_of(final)
                c_ref[z] = coefficient_of(m_ref[z]) * 0.5
            rim_ref[j * LAYERS + z] = jnp.where(row < HALO, first, final)
    for ref in (e_out, h_out, e_mid, h_mid):
        blank_rims(ref)

    def get_e(j, z, start, size):
        if z >= LAYERS:
            return None
        base = (j * LAYERS + z) * cells_x + start - PAD
        if base + size <= e_ref.shape[0]:
            return e_ref[base : base + size, :]
        return pltpu.roll(e_ref[base - 1 : base - 1 + size, :], size - 1, 0)

    def get_h(j, z, start, size):
        return h_ref[j, z, start - PAD : start - PAD + size, :] * 2.0

    def factor(z, start, size):
        return c_ref[z, start - PAD : start - PAD + size, :]

    e, h = Inputs(get_e), Inputs(get_h)
    for new_e, new_h in ((e_mid, h_mid), (e_out, h_out)):
        to_e, to_h = Planes(new_e, ALL_PLANES), Planes(new_h, ALL_PLANES)
        step_h(e, h, to_h, PAD, cells_x, CHUNK)
        step_e(e, to_h, to_e.put, PAD, cells_x, factor, CHUNK)
        e, h = to_e, to_h


def first_steps(e_rows, h_field, material):
    cells_x = h_field.shape[2]
    f32 = jnp.float32
    planes = jax.ShapeDtypeStruct((3, LAYERS, cells_x + 2 * PAD, LANES), f32)
    return pl.pallas_call(
        first_kernel,
        out_shape=(
            jax.ShapeDtypeStruct((LAYERS, cells_x, LANES), f32),
            planes,
            planes,
            jax.ShapeDtypeStruct((8, LANES), f32),
            jax.ShapeDtypeStruct((7 * LAYERS, 2 * HALO, LANES), f32),
        ),
        scratch_shapes=[pltpu.VMEM(planes.shape, f32)] * 2,
        compiler_params=pltpu.CompilerParams(vmem_limit_bytes=VMEM_LIMIT),
        cost_estimate=lasting(2.7),
        name="first_steps",
    )(e_rows, h_field, material)


class Rows:
    def __init__(self, ref):
        self.ref = ref

    def load(self, j, by=0):
        return self.ref[j, :, 8 + by : 40 + by, :]

    def step(self, factor):
        zero = jnp.zeros((1, 32, LANES), jnp.float32)
        e = [self.load(j) for j in range(3)]
        e_z = [jnp.concatenate([e[j][1:], zero], 0) for j in range(2)] + [None]
        e_x = [None, self.load(1, 1), self.load(2, 1)]
        e_y = [pltpu.roll(e[0], LANES - 1, 2), None, pltpu.roll(e[2], LANES - 1, 2)]
        for j, change in enumerate(curl_of_e(e, e_z, e_x, e_y)):
            self.ref[3 + j, :, 8:40, :] = self.load(3 + j) + change
        h = [self.load(3 + j) for j in range(3)]
        h_z = [jnp.concatenate([zero, h[j][:-1]], 0) for j in range(2)] + [None]
        h_x = [None, self.load(4, -1), self.load(5, -1)]
        h_y = [pltpu.roll(h[0], 1, 2), None, pltpu.roll(h[2], 1, 2)]
        for j, change in enumerate(curl_of_h(h, h_z, h_x, h_y)):
            self.ref[j, :, 8:40, :] = e[j] + factor * change


def edge_rows(e_ref, h_ref, c_ref, x_ref, r_ref):
    cells_x = c_ref.shape[1]
    blank = jnp.zeros((LAYERS, PAD - HALO, LANES), jnp.float32)
    zero = jnp.zeros((LAYERS, 8, LANES), jnp.float32)
    for j in range(7):
        rims = x_ref[j * LAYERS : (j + 1) * LAYERS] * SCALES[j]
        if j < 3:
            bases = [(j * LAYERS + z) * cells_x for z in range(LAYERS)]
            first = jnp.stack([e_ref[b : b + 8, :] for b in bases])
            final = jnp.stack([e_ref[b + cells_x - 8 : b + cells_x, :] for b in bases])
        elif j < 6:
            first, final = h_ref[j - 3, :, :8, :] * 2.0, h_ref[j - 3, :, cells_x - 8 :, :] * 2.0
        else:
            first, final = c_ref[:, :8, :], c_ref[:, cells_x - 8 :, :]
        rows = [blank, rims[:, HALO:], first, final, rims[:, :HALO], blank]
        if j < 6:
            r_ref[j] = jnp.concatenate([zero] + rows + [zero], 1)
        else:
            factor = jnp.concatenate(rows, 1)
    edge = Rows(r_ref)
    for _ in range(STEPS):
        edge.step(factor)


def with_rows(value, r_ref, j, z):
    row = lax.broadcasted_iota(jnp.int32, (8, LANES), 0)
    top = jnp.where(row < HALO, r_ref[j, z, 16:24, :], value[:8])
    end = jnp.where(row >= HALO, r_ref[j, z, 24:32, :], value[-8:])
    return jnp.concatenate([top, value[8:-8], end], 0)


def later_kernel(e_in, h_in, c_ref, _, out_ref, token_ref, e_mid, h_mid, h_last):
    cells_x = c_ref.shape[1]
    token_ref[...] = jnp.zeros_like(token_ref)
    for ref in (e_mid, h_mid, h_last):
        blank_rims(ref)

    def finish(j, z, start, value):
        out_ref[j, z, start - PAD : start - PAD + value.shape[0], :] = value

    def factor(z, start, size):
        return c_ref[z, start - PAD : start - PAD + size, :]

    e, h = Planes(e_in, ALL_PLANES), Planes(h_in, ALL_PLANES)
    to_e, to_h = Planes(e_mid, ALL_PLANES), Planes(h_mid, ALL_PLANES)
    step_h(e, h, to_h, PAD, cells_x, CHUNK)
    step_e(e, to_h, to_e.put, PAD, cells_x, factor, CHUNK)
    last_h = Planes(h_last, ALL_PLANES)
    step_h(to_e, to_h, last_h, PAD, cells_x, CHUNK)
    step_e(to_e, last_h, finish, PAD, cells_x, factor, CHUNK)
    for j, z in ALL_PLANES:
        out_ref[3 + j, z] = h_last[j, z, PAD : PAD + cells_x, :]


def later_steps(e, h, coefficient, after):
    cells_x = coefficient.shape[1]
    f32 = jnp.float32
    return pl.pallas_call(
        later_kernel,
        out_shape=(
            jax.ShapeDtypeStruct((6, LAYERS, cells_x, LANES), f32),
            jax.ShapeDtypeStruct((8, LANES), f32),
        ),
        scratch_shapes=[pltpu.VMEM(e.shape, f32)] * 3,
        compiler_params=pltpu.CompilerParams(vmem_limit_bytes=VMEM_LIMIT),
        cost_estimate=lasting(2.7),
        name="later_steps",
    )(e, h, coefficient, after)


def strip_kernel(
    w_ref, low_ref, high_ref, free_ref, e_ref, h_ref, c_ref, x_ref, own_ref, got_ref, edge_ref,
    to_ref, _, factor_ref, out_ref, s_ref, edges_ref, r_ref,
):
    rows = w_ref.shape[2]
    first = BASE - PAD
    mine = [beside(w_ref[j, g]) for j in range(7) for g in range(2)]
    mine = dot32(jnp.concatenate(mine, 0), own_ref[...])
    got = [jnp.concatenate([beside(low_ref[a]), beside(high_ref[a])], 1) for a in range(2)]
    got = dot32(jnp.concatenate(got, 0), got_ref[...])
    factor = []
    for j in range(7):
        for g in range(2):
            i = 2 * j + g
            a, b = divmod(i, 8)
            value = mine[i * rows : (i + 1) * rows]
            value = value + got[a * rows : (a + 1) * rows, b * LANES : (b + 1) * LANES]
            if j < 6:
                s_ref[j, g, first : first + rows, :] = value
            else:
                factor.append(value)
    factor_ref[...] = dot32(jnp.concatenate([beside(f) for f in factor], 1), to_ref[...])
    strip = Strip(s_ref, rows)
    for step in range(STEPS):
        strip.step_h()
        new = strip.step_e(factor)
        for g in range(2):
            for j in range(3):
                strip.store(j, g, new[g][j])
    cells_x = out_ref.shape[2]
    edges_ref[...] = strip.all_edges(cells_x, edge_ref[...])
    edge_rows(e_ref, h_ref, c_ref, x_ref, r_ref)
    for j, z in EVERY:
        value = with_rows(free_ref[j, z], r_ref, j, z)
        value = with_edges(value, edges_ref, (2 * j + z % 2) * cells_x, z // 2, HALO)
        out_ref[j, z] = value if j < 3 else value * 0.5


def strip_run(own_edges, low, high, free, e_field, h_field, coefficient, x_rims, after):
    rows = own_edges.shape[2]
    f32 = jnp.float32
    return pl.pallas_call(
        strip_kernel,
        out_shape=(
            jax.ShapeDtypeStruct((rows, LANES), f32),
            jax.ShapeDtypeStruct(free.shape, f32),
        ),
        scratch_shapes=[
            pltpu.VMEM((6, 2, rows + 2 * (BASE - PAD), LANES), f32),
            pltpu.VMEM((12 * free.shape[2], LAYERS // 2 * LANES), f32),
            pltpu.VMEM((6, LAYERS, 48, LANES), f32),
        ],
        compiler_params=pltpu.CompilerParams(vmem_limit_bytes=VMEM_LIMIT),
        cost_estimate=lasting(4),
        name="strip_run",
    )(
        own_edges, low, high, free, e_field, h_field, coefficient, x_rims,
        *(jnp.asarray(m) for m in strip_matrices()),
        jnp.asarray(edge_matrix()), jnp.asarray(factor_matrix()), after,
    )


def response_kernel(
    c_ref, factor_ref, free_ref, mine_ref, other_ref, near_ref, outside_ref, edge_ref,
    e_out, h_out,
    e_refs, h_refs, s_ref, plane_ref, rim_ref, done_ref, edges_ref, sems,
):
    cells_x = e_out.shape[2]
    copies = []

    def send(j, z, source):
        to = e_out.at[j, z] if j < 3 else h_out.at[j - 3, z]
        copies.append(pltpu.make_async_copy(source, to, sems.at[j, z]))
        copies[-1].start()

    far = [(j, z) for j, z in EVERY if z >= ZINJ + STEPS - (0 if j < 2 else 1)]
    for j, z in far:
        send(j, z, free_ref.at[j, z])
    rows = cells_x + 2 * PAD
    half = rows // 2
    first = BASE - PAD
    own = lax.axis_index("src")
    lane = lane_of((half, LANES))
    for ref, which in ((mine_ref, own), (other_ref, 1 - own)):
        at = pl.ds(pl.multiple_of(which * half, 8), half)
        for part in range(2):
            plane_ref[part, at, :] = ref[part * half : (part + 1) * half, :]
        rim_ref[0, at, :] = jnp.where(lane < 16, unfolded(ref[2 * half :, :], half, 8, 0), 0.0)
    outer = dot32(beside(rim_ref[0]), outside_ref[...])
    planes = jnp.concatenate([beside(plane_ref[part]) for part in range(2)], 0)
    inner = dot32(planes, near_ref[...])
    for part in range(2):
        own_part = outer[:, part * LANES : (part + 1) * LANES]
        rim_ref[part] = inner[part * rows : (part + 1) * rows] + own_part

    def injection(ref, step, start, size):
        cosine = COURANT * math.cos(OMEGA * step)
        sine = COURANT * math.sin(OMEGA * step)
        re, im = ref[0, start : start + size, :], ref[1, start : start + size, :]
        return [cosine * re - sine * im, sine * re + cosine * im, None]

    e, h = Planes(e_refs.at[0]), Planes(h_refs.at[0])
    for j, value in enumerate(injection(plane_ref, 1, 0, rows)):
        e.put(j, ZINJ, first, value)
    strip = ResponseStrip(s_ref, rows)
    s_ref[...] = jnp.zeros_like(s_ref)
    for j, value in enumerate(injection(rim_ref, 1, 0, rows)[:2]):
        strip.store(j, value)
    for step in range(2, STEPS + 1):
        strip.step_h(step == 2)
        new = strip.step_e(factor_ref[...])
        for j, value in enumerate(injection(rim_ref, step, 0, rows)):
            strip.store(j, add(new[j], value))
    edges_ref[...] = strip.all_edges(cells_x, edge_ref[...])

    def factor(z, start, size):
        return c_ref[z, start : start + size, :]

    def finish(j, z, start, value):
        if (j, z) in far:
            return
        size, at = value.shape[0], start - BASE
        if j < 3 and z == ZINJ:
            value = add(value, injection(plane_ref, STEPS, start - first, size)[j])
        value = with_edges(value, edges_ref, j * cells_x + at, z, REACHED)
        value = (value if j < 3 else value * 0.5) + free_ref[j, z, at : at + size, :]
        done_ref[j, z, at : at + size, :] = value
        if at + size == cells_x:
            send(j, z, done_ref.at[j, z])

    for step in range(2, STEPS + 1):
        last = step == STEPS
        new_h = Planes(h_refs.at[step - 1])
        step_h(e, h, new_h, first, rows - (PAD if last else 0), RESPONSE_CHUNK)
        if last:
            for j, z in ALL_PLANES:
                for at, size in chunks(BASE, cells_x, RESPONSE_CHUNK):
                    value = new_h.get(j, z, at, size)
                    if value is not None:
                        finish(3 + j, z, at, value)
            step_e(e, new_h, finish, BASE, cells_x, factor, cells_x)
            break
        new_e = Planes(e_refs.at[step - 1])

        def put(j, z, start, value):
            if z == ZINJ:
                size = value.shape[0]
                value = add(value, injection(plane_ref, step, start - first, size)[j])
            new_e.put(j, z, start, value)

        step_e(e, new_h, put, first, rows, factor, RESPONSE_CHUNK)
        e, h = new_e, new_h
    for copy in copies:
        copy.wait()


def response(c_ext, factor, free, mine, other, cells_x):
    rows = cells_x + 2 * PAD
    tall = cells_x + 2 * BASE
    f32 = jnp.float32
    out = jax.ShapeDtypeStruct((3, LAYERS, cells_x, LANES), f32)
    vmem = pl.BlockSpec(memory_space=pltpu.VMEM)
    return pl.pallas_call(
        response_kernel,
        in_specs=[vmem] * 8,
        out_specs=(pl.BlockSpec(memory_space=pl.ANY),) * 2,
        out_shape=(out, out),
        scratch_shapes=[
            pltpu.VMEM((STEPS - 1, 3, LAYERS, tall, LANES), f32),
            pltpu.VMEM((STEPS, 3, LAYERS, tall, LANES), f32),
            pltpu.VMEM((6, tall, LANES), f32),
            pltpu.VMEM((2, rows, LANES), f32),
            pltpu.VMEM((2, rows, LANES), f32),
            pltpu.VMEM((6, LAYERS, cells_x, LANES), f32),
            pltpu.VMEM((6 * cells_x, min(LAYERS, ZINJ + STEPS) * LANES), f32),
            pltpu.SemaphoreType.DMA((6, LAYERS)),
        ],
        compiler_params=pltpu.CompilerParams(vmem_limit_bytes=RESPONSE_LIMIT),
        cost_estimate=lasting(6.5),
        name="response",
    )(
        c_ext, factor, free, mine, other,
        jnp.asarray(near_matrix()), jnp.asarray(outside_matrix()),
        jnp.asarray(response_edge_matrix()),
    )


def along(block, axis, distance):
    n = lax.axis_size(axis)
    return lax.ppermute(block, axis, [((i - distance) % n, i) for i in range(n)])


def flipped(block, axis, bits):
    return lax.ppermute(block, axis, [(i, i ^ bits) for i in range(lax.axis_size(axis))])


def to_groups(block, n_src, n_tx, flip, distance):
    route = []
    for s in range(n_src):
        for t in range(n_tx):
            route.append((s * n_tx + t, (s ^ flip) * n_tx + (t + distance) % n_tx))
    return lax.ppermute(block, ("src", "tx"), route)


def per_device(orders, offsets, material, e_field, h_field):
    cols_ky = orders.shape[3]
    layers, cells_x, cells_y = material.shape
    n_src, n_tx, n_ty = lax.axis_size("src"), lax.axis_size("tx"), lax.axis_size("ty")
    half = cells_x // 2 + PAD
    e_field = e_field.reshape(-1, cells_y)
    parts = x_stage(
        offsets.T, jnp.swapaxes(orders, 2, 3), n_tx, cells_x, (e_field, h_field, material)
    )
    received = [parts[0]]
    for distance in range(n_tx):
        for flip in range(n_src):
            if distance or flip:
                part = parts[2 * distance + flip]
                received.append(to_groups(part, n_src, n_tx, flip, distance))
    coefficient, e_half, h_half, begun, rims = first_steps(e_field, h_field, material)

    if n_tx == 2:
        x_rims = along(rims, "tx", 1)
    else:
        top, bottom = rims[:, :HALO], rims[:, HALO:]
        x_rims = jnp.concatenate([along(top, "tx", -1), along(bottom, "tx", 1)], 1)
    block = summed(received, begun)
    c_ext, own_edges, to_high, to_low = pack(e_field, h_field, coefficient, x_rims)
    low = along(to_high, "ty", 1)
    high = along(to_low, "ty", -1)
    free, run = later_steps(e_half, h_half, coefficient, to_high)

    blocks = {0: block}
    for bits in range(n_ty - 2, 0, -2):
        blocks[bits] = flipped(block, "ty", bits)
    for bits in range(0, n_ty, 2):
        blocks[bits + 1] = flipped(blocks[bits], "ty", 1)
    mine = y_stage([blocks[b] for b in range(n_ty)], cols_ky, cells_y, half, run)
    other = flipped(mine, "src", 1)
    factor, free = strip_run(
        own_edges, low, high, free, e_field, h_field, coefficient, x_rims, mine
    )
    return response(c_ext, factor, free, mine, other, cells_x)


def solution(mesh):
    in_specs = (
        P("src", None, "tx", "ty"),
        P("src", None),
        P(None, "tx", "ty"),
        P(None, None, "tx", "ty"),
        P(None, None, "tx", "ty"),
    )
    out_specs = (P(None, None, "tx", "ty"), P(None, None, "tx", "ty"))
    return jax.shard_map(
        per_device, mesh=mesh, in_specs=in_specs, out_specs=out_specs, check_vma=False
    )
```

```python
import functools
import math

import jax
import jax.numpy as jnp
import ml_dtypes
import numpy as np
from jax import lax
from jax.experimental import pallas as pl
from jax.experimental.pallas import tpu as pltpu
from jax.sharding import PartitionSpec as P

MX = 512
MY = 512
STEPS = 4
ZINJ = 1
LAYERS = 6

COURANT = 0.5
OMEGA = 0.7
PERMITTIVITY = (1.0, 2.6, 11.9, 2.1)

REACH = 8
SPAN = 2 * REACH
PAD = 8
HALO = 4
CHUNK = 8
RESPONSE_CHUNK = 64
BASE = 16
SLOT = 32
WIDE = 8
REACHED = STEPS - 1
RESPONSE_SLOT = 21
HIGH_SIDE = 10
LANES = 128
VMEM_LIMIT = 24 * 1024 * 1024
RESPONSE_LIMIT = 40 * 1024 * 1024
X_LIMIT = 60_700_000


def split_bf16(table):
    high = table.astype(ml_dtypes.bfloat16)
    low = (table - high.astype(np.float64)).astype(ml_dtypes.bfloat16)
    return high, low


def padded(lanes):
    return -(-lanes // LANES) * LANES


@functools.lru_cache(maxsize=None)
def x_seeds(n_tx, rows_kx, cells_x):
    window = rows_kx + SPAN
    wide = padded(window)
    full = cells_x * n_tx
    turns = [8 << k for k in range((cells_x // 8).bit_length())]
    count = 8 + len(turns) + n_tx
    table = np.zeros((n_tx, -(-count // 8) * 8, 2 * wide), np.float32)
    for own in range(n_tx):
        freq = own * rows_kx - MX // 2 - REACH + np.arange(window)
        tiles = [(own + distance) % n_tx * cells_x for distance in range(n_tx)]
        x = np.array(list(range(-PAD, 8 - PAD)) + turns + tiles)
        angle = np.mod(x[:, None] * freq[None, :], full) * (2.0 * math.pi / full)
        table[own, :count, :window] = np.cos(angle)
        table[own, :count, wide : wide + window] = np.sin(angle)
    return table, len(turns)


@functools.lru_cache(maxsize=None)
def y_tables(n_ty, cols_ky, cells_y):
    full = cells_y * n_ty
    window = cols_ky + SPAN
    edge = np.concatenate([np.arange(-HALO, 0), cells_y + np.arange(HALO)])
    y = np.concatenate([np.arange(cells_y), edge])
    table = np.zeros((n_ty, LANES + 2 * SPAN, 2 * cells_y + LANES))
    for block in range(n_ty):
        freq = block * cols_ky - MY // 2 - REACH + np.arange(window)
        angle = np.mod(freq[:, None] * y[None, :], full) * (2.0 * math.pi / full)
        cos, sin = np.cos(angle), np.sin(angle)

        def placed(re_cols, im_cols):
            out = np.zeros((window, 2 * cells_y + LANES))
            out[:, :cells_y] = re_cols[:, :cells_y]
            out[:, cells_y : 2 * cells_y] = im_cols[:, :cells_y]
            out[:, 2 * cells_y : 2 * cells_y + 2 * HALO] = re_cols[:, cells_y:]
            out[:, 2 * cells_y + 2 * HALO : 2 * cells_y + 4 * HALO] = im_cols[:, cells_y:]
            return out

        from_re = placed(cos, sin)
        from_im = placed(-sin, cos)
        table[block, :cols_ky] = from_re[:cols_ky]
        table[block, cols_ky : 2 * cols_ky] = from_im[:cols_ky]
        table[block, LANES : LANES + SPAN] = from_re[cols_ky:]
        table[block, LANES + SPAN :] = from_im[cols_ky:]
    return split_bf16(table)


@functools.lru_cache(maxsize=None)
def y_phases(n_ty, cols_ky, cells_y):
    full = cells_y * n_ty
    out = np.zeros((n_ty, n_ty, 8, LANES), np.float32)
    for own in range(n_ty):
        for block in range(n_ty):
            freq = block * cols_ky - MY // 2 - REACH + np.arange(cols_ky + SPAN)
            angle = np.mod(freq * own * cells_y, full) * (2.0 * math.pi / full)
            cos, sin = np.cos(angle), np.sin(angle)
            out[own, block, 0, :cols_ky] = cos[:cols_ky]
            out[own, block, 0, cols_ky : 2 * cols_ky] = cos[:cols_ky]
            out[own, block, 1, :cols_ky] = -sin[:cols_ky]
            out[own, block, 1, cols_ky : 2 * cols_ky] = sin[:cols_ky]
            for group in range(LANES // (2 * SPAN)):
                at = group * 2 * SPAN
                out[own, block, 2, at : at + SPAN] = cos[cols_ky:]
                out[own, block, 2, at + SPAN : at + 2 * SPAN] = cos[cols_ky:]
                out[own, block, 3, at : at + SPAN] = -sin[cols_ky:]
                out[own, block, 3, at + SPAN : at + 2 * SPAN] = sin[cols_ky:]
    return out


def lasting(microseconds):
    moved = int(microseconds * 3.69e6)
    return pl.CostEstimate(flops=0, transcendentals=0, bytes_accessed=moved)


def lane_of(shape):
    return lax.broadcasted_iota(jnp.int32, shape, len(shape) - 1)


def rolled(value, shift):
    shift = shift % LANES
    return value if shift == 0 else pltpu.roll(value, shift, 1)


def halves(value):
    high = value.astype(jnp.bfloat16)
    low = (value - high.astype(jnp.float32)).astype(jnp.bfloat16)
    return high, low


def dot32(a, b):
    return jnp.dot(a, b, preferred_element_type=jnp.float32)


def fold_groups(rows, count):
    tiles = rows // 8
    sizes = [8 * (tiles // count + (1 if g < tiles % count else 0)) for g in range(count)]
    starts = [sum(sizes[:g]) for g in range(count)]
    return list(zip(starts, sizes))


def folded_rows(rows, count):
    return fold_groups(rows, count)[0][1]


def folded(value, count):
    groups = fold_groups(value.shape[0], count)
    tall, wide = groups[0][1], LANES // count
    lane = lane_of((tall, LANES))
    total = jnp.zeros((tall, LANES), value.dtype)
    for g, (start, size) in enumerate(groups):
        part = value[start : start + size]
        if size < tall:
            part = jnp.concatenate([part, jnp.zeros((tall - size, LANES), value.dtype)], 0)
        keep = (lane >= wide * g) & (lane < wide * (g + 1))
        total = jnp.where(keep, rolled(part, wide * g), total)
    return total


def unfolded(value, rows, count, at):
    wide = LANES // count
    parts = []
    for g, (_, size) in enumerate(fold_groups(rows, count)):
        parts.append(rolled(value[:size], at - wide * g))
    return jnp.concatenate(parts, 0)


def turned(cos, sin, by_cos, by_sin):
    return cos * by_cos - sin * by_sin, sin * by_cos + cos * by_sin


def fill_table(n_turns, seed_ref, table_ref):
    _, n_tx, rows, both = table_ref.shape
    wide = both // 2

    def row(i):
        return seed_ref[i : i + 1, :wide], seed_ref[i : i + 1, wide:]

    cos, sin = seed_ref[:8, :wide], seed_ref[:8, wide:]
    for k in range(n_turns):
        more = min(8 << k, rows - (8 << k))
        new = turned(cos[:more], sin[:more], *row(8 + k))
        cos, sin = jnp.concatenate([cos, new[0]], 0), jnp.concatenate([sin, new[1]], 0)
    for distance in range(n_tx):
        there = turned(cos, sin, *row(8 + n_turns + distance))
        for part in range(2):
            high, low = halves(there[part])
            table_ref[0, distance, :, part * wide : (part + 1) * wide] = high
            table_ref[1, distance, :, part * wide : (part + 1) * wide] = low


def x_kernel(
    n_turns, offs_in, orders_in, seeds_in, _e, _h, _m, *refs
):
    *out_refs, offs_ref, orders_ref, seed_ref, table_ref, line_ref, acc_ref, q_ref, sems = refs
    own = lax.axis_index("src")
    copies = [
        pltpu.make_async_copy(seeds_in.at[lax.axis_index("tx")], seed_ref, sems.at[0]),
        pltpu.make_async_copy(orders_in, orders_ref, sems.at[1]),
        pltpu.make_async_copy(offs_in, offs_ref, sems.at[2]),
    ]
    for copy in copies:
        copy.start()
    points, _, cols_ky, rows_kx = orders_ref.shape
    _, n_tx, rows, both = table_ref.shape
    half = rows // 2
    acc_ref[...] = jnp.zeros_like(acc_ref)
    line_ref[...] = jnp.zeros_like(line_ref)
    wide = line_ref.shape[4]
    copies[0].wait()
    fill_table(n_turns, seed_ref, table_ref)
    copies[1].wait()
    copies[2].wait()
    for point in range(points):
        down = offs_ref[0, point] + REACH
        across = offs_ref[1, point] + REACH
        for part in range(2):
            for tile in range(rows_kx // wide):
                lanes = slice(tile * wide, (tile + 1) * wide)
                line = line_ref.at[point, part, tile]
                line[pl.ds(across, cols_ky), :] = orders_ref[point, part, :, lanes]
                acc_ref[part, pl.ds(down + tile * wide, wide), :] += line[...].T
    s_re = acc_ref[0]
    s_im = acc_ref[1]
    lane = lane_of(s_re.shape)
    re_by, im_by = rolled(s_re, cols_ky), rolled(s_im, cols_ky)

    def main(re, im_by):
        out = jnp.where(lane < cols_ky, re, im_by)
        return out if 2 * cols_ky == LANES else jnp.where(lane < 2 * cols_ky, out, 0.0)

    def spill(re_back, im_back):
        out = jnp.where(lane < SPAN, re_back, im_back)
        return jnp.where(lane < 2 * SPAN, out, 0.0)

    same = 2 * cols_ky == LANES
    re_back = re_by if same else rolled(s_re, -cols_ky)
    im_back = im_by if same else rolled(s_im, -cols_ky)
    top = [main(s_re, im_by), spill(re_back, rolled(s_im, SPAN - cols_ky))]
    bottom = [main(-s_im, re_by), spill(-im_back, rolled(s_re, SPAN - cols_ky))]
    right = jnp.concatenate([jnp.concatenate(top, 1), jnp.concatenate(bottom, 1)], 0)
    right_h, right_l = halves(right)
    tall = n_tx * rows
    by_high = dot32(table_ref[...].reshape(2 * tall, both), right_h)
    by_low = dot32(table_ref[0].reshape(tall, both), right_l)
    q_ref[...] = by_high[:tall] + (by_high[tall:] + by_low)
    for distance in range(n_tx):
        for flip in range(2):
            start = pl.multiple_of(distance * rows + (own ^ flip) * half, 8)
            block = q_ref[pl.ds(start, half), :]
            out_refs[2 * distance + flip][:half, :] = block[:, :LANES]
            out_refs[2 * distance + flip][half:, :] = folded(block[:, LANES:], 4)


def x_stage(offsets, orders, n_tx, cells_x, beside):
    points, _, cols_ky, rows_kx = orders.shape
    wide = min(rows_kx, LANES)
    seeds, n_turns = x_seeds(n_tx, rows_kx, cells_x)
    rows = cells_x + 2 * PAD
    half = rows // 2
    height = half + folded_rows(half, 4)
    f32 = jnp.float32
    return pl.pallas_call(
        functools.partial(x_kernel, n_turns),
        in_specs=[pl.BlockSpec(memory_space=pltpu.HBM)] * 6,
        out_shape=(jax.ShapeDtypeStruct((height, LANES), f32),) * (2 * n_tx),
        scratch_shapes=[
            pltpu.SMEM(offsets.shape, jnp.int32),
            pltpu.VMEM(orders.shape, f32),
            pltpu.VMEM(seeds.shape[1:], f32),
            pltpu.VMEM((2, n_tx, rows, seeds.shape[2]), jnp.bfloat16),
            pltpu.VMEM((points, 2, rows_kx // wide, LANES, wide), f32),
            pltpu.VMEM((2, seeds.shape[2] // 2, LANES), f32),
            pltpu.VMEM((n_tx * rows, 2 * LANES), f32),
            pltpu.SemaphoreType.DMA((3,)),
        ],
        compiler_params=pltpu.CompilerParams(vmem_limit_bytes=X_LIMIT),
        cost_estimate=lasting(3.5),
        name="x_stage",
    )(offsets, orders, jnp.asarray(seeds), *beside)


def sum_kernel(*refs):
    *part_refs, _, out_ref = refs
    total = part_refs[0][...]
    for ref in part_refs[1:]:
        total = total + ref[...]
    out_ref[...] = total


def summed(parts, after):
    return pl.pallas_call(
        sum_kernel,
        out_shape=jax.ShapeDtypeStruct(parts[0].shape, jnp.float32),
        compiler_params=pltpu.CompilerParams(vmem_limit_bytes=VMEM_LIMIT),
        cost_estimate=lasting(0.4),
        name="sum_parts",
    )(*parts, after)


def y_kernel(cols_ky, half, *refs):
    *block_refs, th_ref, tl_ref, phase_ref, _, out_ref = refs
    n_ty = len(block_refs)
    lane = lane_of((half, LANES))
    mains, spills, numbers = [], [], []
    own = lax.axis_index("ty")
    for number, ref in enumerate(block_refs):
        block = own ^ number
        numbers.append(block)
        phase = phase_ref[own, block]
        main = ref[:half, :]
        if 2 * cols_ky == LANES:
            swapped = rolled(main, cols_ky)
        else:
            swapped = jnp.where(lane < cols_ky, rolled(main, -cols_ky), rolled(main, cols_ky))
        mains.append(main * phase[0:1] + swapped * phase[1:2])
        spill = ref[half:, :]
        small = lane_of(spill.shape)
        other = jnp.where((small & (2 * SPAN - 1)) < SPAN, rolled(spill, -SPAN), rolled(spill, SPAN))
        spills.append(spill * phase[2:3] + other * phase[3:4])
    packed = []
    for first in range(0, n_ty, 4):
        total = None
        for g in range(4):
            part = unfolded(spills[first + g], half, 4, 32 * g)
            total = part if total is None else jnp.where(lane >= 32 * g, part, total)
        packed.append(total)
    left = jnp.concatenate(mains + packed, 1)
    high = left.astype(jnp.bfloat16)
    low = left - high.astype(jnp.float32)
    both = jnp.concatenate([left, low], 0).astype(jnp.bfloat16)

    def table(ref):
        parts = [ref[block, :LANES, :] for block in numbers]
        return jnp.concatenate(parts + [ref[block, LANES:, :] for block in numbers], 0)

    by_high = dot32(both, table(th_ref))
    result = by_high[:half] + (by_high[half:] + dot32(high, table(tl_ref)))
    out_ref[:half, :] = result[:, :LANES]
    out_ref[half : 2 * half, :] = result[:, LANES : 2 * LANES]
    out_ref[2 * half :, :] = folded(result[:, 2 * LANES :], 8)


def y_stage(blocks, cols_ky, cells_y, half, after):
    n_ty = len(blocks)
    t_h, t_l = y_tables(n_ty, cols_ky, cells_y)
    phases = y_phases(n_ty, cols_ky, cells_y)
    height = 2 * half + folded_rows(half, 8)
    return pl.pallas_call(
        functools.partial(y_kernel, cols_ky, half),
        out_shape=jax.ShapeDtypeStruct((height, LANES), jnp.float32),
        compiler_params=pltpu.CompilerParams(vmem_limit_bytes=VMEM_LIMIT),
        cost_estimate=lasting(1.5),
        name="y_stage",
    )(*blocks, jnp.asarray(t_h), jnp.asarray(t_l), jnp.asarray(phases), after)


def coefficient_of(material):
    value = jnp.where(material == 0, COURANT / PERMITTIVITY[0], COURANT / PERMITTIVITY[1])
    value = jnp.where(material == 2, COURANT / PERMITTIVITY[2], value)
    return jnp.where(material == 3, COURANT / PERMITTIVITY[3], value).astype(jnp.float32)


def pack_kernel(
    e_ref, h_ref, c_ref, x_ref, column_ref, message_ref, ext_ref, w_ref, low_ref, high_ref
):
    cells_x = h_ref.shape[2]
    end = BASE + cells_x
    rows = cells_x + 2 * PAD
    lane = lane_of((rows, LANES))
    by_product = []
    blank = jnp.zeros((PAD - HALO, LANES), jnp.float32)
    for j in range(7):
        scale = SCALES[j]
        strips = [jnp.zeros((rows, LANES), jnp.float32)] * 2
        planes = [[], []]
        for z in range(LAYERS):
            if j < 3:
                body = e_ref[pl.ds((j * LAYERS + z) * cells_x, cells_x), :]
            elif j < 6:
                body = h_ref[j - 3, z] * scale
            else:
                body = c_ref[z]
            rims = x_ref[j * LAYERS + z]
            rims = rims if scale == 1 else rims * scale
            full = jnp.concatenate([blank, rims[HALO:], body, rims[:HALO], blank], 0)
            if j == 6:
                ext_ref[z, 0 : BASE - PAD, :] = jnp.zeros((BASE - PAD, LANES), jnp.float32)
                ext_ref[z, BASE - PAD : end + PAD, :] = full
                ext_ref[z, end + PAD : end + BASE, :] = jnp.zeros((BASE - PAD, LANES), jnp.float32)
            g, at = z % 2, (z // 2) * SLOT
            if j in BY_PRODUCT:
                planes[g].append(beside(full))
                continue
            keep = (lane >= at) & (lane < at + 2 * WIDE)
            strips[g] = jnp.where(keep, rolled(full, at + WIDE), strips[g])
        for g in range(2):
            if j in BY_PRODUCT:
                by_product.append(jnp.concatenate(planes[g], 1))
            else:
                w_ref[j, g] = strips[g]
    taken = dot32(jnp.concatenate(by_product, 0), column_ref[...])
    for i, (j, g) in enumerate((j, g) for j in BY_PRODUCT for g in range(2)):
        w_ref[j, g] = taken[i * rows : (i + 1) * rows]
    items = [beside(w_ref[j, g]) for j in range(7) for g in range(2)]
    items += [jnp.zeros_like(items[0])] * (16 - len(items))
    sides = [jnp.concatenate(items[8 * a : 8 * a + 8], 1) for a in range(2)]
    sent = dot32(jnp.concatenate(sides, 0), message_ref[...])
    for a in range(2):
        low_ref[a] = sent[a * rows : (a + 1) * rows, :LANES]
        high_ref[a] = sent[a * rows : (a + 1) * rows, LANES:]


def pack(e_field, h_field, coefficient, x_rims):
    cells_x = h_field.shape[2]
    rows = cells_x + 2 * PAD
    tall = cells_x + 2 * BASE
    f32 = jnp.float32
    return pl.pallas_call(
        pack_kernel,
        out_shape=(
            jax.ShapeDtypeStruct((LAYERS, tall, LANES), f32),
            jax.ShapeDtypeStruct((7, 2, rows, LANES), f32),
            jax.ShapeDtypeStruct((2, rows, LANES), f32),
            jax.ShapeDtypeStruct((2, rows, LANES), f32),
        ),
        compiler_params=pltpu.CompilerParams(vmem_limit_bytes=VMEM_LIMIT),
        cost_estimate=lasting(2.2),
        name="pack",
    )(
        e_field, h_field, coefficient, x_rims,
        jnp.asarray(column_matrix()),
        jnp.asarray(message_matrix()),
    )


def total(terms):
    out = None
    for sign, value in terms:
        if value is None:
            continue
        if out is None:
            out = value if sign > 0 else -value
        else:
            out = out + value if sign > 0 else out - value
    return out


def add(a, b):
    return total([(1, a), (1, b)])


def differ(a, b):
    return total([(1, a), (-1, b)])


def curl_of_e(e, e_z, e_x, e_y):
    return (
        differ(differ(e_z[1], e[1]), differ(e_y[2], e[2])),
        differ(differ(e_x[2], e[2]), differ(e_z[0], e[0])),
        differ(differ(e_y[0], e[0]), differ(e_x[1], e[1])),
    )


def curl_of_h(h, h_z, h_x, h_y):
    return (
        differ(differ(h[2], h_y[2]), differ(h[1], h_z[1])),
        differ(differ(h[0], h_z[0]), differ(h[2], h_x[2])),
        differ(differ(h[1], h_x[1]), differ(h[0], h_y[0])),
    )


def moved(value, shift):
    return None if value is None else rolled(value, shift)


class Planes:
    def __init__(self, ref, live=()):
        self.ref, self.live = ref, set(live)

    def get(self, j, z, start, size):
        return self.ref[j, z, start : start + size, :] if (j, z) in self.live else None

    def put(self, j, z, start, value):
        if value is not None:
            self.ref[j, z, start : start + value.shape[0], :] = value
            self.live.add((j, z))


def chunks(start, size, height):
    return [(at, min(height, start + size - at)) for at in range(start, start + size, height)]


def step_h(e, h, to, start, size, height):
    for at, rows in chunks(start, size, height):
        above = [e.get(j, 0, at, rows) for j in range(3)]
        for z in range(LAYERS):
            own, above = above, [e.get(j, z + 1, at, rows) for j in range(3)]
            e_x = [None] + [e.get(j, z, at + 1, rows) for j in (1, 2)]
            e_y = [moved(own[0], -1), None, moved(own[2], -1)]
            for j, change in enumerate(curl_of_e(own, above[:2] + [None], e_x, e_y)):
                to.put(j, z, at, add(h.get(j, z, at, rows), change))


def step_e(e, h, put, start, size, factor_of, height):
    for at, rows in chunks(start, size, height):
        own = [None] * 3
        for z in range(LAYERS):
            below, own = own, [h.get(j, z, at, rows) for j in range(3)]
            h_x = [None] + [h.get(j, z, at - 1, rows) for j in (1, 2)]
            h_y = [moved(own[0], 1), None, moved(own[2], 1)]
            factor = factor_of(z, at, rows)
            for j, change in enumerate(curl_of_h(own, below[:2] + [None], h_x, h_y)):
                value = e.get(j, z, at, rows)
                put(j, z, at, value if change is None else add(value, factor * change))


class Strip:
    def __init__(self, ref, rows):
        self.ref, self.start, self.rows = ref, BASE - PAD, rows
        self.lane = lane_of((rows, LANES))

    def load(self, j, g, by=0):
        return self.ref[j, g, self.start + by : self.start + by + self.rows, :]

    def store(self, j, g, value):
        self.ref[j, g, self.start : self.start + self.rows, :] = value

    def step_h(self, fresh=False):
        e = [[self.load(j, g) for j in range(3)] for g in range(2)]
        inside = self.lane < 2 * SLOT
        above = [
            [e[1][0], e[1][1], None],
            [jnp.where(inside, rolled(e[0][j], -SLOT), 0.0) for j in range(2)] + [None],
        ]
        for g in range(2):
            e_x = [None, self.load(1, g, 1), self.load(2, g, 1)]
            e_y = [rolled(e[g][0], -1), None, rolled(e[g][2], -1)]
            for j, change in enumerate(curl_of_e(e[g], above[g], e_x, e_y)):
                self.store(3 + j, g, change if fresh else self.load(3 + j, g) + change)

    def step_e(self, factor):
        h = [[self.load(3 + j, g) for j in range(3)] for g in range(2)]
        inside = self.lane >= SLOT
        below = [
            [jnp.where(inside, rolled(h[1][j], SLOT), 0.0) for j in range(2)] + [None],
            [h[0][0], h[0][1], None],
        ]
        new = []
        for g in range(2):
            h_x = [None, self.load(4, g, -1), self.load(5, g, -1)]
            h_y = [rolled(h[g][0], 1), None, rolled(h[g][2], 1)]
            change = curl_of_h(h[g], below[g], h_x, h_y)
            new.append([self.load(j, g) + factor[g] * change[j] for j in range(3)])
        return new

    def all_edges(self, cells_x, matrix):
        values = [
            beside(self.ref[j, g, BASE : BASE + cells_x, :]) for j in range(6) for g in range(2)
        ]
        return dot32(jnp.concatenate(values, 0), matrix)


def beside(value):
    return jnp.concatenate(halves(value), 1)


def matrix_of(pairs, columns, rows=LANES):
    out = np.zeros((rows, columns), ml_dtypes.bfloat16)
    for first_row, first_column, count in pairs:
        for i in range(count):
            out[first_row + i, first_column + i] = 1
    return out


def doubled(matrix):
    blocks = matrix.reshape(-1, LANES, matrix.shape[1])
    return np.concatenate([m for block in blocks for m in (block, block)], 0)


def near_matrix():
    own, at = 2 * REACHED, ZINJ * RESPONSE_SLOT
    pairs = [(0, at + REACHED, own), (LANES - own, at + HIGH_SIDE, own)]
    return doubled(matrix_of(pairs, LANES))


def outside_matrix():
    pairs = []
    for part in range(2):
        lane, at = part * 2 * HALO, part * LANES + ZINJ * RESPONSE_SLOT
        pairs.append((lane + HALO - REACHED, at, REACHED))
        pairs.append((lane + HALO, at + HIGH_SIDE + 2 * REACHED, REACHED))
    return doubled(matrix_of(pairs, 2 * LANES))


def response_edge_matrix():
    pairs = []
    for z in range(min(LAYERS, ZINJ + STEPS)):
        at = z * RESPONSE_SLOT + REACHED
        pairs.append((at, z * LANES, REACHED))
        pairs.append((at + HIGH_SIDE, (z + 1) * LANES - REACHED, REACHED))
    return doubled(matrix_of(pairs, min(LAYERS, ZINJ + STEPS) * LANES))


def factor_matrix():
    pairs = []
    for z in range(LAYERS):
        at, to = z % 2 * LANES + z // 2 * SLOT, z * RESPONSE_SLOT
        pairs.append((at + HALO - REACHED, to, 3 * REACHED))
        pairs.append((at + 16 + WIDE - 2 * REACHED, to + HIGH_SIDE, 3 * REACHED))
    return doubled(matrix_of(pairs, LANES, 2 * LANES))


def edge_matrix():
    pairs = []
    for slot in range(LAYERS // 2):
        pairs.append((slot * SLOT + 4, slot * LANES, HALO))
        pairs.append((slot * SLOT + 20, slot * LANES + LANES - HALO, HALO))
    return doubled(matrix_of(pairs, LAYERS // 2 * LANES))


def column_matrix():
    pairs = []
    for slot in range(LAYERS // 2):
        pairs.append((slot * LANES + LANES - WIDE, slot * SLOT, WIDE))
        pairs.append((slot * LANES, slot * SLOT + WIDE, WIDE))
    return doubled(matrix_of(pairs, LANES, LAYERS // 2 * LANES))


def message_matrix():
    pairs = []
    for item in range(8):
        for slot in range(LAYERS // 2):
            at, to = item * LANES + slot * SLOT, slot * SLOT + HALO * item
            pairs.append((at + 4, to, HALO))
            pairs.append((at + 8, LANES + to, HALO))
    return doubled(matrix_of(pairs, 2 * LANES, 8 * LANES))


def strip_matrices():
    own, got = [], []
    for slot in range(LAYERS // 2):
        at = slot * SLOT
        own += [(at, at + 16, WIDE), (at + 8, at + 4, WIDE)]
        for item in range(8):
            to = item * LANES + at
            got.append((at + HALO * item, to, HALO))
            got.append((LANES + at + HALO * item, to + 24, HALO))
    return doubled(matrix_of(own, LANES)), doubled(matrix_of(got, 8 * LANES, 2 * LANES))


class ResponseStrip:
    def __init__(self, ref, rows):
        self.ref, self.start, self.rows = ref, BASE - PAD, rows
        self.lane = lane_of((rows, LANES))

    def load(self, j, by=0):
        return self.ref[j, self.start + by : self.start + by + self.rows, :]

    def store(self, j, value):
        self.ref[j, self.start : self.start + self.rows, :] = value

    def step_h(self, fresh):
        e = [self.load(j) for j in range(3)]
        inside = self.lane < (LAYERS - 1) * RESPONSE_SLOT
        e_z = [jnp.where(inside, rolled(e[j], -RESPONSE_SLOT), 0.0) for j in range(2)] + [None]
        e_x = [None, self.load(1, 1), self.load(2, 1)]
        e_y = [rolled(e[0], -1), None, rolled(e[2], -1)]
        for j, change in enumerate(curl_of_e(e, e_z, e_x, e_y)):
            self.store(3 + j, change if fresh else self.load(3 + j) + change)

    def step_e(self, factor):
        h = [self.load(3 + j) for j in range(3)]
        inside = self.lane >= RESPONSE_SLOT
        h_z = [jnp.where(inside, rolled(h[j], RESPONSE_SLOT), 0.0) for j in range(2)] + [None]
        h_x = [None, self.load(4, -1), self.load(5, -1)]
        h_y = [rolled(h[0], 1), None, rolled(h[2], 1)]
        change = curl_of_h(h, h_z, h_x, h_y)
        return [self.load(j) + factor * change[j] for j in range(3)]

    def all_edges(self, cells_x, matrix):
        values = [beside(self.ref[j, BASE : BASE + cells_x, :]) for j in range(6)]
        return dot32(jnp.concatenate(values, 0), matrix)


def with_edges(value, edges_ref, start, block, width):
    own = edges_ref[start : start + value.shape[0], block * LANES : (block + 1) * LANES]
    lane = lane_of(own.shape)
    outer = (lane < width) | (lane >= LANES - width)
    return jnp.where(outer, own, value)


SCALES = (1.0, 1.0, 1.0, 2.0, 2.0, 2.0, 0.5)
BY_PRODUCT = (0,)
EVERY = [(j, z) for j in range(6) for z in range(LAYERS)]
ALL_PLANES = EVERY[: 3 * LAYERS]


def blank_rims(ref):
    tall = ref.shape[2]
    for j in range(3):
        for z in range(LAYERS):
            ref[j, z, :PAD, :] = jnp.zeros((PAD, LANES), jnp.float32)
            ref[j, z, tall - PAD :, :] = jnp.zeros((PAD, LANES), jnp.float32)


class Inputs:
    def __init__(self, get):
        self.get = get


def first_kernel(
    e_ref, h_ref, m_ref, c_ref, e_out, h_out, token_ref, rim_ref, e_mid, h_mid
):
    cells_x = h_ref.shape[2]
    token_ref[...] = jnp.zeros_like(token_ref)
    row = lax.broadcasted_iota(jnp.int32, (8, LANES), 0)
    for j in range(7):
        for z in range(LAYERS):
            base = (j * LAYERS + z) * cells_x
            if j < 3:
                first, final = e_ref[base : base + 8, :], e_ref[base + cells_x - 8 : base + cells_x, :]
            else:
                ref = h_ref.at[j - 3, z] if j < 6 else m_ref.at[z]
                first, final = ref[:8, :], ref[cells_x - 8 :, :]
            if j == 6:
                first, final = coefficient_of(first), coefficient_of(final)
                c_ref[z] = coefficient_of(m_ref[z]) * 0.5
            rim_ref[j * LAYERS + z] = jnp.where(row < HALO, first, final)
    for ref in (e_out, h_out, e_mid, h_mid):
        blank_rims(ref)

    def get_e(j, z, start, size):
        if z >= LAYERS:
            return None
        base = (j * LAYERS + z) * cells_x + start - PAD
        if base + size <= e_ref.shape[0]:
            return e_ref[base : base + size, :]
        return pltpu.roll(e_ref[base - 1 : base - 1 + size, :], size - 1, 0)

    def get_h(j, z, start, size):
        return h_ref[j, z, start - PAD : start - PAD + size, :] * 2.0

    def factor(z, start, size):
        return c_ref[z, start - PAD : start - PAD + size, :]

    e, h = Inputs(get_e), Inputs(get_h)
    for new_e, new_h in ((e_mid, h_mid), (e_out, h_out)):
        to_e, to_h = Planes(new_e, ALL_PLANES), Planes(new_h, ALL_PLANES)
        step_h(e, h, to_h, PAD, cells_x, CHUNK)
        step_e(e, to_h, to_e.put, PAD, cells_x, factor, CHUNK)
        e, h = to_e, to_h


def first_steps(e_rows, h_field, material):
    cells_x = h_field.shape[2]
    f32 = jnp.float32
    planes = jax.ShapeDtypeStruct((3, LAYERS, cells_x + 2 * PAD, LANES), f32)
    return pl.pallas_call(
        first_kernel,
        out_shape=(
            jax.ShapeDtypeStruct((LAYERS, cells_x, LANES), f32),
            planes,
            planes,
            jax.ShapeDtypeStruct((8, LANES), f32),
            jax.ShapeDtypeStruct((7 * LAYERS, 2 * HALO, LANES), f32),
        ),
        scratch_shapes=[pltpu.VMEM(planes.shape, f32)] * 2,
        compiler_params=pltpu.CompilerParams(vmem_limit_bytes=VMEM_LIMIT),
        cost_estimate=lasting(2.7),
        name="first_steps",
    )(e_rows, h_field, material)


class Rows:
    def __init__(self, ref):
        self.ref = ref

    def load(self, j, by=0):
        return self.ref[j, :, 8 + by : 40 + by, :]

    def step(self, factor):
        zero = jnp.zeros((1, 32, LANES), jnp.float32)
        e = [self.load(j) for j in range(3)]
        e_z = [jnp.concatenate([e[j][1:], zero], 0) for j in range(2)] + [None]
        e_x = [None, self.load(1, 1), self.load(2, 1)]
        e_y = [pltpu.roll(e[0], LANES - 1, 2), None, pltpu.roll(e[2], LANES - 1, 2)]
        for j, change in enumerate(curl_of_e(e, e_z, e_x, e_y)):
            self.ref[3 + j, :, 8:40, :] = self.load(3 + j) + change
        h = [self.load(3 + j) for j in range(3)]
        h_z = [jnp.concatenate([zero, h[j][:-1]], 0) for j in range(2)] + [None]
        h_x = [None, self.load(4, -1), self.load(5, -1)]
        h_y = [pltpu.roll(h[0], 1, 2), None, pltpu.roll(h[2], 1, 2)]
        for j, change in enumerate(curl_of_h(h, h_z, h_x, h_y)):
            self.ref[j, :, 8:40, :] = e[j] + factor * change


def edge_rows(e_ref, h_ref, c_ref, x_ref, r_ref):
    cells_x = c_ref.shape[1]
    blank = jnp.zeros((LAYERS, PAD - HALO, LANES), jnp.float32)
    zero = jnp.zeros((LAYERS, 8, LANES), jnp.float32)
    for j in range(7):
        rims = x_ref[j * LAYERS : (j + 1) * LAYERS] * SCALES[j]
        if j < 3:
            bases = [(j * LAYERS + z) * cells_x for z in range(LAYERS)]
            first = jnp.stack([e_ref[b : b + 8, :] for b in bases])
            final = jnp.stack([e_ref[b + cells_x - 8 : b + cells_x, :] for b in bases])
        elif j < 6:
            first, final = h_ref[j - 3, :, :8, :] * 2.0, h_ref[j - 3, :, cells_x - 8 :, :] * 2.0
        else:
            first, final = c_ref[:, :8, :], c_ref[:, cells_x - 8 :, :]
        rows = [blank, rims[:, HALO:], first, final, rims[:, :HALO], blank]
        if j < 6:
            r_ref[j] = jnp.concatenate([zero] + rows + [zero], 1)
        else:
            factor = jnp.concatenate(rows, 1)
    edge = Rows(r_ref)
    for _ in range(STEPS):
        edge.step(factor)


def with_rows(value, r_ref, j, z):
    row = lax.broadcasted_iota(jnp.int32, (8, LANES), 0)
    top = jnp.where(row < HALO, r_ref[j, z, 16:24, :], value[:8])
    end = jnp.where(row >= HALO, r_ref[j, z, 24:32, :], value[-8:])
    return jnp.concatenate([top, value[8:-8], end], 0)


def later_kernel(e_in, h_in, c_ref, _, out_ref, token_ref, e_mid, h_mid, h_last):
    cells_x = c_ref.shape[1]
    token_ref[...] = jnp.zeros_like(token_ref)
    for ref in (e_mid, h_mid, h_last):
        blank_rims(ref)

    def finish(j, z, start, value):
        out_ref[j, z, start - PAD : start - PAD + value.shape[0], :] = value

    def factor(z, start, size):
        return c_ref[z, start - PAD : start - PAD + size, :]

    e, h = Planes(e_in, ALL_PLANES), Planes(h_in, ALL_PLANES)
    to_e, to_h = Planes(e_mid, ALL_PLANES), Planes(h_mid, ALL_PLANES)
    step_h(e, h, to_h, PAD, cells_x, CHUNK)
    step_e(e, to_h, to_e.put, PAD, cells_x, factor, CHUNK)
    last_h = Planes(h_last, ALL_PLANES)
    step_h(to_e, to_h, last_h, PAD, cells_x, CHUNK)
    step_e(to_e, last_h, finish, PAD, cells_x, factor, CHUNK)
    for j, z in ALL_PLANES:
        out_ref[3 + j, z] = h_last[j, z, PAD : PAD + cells_x, :]


def later_steps(e, h, coefficient, after):
    cells_x = coefficient.shape[1]
    f32 = jnp.float32
    return pl.pallas_call(
        later_kernel,
        out_shape=(
            jax.ShapeDtypeStruct((6, LAYERS, cells_x, LANES), f32),
            jax.ShapeDtypeStruct((8, LANES), f32),
        ),
        scratch_shapes=[pltpu.VMEM(e.shape, f32)] * 3,
        compiler_params=pltpu.CompilerParams(vmem_limit_bytes=VMEM_LIMIT),
        cost_estimate=lasting(2.7),
        name="later_steps",
    )(e, h, coefficient, after)


def strip_kernel(
    w_ref, low_ref, high_ref, free_ref, e_ref, h_ref, c_ref, x_ref, own_ref, got_ref, edge_ref,
    to_ref, _, factor_ref, out_ref, s_ref, edges_ref, r_ref,
):
    rows = w_ref.shape[2]
    first = BASE - PAD
    mine = [beside(w_ref[j, g]) for j in range(7) for g in range(2)]
    mine = dot32(jnp.concatenate(mine, 0), own_ref[...])
    got = [jnp.concatenate([beside(low_ref[a]), beside(high_ref[a])], 1) for a in range(2)]
    got = dot32(jnp.concatenate(got, 0), got_ref[...])
    factor = []
    for j in range(7):
        for g in range(2):
            i = 2 * j + g
            a, b = divmod(i, 8)
            value = mine[i * rows : (i + 1) * rows]
            value = value + got[a * rows : (a + 1) * rows, b * LANES : (b + 1) * LANES]
            if j < 6:
                s_ref[j, g, first : first + rows, :] = value
            else:
                factor.append(value)
    factor_ref[...] = dot32(jnp.concatenate([beside(f) for f in factor], 1), to_ref[...])
    strip = Strip(s_ref, rows)
    for step in range(STEPS):
        strip.step_h()
        new = strip.step_e(factor)
        for g in range(2):
            for j in range(3):
                strip.store(j, g, new[g][j])
    cells_x = out_ref.shape[2]
    edges_ref[...] = strip.all_edges(cells_x, edge_ref[...])
    edge_rows(e_ref, h_ref, c_ref, x_ref, r_ref)
    for j, z in EVERY:
        value = with_rows(free_ref[j, z], r_ref, j, z)
        value = with_edges(value, edges_ref, (2 * j + z % 2) * cells_x, z // 2, HALO)
        out_ref[j, z] = value if j < 3 else value * 0.5


def strip_run(own_edges, low, high, free, e_field, h_field, coefficient, x_rims, after):
    rows = own_edges.shape[2]
    f32 = jnp.float32
    return pl.pallas_call(
        strip_kernel,
        out_shape=(
            jax.ShapeDtypeStruct((rows, LANES), f32),
            jax.ShapeDtypeStruct(free.shape, f32),
        ),
        scratch_shapes=[
            pltpu.VMEM((6, 2, rows + 2 * (BASE - PAD), LANES), f32),
            pltpu.VMEM((12 * free.shape[2], LAYERS // 2 * LANES), f32),
            pltpu.VMEM((6, LAYERS, 48, LANES), f32),
        ],
        compiler_params=pltpu.CompilerParams(vmem_limit_bytes=VMEM_LIMIT),
        cost_estimate=lasting(4),
        name="strip_run",
    )(
        own_edges, low, high, free, e_field, h_field, coefficient, x_rims,
        *(jnp.asarray(m) for m in strip_matrices()),
        jnp.asarray(edge_matrix()), jnp.asarray(factor_matrix()), after,
    )


def response_kernel(
    c_ref, factor_ref, free_ref, mine_ref, other_ref, near_ref, outside_ref, edge_ref,
    e_out, h_out,
    e_refs, h_refs, s_ref, plane_ref, rim_ref, done_ref, edges_ref, sems,
):
    cells_x = e_out.shape[2]
    copies = []

    def send(j, z, source):
        to = e_out.at[j, z] if j < 3 else h_out.at[j - 3, z]
        copies.append(pltpu.make_async_copy(source, to, sems.at[j, z]))
        copies[-1].start()

    far = [(j, z) for j, z in EVERY if z >= ZINJ + STEPS - (0 if j < 2 else 1)]
    for j, z in far:
        send(j, z, free_ref.at[j, z])
    rows = cells_x + 2 * PAD
    half = rows // 2
    first = BASE - PAD
    own = lax.axis_index("src")
    lane = lane_of((half, LANES))
    for ref, which in ((mine_ref, own), (other_ref, 1 - own)):
        at = pl.ds(pl.multiple_of(which * half, 8), half)
        for part in range(2):
            plane_ref[part, at, :] = ref[part * half : (part + 1) * half, :]
        rim_ref[0, at, :] = jnp.where(lane < 16, unfolded(ref[2 * half :, :], half, 8, 0), 0.0)
    outer = dot32(beside(rim_ref[0]), outside_ref[...])
    planes = jnp.concatenate([beside(plane_ref[part]) for part in range(2)], 0)
    inner = dot32(planes, near_ref[...])
    for part in range(2):
        own_part = outer[:, part * LANES : (part + 1) * LANES]
        rim_ref[part] = inner[part * rows : (part + 1) * rows] + own_part

    def injection(ref, step, start, size):
        cosine = COURANT * math.cos(OMEGA * step)
        sine = COURANT * math.sin(OMEGA * step)
        re, im = ref[0, start : start + size, :], ref[1, start : start + size, :]
        return [cosine * re - sine * im, sine * re + cosine * im, None]

    e, h = Planes(e_refs.at[0]), Planes(h_refs.at[0])
    for j, value in enumerate(injection(plane_ref, 1, 0, rows)):
        e.put(j, ZINJ, first, value)
    strip = ResponseStrip(s_ref, rows)
    s_ref[...] = jnp.zeros_like(s_ref)
    for j, value in enumerate(injection(rim_ref, 1, 0, rows)[:2]):
        strip.store(j, value)
    for step in range(2, STEPS + 1):
        strip.step_h(step == 2)
        new = strip.step_e(factor_ref[...])
        for j, value in enumerate(injection(rim_ref, step, 0, rows)):
            strip.store(j, add(new[j], value))
    edges_ref[...] = strip.all_edges(cells_x, edge_ref[...])

    def factor(z, start, size):
        return c_ref[z, start : start + size, :]

    def finish(j, z, start, value):
        if (j, z) in far:
            return
        size, at = value.shape[0], start - BASE
        if j < 3 and z == ZINJ:
            value = add(value, injection(plane_ref, STEPS, start - first, size)[j])
        value = with_edges(value, edges_ref, j * cells_x + at, z, REACHED)
        value = (value if j < 3 else value * 0.5) + free_ref[j, z, at : at + size, :]
        done_ref[j, z, at : at + size, :] = value
        if at + size == cells_x:
            send(j, z, done_ref.at[j, z])

    for step in range(2, STEPS + 1):
        last = step == STEPS
        new_h = Planes(h_refs.at[step - 1])
        step_h(e, h, new_h, first, rows - (PAD if last else 0), RESPONSE_CHUNK)
        if last:
            for j, z in ALL_PLANES:
                for at, size in chunks(BASE, cells_x, RESPONSE_CHUNK):
                    value = new_h.get(j, z, at, size)
                    if value is not None:
                        finish(3 + j, z, at, value)
            step_e(e, new_h, finish, BASE, cells_x, factor, cells_x)
            break
        new_e = Planes(e_refs.at[step - 1])

        def put(j, z, start, value):
            if z == ZINJ:
                size = value.shape[0]
                value = add(value, injection(plane_ref, step, start - first, size)[j])
            new_e.put(j, z, start, value)

        step_e(e, new_h, put, first, rows, factor, RESPONSE_CHUNK)
        e, h = new_e, new_h
    for copy in copies:
        copy.wait()


def response(c_ext, factor, free, mine, other, cells_x):
    rows = cells_x + 2 * PAD
    tall = cells_x + 2 * BASE
    f32 = jnp.float32
    out = jax.ShapeDtypeStruct((3, LAYERS, cells_x, LANES), f32)
    vmem = pl.BlockSpec(memory_space=pltpu.VMEM)
    return pl.pallas_call(
        response_kernel,
        in_specs=[vmem] * 8,
        out_specs=(pl.BlockSpec(memory_space=pl.ANY),) * 2,
        out_shape=(out, out),
        scratch_shapes=[
            pltpu.VMEM((STEPS - 1, 3, LAYERS, tall, LANES), f32),
            pltpu.VMEM((STEPS, 3, LAYERS, tall, LANES), f32),
            pltpu.VMEM((6, tall, LANES), f32),
            pltpu.VMEM((2, rows, LANES), f32),
            pltpu.VMEM((2, rows, LANES), f32),
            pltpu.VMEM((6, LAYERS, cells_x, LANES), f32),
            pltpu.VMEM((6 * cells_x, min(LAYERS, ZINJ + STEPS) * LANES), f32),
            pltpu.SemaphoreType.DMA((6, LAYERS)),
        ],
        compiler_params=pltpu.CompilerParams(vmem_limit_bytes=RESPONSE_LIMIT),
        cost_estimate=lasting(6.5),
        name="response",
    )(
        c_ext, factor, free, mine, other,
        jnp.asarray(near_matrix()), jnp.asarray(outside_matrix()),
        jnp.asarray(response_edge_matrix()),
    )


def along(block, axis, distance):
    n = lax.axis_size(axis)
    return lax.ppermute(block, axis, [((i - distance) % n, i) for i in range(n)])


def flipped(block, axis, bits):
    return lax.ppermute(block, axis, [(i, i ^ bits) for i in range(lax.axis_size(axis))])


def to_groups(block, n_src, n_tx, flip, distance):
    route = []
    for s in range(n_src):
        for t in range(n_tx):
            route.append((s * n_tx + t, (s ^ flip) * n_tx + (t + distance) % n_tx))
    return lax.ppermute(block, ("src", "tx"), route)


def per_device(orders, offsets, material, e_field, h_field):
    cols_ky = orders.shape[3]
    layers, cells_x, cells_y = material.shape
    n_src, n_tx, n_ty = lax.axis_size("src"), lax.axis_size("tx"), lax.axis_size("ty")
    half = cells_x // 2 + PAD
    e_field = e_field.reshape(-1, cells_y)
    parts = x_stage(
        offsets.T, jnp.swapaxes(orders, 2, 3), n_tx, cells_x, (e_field, h_field, material)
    )
    received = [parts[0]]
    for distance in range(n_tx):
        for flip in range(n_src):
            if distance or flip:
                part = parts[2 * distance + flip]
                received.append(to_groups(part, n_src, n_tx, flip, distance))
    coefficient, e_half, h_half, begun, rims = first_steps(e_field, h_field, material)

    if n_tx == 2:
        x_rims = along(rims, "tx", 1)
    else:
        top, bottom = rims[:, :HALO], rims[:, HALO:]
        x_rims = jnp.concatenate([along(top, "tx", -1), along(bottom, "tx", 1)], 1)
    block = summed(received, begun)
    c_ext, own_edges, to_high, to_low = pack(e_field, h_field, coefficient, x_rims)
    low = along(to_high, "ty", 1)
    high = along(to_low, "ty", -1)
    free, run = later_steps(e_half, h_half, coefficient, block)

    blocks = {0: block}
    for bits in range(n_ty - 2, 0, -2):
        blocks[bits] = flipped(block, "ty", bits)
    for bits in range(0, n_ty, 2):
        blocks[bits + 1] = flipped(blocks[bits], "ty", 1)
    mine = y_stage([blocks[b] for b in range(n_ty)], cols_ky, cells_y, half, run)
    other = flipped(mine, "src", 1)
    factor, free = strip_run(
        own_edges, low, high, free, e_field, h_field, coefficient, x_rims, mine
    )
    return response(c_ext, factor, free, mine, other, cells_x)


def solution(mesh):
    in_specs = (
        P("src", None, "tx", "ty"),
        P("src", None),
        P(None, "tx", "ty"),
        P(None, None, "tx", "ty"),
        P(None, None, "tx", "ty"),
    )
    out_specs = (P(None, None, "tx", "ty"), P(None, None, "tx", "ty"))
    return jax.shard_map(
        per_device, mesh=mesh, in_specs=in_specs, out_specs=out_specs, check_vma=False
    )
```
